32 devices in a mesh: row: 8 (over z, x), space: 4 (over y, core).
Axes of the slice: x: 2, y: 2, z: 4, core: 2. Of those that a mesh axis runs over, the one named last changes fastest.
Arguments:
- features: bfloat16 [512, 128], P(('row', 'space')), may hold values from -6 to 6
- positions: float32 [3, 512], P(None, ('row', 'space')), may hold values from -0.5 to 38, as said below
- species: int32 [512], P(('row', 'space')), may hold values from 0 to 3
- ghost_list: int32 [8, 16, 32], P('row', 'space'), may hold values from 0 to 15
- edge_recv: int32 [16384], P(('row', 'space')), may hold values from 0 to 16, as said below
- edge_send: int32 [16384], P(('row', 'space')), may hold values from 0 to 143
- edge_vec: float32 [3, 16384], P(None, ('row', 'space')), may hold values from -5.8 to 5.8, as said below
- w_msg: bfloat16 [128, 256], replicated, may hold values from -0.5 to 0.5
- w_rad1: float32 [8, 128], replicated, may hold values from -2 to 2
- w_rad2: bfloat16 [128, 256], replicated, may hold values from -0.5 to 0.5
- w_up: bfloat16 [256, 128], replicated, may hold values from -0.375 to 0.375
- w_out: float32 [128], replicated, may hold values from -0.5 to 0.5
- hardness: float32 [4], replicated, may hold values from 2 to 4
- width: float32 [4], replicated, may hold values from 0.8 to 1.6
- chi_shift: float32 [4], replicated, may hold values from -1 to 1
- field: float32 [1], replicated, may hold values from 0.01 to 0.03
Outputs:
- new_features: bfloat16 [512, 128], P(('row', 'space'))
- charges: float32 [512], P(('row', 'space'))
- forces: float32 [3, 512], P(None, ('row', 'space'))
- virial: float32 [6, 512], P(None, ('row', 'space'))
The draws below stay inside these ranges and needn't reach their ends.
Inputs may be any that keep to these rules, and one draw needn't show every extreme that they name: `edge_recv`: in every domain the edges are ordered by receiver; the slots in use fill the first whole blocks of 128 rows, a quarter of the blocks or more, and the other slots hold 16; some domain uses all its slots. `positions`: every two atoms are 1.5 or more apart. `edge_vec`: each edge's length lies between 1.2 and 5.8.
All inputs are finite; a program needn't handle non-finite values.
Results may differ from the reference program's by a relative error of at most 0.0045.
Values may be sent and summed in bfloat16 or wider, within the bound.
No kernel may reach another device: no remote copies, remote signals or barrier semaphores. Data moves between devices by JAX's collectives and lax.ppermute only.
A program may use at most 64 MiB of HBM per device.

```python
import math
import jax
import jax.numpy as jnp
from jax import lax

ATOM_DEV = 16
CH = 128
CAP = 32
EBLK = 128
NRBF = 8
NSPEC = 4
ITERS = 2
ATOMS = 512
EDGE_DEV = 512
EDGES = 16384
N_ROW = 8
N_SPACE = 4


def draw_positions(key, part):
    index = jnp.arange(ATOMS, dtype=jnp.int32)
    domain = index // ATOM_DEV
    local = index % ATOM_DEV
    group = domain // N_SPACE
    lane = domain % N_SPACE
    layers = ATOM_DEV // 16
    first_cell = lane // 4 * 4 + local % 4
    second_cell = lane % 4 * 4 + local // 4 % 4
    third_cell = group * layers + local // 16
    lattice = jnp.stack([first_cell, second_cell, third_cell]).astype(jnp.float32) * 2.5
    jitter = jnp.clip(0.2 * jax.random.normal(key, (3, ATOMS), jnp.float32), -0.5, 0.5)
    return lattice + jitter


def draw_edge_vec(key, part):
    first_key, second_key = jax.random.split(key)
    heading = jax.random.normal(first_key, (3, EDGES), jnp.float32)
    heading = heading / jnp.sqrt(jnp.sum(heading * heading, axis=0) + 1e-06)
    length = jax.random.uniform(second_key, (EDGES,), jnp.float32, 1.2, 5.8)
    return heading * length[None, :]


def draw_edge_recv(key, part):
    domains = EDGES // EDGE_DEV
    blocks = EDGE_DEV // EBLK
    lowest = max(1, blocks // 4)
    first_key, second_key, third_key, fourth_key = jax.random.split(key, 4)
    one_draw = jax.random.randint(first_key, (domains,), lowest, blocks + 1)
    other_draw = jax.random.randint(second_key, (domains,), lowest, blocks + 1)
    live = jnp.minimum(one_draw, other_draw)
    order = jax.random.permutation(third_key, domains)
    live = live.at[order[0]].set(blocks).at[order[1]].set(lowest)
    live_rows = live * EBLK
    chosen = jax.random.randint(fourth_key, (domains, EDGE_DEV), 0, ATOM_DEV)
    slots = jnp.arange(EDGE_DEV, dtype=jnp.int32)[None, :]
    masked = jnp.where(slots < live_rows[:, None], chosen, ATOM_DEV)
    return jnp.sort(masked, axis=1).reshape(-1)


def set_ends(values, own_key, smallest, top_value):
    spot = [jax.random.randint(jax.random.fold_in(own_key, axis), (), 0, length) for axis, length in enumerate(values.shape)]
    widest = values.shape.index(max(values.shape))
    beside = spot[:widest] + [(spot[widest] + 1) % values.shape[widest]] + spot[widest + 1:]
    return values.at[tuple(spot)].set(smallest).at[tuple(beside)].set(top_value)


def block_levels(stream_key, shape, shards, least, high):
    gain, own = 1.0, jax.random.fold_in(stream_key, 6)
    for dim, shards_of in shards:
        heights = jnp.exp(jax.random.uniform(jax.random.fold_in(own, dim), (shards_of,), jnp.float32, least / len(shards), high / len(shards)))
        gain = gain * jnp.repeat(heights, shape[dim] // shards_of).reshape([-1 if axis == dim else 1 for axis in range(len(shape))])
    return gain


def scatter_about(rng, extent, scale, bound, cuts=(), held_as=jnp.bfloat16):
    gain = block_levels(rng, extent, cuts, -0.22, 0.18) if cuts else 1.0
    values = jax.random.normal(rng, extent, jnp.float32) * scale * gain
    return jnp.minimum(jnp.maximum(values, -bound), bound).astype(held_as)


def setup_inputs(seed: int = 0) -> dict:
    key_list = jax.random.split(jax.random.key(seed), 17)
    features = scatter_about(key_list[0], (ATOMS, CH), 1.0, 6.0, ((0, 32),))
    positions = draw_positions(jax.random.fold_in(key_list[16], 71), 0)
    species = set_ends(jax.random.randint(key_list[2], (ATOMS,), 0, NSPEC), jax.random.fold_in(key_list[2], 1), 0, NSPEC - 1).astype(jnp.int32)
    ghost_list = set_ends(jax.random.randint(key_list[3], (N_ROW, N_SPACE * N_SPACE, CAP), 0, ATOM_DEV), jax.random.fold_in(key_list[3], 1), 0, ATOM_DEV - 1).astype(jnp.int32)
    edge_recv = draw_edge_recv(jax.random.fold_in(key_list[16], 71), 0)
    edge_send = set_ends(jax.random.randint(key_list[5], (EDGES,), 0, ATOM_DEV + N_SPACE * CAP), jax.random.fold_in(key_list[5], 1), 0, (ATOM_DEV + N_SPACE * CAP) - 1).astype(jnp.int32)
    edge_vec = draw_edge_vec(jax.random.fold_in(key_list[16], 71), 0)
    w_msg = scatter_about(key_list[7], (CH, 2 * CH), CH ** -0.5, 0.5)
    w_rad1 = scatter_about(key_list[8], (NRBF, CH), NRBF ** -0.5, 2.0, (), jnp.float32)
    w_rad2 = scatter_about(key_list[9], (CH, 2 * CH), CH ** -0.5, 0.5)
    w_up = scatter_about(key_list[10], (2 * CH, CH), (2 * CH) ** -0.5, 0.375)
    w_out = scatter_about(key_list[11], (CH,), CH ** -0.5, 0.5, (), jnp.float32)
    hardness = jnp.clip(jax.random.uniform(key_list[12], (NSPEC,), jnp.float32, 2.0, 4.0), 2.0, 4.0)
    width = jnp.clip(jax.random.uniform(key_list[13], (NSPEC,), jnp.float32, 0.8, 1.6), 0.8, 1.6)
    chi_shift = jnp.clip(jax.random.uniform(key_list[14], (NSPEC,), jnp.float32, -1.0, 1.0), -1.0, 1.0)
    field = jnp.clip(jnp.exp(jax.random.uniform(key_list[15], (1,), jnp.float32, math.log(0.01), math.log(0.03))), 0.01, 0.03)
    return {"features": features, "positions": positions, "species": species, "ghost_list": ghost_list, "edge_recv": edge_recv, "edge_send": edge_send, "edge_vec": edge_vec, "w_msg": w_msg, "w_rad1": w_rad1, "w_rad2": w_rad2, "w_up": w_up, "w_out": w_out, "hardness": hardness, "width": width, "chi_shift": chi_shift, "field": field}


cutoff = 6.0
message_scale = 0.125
two_over_root_pi = 2.0 / math.sqrt(math.pi)
inverse_root_pi = 1.0 / math.sqrt(math.pi)

def lookup(species, table):
    result = jnp.zeros(species.shape, jnp.float32)
    for kind in range(table.shape[0]):
        result = result + jnp.where(species == kind, table[kind], 0.0)
    return result

def pair_block(target, target_labels, source, source_labels, source_charge, forces):
    delta = target[:3, :, None] - source[:3, None, :]
    squared = lax.optimization_barrier(jnp.sum(delta * delta, axis=0))
    same = target_labels[:, None] == source_labels[None, :]
    squared = jnp.where(same, 1.0, squared)
    inverse = lax.rsqrt(squared)
    radius = squared * inverse
    spread = target[3][:, None] * target[3][:, None] + source[3][None, :] * source[3][None, :]
    scale = lax.rsqrt(2.0 * spread)
    scaled = radius * scale
    smear = lax.erf(scaled)
    if forces:
        slope = two_over_root_pi * scale * jnp.exp(-scaled * scaled) * inverse - smear * inverse * inverse
        weight = jnp.where(same, 0.0, source_charge[None, :] * slope * inverse)
        first = lax.optimization_barrier(jnp.sum(weight[None] * delta, axis=2))
        pairs = ((0, 0), (1, 1), (2, 2), (0, 1), (0, 2), (1, 2))
        second = jnp.stack([lax.optimization_barrier(jnp.sum(weight * delta[left] * delta[right], axis=1)) for left, right in pairs])
        return jnp.concatenate([first, second], axis=0)
    kernel = jnp.where(same, 0.0, smear * inverse)
    return lax.optimization_barrier(jnp.sum(kernel * source_charge[None, :], axis=1))

def edge_messages(sender_rows, vectors, projected, w_rad1, w_rad2):
    length = jnp.sqrt(lax.optimization_barrier(jnp.sum(vectors * vectors, axis=0)))
    unit = vectors / length
    order = jnp.arange(1, w_rad1.shape[0] + 1, dtype=jnp.int32).astype(jnp.float32)[:, None]
    ratio = length / cutoff
    envelope = (1.0 - ratio * ratio) * (1.0 - ratio * ratio)
    basis = jnp.sin(order * math.pi * ratio) / ratio * envelope
    radial = jax.nn.silu(jnp.dot(basis.T, w_rad1, precision=lax.Precision.HIGHEST)).astype(jnp.bfloat16)
    filters = jnp.dot(radial, w_rad2, preferred_element_type=jnp.float32)
    picked = jnp.take(projected, sender_rows, axis=0).astype(jnp.float32) * filters
    chans = w_rad1.shape[1]
    scalar = picked[:, :chans]
    carried = picked[:, chans:]
    joined = [scalar, unit[0][:, None] * carried, unit[1][:, None] * carried, unit[2][:, None] * carried]
    return jnp.concatenate(joined, axis=1).astype(jnp.bfloat16)

def reference(features, positions, species, ghost_list, edge_recv, edge_send, edge_vec, w_msg, w_rad1, w_rad2, w_up, w_out, hardness, width, chi_shift, field):
    domains = N_ROW * N_SPACE
    grouped = features.reshape(N_ROW, N_SPACE, ATOM_DEV, CH)
    lists = ghost_list.reshape(N_ROW, N_SPACE, N_SPACE, CAP)

    def pick_rows(rows, chosen):
        return jnp.take(rows, chosen.reshape(-1), axis=0).reshape(N_SPACE, CAP, CH)
    picked = jax.vmap(jax.vmap(pick_rows))(grouped, lists)
    ghosts = picked.transpose(0, 2, 1, 3, 4).reshape(domains, N_SPACE * CAP, CH)
    owned = features.reshape(domains, ATOM_DEV, CH)
    receive = edge_recv.reshape(domains, EDGE_DEV)
    senders = edge_send.reshape(domains, EDGE_DEV)
    vectors = edge_vec.reshape(3, domains, EDGE_DEV).transpose(1, 0, 2)

    def one_domain(item):
        own_rows, ghost_rows, targets, sources, displace = item
        table = jnp.concatenate([own_rows, ghost_rows], axis=0)
        projected = jnp.dot(table, w_msg, preferred_element_type=jnp.float32).astype(jnp.bfloat16)
        message = edge_messages(sources, displace, projected, w_rad1, w_rad2)
        totals = jax.ops.segment_sum(message.astype(jnp.float32), targets, num_segments=ATOM_DEV + 1)
        return totals[:ATOM_DEV]
    summed = lax.map(one_domain, (owned, ghosts, receive, senders, vectors)).reshape(ATOMS, 4 * CH)
    summed = summed * message_scale
    vector_part = summed[:, CH:].reshape(ATOMS, 3, CH)
    invariant = jnp.concatenate([summed[:, :CH], lax.optimization_barrier(jnp.sum(vector_part * vector_part, axis=1))], axis=1).astype(jnp.bfloat16)
    hidden = jax.nn.silu(jnp.dot(invariant, w_up, preferred_element_type=jnp.float32))
    new_features = (features.astype(jnp.float32) + hidden).astype(jnp.bfloat16)
    chi = jnp.dot(hidden, w_out, precision=lax.Precision.HIGHEST) + lookup(species, chi_shift)
    sigma = lookup(species, width)
    diag = lookup(species, hardness) + inverse_root_pi / sigma
    placed = jnp.concatenate([positions, sigma[None, :]], axis=0)
    labels = jnp.arange(ATOMS, dtype=jnp.int32)
    block = min(ATOMS, 256)
    target_blocks = placed.reshape(4, ATOMS // block, block).transpose(1, 0, 2)
    label_blocks = labels.reshape(ATOMS // block, block)

    def couple(vector, forces):

        def one_block(item):
            return pair_block(item[0], item[1], placed, labels, vector, forces)
        result = lax.map(one_block, (target_blocks, label_blocks))
        if forces:
            return result.transpose(1, 0, 2).reshape(9, ATOMS)
        return result.reshape(ATOMS)
    rhs = field[0] * positions[2] - chi
    charges = jnp.zeros_like(rhs)
    residual = rhs
    direction = rhs
    norm_now = jnp.sum(residual * residual)
    for step in range(ITERS):
        image = diag * direction + couple(direction, False)
        alpha = norm_now / jnp.sum(direction * image)
        charges = charges + alpha * direction
        residual = residual - alpha * image
        fresh = jnp.sum(residual * residual)
        direction = residual + fresh / norm_now * direction
        norm_now = fresh
    sums = couple(charges, True)
    pull = -charges[None, :] * sums[:3]
    forces = jnp.concatenate([pull[:2], pull[2:] + (charges * field[0])[None, :]], axis=0)
    virial = 0.5 * charges[None, :] * sums[3:]
    return (new_features, charges, forces, virial)
```

```python
import math

import jax
import jax.numpy as jnp
from jax import lax
from jax.sharding import PartitionSpec as P

ITERS = 2


cutoff = 6.0
message_scale = 0.125
two_over_root_pi = 2.0 / math.sqrt(math.pi)
inverse_root_pi = 1.0 / math.sqrt(math.pi)
replicate_limit = 1024
everywhere = ("row", "space")


def lookup(species, table):
    result = jnp.zeros(species.shape, jnp.float32)
    for kind in range(table.shape[0]):
        result = result + jnp.where(species == kind, table[kind], 0.0)
    return result


def pair_terms(target, target_labels, source, source_labels):
    delta = target[:3, :, None] - source[:3, None, :]
    squared = jnp.sum(delta * delta, axis=0)
    same = target_labels[:, None] == source_labels[None, :]
    squared = jnp.where(same, 1.0, squared)
    inverse = lax.rsqrt(squared)
    radius = squared * inverse
    spread = target[3][:, None] * target[3][:, None] + source[3][None, :] * source[3][None, :]
    scale = lax.rsqrt(2.0 * spread)
    scaled = radius * scale
    smear = lax.erf(scaled)
    return delta, same, inverse, scale, scaled, smear


def coulomb(target, target_labels, source, source_labels):
    _, same, inverse, _, _, smear = pair_terms(target, target_labels, source, source_labels)
    return jnp.where(same, 0.0, smear * inverse)


def pair_forces(target, target_labels, source, source_labels, source_charge):
    delta, same, inverse, scale, scaled, smear = pair_terms(
        target, target_labels, source, source_labels
    )
    slope = (
        two_over_root_pi * scale * jnp.exp(-scaled * scaled) * inverse - smear * inverse * inverse
    )
    weight = jnp.where(same, 0.0, source_charge[None, :] * slope * inverse)
    first = jnp.sum(weight[None] * delta, axis=2)
    pairs = ((0, 0), (1, 1), (2, 2), (0, 1), (0, 2), (1, 2))
    second = jnp.stack(
        [jnp.sum(weight * delta[left] * delta[right], axis=1) for left, right in pairs]
    )
    return jnp.concatenate([first, second], axis=0)


def edge_terms(receive, sender_rows, vectors, projected, w_rad1, w_rad2, atoms):
    length = jnp.sqrt(jnp.sum(vectors * vectors, axis=0))
    unit = vectors / length
    order = jnp.arange(1, w_rad1.shape[0] + 1, dtype=jnp.int32).astype(jnp.float32)[:, None]
    ratio = length / cutoff
    envelope = (1.0 - ratio * ratio) * (1.0 - ratio * ratio)
    basis = jnp.sin(order * math.pi * ratio) / ratio * envelope
    mixed = lax.dot_general(
        basis, w_rad1, (((0,), (0,)), ((), ())), precision=lax.Precision.HIGHEST
    )
    radial = jax.nn.silu(mixed).astype(jnp.bfloat16)
    filters = jnp.dot(radial, w_rad2, preferred_element_type=jnp.float32)
    picked = jnp.take(projected, sender_rows, axis=0).astype(jnp.float32) * filters
    chans = w_rad1.shape[1]
    scalar = picked[:, :chans]
    carried = picked[:, chans:]
    joined = [
        scalar,
        unit[0][:, None] * carried,
        unit[1][:, None] * carried,
        unit[2][:, None] * carried,
    ]
    message = jnp.concatenate(joined, axis=1).astype(jnp.bfloat16)
    onehot = (jnp.arange(atoms, dtype=jnp.int32)[:, None] == receive[None, :]).astype(jnp.bfloat16)
    return jnp.dot(onehot, message, preferred_element_type=jnp.float32)


def gathered(block, devices):
    copies = jnp.broadcast_to(block[None], (devices,) + block.shape)
    return lax.all_to_all(copies, everywhere, split_axis=0, concat_axis=0, tiled=True)


def shards(
    features,
    positions,
    species,
    ghost_list,
    edge_recv,
    edge_send,
    edge_vec,
    w_msg,
    w_rad1,
    w_rad2,
    w_up,
    w_out,
    hardness,
    width,
    chi_shift,
    field,
):
    atoms = features.shape[0]
    chans = features.shape[1]
    lanes = lax.axis_size("space")
    devices = lanes * lax.axis_size("row")
    everybody = devices * atoms
    me = lax.axis_index("row") * lanes + lax.axis_index("space")
    sigma = lookup(species, width)
    diag = lookup(species, hardness) + inverse_root_pi / sigma
    placed = jnp.concatenate([positions, sigma[None, :], diag[None, :]], axis=0)
    everyone = gathered(placed, devices).transpose(1, 0, 2).reshape(5, everybody)
    lists = ghost_list[0]
    outgoing = jnp.take(features, lists.reshape(-1), axis=0).reshape(lanes, lists.shape[1], chans)
    ghost_rows = jnp.einsum(
        "dkc,cf->dkf",
        lax.all_to_all(outgoing, "space", split_axis=0, concat_axis=0, tiled=True),
        w_msg,
        preferred_element_type=jnp.float32,
    ).astype(jnp.bfloat16)
    own_rows = jnp.dot(features, w_msg, preferred_element_type=jnp.float32).astype(jnp.bfloat16)
    projected = jnp.concatenate([own_rows, ghost_rows.reshape(-1, 2 * chans)], axis=0)
    summed = edge_terms(edge_recv, edge_send, edge_vec, projected, w_rad1, w_rad2, atoms)
    summed = summed * message_scale
    vector_part = summed[:, chans:].reshape(atoms, 3, chans)
    invariant = jnp.concatenate(
        [summed[:, :chans], jnp.sum(vector_part * vector_part, axis=1)], axis=1
    ).astype(jnp.bfloat16)
    hidden = jax.nn.silu(jnp.dot(invariant, w_up, preferred_element_type=jnp.float32))
    new_features = (features.astype(jnp.float32) + hidden).astype(jnp.bfloat16)
    chi = jnp.dot(hidden, w_out, precision=lax.Precision.HIGHEST) + lookup(species, chi_shift)
    own_labels = me * atoms + jnp.arange(atoms, dtype=jnp.int32)
    all_labels = jnp.arange(everybody, dtype=jnp.int32)
    rhs = field[0] * positions[2] - chi

    if everybody <= replicate_limit:
        kernel = coulomb(everyone, all_labels, everyone, all_labels)
        residual = gathered(rhs, devices).reshape(everybody)
        all_charges = conjugate(
            residual, lambda v: everyone[4] * v + jnp.sum(kernel * v[None, :], axis=1), jnp.sum
        )
        charges = lax.dynamic_slice(all_charges, (me * atoms,), (atoms,))
    else:
        kernel = coulomb(placed, own_labels, everyone, all_labels)

        def spread(vector):
            return gathered(vector, devices).reshape(everybody)

        charges = conjugate(
            rhs,
            lambda v: diag * v + jnp.sum(kernel * spread(v)[None, :], axis=1),
            lambda v: lax.psum(jnp.sum(v), everywhere),
        )
        all_charges = spread(charges)
    sums = pair_forces(placed, own_labels, everyone, all_labels, all_charges)
    pull = -charges[None, :] * sums[:3]
    forces = jnp.concatenate([pull[:2], pull[2:] + (charges * field[0])[None, :]], axis=0)
    virial = 0.5 * charges[None, :] * sums[3:]
    return (new_features, charges, forces, virial)


def conjugate(rhs, apply, total):
    charges = jnp.zeros_like(rhs)
    residual = rhs
    direction = rhs
    norm_now = total(residual * residual)
    for step in range(ITERS):
        image = apply(direction)
        alpha = norm_now / total(direction * image)
        charges = charges + alpha * direction
        if step + 1 < ITERS:
            residual = residual - alpha * image
            fresh = total(residual * residual)
            direction = residual + fresh / norm_now * direction
            norm_now = fresh
    return charges


def solution(mesh):
    return jax.shard_map(
        shards,
        mesh=mesh,
        in_specs=(
            P(("row", "space"), None),
            P(None, ("row", "space")),
            P(("row", "space")),
            P("row", "space", None),
            P(("row", "space")),
            P(("row", "space")),
            P(None, ("row", "space")),
            P(),
            P(),
            P(),
            P(),
            P(),
            P(),
            P(),
            P(),
            P(),
        ),
        out_specs=(
            P(("row", "space"), None),
            P(("row", "space")),
            P(None, ("row", "space")),
            P(None, ("row", "space")),
        ),
        check_vma=False,
    )
```

```python
import math

import jax
import jax.numpy as jnp
from jax import lax
from jax.sharding import PartitionSpec as P

ITERS = 2


cutoff = 6.0
message_scale = 0.125
two_over_root_pi = 2.0 / math.sqrt(math.pi)
inverse_root_pi = 1.0 / math.sqrt(math.pi)
replicate_limit = 1024
everywhere = ("row", "space")


def lookup(species, table):
    result = jnp.zeros(species.shape, jnp.float32)
    for kind in range(table.shape[0]):
        result = result + jnp.where(species == kind, table[kind], 0.0)
    return result


def pair_terms(target, target_labels, source, source_labels):
    delta = target[:3, :, None] - source[:3, None, :]
    squared = jnp.sum(delta * delta, axis=0)
    same = target_labels[:, None] == source_labels[None, :]
    squared = jnp.where(same, 1.0, squared)
    inverse = lax.rsqrt(squared)
    radius = squared * inverse
    spread = target[3][:, None] * target[3][:, None] + source[3][None, :] * source[3][None, :]
    scale = lax.rsqrt(2.0 * spread)
    scaled = radius * scale
    smear = lax.erf(scaled)
    return delta, same, inverse, scale, scaled, smear


def coulomb(target, target_labels, source, source_labels):
    _, same, inverse, _, _, smear = pair_terms(target, target_labels, source, source_labels)
    return jnp.where(same, 0.0, smear * inverse)


def pair_forces(target, target_labels, source, source_labels, source_charge):
    delta, same, inverse, scale, scaled, smear = pair_terms(
        target, target_labels, source, source_labels
    )
    slope = (
        two_over_root_pi * scale * jnp.exp(-scaled * scaled) * inverse - smear * inverse * inverse
    )
    weight = jnp.where(same, 0.0, source_charge[None, :] * slope * inverse)
    first = jnp.sum(weight[None] * delta, axis=2)
    pairs = ((0, 0), (1, 1), (2, 2), (0, 1), (0, 2), (1, 2))
    second = jnp.stack(
        [jnp.sum(weight * delta[left] * delta[right], axis=1) for left, right in pairs]
    )
    return jnp.concatenate([first, second], axis=0)


def edge_terms(receive, sender_rows, vectors, projected, w_rad1, w_rad2, atoms):
    length = jnp.sqrt(jnp.sum(vectors * vectors, axis=0))
    unit = vectors / length
    order = jnp.arange(1, w_rad1.shape[0] + 1, dtype=jnp.int32).astype(jnp.float32)[:, None]
    ratio = length / cutoff
    envelope = (1.0 - ratio * ratio) * (1.0 - ratio * ratio)
    basis = jnp.sin(order * math.pi * ratio) / ratio * envelope
    mixed = lax.dot_general(
        basis, w_rad1, (((0,), (0,)), ((), ())), precision=lax.Precision.HIGHEST
    )
    radial = jax.nn.silu(mixed).astype(jnp.bfloat16)
    filters = jnp.dot(radial, w_rad2, preferred_element_type=jnp.float32)
    picked = jnp.take(projected, sender_rows, axis=0).astype(jnp.float32) * filters
    chans = w_rad1.shape[1]
    scalar = picked[:, :chans]
    carried = picked[:, chans:]
    joined = [
        scalar,
        unit[0][:, None] * carried,
        unit[1][:, None] * carried,
        unit[2][:, None] * carried,
    ]
    message = jnp.concatenate(joined, axis=1).astype(jnp.bfloat16)
    onehot = (jnp.arange(atoms, dtype=jnp.int32)[:, None] == receive[None, :]).astype(jnp.bfloat16)
    return jnp.dot(onehot, message, preferred_element_type=jnp.float32)


def exchanged(block, axis, step):
    size = lax.axis_size(axis)
    return lax.ppermute(block, axis, [(place, place ^ step) for place in range(size)])


def gathered(block, axes):
    held = block[None]
    for axis in axes:
        size = lax.axis_size(axis)
        if size & (size - 1):
            raise ValueError("size")
        held = jnp.concatenate([held] + [exchanged(held, axis, step) for step in range(1, size)])
    return held


def shards(
    features,
    positions,
    species,
    ghost_list,
    edge_recv,
    edge_send,
    edge_vec,
    w_msg,
    w_rad1,
    w_rad2,
    w_up,
    w_out,
    hardness,
    width,
    chi_shift,
    field,
):
    atoms = features.shape[0]
    chans = features.shape[1]
    lanes = lax.axis_size("space")
    devices = lanes * lax.axis_size("row")
    everybody = devices * atoms
    direct = (everywhere,) if devices <= 32 else ("space", "row")
    sigma = lookup(species, width)
    diag = lookup(species, hardness) + inverse_root_pi / sigma
    placed = jnp.concatenate([positions, sigma[None, :], diag[None, :]], axis=0)
    everyone = gathered(placed, direct).transpose(1, 0, 2).reshape(5, everybody)
    lists = ghost_list[0]
    outgoing = jnp.take(features, lists.reshape(-1), axis=0).reshape(lanes, lists.shape[1], chans)
    if lanes <= 4:
        space = lax.axis_index("space")
        parts = [lax.dynamic_index_in_dim(outgoing, space, 0, False)]
        for step in range(1, lanes):
            part = lax.dynamic_index_in_dim(outgoing, space ^ step, 0, False)
            parts.append(exchanged(part, "space", step))
        incoming = jnp.stack(parts)
    else:
        incoming = lax.all_to_all(outgoing, "space", split_axis=0, concat_axis=0, tiled=True)
    ghost_rows = jnp.einsum(
        "dkc,cf->dkf",
        incoming,
        w_msg,
        preferred_element_type=jnp.float32,
    ).astype(jnp.bfloat16)
    own_rows = jnp.dot(features, w_msg, preferred_element_type=jnp.float32).astype(jnp.bfloat16)
    projected = jnp.concatenate([own_rows, ghost_rows.reshape(-1, 2 * chans)], axis=0)
    if lanes <= 4:
        slots = edge_send - atoms
        width_of = lists.shape[1]
        moved = (slots // width_of ^ space) * width_of + slots % width_of + atoms
        edge_send = jnp.where(edge_send < atoms, edge_send, moved)
    summed = edge_terms(edge_recv, edge_send, edge_vec, projected, w_rad1, w_rad2, atoms)
    summed = summed * message_scale
    vector_part = summed[:, chans:].reshape(atoms, 3, chans)
    invariant = jnp.concatenate(
        [summed[:, :chans], jnp.sum(vector_part * vector_part, axis=1)], axis=1
    ).astype(jnp.bfloat16)
    hidden = jax.nn.silu(jnp.dot(invariant, w_up, preferred_element_type=jnp.float32))
    new_features = (features.astype(jnp.float32) + hidden).astype(jnp.bfloat16)
    chi = jnp.dot(hidden, w_out, precision=lax.Precision.HIGHEST) + lookup(species, chi_shift)
    own_labels = jnp.arange(atoms, dtype=jnp.int32)
    all_labels = jnp.arange(everybody, dtype=jnp.int32)
    rhs = field[0] * positions[2] - chi

    if everybody <= replicate_limit:
        kernel = coulomb(everyone, all_labels, everyone, all_labels)
        residual = gathered(rhs, ("space", "row")).reshape(everybody)
        all_charges = conjugate(
            residual, lambda v: everyone[4] * v + jnp.sum(kernel * v[None, :], axis=1), jnp.sum
        )
        charges = all_charges[:atoms]
    else:
        kernel = coulomb(placed, own_labels, everyone, all_labels)

        def spread(vector):
            return gathered(vector, ("space", "row")).reshape(everybody)

        charges = conjugate(
            rhs,
            lambda v: diag * v + jnp.sum(kernel * spread(v)[None, :], axis=1),
            lambda v: lax.psum(jnp.sum(v), everywhere),
        )
        all_charges = spread(charges)
    sums = pair_forces(placed, own_labels, everyone, all_labels, all_charges)
    pull = -charges[None, :] * sums[:3]
    forces = jnp.concatenate([pull[:2], pull[2:] + (charges * field[0])[None, :]], axis=0)
    virial = 0.5 * charges[None, :] * sums[3:]
    return (new_features, charges, forces, virial)


def conjugate(rhs, apply, total):
    charges = jnp.zeros_like(rhs)
    residual = rhs
    direction = rhs
    norm_now = total(residual * residual)
    for step in range(ITERS):
        image = apply(direction)
        alpha = norm_now / total(direction * image)
        charges = charges + alpha * direction
        if step + 1 < ITERS:
            residual = residual - alpha * image
            fresh = total(residual * residual)
            direction = residual + fresh / norm_now * direction
            norm_now = fresh
    return charges


def solution(mesh):
    return jax.shard_map(
        shards,
        mesh=mesh,
        in_specs=(
            P(("row", "space"), None),
            P(None, ("row", "space")),
            P(("row", "space")),
            P("row", "space", None),
            P(("row", "space")),
            P(("row", "space")),
            P(None, ("row", "space")),
            P(),
            P(),
            P(),
            P(),
            P(),
            P(),
            P(),
            P(),
            P(),
        ),
        out_specs=(
            P(("row", "space"), None),
            P(("row", "space")),
            P(None, ("row", "space")),
            P(None, ("row", "space")),
        ),
        check_vma=False,
    )
```

```python
import math

import jax
import jax.numpy as jnp
from jax import lax
from jax.experimental import pallas as pl
from jax.experimental.pallas import tpu as pltpu
from jax.sharding import PartitionSpec as P

ITERS = 2


cutoff = 6.0
message_scale = 0.125
two_over_root_pi = 2.0 / math.sqrt(math.pi)
inverse_root_pi = 1.0 / math.sqrt(math.pi)
replicate_limit = 1024
everywhere = ("row", "space")


def lookup(species, table):
    result = jnp.zeros(species.shape, jnp.float32)
    for kind in range(table.shape[0]):
        result = result + jnp.where(species == kind, table[kind], 0.0)
    return result


def pair_terms(target, target_labels, source, source_labels):
    delta = target[:3, :, None] - source[:3, None, :]
    squared = jnp.sum(delta * delta, axis=0)
    same = target_labels[:, None] == source_labels[None, :]
    squared = jnp.where(same, 1.0, squared)
    inverse = lax.rsqrt(squared)
    radius = squared * inverse
    spread = target[3][:, None] * target[3][:, None] + source[3][None, :] * source[3][None, :]
    scale = lax.rsqrt(2.0 * spread)
    scaled = radius * scale
    smear = lax.erf(scaled)
    return delta, same, inverse, scale, scaled, smear


def coulomb(target, target_labels, source, source_labels):
    _, same, inverse, _, _, smear = pair_terms(target, target_labels, source, source_labels)
    return jnp.where(same, 0.0, smear * inverse)


def pair_forces(target, target_labels, source, source_labels, source_charge):
    delta, same, inverse, scale, scaled, smear = pair_terms(
        target, target_labels, source, source_labels
    )
    slope = (
        two_over_root_pi * scale * jnp.exp(-scaled * scaled) * inverse - smear * inverse * inverse
    )
    weight = jnp.where(same, 0.0, source_charge[None, :] * slope * inverse)
    first = jnp.sum(weight[None] * delta, axis=2)
    pairs = ((0, 0), (1, 1), (2, 2), (0, 1), (0, 2), (1, 2))
    second = jnp.stack(
        [jnp.sum(weight * delta[left] * delta[right], axis=1) for left, right in pairs]
    )
    return jnp.concatenate([first, second], axis=0)


def edge_terms(receive, sender_rows, vectors, projected, w_rad1, w_rad2, atoms):
    length = jnp.sqrt(jnp.sum(vectors * vectors, axis=0))
    unit = vectors / length
    order = jnp.arange(1, w_rad1.shape[0] + 1, dtype=jnp.int32).astype(jnp.float32)[:, None]
    ratio = length / cutoff
    envelope = (1.0 - ratio * ratio) * (1.0 - ratio * ratio)
    basis = jnp.sin(order * math.pi * ratio) / ratio * envelope
    mixed = lax.dot_general(
        basis, w_rad1, (((0,), (0,)), ((), ())), precision=lax.Precision.HIGHEST
    )
    radial = jax.nn.silu(mixed).astype(jnp.bfloat16)
    filters = jnp.dot(radial, w_rad2, preferred_element_type=jnp.float32)
    picked = jnp.take(projected, sender_rows, axis=0).astype(jnp.float32) * filters
    chans = w_rad1.shape[1]
    scalar = picked[:, :chans]
    carried = picked[:, chans:]
    joined = [
        scalar,
        unit[0][:, None] * carried,
        unit[1][:, None] * carried,
        unit[2][:, None] * carried,
    ]
    message = jnp.concatenate(joined, axis=1).astype(jnp.bfloat16)
    onehot = (jnp.arange(atoms, dtype=jnp.int32)[:, None] == receive[None, :]).astype(jnp.bfloat16)
    return jnp.dot(onehot, message, preferred_element_type=jnp.float32)


def gathered(block, devices):
    copies = jnp.broadcast_to(block[None], (devices,) + block.shape)
    return lax.all_to_all(copies, everywhere, split_axis=0, concat_axis=0, tiled=True)


def shards(
    features,
    positions,
    species,
    ghost_list,
    edge_recv,
    edge_send,
    edge_vec,
    w_msg,
    w_rad1,
    w_rad2,
    w_up,
    w_out,
    hardness,
    width,
    chi_shift,
    field,
):
    atoms = features.shape[0]
    chans = features.shape[1]
    lanes = lax.axis_size("space")
    devices = lanes * lax.axis_size("row")
    everybody = devices * atoms
    me = lax.axis_index("row") * lanes + lax.axis_index("space")
    sigma = lookup(species, width)
    diag = lookup(species, hardness) + inverse_root_pi / sigma
    placed = jnp.concatenate([positions, sigma[None, :], diag[None, :]], axis=0)
    everyone = gathered(placed, devices).transpose(1, 0, 2).reshape(5, everybody)
    lists = ghost_list[0]
    outgoing = jnp.take(features, lists.reshape(-1), axis=0).reshape(lanes, lists.shape[1], chans)
    ghost_rows = jnp.einsum(
        "dkc,cf->dkf",
        lax.all_to_all(outgoing, "space", split_axis=0, concat_axis=0, tiled=True),
        w_msg,
        preferred_element_type=jnp.float32,
    ).astype(jnp.bfloat16)
    own_rows = jnp.dot(features, w_msg, preferred_element_type=jnp.float32).astype(jnp.bfloat16)
    projected = jnp.concatenate([own_rows, ghost_rows.reshape(-1, 2 * chans)], axis=0)
    summed = edge_terms(edge_recv, edge_send, edge_vec, projected, w_rad1, w_rad2, atoms)
    summed = summed * message_scale
    vector_part = summed[:, chans:].reshape(atoms, 3, chans)
    invariant = jnp.concatenate(
        [summed[:, :chans], jnp.sum(vector_part * vector_part, axis=1)], axis=1
    ).astype(jnp.bfloat16)
    hidden = jax.nn.silu(jnp.dot(invariant, w_up, preferred_element_type=jnp.float32))
    new_features = (features.astype(jnp.float32) + hidden).astype(jnp.bfloat16)
    chi = jnp.dot(hidden, w_out, precision=lax.Precision.HIGHEST) + lookup(species, chi_shift)
    own_labels = me * atoms + jnp.arange(atoms, dtype=jnp.int32)
    all_labels = jnp.arange(everybody, dtype=jnp.int32)
    rhs = field[0] * positions[2] - chi

    if everybody <= replicate_limit:
        kernel = coulomb(everyone, all_labels, everyone, all_labels)
        residual = gathered(rhs, devices).reshape(everybody)
        all_charges = conjugate(
            residual, lambda v: everyone[4] * v + jnp.sum(kernel * v[None, :], axis=1), jnp.sum
        )
        charges = lax.dynamic_slice(all_charges, (me * atoms,), (atoms,))
    else:
        kernel = coulomb(placed, own_labels, everyone, all_labels)

        def spread(vector):
            return gathered(vector, devices).reshape(everybody)

        charges = conjugate(
            rhs,
            lambda v: diag * v + jnp.sum(kernel * spread(v)[None, :], axis=1),
            lambda v: lax.psum(jnp.sum(v), everywhere),
        )
        all_charges = spread(charges)
    sums = pair_forces(placed, own_labels, everyone, all_labels, all_charges)
    pull = -charges[None, :] * sums[:3]
    forces = jnp.concatenate([pull[:2], pull[2:] + (charges * field[0])[None, :]], axis=0)
    virial = 0.5 * charges[None, :] * sums[3:]
    return (new_features, charges, forces, virial)


def conjugate(rhs, apply, total):
    charges = jnp.zeros_like(rhs)
    residual = rhs
    direction = rhs
    norm_now = total(residual * residual)
    for step in range(ITERS):
        image = apply(direction)
        alpha = norm_now / total(direction * image)
        charges = charges + alpha * direction
        if step + 1 < ITERS:
            residual = residual - alpha * image
            fresh = total(residual * residual)
            direction = residual + fresh / norm_now * direction
            norm_now = fresh
    return charges


def split3(value):
    first = value.astype(jnp.bfloat16).astype(jnp.float32)
    rest = value - first
    second = rest.astype(jnp.bfloat16).astype(jnp.float32)
    third = (rest - second).astype(jnp.bfloat16).astype(jnp.float32)
    return first, second, third


def over_first(left, right):
    return lax.dot_general(
        left, right, (((0,), (0,)), ((), ())), preferred_element_type=jnp.float32
    )


def over_last(left, right, precision=None):
    return lax.dot_general(
        left,
        right,
        (((1,), (1,)), ((), ())),
        precision=precision,
        preferred_element_type=jnp.float32,
    )


def silu(value):
    return value / (1.0 + jnp.exp(-value))


sine_series = [(-1.0) ** k * math.pi ** (2 * k + 1) / math.factorial(2 * k + 1) for k in range(7)]


def edge_kernel(vec_ref, recv_ref, first_ref, second_ref, filter_ref, combine_ref):
    atoms = combine_ref.shape[0] // 7
    edges = vec_ref.shape[1]
    orders = first_ref.shape[0]
    vec = vec_ref[...]
    east, north, up = vec[0:1], vec[1:2], vec[2:3]
    squared = east * east + north * north + up * up
    inverse = lax.rsqrt(squared)
    ratio = squared * inverse * (1.0 / cutoff)
    envelope = (1.0 - ratio * ratio) * (1.0 - ratio * ratio) * (cutoff * inverse)
    order = lax.broadcasted_iota(jnp.int32, (orders, edges), 0).astype(jnp.float32) + 1.0
    turns = order * ratio
    whole = jnp.floor(turns + 0.5)
    part = turns - whole
    sign = 1.0 - 2.0 * (whole - 2.0 * jnp.floor(whole * 0.5))
    series = jnp.full_like(part, sine_series[-1])
    for coefficient in sine_series[-2::-1]:
        series = series * (part * part) + coefficient
    basis = series * part * (sign * envelope)
    b1, b2, b3 = split3(basis)
    w1, w2, w3 = split3(first_ref[...])
    mixed = over_first(
        jnp.concatenate([w1, w1, w2, w2, w1, w3], axis=0).astype(jnp.bfloat16),
        jnp.concatenate([b1, b2, b1, b2, b3, b1], axis=0).astype(jnp.bfloat16),
    )
    radial = silu(mixed).astype(jnp.bfloat16)
    filter_ref[...] = over_first(second_ref[...], radial)
    local = lax.broadcasted_iota(jnp.int32, (atoms, edges), 0)
    hit = local == recv_ref[...]
    rows = [jnp.where(hit, 1.0, 0.0)]
    low = []
    for component in (east, north, up):
        unit = component * inverse
        high = unit.astype(jnp.bfloat16).astype(jnp.float32)
        rows.append(jnp.where(hit, high, 0.0))
        low.append(jnp.where(hit, unit - high, 0.0))
    combine_ref[...] = jnp.concatenate(rows + low, axis=0).astype(jnp.bfloat16)


def node_kernel(
    space_ref,
    own_ref,
    near_ref,
    side_ref,
    far_ref,
    send_ref,
    filter_ref,
    combine_ref,
    project_ref,
    update_ref,
    out_ref,
    species_ref,
    hardness_ref,
    width_ref,
    shift_ref,
    field_ref,
    positions_ref,
    features_ref,
    block_ref,
):
    atoms = positions_ref.shape[1]
    edges = send_ref.shape[1]
    chans = features_ref.shape[1]
    space = space_ref[0]
    packed = [ref[...].astype(jnp.float32) for ref in (own_ref, near_ref, side_ref, far_ref)]
    lanes = len(packed)
    slots = chans // lanes
    group = jnp.concatenate([value[:atoms] for value in packed], axis=0).astype(jnp.bfloat16)
    picks = jnp.zeros((8, chans), jnp.float32)
    line = lax.broadcasted_iota(jnp.int32, (packed[0].shape[0] - atoms, chans), 0)
    for place, value in enumerate(packed):
        mine = jnp.sum(jnp.where(line == space, value[atoms:], 0.0), axis=0, keepdims=True)
        mine = jnp.broadcast_to(mine, (8, chans))
        picks = picks + (pltpu.roll(mine, place * slots, 1) if place else mine)
    slot_owner = lax.broadcasted_iota(jnp.int32, (1, chans), 1) // slots * atoms
    chosen = slot_owner + picks[0:1].astype(jnp.int32)
    members = lanes * atoms
    fill = jnp.where(
        lax.broadcasted_iota(jnp.int32, (members, chans), 0) == chosen, 1.0, 0.0
    ).astype(jnp.bfloat16)
    send = send_ref[...]
    own = send < atoms
    slot = jnp.where(own, -1, (send - atoms) ^ (space * slots))
    from_slot = jnp.where(
        lax.broadcasted_iota(jnp.int32, (chans, edges), 0) == slot, 1.0, 0.0
    ).astype(jnp.bfloat16)
    from_own = jnp.where(
        lax.broadcasted_iota(jnp.int32, (members, edges), 0) == jnp.where(own, send, -1), 1.0, 0.0
    )
    sender = jnp.dot(fill, from_slot, preferred_element_type=jnp.float32) + from_own
    projected = jnp.dot(group, project_ref[...], preferred_element_type=jnp.float32)
    picked = over_first(projected.astype(jnp.bfloat16), sender.astype(jnp.bfloat16))
    message = (picked * filter_ref[...]).astype(jnp.bfloat16)
    summed = over_last(combine_ref[...], message) * message_scale
    square = jnp.zeros((atoms, chans), jnp.float32)
    for component in range(1, 4):
        high = summed[component * atoms : (component + 1) * atoms, chans:]
        low = summed[(component + 3) * atoms : (component + 4) * atoms, chans:]
        square = square + (high + low) * (high + low)
    invariant = jnp.concatenate([summed[:atoms, :chans], square], axis=1).astype(jnp.bfloat16)
    hidden = silu(jnp.dot(invariant, update_ref[...], preferred_element_type=jnp.float32))
    features_ref[...] = (packed[0][:atoms] + hidden).astype(jnp.bfloat16)
    readout = jnp.broadcast_to(out_ref[...], (8, chans))
    chi = over_last(readout, hidden, lax.Precision.HIGHEST)[0:1]
    species = species_ref[...]

    def table(ref):
        result = jnp.zeros(species.shape, jnp.float32)
        for kind in range(ref.shape[1]):
            result = result + jnp.where(species == kind, ref[:, kind : kind + 1], 0.0)
        return result

    chi = chi + table(shift_ref)
    sigma = table(width_ref)
    diag = table(hardness_ref) + inverse_root_pi / sigma
    positions = positions_ref[...]
    rhs = field_ref[...] * positions[2:3] - chi
    blank = jnp.zeros((2, atoms), jnp.float32)
    block_ref[...] = jnp.concatenate([positions, sigma, diag, rhs, blank], axis=0)


def smeared(scaled):
    decay = jnp.exp(-(scaled * scaled))
    turn = 1.0 / (1.0 + 0.3275911 * scaled)
    series = 1.061405429 * turn - 1.453152027
    series = series * turn + 1.421413741
    series = series * turn - 0.284496736
    series = series * turn + 0.254829592
    return 1.0 - series * turn * decay, decay


def charge_kernel(all_ref, field_ref, charges_ref, forces_ref, virial_ref, matrix_ref):
    count = all_ref.shape[1]
    own = charges_ref.shape[1]
    everyone = all_ref[...]
    columns = everyone.T
    spread_row = everyone[3:4] * everyone[3:4]
    rhs = everyone[5:6]
    diag = everyone[4:5]
    rows = own

    def pairs(start):
        column = columns[start : start + rows]
        delta = [column[:, axis : axis + 1] - everyone[axis : axis + 1] for axis in range(3)]
        squared = delta[0] * delta[0] + delta[1] * delta[1] + delta[2] * delta[2]
        same = lax.broadcasted_iota(jnp.int32, (rows, count), 1) == (
            lax.broadcasted_iota(jnp.int32, (rows, count), 0) + start
        )
        squared = jnp.where(same, 1.0, squared)
        inverse = lax.rsqrt(squared)
        spread = column[:, 3:4] * column[:, 3:4] + spread_row
        scale = lax.rsqrt(2.0 * spread)
        smear, decay = smeared(squared * inverse * scale)
        return delta, same, inverse, scale, jnp.where(same, 0.0, smear * inverse), decay

    image = jnp.zeros((rows, count), jnp.float32)
    for start in range(0, count, rows):
        kernel = pairs(start)[4]
        matrix_ref[start : start + rows, :] = kernel
        image = image + kernel * columns[start : start + rows, 5:6]
    image = diag * rhs + jnp.sum(image, axis=0, keepdims=True)

    def total(value):
        return jnp.sum(value, axis=1, keepdims=True)

    norm = total(rhs * rhs)
    alpha = norm / total(rhs * image)
    residual = rhs - alpha * image
    charges = alpha * rhs
    fresh = total(residual * residual)
    direction = residual + fresh / norm * rhs
    across = jnp.broadcast_to(direction, (8, count)).T
    image = jnp.zeros((rows, count), jnp.float32)
    for start in range(0, count, rows):
        image = image + matrix_ref[start : start + rows, :] * across[start : start + rows, 0:1]
    image = diag * direction + jnp.sum(image, axis=0, keepdims=True)
    charges = charges + fresh / total(direction * image) * direction

    delta, same, inverse, scale, kernel, decay = pairs(0)
    slope = two_over_root_pi * scale * decay * inverse - kernel * inverse
    weight = jnp.where(same, 0.0, charges * slope * inverse)
    pulled = [weight * delta[axis] for axis in range(3)]
    sums = [total(value) for value in pulled]
    for left, right in ((0, 0), (1, 1), (2, 2), (0, 1), (0, 2), (1, 2)):
        sums.append(total(pulled[left] * delta[right]))
    lane = lax.broadcasted_iota(jnp.int32, (rows, 128), 1)
    table = jnp.zeros((rows, 128), jnp.float32)
    for place, value in enumerate(sums):
        table = jnp.where(lane == place, value, table)
    table = table.T
    mine = charges[:, :own]
    charges_ref[...] = mine
    pull = -mine * table[0:3]
    third = lax.broadcasted_iota(jnp.int32, pull.shape, 0) == 2
    forces_ref[...] = pull + jnp.where(third, mine * field_ref[...], 0.0)
    virial_ref[...] = 0.5 * mine * table[3:9]


def whole_specs(count, scalars=0):
    return [pl.BlockSpec(memory_space=pltpu.SMEM)] * scalars + [
        pl.BlockSpec(memory_space=pltpu.VMEM)
    ] * count


def kernel_call(kernel, shapes, arguments, scalars=0, scratch=(), flops=0):
    shapes = tuple(jax.ShapeDtypeStruct(shape, kind) for shape, kind in shapes)
    return pl.pallas_call(
        kernel,
        out_shape=shapes,
        in_specs=whole_specs(len(arguments) - scalars, scalars),
        out_specs=tuple(whole_specs(len(shapes))),
        scratch_shapes=list(scratch),
        compiler_params=pltpu.CompilerParams(vmem_limit_bytes=32 * 1024 * 1024),
        cost_estimate=pl.CostEstimate(flops=flops, bytes_accessed=1 << 20, transcendentals=0),
    )(*arguments)


def exchanged(block, axis, step):
    size = lax.axis_size(axis)
    return lax.ppermute(block, axis, [(place, place ^ step) for place in range(size)])


def few_shards(
    features,
    positions,
    species,
    ghost_list,
    edge_recv,
    edge_send,
    edge_vec,
    w_msg,
    w_rad1,
    w_rad2,
    w_up,
    w_out,
    hardness,
    width,
    chi_shift,
    field,
):
    atoms, chans = features.shape
    edges = edge_recv.shape[0]
    lists = ghost_list[0].astype(jnp.bfloat16)
    lists = jnp.pad(lists, ((0, 16 - lists.shape[0]), (0, chans - lists.shape[1])))
    packed = jnp.concatenate([features, lists], axis=0)
    others = [exchanged(packed, "space", step) for step in range(1, 4)]
    filters, combine = kernel_call(
        edge_kernel,
        [((2 * chans, edges), jnp.float32), ((7 * atoms, edges), jnp.bfloat16)],
        (edge_vec, edge_recv[None], w_rad1, w_rad2),
        flops=1 << 28,
    )
    space = lax.axis_index("space").astype(jnp.int32).reshape(1)
    new_features, block = kernel_call(
        node_kernel,
        [((atoms, chans), jnp.bfloat16), ((8, atoms), jnp.float32)],
        (space, packed, *others, edge_send[None], filters, combine, w_msg, w_up, w_out[None])
        + (species[None], hardness[None], width[None], chi_shift[None], field[None], positions),
        scalars=1,
        flops=1 << 28,
    )
    for axis in ("space", "row"):
        step = 1
        while step < lax.axis_size(axis):
            block = jnp.concatenate([block, exchanged(block, axis, step)], axis=1)
            step = 2 * step
    everybody = block.shape[1]
    charges, forces, virial = kernel_call(
        charge_kernel,
        [((rows, atoms), jnp.float32) for rows in (1, 3, 6)],
        (block, field[None]),
        scratch=[pltpu.VMEM((everybody, everybody), jnp.float32)],
        flops=1 << 28,
    )
    return (new_features, charges[0], forces, virial)


def solution(mesh):
    small = mesh.shape["space"] == 4 and mesh.shape["row"] == 8
    return jax.shard_map(
        few_shards if small else shards,
        mesh=mesh,
        in_specs=(
            P(("row", "space"), None),
            P(None, ("row", "space")),
            P(("row", "space")),
            P("row", "space", None),
            P(("row", "space")),
            P(("row", "space")),
            P(None, ("row", "space")),
            P(),
            P(),
            P(),
            P(),
            P(),
            P(),
            P(),
            P(),
            P(),
        ),
        out_specs=(
            P(("row", "space"), None),
            P(("row", "space")),
            P(None, ("row", "space")),
            P(None, ("row", "space")),
        ),
        check_vma=False,
    )
```

```python
import math

import jax
import jax.numpy as jnp
from jax import lax
from jax.experimental import pallas as pl
from jax.experimental.pallas import tpu as pltpu
from jax.sharding import PartitionSpec as P

ITERS = 2


cutoff = 6.0
message_scale = 0.125
two_over_root_pi = 2.0 / math.sqrt(math.pi)
inverse_root_pi = 1.0 / math.sqrt(math.pi)
replicate_limit = 1024
everywhere = ("row", "space")


def lookup(species, table):
    result = jnp.zeros(species.shape, jnp.float32)
    for kind in range(table.shape[0]):
        result = result + jnp.where(species == kind, table[kind], 0.0)
    return result


def pair_terms(target, target_labels, source, source_labels):
    delta = target[:3, :, None] - source[:3, None, :]
    squared = jnp.sum(delta * delta, axis=0)
    same = target_labels[:, None] == source_labels[None, :]
    squared = jnp.where(same, 1.0, squared)
    inverse = lax.rsqrt(squared)
    radius = squared * inverse
    spread = target[3][:, None] * target[3][:, None] + source[3][None, :] * source[3][None, :]
    scale = lax.rsqrt(2.0 * spread)
    scaled = radius * scale
    smear = lax.erf(scaled)
    return delta, same, inverse, scale, scaled, smear


def coulomb(target, target_labels, source, source_labels):
    _, same, inverse, _, _, smear = pair_terms(target, target_labels, source, source_labels)
    return jnp.where(same, 0.0, smear * inverse)


def pair_forces(target, target_labels, source, source_labels, source_charge):
    delta, same, inverse, scale, scaled, smear = pair_terms(
        target, target_labels, source, source_labels
    )
    slope = (
        two_over_root_pi * scale * jnp.exp(-scaled * scaled) * inverse - smear * inverse * inverse
    )
    weight = jnp.where(same, 0.0, source_charge[None, :] * slope * inverse)
    first = jnp.sum(weight[None] * delta, axis=2)
    pairs = ((0, 0), (1, 1), (2, 2), (0, 1), (0, 2), (1, 2))
    second = jnp.stack(
        [jnp.sum(weight * delta[left] * delta[right], axis=1) for left, right in pairs]
    )
    return jnp.concatenate([first, second], axis=0)


def edge_terms(receive, sender_rows, vectors, projected, w_rad1, w_rad2, atoms):
    length = jnp.sqrt(jnp.sum(vectors * vectors, axis=0))
    unit = vectors / length
    order = jnp.arange(1, w_rad1.shape[0] + 1, dtype=jnp.int32).astype(jnp.float32)[:, None]
    ratio = length / cutoff
    envelope = (1.0 - ratio * ratio) * (1.0 - ratio * ratio)
    basis = jnp.sin(order * math.pi * ratio) / ratio * envelope
    mixed = lax.dot_general(
        basis, w_rad1, (((0,), (0,)), ((), ())), precision=lax.Precision.HIGHEST
    )
    radial = jax.nn.silu(mixed).astype(jnp.bfloat16)
    filters = jnp.dot(radial, w_rad2, preferred_element_type=jnp.float32)
    picked = jnp.take(projected, sender_rows, axis=0).astype(jnp.float32) * filters
    chans = w_rad1.shape[1]
    scalar = picked[:, :chans]
    carried = picked[:, chans:]
    joined = [
        scalar,
        unit[0][:, None] * carried,
        unit[1][:, None] * carried,
        unit[2][:, None] * carried,
    ]
    message = jnp.concatenate(joined, axis=1).astype(jnp.bfloat16)
    onehot = (jnp.arange(atoms, dtype=jnp.int32)[:, None] == receive[None, :]).astype(jnp.bfloat16)
    return jnp.dot(onehot, message, preferred_element_type=jnp.float32)


def gathered(block, devices):
    copies = jnp.broadcast_to(block[None], (devices,) + block.shape)
    return lax.all_to_all(copies, everywhere, split_axis=0, concat_axis=0, tiled=True)


def shards(
    features,
    positions,
    species,
    ghost_list,
    edge_recv,
    edge_send,
    edge_vec,
    w_msg,
    w_rad1,
    w_rad2,
    w_up,
    w_out,
    hardness,
    width,
    chi_shift,
    field,
):
    atoms = features.shape[0]
    chans = features.shape[1]
    lanes = lax.axis_size("space")
    devices = lanes * lax.axis_size("row")
    everybody = devices * atoms
    me = lax.axis_index("row") * lanes + lax.axis_index("space")
    sigma = lookup(species, width)
    diag = lookup(species, hardness) + inverse_root_pi / sigma
    placed = jnp.concatenate([positions, sigma[None, :], diag[None, :]], axis=0)
    everyone = gathered(placed, devices).transpose(1, 0, 2).reshape(5, everybody)
    lists = ghost_list[0]
    outgoing = jnp.take(features, lists.reshape(-1), axis=0).reshape(lanes, lists.shape[1], chans)
    ghost_rows = jnp.einsum(
        "dkc,cf->dkf",
        lax.all_to_all(outgoing, "space", split_axis=0, concat_axis=0, tiled=True),
        w_msg,
        preferred_element_type=jnp.float32,
    ).astype(jnp.bfloat16)
    own_rows = jnp.dot(features, w_msg, preferred_element_type=jnp.float32).astype(jnp.bfloat16)
    projected = jnp.concatenate([own_rows, ghost_rows.reshape(-1, 2 * chans)], axis=0)
    summed = edge_terms(edge_recv, edge_send, edge_vec, projected, w_rad1, w_rad2, atoms)
    summed = summed * message_scale
    vector_part = summed[:, chans:].reshape(atoms, 3, chans)
    invariant = jnp.concatenate(
        [summed[:, :chans], jnp.sum(vector_part * vector_part, axis=1)], axis=1
    ).astype(jnp.bfloat16)
    hidden = jax.nn.silu(jnp.dot(invariant, w_up, preferred_element_type=jnp.float32))
    new_features = (features.astype(jnp.float32) + hidden).astype(jnp.bfloat16)
    chi = jnp.dot(hidden, w_out, precision=lax.Precision.HIGHEST) + lookup(species, chi_shift)
    own_labels = me * atoms + jnp.arange(atoms, dtype=jnp.int32)
    all_labels = jnp.arange(everybody, dtype=jnp.int32)
    rhs = field[0] * positions[2] - chi

    if everybody <= replicate_limit:
        kernel = coulomb(everyone, all_labels, everyone, all_labels)
        residual = gathered(rhs, devices).reshape(everybody)
        all_charges = conjugate(
            residual, lambda v: everyone[4] * v + jnp.sum(kernel * v[None, :], axis=1), jnp.sum
        )
        charges = lax.dynamic_slice(all_charges, (me * atoms,), (atoms,))
    else:
        kernel = coulomb(placed, own_labels, everyone, all_labels)

        def spread(vector):
            return gathered(vector, devices).reshape(everybody)

        charges = conjugate(
            rhs,
            lambda v: diag * v + jnp.sum(kernel * spread(v)[None, :], axis=1),
            lambda v: lax.psum(jnp.sum(v), everywhere),
        )
        all_charges = spread(charges)
    sums = pair_forces(placed, own_labels, everyone, all_labels, all_charges)
    pull = -charges[None, :] * sums[:3]
    forces = jnp.concatenate([pull[:2], pull[2:] + (charges * field[0])[None, :]], axis=0)
    virial = 0.5 * charges[None, :] * sums[3:]
    return (new_features, charges, forces, virial)


def conjugate(rhs, apply, total):
    charges = jnp.zeros_like(rhs)
    residual = rhs
    direction = rhs
    norm_now = total(residual * residual)
    for step in range(ITERS):
        image = apply(direction)
        alpha = norm_now / total(direction * image)
        charges = charges + alpha * direction
        if step + 1 < ITERS:
            residual = residual - alpha * image
            fresh = total(residual * residual)
            direction = residual + fresh / norm_now * direction
            norm_now = fresh
    return charges


def split3(value):
    first = value.astype(jnp.bfloat16).astype(jnp.float32)
    rest = value - first
    second = rest.astype(jnp.bfloat16).astype(jnp.float32)
    third = (rest - second).astype(jnp.bfloat16).astype(jnp.float32)
    return first, second, third


def over_first(left, right):
    return lax.dot_general(
        left, right, (((0,), (0,)), ((), ())), preferred_element_type=jnp.float32
    )


def over_last(left, right, precision=None):
    return lax.dot_general(
        left,
        right,
        (((1,), (1,)), ((), ())),
        precision=precision,
        preferred_element_type=jnp.float32,
    )


def silu(value):
    return value / (1.0 + jnp.exp(-value))


sine_series = [(-1.0) ** k * math.pi ** (2 * k + 1) / math.factorial(2 * k + 1) for k in range(7)]


def pack_kernel(features_ref, lists_ref, packed_ref):
    atoms, chans = features_ref.shape
    packed_ref[:atoms, :] = features_ref[...]
    lists = lists_ref[0].astype(jnp.float32)
    rows, width = lists.shape
    lists = jnp.concatenate([lists, jnp.zeros((rows, chans - width), jnp.float32)], axis=1)
    blank = jnp.zeros((packed_ref.shape[0] - atoms - rows, chans), jnp.float32)
    packed_ref[atoms:, :] = jnp.concatenate([lists, blank], axis=0).astype(jnp.bfloat16)


def edge_kernel(
    vec_ref,
    first_ref,
    second_ref,
    species_ref,
    hardness_ref,
    width_ref,
    shift_ref,
    field_ref,
    positions_ref,
    filter_ref,
    unit_ref,
    base_ref,
):
    edges = vec_ref.shape[1]
    orders = first_ref.shape[0]
    vec = vec_ref[...]
    east, north, up = vec[0:1], vec[1:2], vec[2:3]
    squared = east * east + north * north + up * up
    inverse = lax.rsqrt(squared)
    unit_ref[0:3, :] = vec * inverse
    ratio = squared * inverse * (1.0 / cutoff)
    envelope = (1.0 - ratio * ratio) * (1.0 - ratio * ratio) * (cutoff * inverse)
    order = lax.broadcasted_iota(jnp.int32, (orders, edges), 0).astype(jnp.float32) + 1.0
    turns = order * ratio
    whole = jnp.floor(turns + 0.5)
    part = turns - whole
    sign = 1.0 - 2.0 * (whole - 2.0 * jnp.floor(whole * 0.5))
    series = jnp.full_like(part, sine_series[-1])
    for coefficient in sine_series[-2::-1]:
        series = series * (part * part) + coefficient
    basis = series * part * (sign * envelope)
    b1, b2, b3 = split3(basis)
    w1, w2, w3 = split3(first_ref[...])
    mixed = over_first(
        jnp.concatenate([w1, w1, w2, w2, w1, w3], axis=0).astype(jnp.bfloat16),
        jnp.concatenate([b1, b2, b1, b2, b3, b1], axis=0).astype(jnp.bfloat16),
    )
    radial = silu(mixed).astype(jnp.bfloat16)
    filter_ref[...] = over_first(second_ref[...], radial)
    species = species_ref[...]

    def table(ref):
        result = jnp.zeros(species.shape, jnp.float32)
        for kind in range(ref.shape[1]):
            result = result + jnp.where(species == kind, ref[:, kind : kind + 1], 0.0)
        return result

    positions = positions_ref[...]
    sigma = table(width_ref)
    base_ref[0:3, :] = positions
    base_ref[3:4, :] = sigma
    base_ref[4:5, :] = table(hardness_ref) + inverse_root_pi / sigma
    base_ref[5:6, :] = field_ref[...] * positions[2:3]
    base_ref[6:7, :] = table(shift_ref)
    base_ref[7:8, :] = jnp.zeros_like(sigma)


def node_kernel(
    space_ref,
    own_ref,
    near_ref,
    side_ref,
    far_ref,
    send_ref,
    recv_ref,
    filter_ref,
    unit_ref,
    base_ref,
    project_ref,
    update_ref,
    out_ref,
    features_ref,
    block_ref,
):
    atoms, chans = features_ref.shape
    edges = send_ref.shape[1]
    space = space_ref[0]
    packed = [ref[...].astype(jnp.float32) for ref in (own_ref, near_ref, side_ref, far_ref)]
    lanes = len(packed)
    slots = chans // lanes
    group = jnp.concatenate([value[:atoms] for value in packed], axis=0).astype(jnp.bfloat16)
    picks = jnp.zeros((8, chans), jnp.float32)
    line = lax.broadcasted_iota(jnp.int32, (packed[0].shape[0] - atoms, chans), 0)
    for place, value in enumerate(packed):
        mine = jnp.sum(jnp.where(line == space, value[atoms:], 0.0), axis=0, keepdims=True)
        mine = jnp.broadcast_to(mine, (8, chans))
        picks = picks + (pltpu.roll(mine, place * slots, 1) if place else mine)
    slot_owner = lax.broadcasted_iota(jnp.int32, (1, chans), 1) // slots * atoms
    chosen = slot_owner + picks[0:1].astype(jnp.int32)
    members = lanes * atoms
    fill = jnp.where(
        lax.broadcasted_iota(jnp.int32, (members, chans), 0) == chosen, 1.0, 0.0
    ).astype(jnp.bfloat16)
    send = send_ref[...]
    own = send < atoms
    slot = jnp.where(own, -1, (send - atoms) ^ (space * slots))
    from_slot = jnp.where(
        lax.broadcasted_iota(jnp.int32, (chans, edges), 0) == slot, 1.0, 0.0
    ).astype(jnp.bfloat16)
    from_own = jnp.where(
        lax.broadcasted_iota(jnp.int32, (members, edges), 0) == jnp.where(own, send, -1), 1.0, 0.0
    )
    sender = jnp.dot(fill, from_slot, preferred_element_type=jnp.float32) + from_own
    projected = jnp.dot(group, project_ref[...], preferred_element_type=jnp.float32)
    picked = over_first(projected.astype(jnp.bfloat16), sender.astype(jnp.bfloat16))
    scalar = picked[:chans] * filter_ref[:chans, :]
    carried = picked[chans:] * filter_ref[chans:, :]
    parts = [scalar] + [unit_ref[axis : axis + 1, :] * carried for axis in range(3)]
    message = jnp.concatenate([part.astype(jnp.bfloat16) for part in parts], axis=0)
    hit = lax.broadcasted_iota(jnp.int32, (atoms, edges), 0) == recv_ref[...]
    summed = over_last(jnp.where(hit, 1.0, 0.0).astype(jnp.bfloat16), message) * message_scale
    square = jnp.zeros((atoms, chans), jnp.float32)
    for component in range(1, 4):
        part = summed[:, component * chans : (component + 1) * chans]
        square = square + part * part
    invariant = jnp.concatenate([summed[:, :chans], square], axis=1).astype(jnp.bfloat16)
    hidden = silu(jnp.dot(invariant, update_ref[...], preferred_element_type=jnp.float32))
    features_ref[...] = (packed[0][:atoms] + hidden).astype(jnp.bfloat16)
    readout = jnp.broadcast_to(out_ref[...], (8, chans))
    chi = over_last(readout, hidden, lax.Precision.HIGHEST)[0:1] + base_ref[6:7, :]
    block_ref[0:5, :] = base_ref[0:5, :]
    block_ref[5:6, :] = base_ref[5:6, :] - chi
    block_ref[6:8, :] = jnp.zeros((2, atoms), jnp.float32)


def smeared(scaled):
    decay = jnp.exp(-(scaled * scaled))
    turn = 1.0 / (1.0 + 0.3275911 * scaled)
    series = 1.061405429 * turn - 1.453152027
    series = series * turn + 1.421413741
    series = series * turn - 0.284496736
    series = series * turn + 0.254829592
    return 1.0 - series * turn * decay, decay


def charge_kernel(place_ref, all_ref, field_ref, charges_ref, forces_ref, virial_ref, matrix_ref):
    blocks, _, width = all_ref.shape
    count = blocks * width
    own = charges_ref.shape[1]
    everyone = jnp.concatenate([all_ref[block] for block in range(blocks)], axis=1)
    everyone = pltpu.roll(everyone, lax.rem(count - place_ref[0] * width, count), 1)
    columns = everyone.T
    spread_row = everyone[3:4] * everyone[3:4]
    rhs = everyone[5:6]
    diag = everyone[4:5]
    rows = own

    def pairs(start):
        column = columns[start : start + rows]
        delta = [column[:, axis : axis + 1] - everyone[axis : axis + 1] for axis in range(3)]
        squared = delta[0] * delta[0] + delta[1] * delta[1] + delta[2] * delta[2]
        same = lax.broadcasted_iota(jnp.int32, (rows, count), 1) == (
            lax.broadcasted_iota(jnp.int32, (rows, count), 0) + start
        )
        squared = jnp.where(same, 1.0, squared)
        inverse = lax.rsqrt(squared)
        spread = column[:, 3:4] * column[:, 3:4] + spread_row
        scale = lax.rsqrt(2.0 * spread)
        smear, decay = smeared(squared * inverse * scale)
        return delta, same, inverse, scale, jnp.where(same, 0.0, smear * inverse), decay

    image = jnp.zeros((rows, count), jnp.float32)
    for start in range(0, count, rows):
        kernel = pairs(start)[4]
        matrix_ref[start : start + rows, :] = kernel
        image = image + kernel * columns[start : start + rows, 5:6]
    image = diag * rhs + jnp.sum(image, axis=0, keepdims=True)

    def total(value):
        return jnp.sum(value, axis=1, keepdims=True)

    norm = total(rhs * rhs)
    alpha = norm / total(rhs * image)
    residual = rhs - alpha * image
    charges = alpha * rhs
    fresh = total(residual * residual)
    direction = residual + fresh / norm * rhs
    across = jnp.broadcast_to(direction, (8, count)).T
    image = jnp.zeros((rows, count), jnp.float32)
    for start in range(0, count, rows):
        image = image + matrix_ref[start : start + rows, :] * across[start : start + rows, 0:1]
    image = diag * direction + jnp.sum(image, axis=0, keepdims=True)
    charges = charges + fresh / total(direction * image) * direction

    delta, same, inverse, scale, kernel, decay = pairs(0)
    slope = two_over_root_pi * scale * decay * inverse - kernel * inverse
    weight = jnp.where(same, 0.0, charges * slope * inverse)
    pulled = [weight * delta[axis] for axis in range(3)]
    sums = [total(value) for value in pulled]
    for left, right in ((0, 0), (1, 1), (2, 2), (0, 1), (0, 2), (1, 2)):
        sums.append(total(pulled[left] * delta[right]))
    lane = lax.broadcasted_iota(jnp.int32, (rows, 128), 1)
    table = jnp.zeros((rows, 128), jnp.float32)
    for place, value in enumerate(sums):
        table = jnp.where(lane == place, value, table)
    table = table.T
    mine = charges[:, :own]
    charges_ref[...] = mine
    pull = -mine * table[0:3]
    third = lax.broadcasted_iota(jnp.int32, pull.shape, 0) == 2
    forces_ref[...] = pull + jnp.where(third, mine * field_ref[...], 0.0)
    virial_ref[...] = 0.5 * mine * table[3:9]


def whole_specs(count, scalars=0):
    return [pl.BlockSpec(memory_space=pltpu.SMEM)] * scalars + [
        pl.BlockSpec(memory_space=pltpu.VMEM)
    ] * count


def kernel_call(kernel, shapes, arguments, scalars=0, scratch=(), flops=0):
    shapes = tuple(jax.ShapeDtypeStruct(shape, kind) for shape, kind in shapes)
    return pl.pallas_call(
        kernel,
        out_shape=shapes,
        in_specs=whole_specs(len(arguments) - scalars, scalars),
        out_specs=tuple(whole_specs(len(shapes))),
        scratch_shapes=list(scratch),
        compiler_params=pltpu.CompilerParams(vmem_limit_bytes=32 * 1024 * 1024),
        cost_estimate=pl.CostEstimate(flops=flops, bytes_accessed=1 << 20, transcendentals=0),
    )(*arguments)


def exchanged(block, axis, step):
    size = lax.axis_size(axis)
    return lax.ppermute(block, axis, [(place, place ^ step) for place in range(size)])


def few_shards(
    features,
    positions,
    species,
    ghost_list,
    edge_recv,
    edge_send,
    edge_vec,
    w_msg,
    w_rad1,
    w_rad2,
    w_up,
    w_out,
    hardness,
    width,
    chi_shift,
    field,
):
    atoms, chans = features.shape
    edges = edge_recv.shape[0]
    rows, lanes = lax.axis_size("row"), lax.axis_size("space")
    (packed,) = kernel_call(
        pack_kernel, [((atoms + 16, chans), jnp.bfloat16)], (features, ghost_list)
    )
    others = [exchanged(packed, "space", step) for step in range(1, lanes)]
    filters, units, base = kernel_call(
        edge_kernel,
        [((2 * chans, edges), jnp.float32), ((8, edges), jnp.float32), ((8, atoms), jnp.float32)],
        (edge_vec, w_rad1, w_rad2, species[None], hardness[None], width[None])
        + (chi_shift[None], field[None], positions),
        flops=1 << 28,
    )
    space = lax.axis_index("space").astype(jnp.int32)
    new_features, block = kernel_call(
        node_kernel,
        [((atoms, chans), jnp.bfloat16), ((8, atoms), jnp.float32)],
        (space.reshape(1), packed, *others, edge_send[None], edge_recv[None])
        + (filters, units, base, w_msg, w_up, w_out[None]),
        scalars=1,
        flops=1 << 28,
    )
    block = jnp.concatenate([block, exchanged(block, "space", 1)], axis=1)
    groups = [list(range(core, rows * lanes, 2)) for core in range(2)]
    blocks = len(groups[0])
    block = jnp.broadcast_to(block[None], (blocks,) + block.shape)
    block = lax.all_to_all(block, everywhere, 0, 0, axis_index_groups=groups, tiled=True)
    place = lax.axis_index("row").astype(jnp.int32) * (lanes // 2) + space // 2
    everybody = rows * lanes * atoms
    charges, forces, virial = kernel_call(
        charge_kernel,
        [((count, atoms), jnp.float32) for count in (1, 3, 6)],
        (place.reshape(1), block, field[None]),
        scalars=1,
        scratch=[pltpu.VMEM((everybody, everybody), jnp.float32)],
        flops=1 << 28,
    )
    return (new_features, charges[0], forces, virial)


def solution(mesh):
    small = mesh.shape["space"] == 4 and mesh.shape["row"] == 8
    return jax.shard_map(
        few_shards if small else shards,
        mesh=mesh,
        in_specs=(
            P(("row", "space"), None),
            P(None, ("row", "space")),
            P(("row", "space")),
            P("row", "space", None),
            P(("row", "space")),
            P(("row", "space")),
            P(None, ("row", "space")),
            P(),
            P(),
            P(),
            P(),
            P(),
            P(),
            P(),
            P(),
            P(),
        ),
        out_specs=(
            P(("row", "space"), None),
            P(("row", "space")),
            P(None, ("row", "space")),
            P(None, ("row", "space")),
        ),
        check_vma=False,
    )
```

```python
import math

import jax
import jax.numpy as jnp
from jax import lax
from jax.experimental import pallas as pl
from jax.experimental.pallas import tpu as pltpu
from jax.sharding import PartitionSpec as P

ITERS = 2


cutoff = 6.0
message_scale = 0.125
two_over_root_pi = 2.0 / math.sqrt(math.pi)
inverse_root_pi = 1.0 / math.sqrt(math.pi)
replicate_limit = 1024
everywhere = ("row", "space")


def lookup(species, table):
    result = jnp.zeros(species.shape, jnp.float32)
    for kind in range(table.shape[0]):
        result = result + jnp.where(species == kind, table[kind], 0.0)
    return result


def pair_terms(target, target_labels, source, source_labels):
    delta = target[:3, :, None] - source[:3, None, :]
    squared = jnp.sum(delta * delta, axis=0)
    same = target_labels[:, None] == source_labels[None, :]
    squared = jnp.where(same, 1.0, squared)
    inverse = lax.rsqrt(squared)
    radius = squared * inverse
    spread = target[3][:, None] * target[3][:, None] + source[3][None, :] * source[3][None, :]
    scale = lax.rsqrt(2.0 * spread)
    scaled = radius * scale
    smear = lax.erf(scaled)
    return delta, same, inverse, scale, scaled, smear


def coulomb(target, target_labels, source, source_labels):
    _, same, inverse, _, _, smear = pair_terms(target, target_labels, source, source_labels)
    return jnp.where(same, 0.0, smear * inverse)


def pair_forces(target, target_labels, source, source_labels, source_charge):
    delta, same, inverse, scale, scaled, smear = pair_terms(
        target, target_labels, source, source_labels
    )
    slope = (
        two_over_root_pi * scale * jnp.exp(-scaled * scaled) * inverse - smear * inverse * inverse
    )
    weight = jnp.where(same, 0.0, source_charge[None, :] * slope * inverse)
    first = jnp.sum(weight[None] * delta, axis=2)
    pairs = ((0, 0), (1, 1), (2, 2), (0, 1), (0, 2), (1, 2))
    second = jnp.stack(
        [jnp.sum(weight * delta[left] * delta[right], axis=1) for left, right in pairs]
    )
    return jnp.concatenate([first, second], axis=0)


def edge_terms(receive, sender_rows, vectors, projected, w_rad1, w_rad2, atoms):
    length = jnp.sqrt(jnp.sum(vectors * vectors, axis=0))
    unit = vectors / length
    order = jnp.arange(1, w_rad1.shape[0] + 1, dtype=jnp.int32).astype(jnp.float32)[:, None]
    ratio = length / cutoff
    envelope = (1.0 - ratio * ratio) * (1.0 - ratio * ratio)
    basis = jnp.sin(order * math.pi * ratio) / ratio * envelope
    mixed = lax.dot_general(
        basis, w_rad1, (((0,), (0,)), ((), ())), precision=lax.Precision.HIGHEST
    )
    radial = jax.nn.silu(mixed).astype(jnp.bfloat16)
    filters = jnp.dot(radial, w_rad2, preferred_element_type=jnp.float32)
    picked = jnp.take(projected, sender_rows, axis=0).astype(jnp.float32) * filters
    chans = w_rad1.shape[1]
    scalar = picked[:, :chans]
    carried = picked[:, chans:]
    joined = [
        scalar,
        unit[0][:, None] * carried,
        unit[1][:, None] * carried,
        unit[2][:, None] * carried,
    ]
    message = jnp.concatenate(joined, axis=1).astype(jnp.bfloat16)
    onehot = (jnp.arange(atoms, dtype=jnp.int32)[:, None] == receive[None, :]).astype(jnp.bfloat16)
    return jnp.dot(onehot, message, preferred_element_type=jnp.float32)


def gathered(block, devices):
    copies = jnp.broadcast_to(block[None], (devices,) + block.shape)
    return lax.all_to_all(copies, everywhere, split_axis=0, concat_axis=0, tiled=True)


def shards(
    features,
    positions,
    species,
    ghost_list,
    edge_recv,
    edge_send,
    edge_vec,
    w_msg,
    w_rad1,
    w_rad2,
    w_up,
    w_out,
    hardness,
    width,
    chi_shift,
    field,
):
    atoms = features.shape[0]
    chans = features.shape[1]
    lanes = lax.axis_size("space")
    devices = lanes * lax.axis_size("row")
    everybody = devices * atoms
    me = lax.axis_index("row") * lanes + lax.axis_index("space")
    sigma = lookup(species, width)
    diag = lookup(species, hardness) + inverse_root_pi / sigma
    placed = jnp.concatenate([positions, sigma[None, :], diag[None, :]], axis=0)
    everyone = gathered(placed, devices).transpose(1, 0, 2).reshape(5, everybody)
    lists = ghost_list[0]
    outgoing = jnp.take(features, lists.reshape(-1), axis=0).reshape(lanes, lists.shape[1], chans)
    ghost_rows = jnp.einsum(
        "dkc,cf->dkf",
        lax.all_to_all(outgoing, "space", split_axis=0, concat_axis=0, tiled=True),
        w_msg,
        preferred_element_type=jnp.float32,
    ).astype(jnp.bfloat16)
    own_rows = jnp.dot(features, w_msg, preferred_element_type=jnp.float32).astype(jnp.bfloat16)
    projected = jnp.concatenate([own_rows, ghost_rows.reshape(-1, 2 * chans)], axis=0)
    summed = edge_terms(edge_recv, edge_send, edge_vec, projected, w_rad1, w_rad2, atoms)
    summed = summed * message_scale
    vector_part = summed[:, chans:].reshape(atoms, 3, chans)
    invariant = jnp.concatenate(
        [summed[:, :chans], jnp.sum(vector_part * vector_part, axis=1)], axis=1
    ).astype(jnp.bfloat16)
    hidden = jax.nn.silu(jnp.dot(invariant, w_up, preferred_element_type=jnp.float32))
    new_features = (features.astype(jnp.float32) + hidden).astype(jnp.bfloat16)
    chi = jnp.dot(hidden, w_out, precision=lax.Precision.HIGHEST) + lookup(species, chi_shift)
    own_labels = me * atoms + jnp.arange(atoms, dtype=jnp.int32)
    all_labels = jnp.arange(everybody, dtype=jnp.int32)
    rhs = field[0] * positions[2] - chi

    if everybody <= replicate_limit:
        kernel = coulomb(everyone, all_labels, everyone, all_labels)
        residual = gathered(rhs, devices).reshape(everybody)
        all_charges = conjugate(
            residual, lambda v: everyone[4] * v + jnp.sum(kernel * v[None, :], axis=1), jnp.sum
        )
        charges = lax.dynamic_slice(all_charges, (me * atoms,), (atoms,))
    else:
        kernel = coulomb(placed, own_labels, everyone, all_labels)

        def spread(vector):
            return gathered(vector, devices).reshape(everybody)

        charges = conjugate(
            rhs,
            lambda v: diag * v + jnp.sum(kernel * spread(v)[None, :], axis=1),
            lambda v: lax.psum(jnp.sum(v), everywhere),
        )
        all_charges = spread(charges)
    sums = pair_forces(placed, own_labels, everyone, all_labels, all_charges)
    pull = -charges[None, :] * sums[:3]
    forces = jnp.concatenate([pull[:2], pull[2:] + (charges * field[0])[None, :]], axis=0)
    virial = 0.5 * charges[None, :] * sums[3:]
    return (new_features, charges, forces, virial)


def conjugate(rhs, apply, total):
    charges = jnp.zeros_like(rhs)
    residual = rhs
    direction = rhs
    norm_now = total(residual * residual)
    for step in range(ITERS):
        image = apply(direction)
        alpha = norm_now / total(direction * image)
        charges = charges + alpha * direction
        if step + 1 < ITERS:
            residual = residual - alpha * image
            fresh = total(residual * residual)
            direction = residual + fresh / norm_now * direction
            norm_now = fresh
    return charges


def split3(value):
    first = value.astype(jnp.bfloat16).astype(jnp.float32)
    rest = value - first
    second = rest.astype(jnp.bfloat16).astype(jnp.float32)
    third = (rest - second).astype(jnp.bfloat16).astype(jnp.float32)
    return first, second, third


def over_first(left, right):
    return lax.dot_general(
        left, right, (((0,), (0,)), ((), ())), preferred_element_type=jnp.float32
    )


def over_last(left, right, precision=None):
    return lax.dot_general(
        left,
        right,
        (((1,), (1,)), ((), ())),
        precision=precision,
        preferred_element_type=jnp.float32,
    )


def silu(value):
    return value / (1.0 + jnp.exp(-value))


sine_series = [(-1.0) ** k * math.pi ** (2 * k + 1) / math.factorial(2 * k + 1) for k in range(7)]


def fetched(pairs, semaphores):
    copies = [
        pltpu.make_async_copy(source, target, semaphores.at[place])
        for place, (source, target) in enumerate(pairs)
    ]
    for copy in copies:
        copy.start()
    return copies


def pack_kernel(features_ref, lists_ref, packed_ref, held_ref, semaphores):
    atoms, chans = features_ref.shape
    copies = fetched(
        [(lists_ref, held_ref), (features_ref, packed_ref.at[pl.ds(0, atoms)])], semaphores
    )
    copies[0].wait()
    lists = held_ref[0].astype(jnp.float32)
    rows, width = lists.shape
    lists = jnp.concatenate([lists, jnp.zeros((rows, chans - width), jnp.float32)], axis=1)
    blank = jnp.zeros((packed_ref.shape[0] - atoms - rows, chans), jnp.float32)
    packed_ref[atoms:, :] = jnp.concatenate([lists, blank], axis=0).astype(jnp.bfloat16)
    copies[1].wait()


def edge_kernel(*refs):
    own, kept = refs[:9], refs[9:14]
    filter_ref, unit_ref, base_ref = refs[14:17]
    moved, held, semaphores = refs[17:22], refs[22:31], refs[31]
    copies = fetched(list(zip(own + kept, held + moved)), semaphores)
    for copy in copies:
        copy.wait()
    vec_ref, first_ref, second_ref, species_ref = held[:4]
    hardness_ref, width_ref, shift_ref, field_ref, positions_ref = held[4:]
    edges = vec_ref.shape[1]
    orders = first_ref.shape[0]
    vec = vec_ref[...]
    east, north, up = vec[0:1], vec[1:2], vec[2:3]
    squared = east * east + north * north + up * up
    inverse = lax.rsqrt(squared)
    unit_ref[0:3, :] = vec * inverse
    ratio = squared * inverse * (1.0 / cutoff)
    envelope = (1.0 - ratio * ratio) * (1.0 - ratio * ratio) * (cutoff * inverse)
    order = lax.broadcasted_iota(jnp.int32, (orders, edges), 0).astype(jnp.float32) + 1.0
    turns = order * ratio
    whole = jnp.floor(turns + 0.5)
    part = turns - whole
    sign = 1.0 - 2.0 * (whole - 2.0 * jnp.floor(whole * 0.5))
    series = jnp.full_like(part, sine_series[-1])
    for coefficient in sine_series[-2::-1]:
        series = series * (part * part) + coefficient
    basis = series * part * (sign * envelope)
    b1, b2, b3 = split3(basis)
    w1, w2, w3 = split3(first_ref[...])
    mixed = over_first(
        jnp.concatenate([w1, w1, w2, w2, w1, w3], axis=0).astype(jnp.bfloat16),
        jnp.concatenate([b1, b2, b1, b2, b3, b1], axis=0).astype(jnp.bfloat16),
    )
    radial = silu(mixed).astype(jnp.bfloat16)
    filter_ref[...] = over_first(second_ref[...], radial)
    species = species_ref[...]

    def table(ref):
        result = jnp.zeros(species.shape, jnp.float32)
        for kind in range(ref.shape[1]):
            result = result + jnp.where(species == kind, ref[:, kind : kind + 1], 0.0)
        return result

    positions = positions_ref[...]
    sigma = table(width_ref)
    base_ref[0:3, :] = positions
    base_ref[3:4, :] = sigma
    base_ref[4:5, :] = table(hardness_ref) + inverse_root_pi / sigma
    base_ref[5:6, :] = field_ref[...] * positions[2:3]
    base_ref[6:7, :] = table(shift_ref)
    base_ref[7:8, :] = jnp.zeros_like(sigma)


def node_kernel(
    space_ref,
    own_ref,
    near_ref,
    side_ref,
    far_ref,
    send_ref,
    recv_ref,
    filter_ref,
    unit_ref,
    base_ref,
    project_ref,
    update_ref,
    out_ref,
    features_ref,
    block_ref,
):
    atoms, chans = features_ref.shape
    edges = send_ref.shape[1]
    space = space_ref[0]
    packed = [ref[...].astype(jnp.float32) for ref in (own_ref, near_ref, side_ref, far_ref)]
    lanes = len(packed)
    slots = chans // lanes
    group = jnp.concatenate([value[:atoms] for value in packed], axis=0).astype(jnp.bfloat16)
    picks = jnp.zeros((8, chans), jnp.float32)
    line = lax.broadcasted_iota(jnp.int32, (packed[0].shape[0] - atoms, chans), 0)
    for place, value in enumerate(packed):
        mine = jnp.sum(jnp.where(line == space, value[atoms:], 0.0), axis=0, keepdims=True)
        mine = jnp.broadcast_to(mine, (8, chans))
        picks = picks + (pltpu.roll(mine, place * slots, 1) if place else mine)
    slot_owner = lax.broadcasted_iota(jnp.int32, (1, chans), 1) // slots * atoms
    chosen = slot_owner + picks[0:1].astype(jnp.int32)
    members = lanes * atoms
    fill = jnp.where(
        lax.broadcasted_iota(jnp.int32, (members, chans), 0) == chosen, 1.0, 0.0
    ).astype(jnp.bfloat16)
    send = send_ref[...]
    own = send < atoms
    slot = jnp.where(own, -1, (send - atoms) ^ (space * slots))
    from_slot = jnp.where(
        lax.broadcasted_iota(jnp.int32, (chans, edges), 0) == slot, 1.0, 0.0
    ).astype(jnp.bfloat16)
    from_own = jnp.where(
        lax.broadcasted_iota(jnp.int32, (members, edges), 0) == jnp.where(own, send, -1), 1.0, 0.0
    )
    sender = jnp.dot(fill, from_slot, preferred_element_type=jnp.float32) + from_own
    projected = jnp.dot(group, project_ref[...], preferred_element_type=jnp.float32)
    picked = over_first(projected.astype(jnp.bfloat16), sender.astype(jnp.bfloat16))
    scalar = picked[:chans] * filter_ref[:chans, :]
    carried = picked[chans:] * filter_ref[chans:, :]
    parts = [scalar] + [unit_ref[axis : axis + 1, :] * carried for axis in range(3)]
    message = jnp.concatenate([part.astype(jnp.bfloat16) for part in parts], axis=0)
    hit = lax.broadcasted_iota(jnp.int32, (atoms, edges), 0) == recv_ref[...]
    summed = over_last(jnp.where(hit, 1.0, 0.0).astype(jnp.bfloat16), message) * message_scale
    square = jnp.zeros((atoms, chans), jnp.float32)
    for component in range(1, 4):
        part = summed[:, component * chans : (component + 1) * chans]
        square = square + part * part
    invariant = jnp.concatenate([summed[:, :chans], square], axis=1).astype(jnp.bfloat16)
    hidden = silu(jnp.dot(invariant, update_ref[...], preferred_element_type=jnp.float32))
    features_ref[...] = (packed[0][:atoms] + hidden).astype(jnp.bfloat16)
    readout = jnp.broadcast_to(out_ref[...], (8, chans))
    chi = over_last(readout, hidden, lax.Precision.HIGHEST)[0:1] + base_ref[6:7, :]
    rhs = base_ref[5:6, :] - chi
    wide = jnp.zeros((1, chans - atoms), jnp.float32)
    rows = [base_ref[0:1, :], jnp.zeros((2, atoms), jnp.float32), rhs]
    rows = rows + [base_ref[place : place + 1, :] for place in range(4, 0, -1)]
    block = jnp.concatenate(
        [jnp.concatenate(rows, axis=0), jnp.broadcast_to(wide, (8, chans - atoms))], axis=1
    )
    block = pltpu.roll(block, 0, 1, stride=atoms, stride_axis=0)
    row = jnp.sum(block, axis=0, keepdims=True)
    block_ref[...] = jnp.broadcast_to(row[None], block_ref.shape)


def smeared(scaled):
    decay = jnp.exp(-(scaled * scaled))
    turn = 1.0 / (1.0 + 0.3275911 * scaled)
    series = 1.061405429 * turn - 1.453152027
    series = series * turn + 1.421413741
    series = series * turn - 0.284496736
    series = series * turn + 0.254829592
    return 1.0 - series * turn * decay, decay


def charge_kernel(place_ref, all_ref, field_ref, charges_ref, forces_ref, virial_ref, matrix_ref):
    blocks, _, lanes = all_ref.shape
    own = charges_ref.shape[1]
    count = blocks * own
    fit = lanes // own
    segment = lax.broadcasted_iota(jnp.int32, (8, lanes), 1) // own
    tiles = []
    for first in range(0, blocks, fit):
        tile = jnp.zeros((8, lanes), jnp.float32)
        for place in range(fit):
            row = jnp.broadcast_to(all_ref[first + place], (8, lanes))
            row = pltpu.roll(row, 0, 1, stride=own, stride_axis=0)
            row = pltpu.roll(row, place * own, 1) if place else row
            tile = jnp.where(segment == place, row, tile)
        tiles.append(tile)
    everyone = jnp.concatenate(tiles, axis=1)
    everyone = pltpu.roll(everyone, lax.rem(count - place_ref[0] * own, count), 1)
    columns = everyone.T
    spread_row = everyone[3:4] * everyone[3:4]
    rhs = everyone[5:6]
    diag = everyone[4:5]
    rows = own

    def pairs(start):
        column = columns[start : start + rows]
        delta = [column[:, axis : axis + 1] - everyone[axis : axis + 1] for axis in range(3)]
        squared = delta[0] * delta[0] + delta[1] * delta[1] + delta[2] * delta[2]
        same = lax.broadcasted_iota(jnp.int32, (rows, count), 1) == (
            lax.broadcasted_iota(jnp.int32, (rows, count), 0) + start
        )
        squared = jnp.where(same, 1.0, squared)
        inverse = lax.rsqrt(squared)
        spread = column[:, 3:4] * column[:, 3:4] + spread_row
        scale = lax.rsqrt(2.0 * spread)
        smear, decay = smeared(squared * inverse * scale)
        return delta, same, inverse, scale, jnp.where(same, 0.0, smear * inverse), decay

    image = jnp.zeros((rows, count), jnp.float32)
    for start in range(0, count, rows):
        kernel = pairs(start)[4]
        matrix_ref[start : start + rows, :] = kernel
        image = image + kernel * columns[start : start + rows, 5:6]
    image = diag * rhs + jnp.sum(image, axis=0, keepdims=True)

    def total(value):
        return jnp.sum(value, axis=1, keepdims=True)

    norm = total(rhs * rhs)
    alpha = norm / total(rhs * image)
    residual = rhs - alpha * image
    charges = alpha * rhs
    fresh = total(residual * residual)
    direction = residual + fresh / norm * rhs
    across = jnp.broadcast_to(direction, (8, count)).T
    image = jnp.zeros((rows, count), jnp.float32)
    for start in range(0, count, rows):
        image = image + matrix_ref[start : start + rows, :] * across[start : start + rows, 0:1]
    image = diag * direction + jnp.sum(image, axis=0, keepdims=True)
    charges = charges + fresh / total(direction * image) * direction

    delta, same, inverse, scale, kernel, decay = pairs(0)
    slope = two_over_root_pi * scale * decay * inverse - kernel * inverse
    weight = jnp.where(same, 0.0, charges * slope * inverse)
    pulled = [weight * delta[axis] for axis in range(3)]
    sums = [total(value) for value in pulled]
    for left, right in ((0, 0), (1, 1), (2, 2), (0, 1), (0, 2), (1, 2)):
        sums.append(total(pulled[left] * delta[right]))
    lane = lax.broadcasted_iota(jnp.int32, (rows, 128), 1)
    table = jnp.zeros((rows, 128), jnp.float32)
    for place, value in enumerate(sums):
        table = jnp.where(lane == place, value, table)
    table = table.T
    mine = charges[:, :own]
    charges_ref[...] = mine
    pull = -mine * table[0:3]
    third = lax.broadcasted_iota(jnp.int32, pull.shape, 0) == 2
    forces_ref[...] = pull + jnp.where(third, mine * field_ref[...], 0.0)
    virial_ref[...] = 0.5 * mine * table[3:9]


def kernel_call(kernel, shapes, arguments, scalars=0, far=0, scratch=(), flops=0):
    shapes = tuple(jax.ShapeDtypeStruct(shape, kind) for shape, kind in shapes)
    spaces = [pltpu.SMEM] * scalars + [pltpu.HBM] * far
    spaces = spaces + [pltpu.VMEM] * (len(arguments) - len(spaces))
    return pl.pallas_call(
        kernel,
        out_shape=shapes,
        in_specs=[pl.BlockSpec(memory_space=space) for space in spaces],
        out_specs=tuple(pl.BlockSpec(memory_space=pltpu.VMEM) for _ in shapes),
        scratch_shapes=list(scratch),
        compiler_params=pltpu.CompilerParams(vmem_limit_bytes=32 * 1024 * 1024),
        cost_estimate=pl.CostEstimate(flops=flops, bytes_accessed=1 << 20, transcendentals=0),
    )(*arguments)


def shape_of(value):
    return (value.shape, value.dtype)


def exchanged(block, axis, step):
    size = lax.axis_size(axis)
    return lax.ppermute(block, axis, [(place, place ^ step) for place in range(size)])


def few_shards(
    features,
    positions,
    species,
    ghost_list,
    edge_recv,
    edge_send,
    edge_vec,
    w_msg,
    w_rad1,
    w_rad2,
    w_up,
    w_out,
    hardness,
    width,
    chi_shift,
    field,
):
    atoms, chans = features.shape
    edges = edge_recv.shape[0]
    rows, lanes = lax.axis_size("row"), lax.axis_size("space")
    (packed,) = kernel_call(
        pack_kernel,
        [((atoms + 16, chans), jnp.bfloat16)],
        (features, ghost_list),
        far=2,
        scratch=[pltpu.VMEM(*shape_of(ghost_list)), pltpu.SemaphoreType.DMA((2,))],
    )
    others = [exchanged(packed, "space", step) for step in range(1, lanes)]
    own = (edge_vec, w_rad1, w_rad2, species[None], hardness[None], width[None])
    own = own + (chi_shift[None], field[None], positions)
    kept = (edge_send[None], edge_recv[None], w_msg, w_up, w_out[None])
    filters, units, base, *kept = kernel_call(
        edge_kernel,
        [((2 * chans, edges), jnp.float32), ((8, edges), jnp.float32), ((8, atoms), jnp.float32)]
        + [shape_of(value) for value in kept],
        own + kept,
        far=len(own + kept),
        scratch=[pltpu.VMEM(*shape_of(value)) for value in own]
        + [pltpu.SemaphoreType.DMA((len(own + kept),))],
        flops=1 << 28,
    )
    send, receive, project, update, readout = kept
    space = lax.axis_index("space").astype(jnp.int32)
    devices = rows * lanes
    new_features, block = kernel_call(
        node_kernel,
        [((atoms, chans), jnp.bfloat16), ((devices, 1, chans), jnp.float32)],
        (space.reshape(1), packed, *others, send, receive)
        + (filters, units, base, project, update, readout),
        scalars=1,
        flops=1 << 28,
    )
    block = lax.all_to_all(block, everywhere, 0, 0, tiled=True)
    place = lax.axis_index("row").astype(jnp.int32) * lanes + space
    everybody = rows * lanes * atoms
    charges, forces, virial = kernel_call(
        charge_kernel,
        [((count, atoms), jnp.float32) for count in (1, 3, 6)],
        (place.reshape(1), block, field[None]),
        scalars=1,
        scratch=[pltpu.VMEM((everybody, everybody), jnp.float32)],
        flops=1 << 28,
    )
    return (new_features, charges[0], forces, virial)


def solution(mesh):
    small = mesh.shape["space"] == 4 and mesh.shape["row"] == 8
    return jax.shard_map(
        few_shards if small else shards,
        mesh=mesh,
        in_specs=(
            P(("row", "space"), None),
            P(None, ("row", "space")),
            P(("row", "space")),
            P("row", "space", None),
            P(("row", "space")),
            P(("row", "space")),
            P(None, ("row", "space")),
            P(),
            P(),
            P(),
            P(),
            P(),
            P(),
            P(),
            P(),
            P(),
        ),
        out_specs=(
            P(("row", "space"), None),
            P(("row", "space")),
            P(None, ("row", "space")),
            P(None, ("row", "space")),
        ),
        check_vma=False,
    )
```

```python
import math

import jax
import jax.numpy as jnp
from jax import lax
from jax.experimental import pallas as pl
from jax.experimental.pallas import tpu as pltpu
from jax.sharding import PartitionSpec as P

ITERS = 2


cutoff = 6.0
message_scale = 0.125
two_over_root_pi = 2.0 / math.sqrt(math.pi)
inverse_root_pi = 1.0 / math.sqrt(math.pi)
replicate_limit = 1024
everywhere = ("row", "space")


def lookup(species, table):
    result = jnp.zeros(species.shape, jnp.float32)
    for kind in range(table.shape[0]):
        result = result + jnp.where(species == kind, table[kind], 0.0)
    return result


def pair_terms(target, target_labels, source, source_labels):
    delta = target[:3, :, None] - source[:3, None, :]
    squared = jnp.sum(delta * delta, axis=0)
    same = target_labels[:, None] == source_labels[None, :]
    squared = jnp.where(same, 1.0, squared)
    inverse = lax.rsqrt(squared)
    radius = squared * inverse
    spread = target[3][:, None] * target[3][:, None] + source[3][None, :] * source[3][None, :]
    scale = lax.rsqrt(2.0 * spread)
    scaled = radius * scale
    smear = lax.erf(scaled)
    return delta, same, inverse, scale, scaled, smear


def coulomb(target, target_labels, source, source_labels):
    _, same, inverse, _, _, smear = pair_terms(target, target_labels, source, source_labels)
    return jnp.where(same, 0.0, smear * inverse)


def pair_forces(target, target_labels, source, source_labels, source_charge):
    delta, same, inverse, scale, scaled, smear = pair_terms(
        target, target_labels, source, source_labels
    )
    slope = (
        two_over_root_pi * scale * jnp.exp(-scaled * scaled) * inverse - smear * inverse * inverse
    )
    weight = jnp.where(same, 0.0, source_charge[None, :] * slope * inverse)
    first = jnp.sum(weight[None] * delta, axis=2)
    pairs = ((0, 0), (1, 1), (2, 2), (0, 1), (0, 2), (1, 2))
    second = jnp.stack(
        [jnp.sum(weight * delta[left] * delta[right], axis=1) for left, right in pairs]
    )
    return jnp.concatenate([first, second], axis=0)


def edge_terms(receive, sender_rows, vectors, projected, w_rad1, w_rad2, atoms):
    length = jnp.sqrt(jnp.sum(vectors * vectors, axis=0))
    unit = vectors / length
    order = jnp.arange(1, w_rad1.shape[0] + 1, dtype=jnp.int32).astype(jnp.float32)[:, None]
    ratio = length / cutoff
    envelope = (1.0 - ratio * ratio) * (1.0 - ratio * ratio)
    basis = jnp.sin(order * math.pi * ratio) / ratio * envelope
    mixed = lax.dot_general(
        basis, w_rad1, (((0,), (0,)), ((), ())), precision=lax.Precision.HIGHEST
    )
    radial = jax.nn.silu(mixed).astype(jnp.bfloat16)
    filters = jnp.dot(radial, w_rad2, preferred_element_type=jnp.float32)
    picked = jnp.take(projected, sender_rows, axis=0).astype(jnp.float32) * filters
    chans = w_rad1.shape[1]
    scalar = picked[:, :chans]
    carried = picked[:, chans:]
    joined = [
        scalar,
        unit[0][:, None] * carried,
        unit[1][:, None] * carried,
        unit[2][:, None] * carried,
    ]
    message = jnp.concatenate(joined, axis=1).astype(jnp.bfloat16)
    onehot = (jnp.arange(atoms, dtype=jnp.int32)[:, None] == receive[None, :]).astype(jnp.bfloat16)
    return jnp.dot(onehot, message, preferred_element_type=jnp.float32)


def gathered(block, devices):
    copies = jnp.broadcast_to(block[None], (devices,) + block.shape)
    return lax.all_to_all(copies, everywhere, split_axis=0, concat_axis=0, tiled=True)


def shards(
    features,
    positions,
    species,
    ghost_list,
    edge_recv,
    edge_send,
    edge_vec,
    w_msg,
    w_rad1,
    w_rad2,
    w_up,
    w_out,
    hardness,
    width,
    chi_shift,
    field,
):
    atoms = features.shape[0]
    chans = features.shape[1]
    lanes = lax.axis_size("space")
    devices = lanes * lax.axis_size("row")
    everybody = devices * atoms
    me = lax.axis_index("row") * lanes + lax.axis_index("space")
    sigma = lookup(species, width)
    diag = lookup(species, hardness) + inverse_root_pi / sigma
    placed = jnp.concatenate([positions, sigma[None, :], diag[None, :]], axis=0)
    everyone = gathered(placed, devices).transpose(1, 0, 2).reshape(5, everybody)
    lists = ghost_list[0]
    outgoing = jnp.take(features, lists.reshape(-1), axis=0).reshape(lanes, lists.shape[1], chans)
    ghost_rows = jnp.einsum(
        "dkc,cf->dkf",
        lax.all_to_all(outgoing, "space", split_axis=0, concat_axis=0, tiled=True),
        w_msg,
        preferred_element_type=jnp.float32,
    ).astype(jnp.bfloat16)
    own_rows = jnp.dot(features, w_msg, preferred_element_type=jnp.float32).astype(jnp.bfloat16)
    projected = jnp.concatenate([own_rows, ghost_rows.reshape(-1, 2 * chans)], axis=0)
    summed = edge_terms(edge_recv, edge_send, edge_vec, projected, w_rad1, w_rad2, atoms)
    summed = summed * message_scale
    vector_part = summed[:, chans:].reshape(atoms, 3, chans)
    invariant = jnp.concatenate(
        [summed[:, :chans], jnp.sum(vector_part * vector_part, axis=1)], axis=1
    ).astype(jnp.bfloat16)
    hidden = jax.nn.silu(jnp.dot(invariant, w_up, preferred_element_type=jnp.float32))
    new_features = (features.astype(jnp.float32) + hidden).astype(jnp.bfloat16)
    chi = jnp.dot(hidden, w_out, precision=lax.Precision.HIGHEST) + lookup(species, chi_shift)
    own_labels = me * atoms + jnp.arange(atoms, dtype=jnp.int32)
    all_labels = jnp.arange(everybody, dtype=jnp.int32)
    rhs = field[0] * positions[2] - chi

    if everybody <= replicate_limit:
        kernel = coulomb(everyone, all_labels, everyone, all_labels)
        residual = gathered(rhs, devices).reshape(everybody)
        all_charges = conjugate(
            residual, lambda v: everyone[4] * v + jnp.sum(kernel * v[None, :], axis=1), jnp.sum
        )
        charges = lax.dynamic_slice(all_charges, (me * atoms,), (atoms,))
    else:
        kernel = coulomb(placed, own_labels, everyone, all_labels)

        def spread(vector):
            return gathered(vector, devices).reshape(everybody)

        charges = conjugate(
            rhs,
            lambda v: diag * v + jnp.sum(kernel * spread(v)[None, :], axis=1),
            lambda v: lax.psum(jnp.sum(v), everywhere),
        )
        all_charges = spread(charges)
    sums = pair_forces(placed, own_labels, everyone, all_labels, all_charges)
    pull = -charges[None, :] * sums[:3]
    forces = jnp.concatenate([pull[:2], pull[2:] + (charges * field[0])[None, :]], axis=0)
    virial = 0.5 * charges[None, :] * sums[3:]
    return (new_features, charges, forces, virial)


def conjugate(rhs, apply, total):
    charges = jnp.zeros_like(rhs)
    residual = rhs
    direction = rhs
    norm_now = total(residual * residual)
    for step in range(ITERS):
        image = apply(direction)
        alpha = norm_now / total(direction * image)
        charges = charges + alpha * direction
        if step + 1 < ITERS:
            residual = residual - alpha * image
            fresh = total(residual * residual)
            direction = residual + fresh / norm_now * direction
            norm_now = fresh
    return charges


def split3(value):
    first = value.astype(jnp.bfloat16).astype(jnp.float32)
    rest = value - first
    second = rest.astype(jnp.bfloat16).astype(jnp.float32)
    third = (rest - second).astype(jnp.bfloat16).astype(jnp.float32)
    return first, second, third


def over_first(left, right):
    return lax.dot_general(
        left, right, (((0,), (0,)), ((), ())), preferred_element_type=jnp.float32
    )


def over_last(left, right, precision=None):
    return lax.dot_general(
        left,
        right,
        (((1,), (1,)), ((), ())),
        precision=precision,
        preferred_element_type=jnp.float32,
    )


def silu(value):
    return value / (1.0 + jnp.exp(-value))


sine_series = [(-1.0) ** k * math.pi ** (2 * k + 1) / math.factorial(2 * k + 1) for k in range(7)]


def fetched(pairs, semaphores):
    copies = [
        pltpu.make_async_copy(source, target, semaphores.at[place])
        for place, (source, target) in enumerate(pairs)
    ]
    for copy in copies:
        copy.start()
    return copies


def pack_kernel(features_ref, lists_ref, packed_ref, held_ref, semaphores):
    atoms, chans = features_ref.shape
    copies = fetched(
        [(lists_ref, held_ref), (features_ref, packed_ref.at[pl.ds(0, atoms)])], semaphores
    )
    copies[0].wait()
    lists = held_ref[0].astype(jnp.float32)
    rows, width = lists.shape
    lists = jnp.concatenate([lists, jnp.zeros((rows, chans - width), jnp.float32)], axis=1)
    blank = jnp.zeros((packed_ref.shape[0] - atoms - rows, chans), jnp.float32)
    packed_ref[atoms:, :] = jnp.concatenate([lists, blank], axis=0).astype(jnp.bfloat16)
    copies[1].wait()


def edge_kernel(field_ref, *refs):
    own, kept = refs[:8], refs[8:13]
    filter_ref, unit_ref, base_ref = refs[13:16]
    moved, held, semaphores = refs[16:21], refs[21:29], refs[29]
    copies = fetched(list(zip(own + kept, held + moved)), semaphores)
    for copy in copies:
        copy.wait()
    vec_ref, first_ref, second_ref, species_ref = held[:4]
    hardness_ref, width_ref, shift_ref, positions_ref = held[4:]
    edges = vec_ref.shape[1]
    orders = first_ref.shape[0]
    vec = vec_ref[...]
    east, north, up = vec[0:1], vec[1:2], vec[2:3]
    squared = east * east + north * north + up * up
    inverse = lax.rsqrt(squared)
    unit_ref[0:3, :] = vec * inverse
    ratio = squared * inverse * (1.0 / cutoff)
    envelope = (1.0 - ratio * ratio) * (1.0 - ratio * ratio) * (cutoff * inverse)
    order = lax.broadcasted_iota(jnp.int32, (orders, edges), 0).astype(jnp.float32) + 1.0
    turns = order * ratio
    whole = jnp.floor(turns + 0.5)
    part = turns - whole
    sign = 1.0 - 2.0 * (whole - 2.0 * jnp.floor(whole * 0.5))
    series = jnp.full_like(part, sine_series[-1])
    for coefficient in sine_series[-2::-1]:
        series = series * (part * part) + coefficient
    basis = series * part * (sign * envelope)
    b1, b2, b3 = split3(basis)
    w1, w2, w3 = split3(first_ref[...])
    mixed = over_first(
        jnp.concatenate([w1, w1, w2, w2, w1, w3], axis=0).astype(jnp.bfloat16),
        jnp.concatenate([b1, b2, b1, b2, b3, b1], axis=0).astype(jnp.bfloat16),
    )
    radial = silu(mixed).astype(jnp.bfloat16)
    filter_ref[...] = over_first(second_ref[...], radial)
    species = species_ref[...]

    def table(ref):
        result = jnp.zeros(species.shape, jnp.float32)
        for kind in range(ref.shape[1]):
            result = result + jnp.where(species == kind, ref[:, kind : kind + 1], 0.0)
        return result

    positions = positions_ref[...]
    sigma = table(width_ref)
    base_ref[0:3, :] = positions
    base_ref[3:4, :] = sigma
    base_ref[4:5, :] = table(hardness_ref) + inverse_root_pi / sigma
    base_ref[5:6, :] = field_ref[0] * positions[2:3]
    base_ref[6:7, :] = table(shift_ref)
    base_ref[7:8, :] = jnp.zeros_like(sigma)


def node_kernel(
    space_ref,
    own_ref,
    near_ref,
    side_ref,
    far_ref,
    send_ref,
    recv_ref,
    filter_ref,
    unit_ref,
    base_ref,
    project_ref,
    update_ref,
    out_ref,
    features_ref,
    block_ref,
):
    atoms, chans = features_ref.shape
    edges = send_ref.shape[1]
    space = space_ref[0]
    packed = [ref[...].astype(jnp.float32) for ref in (own_ref, near_ref, side_ref, far_ref)]
    lanes = len(packed)
    slots = chans // lanes
    group = jnp.concatenate([value[:atoms] for value in packed], axis=0).astype(jnp.bfloat16)
    picks = jnp.zeros((8, chans), jnp.float32)
    line = lax.broadcasted_iota(jnp.int32, (packed[0].shape[0] - atoms, chans), 0)
    for place, value in enumerate(packed):
        mine = jnp.sum(jnp.where(line == space, value[atoms:], 0.0), axis=0, keepdims=True)
        mine = jnp.broadcast_to(mine, (8, chans))
        picks = picks + (pltpu.roll(mine, place * slots, 1) if place else mine)
    slot_owner = lax.broadcasted_iota(jnp.int32, (1, chans), 1) // slots * atoms
    chosen = slot_owner + picks[0:1].astype(jnp.int32)
    members = lanes * atoms
    fill = jnp.where(
        lax.broadcasted_iota(jnp.int32, (members, chans), 0) == chosen, 1.0, 0.0
    ).astype(jnp.bfloat16)
    send = send_ref[...]
    own = send < atoms
    slot = jnp.where(own, -1, (send - atoms) ^ (space * slots))
    from_slot = jnp.where(
        lax.broadcasted_iota(jnp.int32, (chans, edges), 0) == slot, 1.0, 0.0
    ).astype(jnp.bfloat16)
    from_own = jnp.where(
        lax.broadcasted_iota(jnp.int32, (members, edges), 0) == jnp.where(own, send, -1), 1.0, 0.0
    )
    sender = jnp.dot(fill, from_slot, preferred_element_type=jnp.float32) + from_own
    projected = jnp.dot(group, project_ref[...], preferred_element_type=jnp.float32)
    picked = over_first(projected.astype(jnp.bfloat16), sender.astype(jnp.bfloat16))
    scalar = picked[:chans] * filter_ref[:chans, :]
    carried = picked[chans:] * filter_ref[chans:, :]
    parts = [scalar] + [unit_ref[axis : axis + 1, :] * carried for axis in range(3)]
    message = jnp.concatenate([part.astype(jnp.bfloat16) for part in parts], axis=0)
    hit = lax.broadcasted_iota(jnp.int32, (atoms, edges), 0) == recv_ref[...]
    summed = over_last(jnp.where(hit, 1.0, 0.0).astype(jnp.bfloat16), message) * message_scale
    square = jnp.zeros((atoms, chans), jnp.float32)
    for component in range(1, 4):
        part = summed[:, component * chans : (component + 1) * chans]
        square = square + part * part
    invariant = jnp.concatenate([summed[:, :chans], square], axis=1).astype(jnp.bfloat16)
    hidden = silu(jnp.dot(invariant, update_ref[...], preferred_element_type=jnp.float32))
    features_ref[...] = (packed[0][:atoms] + hidden).astype(jnp.bfloat16)
    readout = jnp.broadcast_to(out_ref[...], (8, chans))
    chi = over_last(readout, hidden, lax.Precision.HIGHEST)[0:1] + base_ref[6:7, :]
    rhs = base_ref[5:6, :] - chi
    wide = jnp.zeros((1, chans - atoms), jnp.float32)
    rows = [base_ref[0:1, :], jnp.zeros((2, atoms), jnp.float32), rhs]
    rows = rows + [base_ref[place : place + 1, :] for place in range(4, 0, -1)]
    block = jnp.concatenate(
        [jnp.concatenate(rows, axis=0), jnp.broadcast_to(wide, (8, chans - atoms))], axis=1
    )
    block = pltpu.roll(block, 0, 1, stride=atoms, stride_axis=0)
    row = jnp.sum(block, axis=0, keepdims=True)
    block_ref[...] = jnp.broadcast_to(row[None], block_ref.shape)


def smeared(scaled):
    decay = jnp.exp(-(scaled * scaled))
    turn = 1.0 / (1.0 + 0.3275911 * scaled)
    series = 1.061405429 * turn - 1.453152027
    series = series * turn + 1.421413741
    series = series * turn - 0.284496736
    series = series * turn + 0.254829592
    return 1.0 - series * turn * decay, decay


def charge_kernel(place_ref, field_ref, all_ref, charges_ref, forces_ref, virial_ref, matrix_ref):
    blocks, _, lanes = all_ref.shape
    own = charges_ref.shape[1]
    count = blocks * own
    fit = lanes // own
    segment = lax.broadcasted_iota(jnp.int32, (8, lanes), 1) // own
    tiles = []
    for first in range(0, blocks, fit):
        tile = jnp.zeros((8, lanes), jnp.float32)
        for place in range(fit):
            row = jnp.broadcast_to(all_ref[first + place], (8, lanes))
            row = pltpu.roll(row, 0, 1, stride=own, stride_axis=0)
            row = pltpu.roll(row, place * own, 1) if place else row
            tile = jnp.where(segment == place, row, tile)
        tiles.append(tile)
    everyone = jnp.concatenate(tiles, axis=1)
    everyone = pltpu.roll(everyone, lax.rem(count - place_ref[0] * own, count), 1)
    columns = everyone.T
    spread_row = everyone[3:4] * everyone[3:4]
    rhs = everyone[5:6]
    diag = everyone[4:5]
    rows = own

    def pairs(start):
        column = columns[start : start + rows]
        delta = [column[:, axis : axis + 1] - everyone[axis : axis + 1] for axis in range(3)]
        squared = delta[0] * delta[0] + delta[1] * delta[1] + delta[2] * delta[2]
        same = lax.broadcasted_iota(jnp.int32, (rows, count), 1) == (
            lax.broadcasted_iota(jnp.int32, (rows, count), 0) + start
        )
        squared = jnp.where(same, 1.0, squared)
        inverse = lax.rsqrt(squared)
        spread = column[:, 3:4] * column[:, 3:4] + spread_row
        scale = lax.rsqrt(2.0 * spread)
        smear, decay = smeared(squared * inverse * scale)
        return delta, same, inverse, scale, jnp.where(same, 0.0, smear * inverse), decay

    image = jnp.zeros((rows, count), jnp.float32)
    for start in range(0, count, rows):
        kernel = pairs(start)[4]
        matrix_ref[start : start + rows, :] = kernel
        image = image + kernel * columns[start : start + rows, 5:6]
    image = diag * rhs + jnp.sum(image, axis=0, keepdims=True)

    def total(value):
        return jnp.sum(value, axis=1, keepdims=True)

    norm = total(rhs * rhs)
    alpha = norm / total(rhs * image)
    residual = rhs - alpha * image
    charges = alpha * rhs
    fresh = total(residual * residual)
    direction = residual + fresh / norm * rhs
    across = jnp.broadcast_to(direction, (8, count)).T
    image = jnp.zeros((rows, count), jnp.float32)
    for start in range(0, count, rows):
        image = image + matrix_ref[start : start + rows, :] * across[start : start + rows, 0:1]
    image = diag * direction + jnp.sum(image, axis=0, keepdims=True)
    charges = charges + fresh / total(direction * image) * direction

    delta, same, inverse, scale, kernel, decay = pairs(0)
    slope = two_over_root_pi * scale * decay * inverse - kernel * inverse
    weight = jnp.where(same, 0.0, charges * slope * inverse)
    pulled = [weight * delta[axis] for axis in range(3)]
    sums = [total(value) for value in pulled]
    for left, right in ((0, 0), (1, 1), (2, 2), (0, 1), (0, 2), (1, 2)):
        sums.append(total(pulled[left] * delta[right]))
    lane = lax.broadcasted_iota(jnp.int32, (rows, 128), 1)
    table = jnp.zeros((rows, 128), jnp.float32)
    for place, value in enumerate(sums):
        table = jnp.where(lane == place, value, table)
    table = table.T
    mine = charges[:, :own]
    charges_ref[...] = mine
    pull = -mine * table[0:3]
    third = lax.broadcasted_iota(jnp.int32, pull.shape, 0) == 2
    forces_ref[...] = pull + jnp.where(third, mine * field_ref[0], 0.0)
    virial_ref[...] = 0.5 * mine * table[3:9]


def kernel_call(kernel, shapes, arguments, scalars=0, far=0, scratch=(), flops=0):
    shapes = tuple(jax.ShapeDtypeStruct(shape, kind) for shape, kind in shapes)
    spaces = [pltpu.SMEM] * scalars + [pltpu.HBM] * far
    spaces = spaces + [pltpu.VMEM] * (len(arguments) - len(spaces))
    arguments = [
        pltpu.with_memory_space_constraint(value, space) if space is pltpu.HBM else value
        for value, space in zip(arguments, spaces)
    ]
    return pl.pallas_call(
        kernel,
        out_shape=shapes,
        in_specs=[pl.BlockSpec(memory_space=space) for space in spaces],
        out_specs=tuple(pl.BlockSpec(memory_space=pltpu.VMEM) for _ in shapes),
        scratch_shapes=list(scratch),
        compiler_params=pltpu.CompilerParams(vmem_limit_bytes=32 * 1024 * 1024),
        cost_estimate=pl.CostEstimate(flops=flops, bytes_accessed=1 << 20, transcendentals=0),
    )(*arguments)


def shape_of(value):
    return (value.shape, value.dtype)


def exchanged(block, axis, step):
    size = lax.axis_size(axis)
    return lax.ppermute(block, axis, [(place, place ^ step) for place in range(size)])


def few_shards(
    features,
    positions,
    species,
    ghost_list,
    edge_recv,
    edge_send,
    edge_vec,
    w_msg,
    w_rad1,
    w_rad2,
    w_up,
    w_out,
    hardness,
    width,
    chi_shift,
    field,
):
    atoms, chans = features.shape
    edges = edge_recv.shape[0]
    rows, lanes = lax.axis_size("row"), lax.axis_size("space")
    (packed,) = kernel_call(
        pack_kernel,
        [((atoms + 16, chans), jnp.bfloat16)],
        (features, ghost_list),
        far=2,
        scratch=[pltpu.VMEM(*shape_of(ghost_list)), pltpu.SemaphoreType.DMA((2,))],
    )
    others = [exchanged(packed, "space", step) for step in range(1, lanes)]
    own = (edge_vec, w_rad1, w_rad2, species[None], hardness[None], width[None])
    own = own + (chi_shift[None], positions)
    kept = (edge_send[None], edge_recv[None], w_msg, w_up, w_out[None])
    filters, units, base, *kept = kernel_call(
        edge_kernel,
        [((2 * chans, edges), jnp.float32), ((8, edges), jnp.float32), ((8, atoms), jnp.float32)]
        + [shape_of(value) for value in kept],
        (field,) + own + kept,
        scalars=1,
        far=len(own + kept),
        scratch=[pltpu.VMEM(*shape_of(value)) for value in own]
        + [pltpu.SemaphoreType.DMA((len(own + kept),))],
        flops=1 << 28,
    )
    send, receive, project, update, readout = kept
    space = lax.axis_index("space").astype(jnp.int32)
    devices = rows * lanes
    new_features, block = kernel_call(
        node_kernel,
        [((atoms, chans), jnp.bfloat16), ((devices, 1, chans), jnp.float32)],
        (space.reshape(1), packed, *others, send, receive)
        + (filters, units, base, project, update, readout),
        scalars=1,
        flops=1 << 28,
    )
    block = lax.all_to_all(block, everywhere, 0, 0, tiled=True)
    place = lax.axis_index("row").astype(jnp.int32) * lanes + space
    everybody = rows * lanes * atoms
    charges, forces, virial = kernel_call(
        charge_kernel,
        [((count, atoms), jnp.float32) for count in (1, 3, 6)],
        (place.reshape(1), field, block),
        scalars=2,
        scratch=[pltpu.VMEM((everybody, everybody), jnp.float32)],
        flops=1 << 28,
    )
    return (new_features, charges[0], forces, virial)


def solution(mesh):
    small = mesh.shape["space"] == 4 and mesh.shape["row"] == 8
    return jax.shard_map(
        few_shards if small else shards,
        mesh=mesh,
        in_specs=(
            P(("row", "space"), None),
            P(None, ("row", "space")),
            P(("row", "space")),
            P("row", "space", None),
            P(("row", "space")),
            P(("row", "space")),
            P(None, ("row", "space")),
            P(),
            P(),
            P(),
            P(),
            P(),
            P(),
            P(),
            P(),
            P(),
        ),
        out_specs=(
            P(("row", "space"), None),
            P(("row", "space")),
            P(None, ("row", "space")),
            P(None, ("row", "space")),
        ),
        check_vma=False,
    )
```

```python
import math

import jax
import jax.numpy as jnp
from jax import lax
from jax.experimental import pallas as pl
from jax.experimental.pallas import tpu as pltpu
from jax.sharding import PartitionSpec as P

ITERS = 2


cutoff = 6.0
message_scale = 0.125
two_over_root_pi = 2.0 / math.sqrt(math.pi)
inverse_root_pi = 1.0 / math.sqrt(math.pi)
replicate_limit = 1024
everywhere = ("row", "space")


def lookup(species, table):
    result = jnp.zeros(species.shape, jnp.float32)
    for kind in range(table.shape[0]):
        result = result + jnp.where(species == kind, table[kind], 0.0)
    return result


def pair_terms(target, target_labels, source, source_labels):
    delta = target[:3, :, None] - source[:3, None, :]
    squared = jnp.sum(delta * delta, axis=0)
    same = target_labels[:, None] == source_labels[None, :]
    squared = jnp.where(same, 1.0, squared)
    inverse = lax.rsqrt(squared)
    radius = squared * inverse
    spread = target[3][:, None] * target[3][:, None] + source[3][None, :] * source[3][None, :]
    scale = lax.rsqrt(2.0 * spread)
    scaled = radius * scale
    smear = lax.erf(scaled)
    return delta, same, inverse, scale, scaled, smear


def coulomb(target, target_labels, source, source_labels):
    _, same, inverse, _, _, smear = pair_terms(target, target_labels, source, source_labels)
    return jnp.where(same, 0.0, smear * inverse)


def pair_forces(target, target_labels, source, source_labels, source_charge):
    delta, same, inverse, scale, scaled, smear = pair_terms(
        target, target_labels, source, source_labels
    )
    slope = (
        two_over_root_pi * scale * jnp.exp(-scaled * scaled) * inverse - smear * inverse * inverse
    )
    weight = jnp.where(same, 0.0, source_charge[None, :] * slope * inverse)
    first = jnp.sum(weight[None] * delta, axis=2)
    pairs = ((0, 0), (1, 1), (2, 2), (0, 1), (0, 2), (1, 2))
    second = jnp.stack(
        [jnp.sum(weight * delta[left] * delta[right], axis=1) for left, right in pairs]
    )
    return jnp.concatenate([first, second], axis=0)


def edge_terms(receive, sender_rows, vectors, projected, w_rad1, w_rad2, atoms):
    length = jnp.sqrt(jnp.sum(vectors * vectors, axis=0))
    unit = vectors / length
    order = jnp.arange(1, w_rad1.shape[0] + 1, dtype=jnp.int32).astype(jnp.float32)[:, None]
    ratio = length / cutoff
    envelope = (1.0 - ratio * ratio) * (1.0 - ratio * ratio)
    basis = jnp.sin(order * math.pi * ratio) / ratio * envelope
    mixed = lax.dot_general(
        basis, w_rad1, (((0,), (0,)), ((), ())), precision=lax.Precision.HIGHEST
    )
    radial = jax.nn.silu(mixed).astype(jnp.bfloat16)
    filters = jnp.dot(radial, w_rad2, preferred_element_type=jnp.float32)
    picked = jnp.take(projected, sender_rows, axis=0).astype(jnp.float32) * filters
    chans = w_rad1.shape[1]
    scalar = picked[:, :chans]
    carried = picked[:, chans:]
    joined = [
        scalar,
        unit[0][:, None] * carried,
        unit[1][:, None] * carried,
        unit[2][:, None] * carried,
    ]
    message = jnp.concatenate(joined, axis=1).astype(jnp.bfloat16)
    onehot = (jnp.arange(atoms, dtype=jnp.int32)[:, None] == receive[None, :]).astype(jnp.bfloat16)
    return jnp.dot(onehot, message, preferred_element_type=jnp.float32)


def gathered(block, devices):
    copies = jnp.broadcast_to(block[None], (devices,) + block.shape)
    return lax.all_to_all(copies, everywhere, split_axis=0, concat_axis=0, tiled=True)


def shards(
    features,
    positions,
    species,
    ghost_list,
    edge_recv,
    edge_send,
    edge_vec,
    w_msg,
    w_rad1,
    w_rad2,
    w_up,
    w_out,
    hardness,
    width,
    chi_shift,
    field,
):
    atoms = features.shape[0]
    chans = features.shape[1]
    lanes = lax.axis_size("space")
    devices = lanes * lax.axis_size("row")
    everybody = devices * atoms
    me = lax.axis_index("row") * lanes + lax.axis_index("space")
    sigma = lookup(species, width)
    diag = lookup(species, hardness) + inverse_root_pi / sigma
    placed = jnp.concatenate([positions, sigma[None, :], diag[None, :]], axis=0)
    everyone = gathered(placed, devices).transpose(1, 0, 2).reshape(5, everybody)
    lists = ghost_list[0]
    outgoing = jnp.take(features, lists.reshape(-1), axis=0).reshape(lanes, lists.shape[1], chans)
    ghost_rows = jnp.einsum(
        "dkc,cf->dkf",
        lax.all_to_all(outgoing, "space", split_axis=0, concat_axis=0, tiled=True),
        w_msg,
        preferred_element_type=jnp.float32,
    ).astype(jnp.bfloat16)
    own_rows = jnp.dot(features, w_msg, preferred_element_type=jnp.float32).astype(jnp.bfloat16)
    projected = jnp.concatenate([own_rows, ghost_rows.reshape(-1, 2 * chans)], axis=0)
    summed = edge_terms(edge_recv, edge_send, edge_vec, projected, w_rad1, w_rad2, atoms)
    summed = summed * message_scale
    vector_part = summed[:, chans:].reshape(atoms, 3, chans)
    invariant = jnp.concatenate(
        [summed[:, :chans], jnp.sum(vector_part * vector_part, axis=1)], axis=1
    ).astype(jnp.bfloat16)
    hidden = jax.nn.silu(jnp.dot(invariant, w_up, preferred_element_type=jnp.float32))
    new_features = (features.astype(jnp.float32) + hidden).astype(jnp.bfloat16)
    chi = jnp.dot(hidden, w_out, precision=lax.Precision.HIGHEST) + lookup(species, chi_shift)
    own_labels = me * atoms + jnp.arange(atoms, dtype=jnp.int32)
    all_labels = jnp.arange(everybody, dtype=jnp.int32)
    rhs = field[0] * positions[2] - chi

    if everybody <= replicate_limit:
        kernel = coulomb(everyone, all_labels, everyone, all_labels)
        residual = gathered(rhs, devices).reshape(everybody)
        all_charges = conjugate(
            residual, lambda v: everyone[4] * v + jnp.sum(kernel * v[None, :], axis=1), jnp.sum
        )
        charges = lax.dynamic_slice(all_charges, (me * atoms,), (atoms,))
    else:
        kernel = coulomb(placed, own_labels, everyone, all_labels)

        def spread(vector):
            return gathered(vector, devices).reshape(everybody)

        charges = conjugate(
            rhs,
            lambda v: diag * v + jnp.sum(kernel * spread(v)[None, :], axis=1),
            lambda v: lax.psum(jnp.sum(v), everywhere),
        )
        all_charges = spread(charges)
    sums = pair_forces(placed, own_labels, everyone, all_labels, all_charges)
    pull = -charges[None, :] * sums[:3]
    forces = jnp.concatenate([pull[:2], pull[2:] + (charges * field[0])[None, :]], axis=0)
    virial = 0.5 * charges[None, :] * sums[3:]
    return (new_features, charges, forces, virial)


def conjugate(rhs, apply, total):
    charges = jnp.zeros_like(rhs)
    residual = rhs
    direction = rhs
    norm_now = total(residual * residual)
    for step in range(ITERS):
        image = apply(direction)
        alpha = norm_now / total(direction * image)
        charges = charges + alpha * direction
        if step + 1 < ITERS:
            residual = residual - alpha * image
            fresh = total(residual * residual)
            direction = residual + fresh / norm_now * direction
            norm_now = fresh
    return charges


def split3(value):
    first = value.astype(jnp.bfloat16).astype(jnp.float32)
    rest = value - first
    second = rest.astype(jnp.bfloat16).astype(jnp.float32)
    third = (rest - second).astype(jnp.bfloat16).astype(jnp.float32)
    return first, second, third


def over_first(left, right):
    return lax.dot_general(
        left, right, (((0,), (0,)), ((), ())), preferred_element_type=jnp.float32
    )


def over_last(left, right, precision=None):
    return lax.dot_general(
        left,
        right,
        (((1,), (1,)), ((), ())),
        precision=precision,
        preferred_element_type=jnp.float32,
    )


def silu(value):
    return value / (1.0 + jnp.exp(-value))


def silu_half(value):
    return (0.5 * value) * (1.0 + jnp.tanh(0.5 * value))


sine_series = [(-1.0) ** k * math.pi ** (2 * k + 1) / math.factorial(2 * k + 1) for k in range(7)]


def fetched(pairs, semaphores):
    copies = [
        pltpu.make_async_copy(source, target, semaphores.at[place])
        for place, (source, target) in enumerate(pairs)
    ]
    for copy in copies:
        copy.start()
    return copies


rhs_segment = 3


def pack_kernel(*refs):
    count = (len(refs) - 3) // 2
    features_ref, lists_ref, packed_ref = refs[0], refs[1], refs[count + 1]
    held_ref, semaphores = refs[-2:]
    atoms, chans = features_ref.shape
    pairs = [(lists_ref, held_ref), (features_ref, packed_ref.at[pl.ds(0, atoms)])]
    copies = fetched(pairs + list(zip(refs[2 : count + 1], refs[count + 2 : -2])), semaphores)
    copies[0].wait()
    lists = held_ref[0].astype(jnp.float32)
    rows, width = lists.shape
    lists = jnp.concatenate([lists, jnp.zeros((rows, chans - width), jnp.float32)], axis=1)
    blank = jnp.zeros((packed_ref.shape[0] - atoms - rows, chans), jnp.float32)
    packed_ref[atoms:, :] = jnp.concatenate([lists, blank], axis=0).astype(jnp.bfloat16)
    for copy in copies[1:]:
        copy.wait()


def edge_kernel(
    field_ref,
    space_ref,
    vec_ref,
    first_ref,
    second_ref,
    species_ref,
    hardness_ref,
    width_ref,
    shift_ref,
    positions_ref,
    send_ref,
    recv_ref,
    project_ref,
    filter_ref,
    unit_ref,
    row_ref,
    slot_ref,
    local_ref,
    hit_ref,
    turned_ref,
):
    edges = vec_ref.shape[1]
    orders = first_ref.shape[0]
    vec = vec_ref[...]
    east, north, up = vec[0:1], vec[1:2], vec[2:3]
    squared = east * east + north * north + up * up
    inverse = lax.rsqrt(squared)
    unit_ref[0:3, :] = vec * inverse
    ratio = squared * inverse * (1.0 / cutoff)
    envelope = (1.0 - ratio * ratio) * (1.0 - ratio * ratio) * (cutoff * inverse)
    order = lax.broadcasted_iota(jnp.int32, (orders, edges), 0).astype(jnp.float32) + 1.0
    turns = order * ratio
    whole = jnp.floor(turns + 0.5)
    part = turns - whole
    sign = 1.0 - 2.0 * (whole - 2.0 * jnp.floor(whole * 0.5))
    series = jnp.full_like(part, sine_series[-1])
    for coefficient in sine_series[-2::-1]:
        series = series * (part * part) + coefficient
    basis = series * part * (sign * envelope)
    b1, b2, b3 = split3(basis)
    w1, w2, w3 = split3(first_ref[...])
    mixed = over_first(
        jnp.concatenate([w1, w1, w2, w2, w1, w3], axis=0).astype(jnp.bfloat16),
        jnp.concatenate([b1, b2, b1, b2, b3, b1], axis=0).astype(jnp.bfloat16),
    )
    radial = silu_half(mixed).astype(jnp.bfloat16)
    filter_ref[...] = over_first(second_ref[...], radial)
    species = species_ref[...]

    def table(ref):
        result = jnp.zeros(species.shape, jnp.float32)
        for kind in range(ref.shape[1]):
            result = result + jnp.where(species == kind, ref[:, kind : kind + 1], 0.0)
        return result

    positions = positions_ref[...]
    sigma = table(width_ref)
    atoms = species.shape[1]
    chans = row_ref.shape[1]
    diag = table(hardness_ref) + inverse_root_pi / sigma
    rhs = field_ref[0] * positions[2:3] - table(shift_ref)
    blank = jnp.zeros((2, atoms), jnp.float32)
    rows = [positions[0:1], blank, rhs, diag, sigma, positions[2:3], positions[1:2]]
    block = jnp.concatenate(
        [jnp.concatenate(rows, axis=0), jnp.zeros((8, chans - atoms), jnp.float32)], axis=1
    )
    block = pltpu.roll(block, 0, 1, stride=atoms, stride_axis=0)
    row_ref[...] = jnp.sum(block, axis=0, keepdims=True)
    lanes = local_ref.shape[0] // atoms
    slots = chans // lanes
    send = send_ref[...]
    own = send < atoms
    slot = jnp.where(own, -1, (send - atoms) ^ (space_ref[0] * slots))
    local = jnp.where(own, send, -1)

    def chosen(ref, index):
        hit = lax.broadcasted_iota(jnp.int32, ref.shape, 0) == index
        ref[...] = jnp.where(hit, 1.0, 0.0).astype(ref.dtype)

    chosen(slot_ref, slot)
    chosen(local_ref, local)
    chosen(hit_ref, recv_ref[...])
    turned_ref[...] = project_ref[...].astype(jnp.float32).T.astype(jnp.bfloat16)


def node_kernel(
    space_ref,
    own_ref,
    near_ref,
    side_ref,
    far_ref,
    filter_ref,
    unit_ref,
    row_ref,
    slot_ref,
    local_ref,
    hit_ref,
    turned_ref,
    update_ref,
    out_ref,
    features_ref,
    block_ref,
):
    atoms, chans = features_ref.shape
    space = space_ref[0]
    packed = [ref[...].astype(jnp.float32) for ref in (own_ref, near_ref, side_ref, far_ref)]
    lanes = len(packed)
    slots = chans // lanes
    group = jnp.concatenate([value[:atoms] for value in packed], axis=0).astype(jnp.bfloat16)
    picks = jnp.zeros((8, chans), jnp.float32)
    line = lax.broadcasted_iota(jnp.int32, (8, chans), 0)
    for place, value in enumerate(packed):
        mine = jnp.where(line == space, value[atoms : atoms + 8], 0.0)
        picks = picks + (pltpu.roll(mine, place * slots, 1) if place else mine)
    slot_owner = lax.broadcasted_iota(jnp.int32, (1, chans), 1) // slots * atoms
    chosen = slot_owner + jnp.sum(picks, axis=0, keepdims=True).astype(jnp.int32)
    fill = jnp.where(
        lax.broadcasted_iota(jnp.int32, (lanes * atoms, chans), 0) == chosen, 1.0, 0.0
    ).astype(jnp.bfloat16)
    sender = jnp.dot(fill, slot_ref[...], preferred_element_type=jnp.float32) + local_ref[...]
    projected = over_last(turned_ref[...], group).astype(jnp.bfloat16)
    picked = jnp.dot(projected, sender.astype(jnp.bfloat16), preferred_element_type=jnp.float32)
    scalar = picked[:chans] * filter_ref[:chans, :]
    carried = picked[chans:] * filter_ref[chans:, :]
    parts = [scalar] + [unit_ref[axis : axis + 1, :] * carried for axis in range(3)]
    message = jnp.concatenate([part.astype(jnp.bfloat16) for part in parts], axis=0)
    summed = over_last(hit_ref[...], message) * message_scale
    square = jnp.zeros((atoms, chans), jnp.float32)
    for component in range(1, 4):
        part = summed[:, component * chans : (component + 1) * chans]
        square = square + part * part
    invariant = jnp.concatenate([summed[:, :chans], square], axis=1).astype(jnp.bfloat16)
    hidden = silu(jnp.dot(invariant, update_ref[...], preferred_element_type=jnp.float32))
    features_ref[...] = (packed[0][:atoms] + hidden).astype(jnp.bfloat16)
    chi = jnp.sum(hidden * out_ref[...], axis=1, keepdims=True)
    lane = lax.broadcasted_iota(jnp.int32, (atoms, chans), 1)
    atom = lax.broadcasted_iota(jnp.int32, (atoms, chans), 0)
    place = lane == atom + rhs_segment * atoms
    row = row_ref[...] - jnp.sum(jnp.where(place, chi, 0.0), axis=0, keepdims=True)
    block_ref[...] = jnp.broadcast_to(row[None], block_ref.shape)


def reciprocal(value):
    rough = pl.reciprocal(value, approx=True)
    return rough * (2.0 - value * rough)


def smeared(scaled):
    decay = jnp.exp2(scaled * scaled * -math.log2(math.e))
    turn = reciprocal(1.0 + 0.3275911 * scaled)
    series = 1.061405429 * turn - 1.453152027
    series = series * turn + 1.421413741
    series = series * turn - 0.284496736
    series = series * turn + 0.254829592
    return 1.0 - series * turn * decay, decay


def charge_kernel(
    place_ref, field_ref, all_ref, charges_ref, forces_ref, virial_ref, matrix_ref, side_ref
):
    blocks, _, lanes = all_ref.shape
    own = charges_ref.shape[1]
    count = blocks * own
    fit = lanes // own
    segment = lax.broadcasted_iota(jnp.int32, (8, lanes), 1) // own
    tiles = []
    for first in range(0, blocks, fit):
        tile = jnp.zeros((8, lanes), jnp.float32)
        for place in range(fit):
            row = jnp.broadcast_to(all_ref[first + place], (8, lanes))
            row = pltpu.roll(row, 0, 1, stride=own, stride_axis=0)
            row = pltpu.roll(row, place * own, 1) if place else row
            tile = jnp.where(segment == place, row, tile)
        tiles.append(tile)
    everyone = jnp.concatenate(tiles, axis=1)
    everyone = pltpu.roll(everyone, lax.rem(count - place_ref[0] * own, count), 1)
    columns = everyone.T
    diag, rhs = everyone[4:5], everyone[5:6]
    rows = own
    spread_row = 2.0 * everyone[3:4] * everyone[3:4]
    tiles = count // lanes
    lane = lax.broadcasted_iota(jnp.int32, (rows, lanes), 1)
    line = lax.broadcasted_iota(jnp.int32, (rows, lanes), 0)

    def part(row, tile):
        return row[:, tile * lanes : (tile + 1) * lanes]

    def spread(column):
        return jnp.broadcast_to(column, (rows, lanes))

    above = [jnp.zeros((rows, lanes), jnp.float32) for _ in range(tiles)]
    kept = []
    for start in range(0, count, rows):
        first = start // lanes
        column = columns[start : start + rows]
        place = [spread(column[:, axis : axis + 1]) for axis in range(3)]
        wide = spread(2.0 * column[:, 3:4] * column[:, 3:4])
        value = spread(column[:, 5:6])
        below = jnp.zeros((rows, lanes), jnp.float32)
        for tile in range(first, tiles):
            delta = [place[axis] - part(everyone[axis : axis + 1], tile) for axis in range(3)]
            squared = delta[0] * delta[0] + delta[1] * delta[1] + delta[2] * delta[2]
            if tile == first:
                same = lane == line + (start - first * lanes)
                squared = jnp.where(same, 1.0, squared)
            inverse = lax.rsqrt(squared)
            scale = lax.rsqrt(wide + part(spread_row, tile))
            smear, decay = smeared(squared * inverse * scale)
            kernel = smear * inverse
            if start == 0:
                slope = (two_over_root_pi * scale * decay - kernel) * inverse * inverse
                slope = jnp.where(same, 0.0, slope) if tile == first else slope
                kept.append((delta, slope))
            if tile == first:
                kernel = jnp.where(same, 0.0, kernel)
            else:
                below = below + kernel * part(rhs, tile)
            above[tile] = above[tile] + kernel * value
            matrix_ref[start : start + rows, tile * lanes : (tile + 1) * lanes] = kernel
        if first + 1 < tiles:
            side_ref[start : start + rows, :] = below
    image = []
    for tile in range(tiles):
        value = jnp.sum(above[tile], axis=0, keepdims=True)
        if tile + 1 < tiles:
            below = side_ref[tile * lanes : (tile + 1) * lanes, :].T
            value = value + jnp.sum(below, axis=0, keepdims=True)
        image.append(value)
    image = diag * rhs + jnp.concatenate(image, axis=1)

    def total(value):
        return jnp.sum(value, axis=1, keepdims=True)

    norm = total(rhs * rhs)
    alpha = norm / total(rhs * image)
    residual = rhs - alpha * image
    fresh = total(residual * residual)
    direction = residual + fresh / norm * rhs
    across = jnp.broadcast_to(direction, (8, count)).T
    onto = [jnp.zeros((rows, lanes), jnp.float32) for _ in range(tiles)]
    above = [jnp.zeros((rows, lanes), jnp.float32) for _ in range(tiles)]
    for start in range(0, count, rows):
        first = start // lanes
        value = spread(across[start : start + rows, 0:1])
        for tile in range(first, tiles):
            sums = onto if tile == first else above
            kernel = matrix_ref[start : start + rows, tile * lanes : (tile + 1) * lanes]
            sums[tile] = sums[tile] + kernel * value
    curved = jnp.zeros((rows, lanes), jnp.float32)
    for tile in range(tiles):
        curved = curved + (onto[tile] + 2.0 * above[tile]) * part(direction, tile)
    curved = jnp.sum(curved, axis=0, keepdims=True)
    for tile in range(tiles):
        curved = curved + part(diag * direction * direction, tile)
    charges = alpha * rhs + fresh / total(curved) * direction

    sums = [jnp.zeros((rows, lanes), jnp.float32) for _ in range(9)]
    for tile, (delta, slope) in enumerate(kept):
        weight = part(charges, tile) * slope
        pulled = [weight * delta[axis] for axis in range(3)]
        terms = pulled + [
            pulled[left] * delta[right]
            for left, right in ((0, 0), (1, 1), (2, 2), (0, 1), (0, 2), (1, 2))
        ]
        sums = [old + term for old, term in zip(sums, terms)]
    table = jnp.zeros((rows, lanes), jnp.float32)
    for place, value in enumerate(sums):
        table = jnp.where(lane == place, total(value), table)
    table = table.T
    mine = charges[:, :own]
    charges_ref[...] = mine
    pull = -mine * table[0:3]
    third = lax.broadcasted_iota(jnp.int32, pull.shape, 0) == 2
    forces_ref[...] = pull + jnp.where(third, mine * field_ref[0], 0.0)
    virial_ref[...] = 0.5 * mine * table[3:9]


def kernel_call(kernel, shapes, arguments, scalars=0, far=0, scratch=(), flops=0):
    shapes = tuple(jax.ShapeDtypeStruct(shape, kind) for shape, kind in shapes)
    spaces = [pltpu.SMEM] * scalars + [pltpu.HBM] * far
    spaces = spaces + [pltpu.VMEM] * (len(arguments) - len(spaces))
    arguments = [
        pltpu.with_memory_space_constraint(value, space) if space is pltpu.HBM else value
        for value, space in zip(arguments, spaces)
    ]
    return pl.pallas_call(
        kernel,
        out_shape=shapes,
        in_specs=[pl.BlockSpec(memory_space=space) for space in spaces],
        out_specs=tuple(pl.BlockSpec(memory_space=pltpu.VMEM) for _ in shapes),
        scratch_shapes=list(scratch),
        compiler_params=pltpu.CompilerParams(vmem_limit_bytes=32 * 1024 * 1024),
        cost_estimate=pl.CostEstimate(flops=flops, bytes_accessed=1 << 20, transcendentals=0),
    )(*arguments)


def exchanged(block, axis, step):
    size = lax.axis_size(axis)
    return lax.ppermute(block, axis, [(place, place ^ step) for place in range(size)])


def few_shards(
    features,
    positions,
    species,
    ghost_list,
    edge_recv,
    edge_send,
    edge_vec,
    w_msg,
    w_rad1,
    w_rad2,
    w_up,
    w_out,
    hardness,
    width,
    chi_shift,
    field,
):
    atoms, chans = features.shape
    edges = edge_recv.shape[0]
    rows, lanes = lax.axis_size("row"), lax.axis_size("space")
    rest = (edge_vec, w_rad1, w_rad2, species[None], hardness[None], width[None])
    rest = rest + (chi_shift[None], positions, edge_send[None], edge_recv[None], w_msg)
    rest = rest + (w_up, w_out[None])
    packed, *rest = kernel_call(
        pack_kernel,
        [((atoms + 16, chans), jnp.bfloat16)] + [(value.shape, value.dtype) for value in rest],
        (features, ghost_list) + rest,
        far=2 + len(rest),
        scratch=[
            pltpu.VMEM(ghost_list.shape, ghost_list.dtype),
            pltpu.SemaphoreType.DMA((2 + len(rest),)),
        ],
    )
    others = [exchanged(packed, "space", step) for step in range(1, lanes)]
    space = lax.axis_index("space").astype(jnp.int32)
    parts = kernel_call(
        edge_kernel,
        [
            ((2 * chans, edges), jnp.float32),
            ((8, edges), jnp.float32),
            ((1, chans), jnp.float32),
            ((chans, edges), jnp.bfloat16),
            ((lanes * atoms, edges), jnp.float32),
            ((atoms, edges), jnp.bfloat16),
            ((2 * chans, chans), jnp.bfloat16),
        ],
        (field, space.reshape(1), *rest[:-2]),
        scalars=2,
        flops=1 << 28,
    )
    devices = rows * lanes
    new_features, block = kernel_call(
        node_kernel,
        [((atoms, chans), jnp.bfloat16), ((devices, 1, chans), jnp.float32)],
        (space.reshape(1), packed, *others, *parts, *rest[-2:]),
        scalars=1,
        flops=1 << 28,
    )
    block = lax.all_to_all(block, everywhere, 0, 0, tiled=True)
    place = lax.axis_index("row").astype(jnp.int32) * lanes + space
    everybody = rows * lanes * atoms
    charges, forces, virial = kernel_call(
        charge_kernel,
        [((count, atoms), jnp.float32) for count in (1, 3, 6)],
        (place.reshape(1), field, block),
        scalars=2,
        scratch=[
            pltpu.VMEM((everybody, everybody), jnp.float32),
            pltpu.VMEM((everybody, chans), jnp.float32),
        ],
        flops=1 << 28,
    )
    return (new_features, charges[0], forces, virial)


def solution(mesh):
    small = mesh.shape["space"] == 4 and mesh.shape["row"] == 8
    return jax.shard_map(
        few_shards if small else shards,
        mesh=mesh,
        in_specs=(
            P(("row", "space"), None),
            P(None, ("row", "space")),
            P(("row", "space")),
            P("row", "space", None),
            P(("row", "space")),
            P(("row", "space")),
            P(None, ("row", "space")),
            P(),
            P(),
            P(),
            P(),
            P(),
            P(),
            P(),
            P(),
            P(),
        ),
        out_specs=(
            P(("row", "space"), None),
            P(("row", "space")),
            P(None, ("row", "space")),
            P(None, ("row", "space")),
        ),
        check_vma=False,
    )
```

```python
import math

import jax
import jax.numpy as jnp
from jax import lax
from jax.experimental import pallas as pl
from jax.experimental.pallas import tpu as pltpu
from jax.sharding import PartitionSpec as P

ITERS = 2


cutoff = 6.0
message_scale = 0.125
two_over_root_pi = 2.0 / math.sqrt(math.pi)
inverse_root_pi = 1.0 / math.sqrt(math.pi)
replicate_limit = 1024
everywhere = ("row", "space")


def lookup(species, table):
    result = jnp.zeros(species.shape, jnp.float32)
    for kind in range(table.shape[0]):
        result = result + jnp.where(species == kind, table[kind], 0.0)
    return result


def pair_terms(target, target_labels, source, source_labels):
    delta = target[:3, :, None] - source[:3, None, :]
    squared = jnp.sum(delta * delta, axis=0)
    same = target_labels[:, None] == source_labels[None, :]
    squared = jnp.where(same, 1.0, squared)
    inverse = lax.rsqrt(squared)
    radius = squared * inverse
    spread = target[3][:, None] * target[3][:, None] + source[3][None, :] * source[3][None, :]
    scale = lax.rsqrt(2.0 * spread)
    scaled = radius * scale
    smear = lax.erf(scaled)
    return delta, same, inverse, scale, scaled, smear


def coulomb(target, target_labels, source, source_labels):
    _, same, inverse, _, _, smear = pair_terms(target, target_labels, source, source_labels)
    return jnp.where(same, 0.0, smear * inverse)


def pair_forces(target, target_labels, source, source_labels, source_charge):
    delta, same, inverse, scale, scaled, smear = pair_terms(
        target, target_labels, source, source_labels
    )
    slope = (
        two_over_root_pi * scale * jnp.exp(-scaled * scaled) * inverse - smear * inverse * inverse
    )
    weight = jnp.where(same, 0.0, source_charge[None, :] * slope * inverse)
    first = jnp.sum(weight[None] * delta, axis=2)
    pairs = ((0, 0), (1, 1), (2, 2), (0, 1), (0, 2), (1, 2))
    second = jnp.stack(
        [jnp.sum(weight * delta[left] * delta[right], axis=1) for left, right in pairs]
    )
    return jnp.concatenate([first, second], axis=0)


def edge_terms(receive, sender_rows, vectors, projected, w_rad1, w_rad2, atoms):
    length = jnp.sqrt(jnp.sum(vectors * vectors, axis=0))
    unit = vectors / length
    order = jnp.arange(1, w_rad1.shape[0] + 1, dtype=jnp.int32).astype(jnp.float32)[:, None]
    ratio = length / cutoff
    envelope = (1.0 - ratio * ratio) * (1.0 - ratio * ratio)
    basis = jnp.sin(order * math.pi * ratio) / ratio * envelope
    mixed = lax.dot_general(
        basis, w_rad1, (((0,), (0,)), ((), ())), precision=lax.Precision.HIGHEST
    )
    radial = jax.nn.silu(mixed).astype(jnp.bfloat16)
    filters = jnp.dot(radial, w_rad2, preferred_element_type=jnp.float32)
    picked = jnp.take(projected, sender_rows, axis=0).astype(jnp.float32) * filters
    chans = w_rad1.shape[1]
    scalar = picked[:, :chans]
    carried = picked[:, chans:]
    joined = [
        scalar,
        unit[0][:, None] * carried,
        unit[1][:, None] * carried,
        unit[2][:, None] * carried,
    ]
    message = jnp.concatenate(joined, axis=1).astype(jnp.bfloat16)
    onehot = (jnp.arange(atoms, dtype=jnp.int32)[:, None] == receive[None, :]).astype(jnp.bfloat16)
    return jnp.dot(onehot, message, preferred_element_type=jnp.float32)


def gathered(block, devices):
    copies = jnp.broadcast_to(block[None], (devices,) + block.shape)
    return lax.all_to_all(copies, everywhere, split_axis=0, concat_axis=0, tiled=True)


def shards(
    features,
    positions,
    species,
    ghost_list,
    edge_recv,
    edge_send,
    edge_vec,
    w_msg,
    w_rad1,
    w_rad2,
    w_up,
    w_out,
    hardness,
    width,
    chi_shift,
    field,
):
    atoms = features.shape[0]
    chans = features.shape[1]
    lanes = lax.axis_size("space")
    devices = lanes * lax.axis_size("row")
    everybody = devices * atoms
    me = lax.axis_index("row") * lanes + lax.axis_index("space")
    sigma = lookup(species, width)
    diag = lookup(species, hardness) + inverse_root_pi / sigma
    placed = jnp.concatenate([positions, sigma[None, :], diag[None, :]], axis=0)
    everyone = gathered(placed, devices).transpose(1, 0, 2).reshape(5, everybody)
    lists = ghost_list[0]
    outgoing = jnp.take(features, lists.reshape(-1), axis=0).reshape(lanes, lists.shape[1], chans)
    ghost_rows = jnp.einsum(
        "dkc,cf->dkf",
        lax.all_to_all(outgoing, "space", split_axis=0, concat_axis=0, tiled=True),
        w_msg,
        preferred_element_type=jnp.float32,
    ).astype(jnp.bfloat16)
    own_rows = jnp.dot(features, w_msg, preferred_element_type=jnp.float32).astype(jnp.bfloat16)
    projected = jnp.concatenate([own_rows, ghost_rows.reshape(-1, 2 * chans)], axis=0)
    summed = edge_terms(edge_recv, edge_send, edge_vec, projected, w_rad1, w_rad2, atoms)
    summed = summed * message_scale
    vector_part = summed[:, chans:].reshape(atoms, 3, chans)
    invariant = jnp.concatenate(
        [summed[:, :chans], jnp.sum(vector_part * vector_part, axis=1)], axis=1
    ).astype(jnp.bfloat16)
    hidden = jax.nn.silu(jnp.dot(invariant, w_up, preferred_element_type=jnp.float32))
    new_features = (features.astype(jnp.float32) + hidden).astype(jnp.bfloat16)
    chi = jnp.dot(hidden, w_out, precision=lax.Precision.HIGHEST) + lookup(species, chi_shift)
    own_labels = me * atoms + jnp.arange(atoms, dtype=jnp.int32)
    all_labels = jnp.arange(everybody, dtype=jnp.int32)
    rhs = field[0] * positions[2] - chi

    if everybody <= replicate_limit:
        kernel = coulomb(everyone, all_labels, everyone, all_labels)
        residual = gathered(rhs, devices).reshape(everybody)
        all_charges = conjugate(
            residual, lambda v: everyone[4] * v + jnp.sum(kernel * v[None, :], axis=1), jnp.sum
        )
        charges = lax.dynamic_slice(all_charges, (me * atoms,), (atoms,))
    else:
        kernel = coulomb(placed, own_labels, everyone, all_labels)

        def spread(vector):
            return gathered(vector, devices).reshape(everybody)

        charges = conjugate(
            rhs,
            lambda v: diag * v + jnp.sum(kernel * spread(v)[None, :], axis=1),
            lambda v: lax.psum(jnp.sum(v), everywhere),
        )
        all_charges = spread(charges)
    sums = pair_forces(placed, own_labels, everyone, all_labels, all_charges)
    pull = -charges[None, :] * sums[:3]
    forces = jnp.concatenate([pull[:2], pull[2:] + (charges * field[0])[None, :]], axis=0)
    virial = 0.5 * charges[None, :] * sums[3:]
    return (new_features, charges, forces, virial)


def conjugate(rhs, apply, total):
    charges = jnp.zeros_like(rhs)
    residual = rhs
    direction = rhs
    norm_now = total(residual * residual)
    for step in range(ITERS):
        image = apply(direction)
        alpha = norm_now / total(direction * image)
        charges = charges + alpha * direction
        if step + 1 < ITERS:
            residual = residual - alpha * image
            fresh = total(residual * residual)
            direction = residual + fresh / norm_now * direction
            norm_now = fresh
    return charges


def split3(value):
    first = value.astype(jnp.bfloat16).astype(jnp.float32)
    rest = value - first
    second = rest.astype(jnp.bfloat16).astype(jnp.float32)
    third = (rest - second).astype(jnp.bfloat16).astype(jnp.float32)
    return first, second, third


def over_first(left, right):
    return lax.dot_general(
        left, right, (((0,), (0,)), ((), ())), preferred_element_type=jnp.float32
    )


def over_last(left, right, precision=None):
    return lax.dot_general(
        left,
        right,
        (((1,), (1,)), ((), ())),
        precision=precision,
        preferred_element_type=jnp.float32,
    )


def silu(value):
    return value / (1.0 + jnp.exp(-value))


def silu_half(value):
    return (0.5 * value) * (1.0 + jnp.tanh(0.5 * value))


sine_series = [(-1.0) ** k * math.pi ** (2 * k + 1) / math.factorial(2 * k + 1) for k in range(7)]


def fetched(pairs, semaphores):
    copies = [
        pltpu.make_async_copy(source, target, semaphores.at[place])
        for place, (source, target) in enumerate(pairs)
    ]
    for copy in copies:
        copy.start()
    return copies


rhs_segment = 3


def pack_kernel(*refs):
    count = (len(refs) - 3) // 2
    features_ref, lists_ref, packed_ref = refs[0], refs[1], refs[count + 1]
    held_ref, semaphores = refs[-2:]
    atoms, chans = features_ref.shape
    pairs = [(lists_ref, held_ref), (features_ref, packed_ref.at[pl.ds(0, atoms)])]
    copies = fetched(pairs + list(zip(refs[2 : count + 1], refs[count + 2 : -2])), semaphores)
    copies[0].wait()
    lists = held_ref[0].astype(jnp.float32)
    rows, width = lists.shape
    lists = jnp.concatenate([lists, jnp.zeros((rows, chans - width), jnp.float32)], axis=1)
    blank = jnp.zeros((packed_ref.shape[0] - atoms - rows, chans), jnp.float32)
    packed_ref[atoms:, :] = jnp.concatenate([lists, blank], axis=0).astype(jnp.bfloat16)
    for copy in copies[1:]:
        copy.wait()


def edge_kernel(
    field_ref,
    space_ref,
    vec_ref,
    first_ref,
    second_ref,
    species_ref,
    hardness_ref,
    width_ref,
    shift_ref,
    positions_ref,
    send_ref,
    recv_ref,
    project_ref,
    filter_ref,
    unit_ref,
    row_ref,
    slot_ref,
    local_ref,
    hit_ref,
    turned_ref,
):
    edges = vec_ref.shape[1]
    orders = first_ref.shape[0]
    vec = vec_ref[...]
    east, north, up = vec[0:1], vec[1:2], vec[2:3]
    squared = east * east + north * north + up * up
    inverse = lax.rsqrt(squared)
    unit_ref[0:3, :] = vec * inverse
    ratio = squared * inverse * (1.0 / cutoff)
    envelope = (1.0 - ratio * ratio) * (1.0 - ratio * ratio) * (cutoff * inverse)
    order = lax.broadcasted_iota(jnp.int32, (orders, edges), 0).astype(jnp.float32) + 1.0
    turns = order * ratio
    whole = jnp.floor(turns + 0.5)
    part = turns - whole
    sign = 1.0 - 2.0 * (whole - 2.0 * jnp.floor(whole * 0.5))
    series = jnp.full_like(part, sine_series[-1])
    for coefficient in sine_series[-2::-1]:
        series = series * (part * part) + coefficient
    basis = series * part * (sign * envelope)
    b1, b2, b3 = split3(basis)
    w1, w2, w3 = split3(first_ref[...])
    mixed = over_first(
        jnp.concatenate([w1, w1, w2, w2, w1, w3], axis=0).astype(jnp.bfloat16),
        jnp.concatenate([b1, b2, b1, b2, b3, b1], axis=0).astype(jnp.bfloat16),
    )
    radial = silu_half(mixed).astype(jnp.bfloat16)
    filter_ref[...] = over_first(second_ref[...], radial)
    species = species_ref[...]

    def table(ref):
        result = jnp.zeros(species.shape, jnp.float32)
        for kind in range(ref.shape[1]):
            result = result + jnp.where(species == kind, ref[:, kind : kind + 1], 0.0)
        return result

    positions = positions_ref[...]
    sigma = table(width_ref)
    atoms = species.shape[1]
    chans = row_ref.shape[1]
    diag = table(hardness_ref) + inverse_root_pi / sigma
    rhs = field_ref[0] * positions[2:3] - table(shift_ref)
    blank = jnp.zeros((2, atoms), jnp.float32)
    rows = [positions[0:1], blank, rhs, diag, sigma, positions[2:3], positions[1:2]]
    block = jnp.concatenate(
        [jnp.concatenate(rows, axis=0), jnp.zeros((8, chans - atoms), jnp.float32)], axis=1
    )
    block = pltpu.roll(block, 0, 1, stride=atoms, stride_axis=0)
    row_ref[...] = jnp.sum(block, axis=0, keepdims=True)
    lanes = local_ref.shape[0] // atoms
    slots = chans // lanes
    send = send_ref[...]
    own = send < atoms
    slot = jnp.where(own, -1, (send - atoms) ^ (space_ref[0] * slots))
    local = jnp.where(own, send, -1)

    def chosen(ref, index):
        hit = lax.broadcasted_iota(jnp.int32, ref.shape, 0) == index
        ref[...] = jnp.where(hit, 1.0, 0.0).astype(ref.dtype)

    chosen(slot_ref, slot)
    chosen(local_ref, local)
    chosen(hit_ref, recv_ref[...])
    turned_ref[...] = project_ref[...].astype(jnp.float32).T.astype(jnp.bfloat16)


def node_kernel(
    space_ref,
    own_ref,
    near_ref,
    side_ref,
    far_ref,
    filter_ref,
    unit_ref,
    row_ref,
    slot_ref,
    local_ref,
    hit_ref,
    turned_ref,
    update_ref,
    out_ref,
    features_ref,
    block_ref,
):
    atoms, chans = features_ref.shape
    space = space_ref[0]
    packed = [ref[...].astype(jnp.float32) for ref in (own_ref, near_ref, side_ref, far_ref)]
    lanes = len(packed)
    slots = chans // lanes
    group = jnp.concatenate([value[:atoms] for value in packed], axis=0).astype(jnp.bfloat16)
    picks = jnp.zeros((8, chans), jnp.float32)
    line = lax.broadcasted_iota(jnp.int32, (8, chans), 0)
    for place, value in enumerate(packed):
        mine = jnp.where(line == space, value[atoms : atoms + 8], 0.0)
        picks = picks + (pltpu.roll(mine, place * slots, 1) if place else mine)
    slot_owner = lax.broadcasted_iota(jnp.int32, (1, chans), 1) // slots * atoms
    chosen = slot_owner + jnp.sum(picks, axis=0, keepdims=True).astype(jnp.int32)
    fill = jnp.where(
        lax.broadcasted_iota(jnp.int32, (lanes * atoms, chans), 0) == chosen, 1.0, 0.0
    ).astype(jnp.bfloat16)
    sender = jnp.dot(fill, slot_ref[...], preferred_element_type=jnp.float32) + local_ref[...]
    projected = over_last(turned_ref[...], group).astype(jnp.bfloat16)
    picked = jnp.dot(projected, sender.astype(jnp.bfloat16), preferred_element_type=jnp.float32)
    scalar = picked[:chans] * filter_ref[:chans, :]
    carried = picked[chans:] * filter_ref[chans:, :]
    parts = [scalar] + [unit_ref[axis : axis + 1, :] * carried for axis in range(3)]
    message = jnp.concatenate([part.astype(jnp.bfloat16) for part in parts], axis=0)
    summed = over_last(hit_ref[...], message) * message_scale
    square = jnp.zeros((atoms, chans), jnp.float32)
    for component in range(1, 4):
        part = summed[:, component * chans : (component + 1) * chans]
        square = square + part * part
    invariant = jnp.concatenate([summed[:, :chans], square], axis=1).astype(jnp.bfloat16)
    hidden = silu(jnp.dot(invariant, update_ref[...], preferred_element_type=jnp.float32))
    features_ref[...] = (packed[0][:atoms] + hidden).astype(jnp.bfloat16)
    chi = jnp.sum(hidden * out_ref[...], axis=1, keepdims=True)
    lane = lax.broadcasted_iota(jnp.int32, (atoms, chans), 1)
    atom = lax.broadcasted_iota(jnp.int32, (atoms, chans), 0)
    place = lane == atom + rhs_segment * atoms
    row = row_ref[...] - jnp.sum(jnp.where(place, chi, 0.0), axis=0, keepdims=True)
    block_ref[...] = jnp.broadcast_to(row[None], block_ref.shape)


def reciprocal(value):
    rough = pl.reciprocal(value, approx=True)
    return rough * (2.0 - value * rough)


def smeared(scaled):
    decay = jnp.exp2(scaled * scaled * -math.log2(math.e))
    turn = reciprocal(1.0 + 0.3275911 * scaled)
    series = 1.061405429 * turn - 1.453152027
    series = series * turn + 1.421413741
    series = series * turn - 0.284496736
    series = series * turn + 0.254829592
    return 1.0 - series * turn * decay, decay


def charge_kernel(
    place_ref, field_ref, all_ref, charges_ref, forces_ref, virial_ref, matrix_ref, side_ref
):
    blocks, _, lanes = all_ref.shape
    own = charges_ref.shape[1]
    count = blocks * own
    fit = lanes // own
    segment = lax.broadcasted_iota(jnp.int32, (8, lanes), 1) // own
    tiles = []
    for first in range(0, blocks, fit):
        tile = jnp.zeros((8, lanes), jnp.float32)
        for place in range(fit):
            row = jnp.broadcast_to(all_ref[first + place], (8, lanes))
            row = pltpu.roll(row, 0, 1, stride=own, stride_axis=0)
            row = pltpu.roll(row, place * own, 1) if place else row
            tile = jnp.where(segment == place, row, tile)
        tiles.append(tile)
    everyone = jnp.concatenate(tiles, axis=1)
    everyone = pltpu.roll(everyone, lax.rem(count - place_ref[0] * own, count), 1)
    columns = everyone.T
    diag, rhs = everyone[4:5], everyone[5:6]
    rows = own
    spread_row = 2.0 * everyone[3:4] * everyone[3:4]
    tiles = count // lanes
    lane = lax.broadcasted_iota(jnp.int32, (rows, lanes), 1)
    line = lax.broadcasted_iota(jnp.int32, (rows, lanes), 0)

    def part(row, tile):
        return row[:, tile * lanes : (tile + 1) * lanes]

    def spread(column):
        return jnp.broadcast_to(column, (rows, lanes))

    above = [jnp.zeros((rows, lanes), jnp.float32) for _ in range(tiles)]
    kept = []
    for start in range(0, count, rows):
        first = start // lanes
        column = columns[start : start + rows]
        place = [spread(column[:, axis : axis + 1]) for axis in range(3)]
        wide = spread(2.0 * column[:, 3:4] * column[:, 3:4])
        value = spread(column[:, 5:6])
        below = jnp.zeros((rows, lanes), jnp.float32)
        for tile in range(first, tiles):
            delta = [place[axis] - part(everyone[axis : axis + 1], tile) for axis in range(3)]
            squared = delta[0] * delta[0] + delta[1] * delta[1] + delta[2] * delta[2]
            if tile == first:
                same = lane == line + (start - first * lanes)
                squared = jnp.where(same, 1.0, squared)
            inverse = lax.rsqrt(squared)
            scale = lax.rsqrt(wide + part(spread_row, tile))
            smear, decay = smeared(squared * inverse * scale)
            kernel = smear * inverse
            if start == 0:
                slope = (two_over_root_pi * scale * decay - kernel) * inverse * inverse
                slope = jnp.where(same, 0.0, slope) if tile == first else slope
                kept.append((delta, slope))
            if tile == first:
                kernel = jnp.where(same, 0.0, kernel)
            else:
                below = below + kernel * part(rhs, tile)
            above[tile] = above[tile] + kernel * value
            matrix_ref[start : start + rows, tile * lanes : (tile + 1) * lanes] = kernel
        if first + 1 < tiles:
            side_ref[start : start + rows, :] = below
    image = []
    for tile in range(tiles):
        value = jnp.sum(above[tile], axis=0, keepdims=True)
        if tile + 1 < tiles:
            below = side_ref[tile * lanes : (tile + 1) * lanes, :].T
            value = value + jnp.sum(below, axis=0, keepdims=True)
        image.append(value)
    image = diag * rhs + jnp.concatenate(image, axis=1)

    def total(value):
        return jnp.sum(value, axis=1, keepdims=True)

    norm = total(rhs * rhs)
    alpha = norm / total(rhs * image)
    residual = rhs - alpha * image
    fresh = total(residual * residual)
    direction = residual + fresh / norm * rhs
    across = jnp.broadcast_to(direction, (8, count)).T
    onto = [jnp.zeros((rows, lanes), jnp.float32) for _ in range(tiles)]
    above = [jnp.zeros((rows, lanes), jnp.float32) for _ in range(tiles)]
    for start in range(0, count, rows):
        first = start // lanes
        value = spread(across[start : start + rows, 0:1])
        for tile in range(first, tiles):
            sums = onto if tile == first else above
            kernel = matrix_ref[start : start + rows, tile * lanes : (tile + 1) * lanes]
            sums[tile] = sums[tile] + kernel * value
    curved = jnp.zeros((rows, lanes), jnp.float32)
    for tile in range(tiles):
        curved = curved + (onto[tile] + 2.0 * above[tile]) * part(direction, tile)
    curved = jnp.sum(curved, axis=0, keepdims=True)
    for tile in range(tiles):
        curved = curved + part(diag * direction * direction, tile)
    charges = alpha * rhs + fresh / total(curved) * direction

    sums = [jnp.zeros((rows, lanes), jnp.float32) for _ in range(9)]
    for tile, (delta, slope) in enumerate(kept):
        weight = part(charges, tile) * slope
        pulled = [weight * delta[axis] for axis in range(3)]
        terms = pulled + [
            pulled[left] * delta[right]
            for left, right in ((0, 0), (1, 1), (2, 2), (0, 1), (0, 2), (1, 2))
        ]
        sums = [old + term for old, term in zip(sums, terms)]
    table = jnp.zeros((rows, lanes), jnp.float32)
    for place, value in enumerate(sums):
        table = jnp.where(lane == place, total(value), table)
    table = table.T
    mine = charges[:, :own]
    charges_ref[...] = mine
    pull = -mine * table[0:3]
    third = lax.broadcasted_iota(jnp.int32, pull.shape, 0) == 2
    forces_ref[...] = pull + jnp.where(third, mine * field_ref[0], 0.0)
    virial_ref[...] = 0.5 * mine * table[3:9]


def kernel_call(kernel, shapes, arguments, scalars=0, far=0, scratch=(), flops=0):
    shapes = tuple(jax.ShapeDtypeStruct(shape, kind) for shape, kind in shapes)
    spaces = [pltpu.SMEM] * scalars + [pltpu.HBM] * far
    spaces = spaces + [pltpu.VMEM] * (len(arguments) - len(spaces))
    arguments = [
        pltpu.with_memory_space_constraint(value, space) if space is pltpu.HBM else value
        for value, space in zip(arguments, spaces)
    ]
    return pl.pallas_call(
        kernel,
        out_shape=shapes,
        in_specs=[pl.BlockSpec(memory_space=space) for space in spaces],
        out_specs=tuple(pl.BlockSpec(memory_space=pltpu.VMEM) for _ in shapes),
        scratch_shapes=list(scratch),
        compiler_params=pltpu.CompilerParams(vmem_limit_bytes=32 * 1024 * 1024),
        cost_estimate=pl.CostEstimate(flops=flops, bytes_accessed=1 << 20, transcendentals=0),
    )(*arguments)


def exchanged(block, axis, step):
    size = lax.axis_size(axis)
    return lax.ppermute(block, axis, [(place, place ^ step) for place in range(size)])


def few_shards(
    features,
    positions,
    species,
    ghost_list,
    edge_recv,
    edge_send,
    edge_vec,
    w_msg,
    w_rad1,
    w_rad2,
    w_up,
    w_out,
    hardness,
    width,
    chi_shift,
    field,
):
    atoms, chans = features.shape
    edges = edge_recv.shape[0]
    rows, lanes = lax.axis_size("row"), lax.axis_size("space")
    rest = (edge_vec, w_rad1, w_rad2, species[None], hardness[None], width[None])
    rest = rest + (chi_shift[None], positions, edge_send[None], edge_recv[None], w_msg)
    rest = rest + (w_up, w_out[None])
    packed, *rest = kernel_call(
        pack_kernel,
        [((atoms + 16, chans), jnp.bfloat16)] + [(value.shape, value.dtype) for value in rest],
        (features, ghost_list) + rest,
        far=2 + len(rest),
        scratch=[
            pltpu.VMEM(ghost_list.shape, ghost_list.dtype),
            pltpu.SemaphoreType.DMA((2 + len(rest),)),
        ],
    )
    others = [exchanged(packed, "space", step) for step in range(1, lanes)]
    space = lax.axis_index("space").astype(jnp.int32)
    parts = kernel_call(
        edge_kernel,
        [
            ((2 * chans, edges), jnp.float32),
            ((8, edges), jnp.float32),
            ((1, chans), jnp.float32),
            ((chans, edges), jnp.bfloat16),
            ((lanes * atoms, edges), jnp.float32),
            ((atoms, edges), jnp.bfloat16),
            ((2 * chans, chans), jnp.bfloat16),
        ],
        (field, space.reshape(1), *rest[:-2]),
        scalars=2,
        flops=1 << 28,
    )
    devices = rows * lanes
    new_features, block = kernel_call(
        node_kernel,
        [((atoms, chans), jnp.bfloat16), ((devices, 1, chans), jnp.float32)],
        (space.reshape(1), packed, *others, *parts, *rest[-2:]),
        scalars=1,
        flops=1 << 28,
    )
    order = [list(range(devices - 1, -1, -1))]
    block = lax.all_to_all(block, everywhere, 0, 0, axis_index_groups=order, tiled=True)
    place = devices - 1 - (lax.axis_index("row").astype(jnp.int32) * lanes + space)
    everybody = rows * lanes * atoms
    charges, forces, virial = kernel_call(
        charge_kernel,
        [((count, atoms), jnp.float32) for count in (1, 3, 6)],
        (place.reshape(1), field, block),
        scalars=2,
        scratch=[
            pltpu.VMEM((everybody, everybody), jnp.float32),
            pltpu.VMEM((everybody, chans), jnp.float32),
        ],
        flops=1 << 28,
    )
    return (new_features, charges[0], forces, virial)


def solution(mesh):
    small = mesh.shape["space"] == 4 and mesh.shape["row"] == 8
    return jax.shard_map(
        few_shards if small else shards,
        mesh=mesh,
        in_specs=(
            P(("row", "space"), None),
            P(None, ("row", "space")),
            P(("row", "space")),
            P("row", "space", None),
            P(("row", "space")),
            P(("row", "space")),
            P(None, ("row", "space")),
            P(),
            P(),
            P(),
            P(),
            P(),
            P(),
            P(),
            P(),
            P(),
        ),
        out_specs=(
            P(("row", "space"), None),
            P(("row", "space")),
            P(None, ("row", "space")),
            P(None, ("row", "space")),
        ),
        check_vma=False,
    )
```

```python
import math

import jax
import jax.numpy as jnp
from jax import lax
from jax.experimental import pallas as pl
from jax.experimental.pallas import tpu as pltpu
from jax.sharding import PartitionSpec as P

ITERS = 2


cutoff = 6.0
message_scale = 0.125
two_over_root_pi = 2.0 / math.sqrt(math.pi)
inverse_root_pi = 1.0 / math.sqrt(math.pi)
replicate_limit = 1024
everywhere = ("row", "space")


def lookup(species, table):
    result = jnp.zeros(species.shape, jnp.float32)
    for kind in range(table.shape[0]):
        result = result + jnp.where(species == kind, table[kind], 0.0)
    return result


def pair_terms(target, target_labels, source, source_labels):
    delta = target[:3, :, None] - source[:3, None, :]
    squared = jnp.sum(delta * delta, axis=0)
    same = target_labels[:, None] == source_labels[None, :]
    squared = jnp.where(same, 1.0, squared)
    inverse = lax.rsqrt(squared)
    radius = squared * inverse
    spread = target[3][:, None] * target[3][:, None] + source[3][None, :] * source[3][None, :]
    scale = lax.rsqrt(2.0 * spread)
    scaled = radius * scale
    smear = lax.erf(scaled)
    return delta, same, inverse, scale, scaled, smear


def coulomb(target, target_labels, source, source_labels):
    _, same, inverse, _, _, smear = pair_terms(target, target_labels, source, source_labels)
    return jnp.where(same, 0.0, smear * inverse)


def pair_forces(target, target_labels, source, source_labels, source_charge):
    delta, same, inverse, scale, scaled, smear = pair_terms(
        target, target_labels, source, source_labels
    )
    slope = (
        two_over_root_pi * scale * jnp.exp(-scaled * scaled) * inverse - smear * inverse * inverse
    )
    weight = jnp.where(same, 0.0, source_charge[None, :] * slope * inverse)
    first = jnp.sum(weight[None] * delta, axis=2)
    pairs = ((0, 0), (1, 1), (2, 2), (0, 1), (0, 2), (1, 2))
    second = jnp.stack(
        [jnp.sum(weight * delta[left] * delta[right], axis=1) for left, right in pairs]
    )
    return jnp.concatenate([first, second], axis=0)


def edge_terms(receive, sender_rows, vectors, projected, w_rad1, w_rad2, atoms):
    length = jnp.sqrt(jnp.sum(vectors * vectors, axis=0))
    unit = vectors / length
    order = jnp.arange(1, w_rad1.shape[0] + 1, dtype=jnp.int32).astype(jnp.float32)[:, None]
    ratio = length / cutoff
    envelope = (1.0 - ratio * ratio) * (1.0 - ratio * ratio)
    basis = jnp.sin(order * math.pi * ratio) / ratio * envelope
    mixed = lax.dot_general(
        basis, w_rad1, (((0,), (0,)), ((), ())), precision=lax.Precision.HIGHEST
    )
    radial = jax.nn.silu(mixed).astype(jnp.bfloat16)
    filters = jnp.dot(radial, w_rad2, preferred_element_type=jnp.float32)
    picked = jnp.take(projected, sender_rows, axis=0).astype(jnp.float32) * filters
    chans = w_rad1.shape[1]
    scalar = picked[:, :chans]
    carried = picked[:, chans:]
    joined = [
        scalar,
        unit[0][:, None] * carried,
        unit[1][:, None] * carried,
        unit[2][:, None] * carried,
    ]
    message = jnp.concatenate(joined, axis=1).astype(jnp.bfloat16)
    onehot = (jnp.arange(atoms, dtype=jnp.int32)[:, None] == receive[None, :]).astype(jnp.bfloat16)
    return jnp.dot(onehot, message, preferred_element_type=jnp.float32)


def gathered(block, devices):
    copies = jnp.broadcast_to(block[None], (devices,) + block.shape)
    return lax.all_to_all(copies, everywhere, split_axis=0, concat_axis=0, tiled=True)


def shards(
    features,
    positions,
    species,
    ghost_list,
    edge_recv,
    edge_send,
    edge_vec,
    w_msg,
    w_rad1,
    w_rad2,
    w_up,
    w_out,
    hardness,
    width,
    chi_shift,
    field,
):
    atoms = features.shape[0]
    chans = features.shape[1]
    lanes = lax.axis_size("space")
    devices = lanes * lax.axis_size("row")
    everybody = devices * atoms
    me = lax.axis_index("row") * lanes + lax.axis_index("space")
    sigma = lookup(species, width)
    diag = lookup(species, hardness) + inverse_root_pi / sigma
    placed = jnp.concatenate([positions, sigma[None, :], diag[None, :]], axis=0)
    everyone = gathered(placed, devices).transpose(1, 0, 2).reshape(5, everybody)
    lists = ghost_list[0]
    outgoing = jnp.take(features, lists.reshape(-1), axis=0).reshape(lanes, lists.shape[1], chans)
    ghost_rows = jnp.einsum(
        "dkc,cf->dkf",
        lax.all_to_all(outgoing, "space", split_axis=0, concat_axis=0, tiled=True),
        w_msg,
        preferred_element_type=jnp.float32,
    ).astype(jnp.bfloat16)
    own_rows = jnp.dot(features, w_msg, preferred_element_type=jnp.float32).astype(jnp.bfloat16)
    projected = jnp.concatenate([own_rows, ghost_rows.reshape(-1, 2 * chans)], axis=0)
    summed = edge_terms(edge_recv, edge_send, edge_vec, projected, w_rad1, w_rad2, atoms)
    summed = summed * message_scale
    vector_part = summed[:, chans:].reshape(atoms, 3, chans)
    invariant = jnp.concatenate(
        [summed[:, :chans], jnp.sum(vector_part * vector_part, axis=1)], axis=1
    ).astype(jnp.bfloat16)
    hidden = jax.nn.silu(jnp.dot(invariant, w_up, preferred_element_type=jnp.float32))
    new_features = (features.astype(jnp.float32) + hidden).astype(jnp.bfloat16)
    chi = jnp.dot(hidden, w_out, precision=lax.Precision.HIGHEST) + lookup(species, chi_shift)
    own_labels = me * atoms + jnp.arange(atoms, dtype=jnp.int32)
    all_labels = jnp.arange(everybody, dtype=jnp.int32)
    rhs = field[0] * positions[2] - chi

    if everybody <= replicate_limit:
        kernel = coulomb(everyone, all_labels, everyone, all_labels)
        residual = gathered(rhs, devices).reshape(everybody)
        all_charges = conjugate(
            residual, lambda v: everyone[4] * v + jnp.sum(kernel * v[None, :], axis=1), jnp.sum
        )
        charges = lax.dynamic_slice(all_charges, (me * atoms,), (atoms,))
    else:
        kernel = coulomb(placed, own_labels, everyone, all_labels)

        def spread(vector):
            return gathered(vector, devices).reshape(everybody)

        charges = conjugate(
            rhs,
            lambda v: diag * v + jnp.sum(kernel * spread(v)[None, :], axis=1),
            lambda v: lax.psum(jnp.sum(v), everywhere),
        )
        all_charges = spread(charges)
    sums = pair_forces(placed, own_labels, everyone, all_labels, all_charges)
    pull = -charges[None, :] * sums[:3]
    forces = jnp.concatenate([pull[:2], pull[2:] + (charges * field[0])[None, :]], axis=0)
    virial = 0.5 * charges[None, :] * sums[3:]
    return (new_features, charges, forces, virial)


def conjugate(rhs, apply, total):
    charges = jnp.zeros_like(rhs)
    residual = rhs
    direction = rhs
    norm_now = total(residual * residual)
    for step in range(ITERS):
        image = apply(direction)
        alpha = norm_now / total(direction * image)
        charges = charges + alpha * direction
        if step + 1 < ITERS:
            residual = residual - alpha * image
            fresh = total(residual * residual)
            direction = residual + fresh / norm_now * direction
            norm_now = fresh
    return charges


def split3(value):
    first = value.astype(jnp.bfloat16).astype(jnp.float32)
    rest = value - first
    second = rest.astype(jnp.bfloat16).astype(jnp.float32)
    third = (rest - second).astype(jnp.bfloat16).astype(jnp.float32)
    return first, second, third


def over_first(left, right):
    return lax.dot_general(
        left, right, (((0,), (0,)), ((), ())), preferred_element_type=jnp.float32
    )


def over_last(left, right, precision=None):
    return lax.dot_general(
        left,
        right,
        (((1,), (1,)), ((), ())),
        precision=precision,
        preferred_element_type=jnp.float32,
    )


def silu(value):
    return value / (1.0 + jnp.exp(-value))


def silu_half(value):
    return (0.5 * value) * (1.0 + jnp.tanh(0.5 * value))


sine_series = [(-1.0) ** k * math.pi ** (2 * k + 1) / math.factorial(2 * k + 1) for k in range(7)]


def fetched(pairs, semaphores):
    copies = [
        pltpu.make_async_copy(source, target, semaphores.at[place])
        for place, (source, target) in enumerate(pairs)
    ]
    for copy in copies:
        copy.start()
    return copies


rhs_segment = 3


def pack_kernel(*refs):
    count = (len(refs) - 3) // 2
    features_ref, lists_ref, packed_ref = refs[0], refs[1], refs[count + 1]
    held_ref, semaphores = refs[-2:]
    atoms, chans = features_ref.shape
    pairs = [(lists_ref, held_ref), (features_ref, packed_ref.at[pl.ds(0, atoms)])]
    copies = fetched(pairs + list(zip(refs[2 : count + 1], refs[count + 2 : -2])), semaphores)
    copies[0].wait()
    lists = held_ref[0].astype(jnp.float32)
    rows, width = lists.shape
    lists = jnp.concatenate([lists, jnp.zeros((rows, chans - width), jnp.float32)], axis=1)
    blank = jnp.zeros((packed_ref.shape[0] - atoms - rows, chans), jnp.float32)
    packed_ref[atoms:, :] = jnp.concatenate([lists, blank], axis=0).astype(jnp.bfloat16)
    for copy in copies[1:]:
        copy.wait()


def edge_kernel(
    field_ref,
    space_ref,
    vec_ref,
    first_ref,
    second_ref,
    species_far,
    hardness_far,
    width_far,
    shift_far,
    positions_far,
    send_far,
    recv_far,
    project_far,
    update_far,
    out_far,
    filter_ref,
    unit_ref,
    row_ref,
    slot_ref,
    local_ref,
    hit_ref,
    turned_ref,
    upward_ref,
    read_ref,
    species_ref,
    hardness_ref,
    width_ref,
    shift_ref,
    positions_ref,
    send_ref,
    recv_ref,
    project_ref,
    update_ref,
    out_ref,
    semaphores,
):
    far = (send_far, recv_far, project_far, update_far, species_far, hardness_far)
    far = far + (width_far, shift_far, positions_far, out_far)
    near = (send_ref, recv_ref, project_ref, update_ref, species_ref, hardness_ref)
    near = near + (width_ref, shift_ref, positions_ref, out_ref)
    copies = fetched(list(zip(far, near)), semaphores)
    edges = vec_ref.shape[1]
    orders = first_ref.shape[0]
    vec = vec_ref[...]
    east, north, up = vec[0:1], vec[1:2], vec[2:3]
    squared = east * east + north * north + up * up
    inverse = lax.rsqrt(squared)
    unit_ref[0:3, :] = vec * inverse
    ratio = squared * inverse * (1.0 / cutoff)
    envelope = (1.0 - ratio * ratio) * (1.0 - ratio * ratio) * (cutoff * inverse)
    order = lax.broadcasted_iota(jnp.int32, (orders, edges), 0).astype(jnp.float32) + 1.0
    turns = order * ratio
    whole = jnp.floor(turns + 0.5)
    part = turns - whole
    sign = 1.0 - 2.0 * (whole - 2.0 * jnp.floor(whole * 0.5))
    series = jnp.full_like(part, sine_series[-1])
    for coefficient in sine_series[-2::-1]:
        series = series * (part * part) + coefficient
    basis = series * part * (sign * envelope)
    b1, b2, b3 = split3(basis)
    w1, w2, w3 = split3(first_ref[...])
    mixed = over_first(
        jnp.concatenate([w1, w1, w2, w2, w1, w3], axis=0).astype(jnp.bfloat16),
        jnp.concatenate([b1, b2, b1, b2, b3, b1], axis=0).astype(jnp.bfloat16),
    )
    radial = silu_half(mixed).astype(jnp.bfloat16)
    filter_ref[...] = over_first(second_ref[...], radial)
    for copy in copies:
        copy.wait()
    species = species_ref[...]

    def table(ref):
        result = jnp.zeros(species.shape, jnp.float32)
        for kind in range(ref.shape[1]):
            result = result + jnp.where(species == kind, ref[:, kind : kind + 1], 0.0)
        return result

    positions = positions_ref[...]
    sigma = table(width_ref)
    atoms = species.shape[1]
    chans = row_ref.shape[1]
    diag = table(hardness_ref) + inverse_root_pi / sigma
    rhs = field_ref[0] * positions[2:3] - table(shift_ref)
    blank = jnp.zeros((2, atoms), jnp.float32)
    rows = [positions[0:1], blank, rhs, diag, sigma, positions[2:3], positions[1:2]]
    block = jnp.concatenate(
        [jnp.concatenate(rows, axis=0), jnp.zeros((8, chans - atoms), jnp.float32)], axis=1
    )
    block = pltpu.roll(block, 0, 1, stride=atoms, stride_axis=0)
    row_ref[...] = jnp.sum(block, axis=0, keepdims=True)
    lanes = local_ref.shape[0] // atoms
    slots = chans // lanes
    send = send_ref[...]
    own = send < atoms
    slot = jnp.where(own, -1, (send - atoms) ^ (space_ref[0] * slots))
    local = jnp.where(own, send, -1)

    def chosen(ref, index):
        hit = lax.broadcasted_iota(jnp.int32, ref.shape, 0) == index
        ref[...] = jnp.where(hit, 1.0, 0.0).astype(ref.dtype)

    chosen(slot_ref, slot)
    chosen(local_ref, local)
    chosen(hit_ref, recv_ref[...])
    turned_ref[...] = project_ref[...].astype(jnp.float32).T.astype(jnp.bfloat16)
    upward_ref[...] = update_ref[...].astype(jnp.float32).T.astype(jnp.bfloat16)
    read_ref[...] = jnp.broadcast_to(out_ref[...], (atoms, chans)).T


def node_kernel(
    space_ref,
    own_ref,
    near_ref,
    side_ref,
    far_ref,
    filter_ref,
    unit_ref,
    row_ref,
    slot_ref,
    local_ref,
    hit_ref,
    turned_ref,
    upward_ref,
    read_ref,
    features_ref,
    block_ref,
):
    atoms, chans = features_ref.shape
    space = space_ref[0]
    packed = [ref[...].astype(jnp.float32) for ref in (own_ref, near_ref, side_ref, far_ref)]
    lanes = len(packed)
    slots = chans // lanes
    group = jnp.concatenate([value[:atoms] for value in packed], axis=0).astype(jnp.bfloat16)
    picks = jnp.zeros((8, chans), jnp.float32)
    line = lax.broadcasted_iota(jnp.int32, (8, chans), 0)
    for place, value in enumerate(packed):
        mine = jnp.where(line == space, value[atoms : atoms + 8], 0.0)
        picks = picks + (pltpu.roll(mine, place * slots, 1) if place else mine)
    slot_owner = lax.broadcasted_iota(jnp.int32, (1, chans), 1) // slots * atoms
    chosen = slot_owner + jnp.sum(picks, axis=0, keepdims=True).astype(jnp.int32)
    fill = jnp.where(
        lax.broadcasted_iota(jnp.int32, (lanes * atoms, chans), 0) == chosen, 1.0, 0.0
    ).astype(jnp.bfloat16)
    sender = jnp.dot(fill, slot_ref[...], preferred_element_type=jnp.float32) + local_ref[...]
    projected = over_last(turned_ref[...], group).astype(jnp.bfloat16)
    picked = jnp.dot(projected, sender.astype(jnp.bfloat16), preferred_element_type=jnp.float32)
    scalar = picked[:chans] * filter_ref[:chans, :]
    carried = picked[chans:] * filter_ref[chans:, :]
    parts = [scalar] + [unit_ref[axis : axis + 1, :] * carried for axis in range(3)]
    message = jnp.concatenate([part.astype(jnp.bfloat16) for part in parts], axis=0)
    summed = over_last(message, hit_ref[...]) * message_scale
    square = jnp.zeros((chans, atoms), jnp.float32)
    for component in range(1, 4):
        part = summed[component * chans : (component + 1) * chans]
        square = square + part * part
    invariant = jnp.concatenate([summed[:chans], square], axis=0).astype(jnp.bfloat16)
    hidden = silu(jnp.dot(upward_ref[...], invariant, preferred_element_type=jnp.float32))
    chi = jnp.sum(hidden * read_ref[...], axis=0, keepdims=True)
    chi = jnp.concatenate([chi, jnp.zeros((1, chans - atoms), jnp.float32)], axis=1)
    row = row_ref[...] - pltpu.roll(chi, rhs_segment * atoms, 1)
    block_ref[...] = jnp.broadcast_to(row[None], block_ref.shape)
    features_ref[...] = (packed[0][:atoms] + hidden.T).astype(jnp.bfloat16)


def reciprocal(value):
    rough = pl.reciprocal(value, approx=True)
    return rough * (2.0 - value * rough)


def smeared(scaled):
    decay = jnp.exp2(scaled * scaled * -math.log2(math.e))
    turn = reciprocal(1.0 + 0.3275911 * scaled)
    series = 1.061405429 * turn - 1.453152027
    series = series * turn + 1.421413741
    series = series * turn - 0.284496736
    series = series * turn + 0.254829592
    return 1.0 - series * turn * decay, decay


def charge_kernel(
    place_ref,
    field_ref,
    all_ref,
    ready_ref,
    charges_ref,
    forces_ref,
    virial_ref,
    features_ref,
    matrix_ref,
    side_ref,
    value_ref,
):
    features_ref[...] = ready_ref[...]
    blocks, _, lanes = all_ref.shape
    own = charges_ref.shape[1]
    count = blocks * own
    fit = lanes // own
    segment = lax.broadcasted_iota(jnp.int32, (8, lanes), 1) // own
    tiles = []
    for first in range(0, blocks, fit):
        tile = jnp.zeros((8, lanes), jnp.float32)
        for place in range(fit):
            row = all_ref[lax.rem(place_ref[0] + first + place, blocks)]
            row = pltpu.roll(jnp.broadcast_to(row, (8, lanes)), 0, 1, stride=own, stride_axis=0)
            row = pltpu.roll(row, place * own, 1) if place else row
            tile = jnp.where(segment == place, row, tile)
        tiles.append(tile)
    everyone = jnp.concatenate(tiles, axis=1)
    columns = everyone.T
    diag, rhs = everyone[4:5], everyone[5:6]
    rows = own
    spread_row = 2.0 * everyone[3:4] * everyone[3:4]
    tiles = count // lanes
    lane = lax.broadcasted_iota(jnp.int32, (rows, lanes), 1)
    line = lax.broadcasted_iota(jnp.int32, (rows, lanes), 0)

    def part(row, tile):
        return row[:, tile * lanes : (tile + 1) * lanes]

    def spread(column):
        return jnp.broadcast_to(column, (rows, lanes))

    above = [jnp.zeros((rows, lanes), jnp.float32) for _ in range(tiles)]
    kept = []
    for start in range(0, count, rows):
        first = start // lanes
        column = columns[start : start + rows]
        place = [spread(column[:, axis : axis + 1]) for axis in range(3)]
        wide = spread(2.0 * column[:, 3:4] * column[:, 3:4])
        value = spread(column[:, 5:6])
        value_ref[start : start + rows, :] = value
        below = jnp.zeros((rows, lanes), jnp.float32)
        for tile in range(first, tiles):
            delta = [place[axis] - part(everyone[axis : axis + 1], tile) for axis in range(3)]
            squared = delta[0] * delta[0] + delta[1] * delta[1] + delta[2] * delta[2]
            if tile == first:
                same = lane == line + (start - first * lanes)
                squared = jnp.where(same, 1.0, squared)
            inverse = lax.rsqrt(squared)
            scale = lax.rsqrt(wide + part(spread_row, tile))
            smear, decay = smeared(squared * inverse * scale)
            kernel = smear * inverse
            if start == 0:
                slope = (two_over_root_pi * scale * decay - kernel) * inverse * inverse
                slope = jnp.where(same, 0.0, slope) if tile == first else slope
                kept.append((delta, slope))
            if tile == first:
                kernel = jnp.where(same, 0.0, kernel)
            else:
                below = below + kernel * part(rhs, tile)
            above[tile] = above[tile] + kernel * value
            matrix_ref[start : start + rows, tile * lanes : (tile + 1) * lanes] = kernel
        if first + 1 < tiles:
            side_ref[start : start + rows, :] = below
    image = []
    for tile in range(tiles):
        value = jnp.sum(above[tile], axis=0, keepdims=True)
        if tile + 1 < tiles:
            below = side_ref[tile * lanes : (tile + 1) * lanes, :].T
            value = value + jnp.sum(below, axis=0, keepdims=True)
        image.append(value)
    image = diag * rhs + jnp.concatenate(image, axis=1)
    across = jnp.broadcast_to(image, (8, count)).T

    def total(value):
        return jnp.sum(value, axis=1, keepdims=True)

    norm = total(rhs * rhs)
    alpha = norm / total(rhs * image)
    residual = rhs - alpha * image
    fresh = total(residual * residual)
    again = fresh / norm
    direction = residual + again * rhs
    onto = [jnp.zeros((rows, lanes), jnp.float32) for _ in range(tiles)]
    above = [jnp.zeros((rows, lanes), jnp.float32) for _ in range(tiles)]
    for start in range(0, count, rows):
        first = start // lanes
        value = (1.0 + again) * value_ref[start : start + rows, :]
        value = value - alpha * spread(across[start : start + rows, 0:1])
        for tile in range(first, tiles):
            sums = onto if tile == first else above
            kernel = matrix_ref[start : start + rows, tile * lanes : (tile + 1) * lanes]
            sums[tile] = sums[tile] + kernel * value
    curved = jnp.zeros((rows, lanes), jnp.float32)
    for tile in range(tiles):
        curved = curved + (onto[tile] + 2.0 * above[tile]) * part(direction, tile)
    curved = jnp.sum(curved, axis=0, keepdims=True)
    for tile in range(tiles):
        curved = curved + part(diag * direction * direction, tile)
    charges = alpha * rhs + fresh / total(curved) * direction

    sums = [jnp.zeros((rows, lanes), jnp.float32) for _ in range(9)]
    for tile, (delta, slope) in enumerate(kept):
        weight = part(charges, tile) * slope
        pulled = [weight * delta[axis] for axis in range(3)]
        terms = pulled + [
            pulled[left] * delta[right]
            for left, right in ((0, 0), (1, 1), (2, 2), (0, 1), (0, 2), (1, 2))
        ]
        sums = [old + term for old, term in zip(sums, terms)]
    table = jnp.zeros((rows, lanes), jnp.float32)
    for place, value in enumerate(sums):
        table = jnp.where(lane == place, total(value), table)
    table = table.T
    mine = charges[:, :own]
    charges_ref[...] = mine
    pull = -mine * table[0:3]
    third = lax.broadcasted_iota(jnp.int32, pull.shape, 0) == 2
    forces_ref[...] = pull + jnp.where(third, mine * field_ref[0], 0.0)
    virial_ref[...] = 0.5 * mine * table[3:9]


def kernel_call(kernel, shapes, arguments, scalars=0, near=0, far=0, scratch=(), flops=0):
    shapes = tuple(jax.ShapeDtypeStruct(shape, kind) for shape, kind in shapes)
    spaces = [pltpu.SMEM] * scalars + [pltpu.VMEM] * near + [pltpu.HBM] * far
    spaces = spaces + [pltpu.VMEM] * (len(arguments) - len(spaces))
    arguments = [
        pltpu.with_memory_space_constraint(value, space) if space is pltpu.HBM else value
        for value, space in zip(arguments, spaces)
    ]
    return pl.pallas_call(
        kernel,
        out_shape=shapes,
        in_specs=[pl.BlockSpec(memory_space=space) for space in spaces],
        out_specs=tuple(pl.BlockSpec(memory_space=pltpu.VMEM) for _ in shapes),
        scratch_shapes=list(scratch),
        compiler_params=pltpu.CompilerParams(vmem_limit_bytes=32 * 1024 * 1024),
        cost_estimate=pl.CostEstimate(flops=flops, bytes_accessed=1 << 20, transcendentals=0),
    )(*arguments)


def exchanged(block, axis, step):
    size = lax.axis_size(axis)
    return lax.ppermute(block, axis, [(place, place ^ step) for place in range(size)])


def few_shards(
    features,
    positions,
    species,
    ghost_list,
    edge_recv,
    edge_send,
    edge_vec,
    w_msg,
    w_rad1,
    w_rad2,
    w_up,
    w_out,
    hardness,
    width,
    chi_shift,
    field,
):
    atoms, chans = features.shape
    edges = edge_recv.shape[0]
    rows, lanes = lax.axis_size("row"), lax.axis_size("space")
    first = (edge_vec, w_rad1, w_rad2)
    packed, *first = kernel_call(
        pack_kernel,
        [((atoms + 16, chans), jnp.bfloat16)] + [(value.shape, value.dtype) for value in first],
        (features, ghost_list) + first,
        far=2 + len(first),
        scratch=[
            pltpu.VMEM(ghost_list.shape, ghost_list.dtype),
            pltpu.SemaphoreType.DMA((2 + len(first),)),
        ],
    )
    others = [exchanged(packed, "space", step) for step in range(1, lanes)]
    space = lax.axis_index("space").astype(jnp.int32)
    rest = (species[None], hardness[None], width[None], chi_shift[None], positions)
    rest = rest + (edge_send[None], edge_recv[None], w_msg, w_up, w_out[None])
    parts = kernel_call(
        edge_kernel,
        [
            ((2 * chans, edges), jnp.float32),
            ((8, edges), jnp.float32),
            ((1, chans), jnp.float32),
            ((chans, edges), jnp.bfloat16),
            ((lanes * atoms, edges), jnp.float32),
            ((atoms, edges), jnp.bfloat16),
            ((2 * chans, chans), jnp.bfloat16),
            ((chans, 2 * chans), jnp.bfloat16),
            ((chans, atoms), jnp.float32),
        ],
        (field, space.reshape(1), *first, *rest),
        scalars=2,
        near=len(first),
        far=len(rest),
        scratch=[pltpu.VMEM(value.shape, value.dtype) for value in rest]
        + [pltpu.SemaphoreType.DMA((len(rest),))],
        flops=1 << 28,
    )
    devices = rows * lanes
    ready, block = kernel_call(
        node_kernel,
        [((atoms, chans), jnp.bfloat16), ((devices, 1, chans), jnp.float32)],
        (space.reshape(1), packed, *others, *parts),
        scalars=1,
        flops=1 << 28,
    )
    block = lax.all_to_all(block, everywhere, 0, 0, tiled=True)
    place = lax.axis_index("row").astype(jnp.int32) * lanes + space
    everybody = rows * lanes * atoms
    charges, forces, virial, new_features = kernel_call(
        charge_kernel,
        [((count, atoms), jnp.float32) for count in (1, 3, 6)]
        + [((atoms, chans), jnp.bfloat16)],
        (place.reshape(1), field, block, ready),
        scalars=2,
        scratch=[
            pltpu.VMEM((everybody, everybody), jnp.float32),
            pltpu.VMEM((everybody, chans), jnp.float32),
            pltpu.VMEM((everybody, chans), jnp.float32),
        ],
        flops=1 << 28,
    )
    return (new_features, charges[0], forces, virial)


def solution(mesh):
    small = mesh.shape["space"] == 4 and mesh.shape["row"] == 8
    return jax.shard_map(
        few_shards if small else shards,
        mesh=mesh,
        in_specs=(
            P(("row", "space"), None),
            P(None, ("row", "space")),
            P(("row", "space")),
            P("row", "space", None),
            P(("row", "space")),
            P(("row", "space")),
            P(None, ("row", "space")),
            P(),
            P(),
            P(),
            P(),
            P(),
            P(),
            P(),
            P(),
            P(),
        ),
        out_specs=(
            P(("row", "space"), None),
            P(("row", "space")),
            P(None, ("row", "space")),
            P(None, ("row", "space")),
        ),
        check_vma=False,
    )
```

```python
import math

import jax
import jax.numpy as jnp
from jax import lax
from jax.experimental import pallas as pl
from jax.experimental.pallas import tpu as pltpu
from jax.sharding import PartitionSpec as P

ITERS = 2


cutoff = 6.0
message_scale = 0.125
two_over_root_pi = 2.0 / math.sqrt(math.pi)
inverse_root_pi = 1.0 / math.sqrt(math.pi)
replicate_limit = 1024
everywhere = ("row", "space")


def lookup(species, table):
    result = jnp.zeros(species.shape, jnp.float32)
    for kind in range(table.shape[0]):
        result = result + jnp.where(species == kind, table[kind], 0.0)
    return result


def pair_terms(target, target_labels, source, source_labels):
    delta = target[:3, :, None] - source[:3, None, :]
    squared = jnp.sum(delta * delta, axis=0)
    same = target_labels[:, None] == source_labels[None, :]
    squared = jnp.where(same, 1.0, squared)
    inverse = lax.rsqrt(squared)
    radius = squared * inverse
    spread = target[3][:, None] * target[3][:, None] + source[3][None, :] * source[3][None, :]
    scale = lax.rsqrt(2.0 * spread)
    scaled = radius * scale
    smear = lax.erf(scaled)
    return delta, same, inverse, scale, scaled, smear


def coulomb(target, target_labels, source, source_labels):
    _, same, inverse, _, _, smear = pair_terms(target, target_labels, source, source_labels)
    return jnp.where(same, 0.0, smear * inverse)


def pair_forces(target, target_labels, source, source_labels, source_charge):
    delta, same, inverse, scale, scaled, smear = pair_terms(
        target, target_labels, source, source_labels
    )
    slope = (
        two_over_root_pi * scale * jnp.exp(-scaled * scaled) * inverse - smear * inverse * inverse
    )
    weight = jnp.where(same, 0.0, source_charge[None, :] * slope * inverse)
    first = jnp.sum(weight[None] * delta, axis=2)
    pairs = ((0, 0), (1, 1), (2, 2), (0, 1), (0, 2), (1, 2))
    second = jnp.stack(
        [jnp.sum(weight * delta[left] * delta[right], axis=1) for left, right in pairs]
    )
    return jnp.concatenate([first, second], axis=0)


def edge_terms(receive, sender_rows, vectors, projected, w_rad1, w_rad2, atoms):
    length = jnp.sqrt(jnp.sum(vectors * vectors, axis=0))
    unit = vectors / length
    order = jnp.arange(1, w_rad1.shape[0] + 1, dtype=jnp.int32).astype(jnp.float32)[:, None]
    ratio = length / cutoff
    envelope = (1.0 - ratio * ratio) * (1.0 - ratio * ratio)
    basis = jnp.sin(order * math.pi * ratio) / ratio * envelope
    mixed = lax.dot_general(
        basis, w_rad1, (((0,), (0,)), ((), ())), precision=lax.Precision.HIGHEST
    )
    radial = jax.nn.silu(mixed).astype(jnp.bfloat16)
    filters = jnp.dot(radial, w_rad2, preferred_element_type=jnp.float32)
    picked = jnp.take(projected, sender_rows, axis=0).astype(jnp.float32) * filters
    chans = w_rad1.shape[1]
    scalar = picked[:, :chans]
    carried = picked[:, chans:]
    joined = [
        scalar,
        unit[0][:, None] * carried,
        unit[1][:, None] * carried,
        unit[2][:, None] * carried,
    ]
    message = jnp.concatenate(joined, axis=1).astype(jnp.bfloat16)
    onehot = (jnp.arange(atoms, dtype=jnp.int32)[:, None] == receive[None, :]).astype(jnp.bfloat16)
    return jnp.dot(onehot, message, preferred_element_type=jnp.float32)


def gathered(block, devices):
    copies = jnp.broadcast_to(block[None], (devices,) + block.shape)
    return lax.all_to_all(copies, everywhere, split_axis=0, concat_axis=0, tiled=True)


def shards(
    features,
    positions,
    species,
    ghost_list,
    edge_recv,
    edge_send,
    edge_vec,
    w_msg,
    w_rad1,
    w_rad2,
    w_up,
    w_out,
    hardness,
    width,
    chi_shift,
    field,
):
    atoms = features.shape[0]
    chans = features.shape[1]
    lanes = lax.axis_size("space")
    devices = lanes * lax.axis_size("row")
    everybody = devices * atoms
    me = lax.axis_index("row") * lanes + lax.axis_index("space")
    sigma = lookup(species, width)
    diag = lookup(species, hardness) + inverse_root_pi / sigma
    placed = jnp.concatenate([positions, sigma[None, :], diag[None, :]], axis=0)
    everyone = gathered(placed, devices).transpose(1, 0, 2).reshape(5, everybody)
    lists = ghost_list[0]
    outgoing = jnp.take(features, lists.reshape(-1), axis=0).reshape(lanes, lists.shape[1], chans)
    ghost_rows = jnp.einsum(
        "dkc,cf->dkf",
        lax.all_to_all(outgoing, "space", split_axis=0, concat_axis=0, tiled=True),
        w_msg,
        preferred_element_type=jnp.float32,
    ).astype(jnp.bfloat16)
    own_rows = jnp.dot(features, w_msg, preferred_element_type=jnp.float32).astype(jnp.bfloat16)
    projected = jnp.concatenate([own_rows, ghost_rows.reshape(-1, 2 * chans)], axis=0)
    summed = edge_terms(edge_recv, edge_send, edge_vec, projected, w_rad1, w_rad2, atoms)
    summed = summed * message_scale
    vector_part = summed[:, chans:].reshape(atoms, 3, chans)
    invariant = jnp.concatenate(
        [summed[:, :chans], jnp.sum(vector_part * vector_part, axis=1)], axis=1
    ).astype(jnp.bfloat16)
    hidden = jax.nn.silu(jnp.dot(invariant, w_up, preferred_element_type=jnp.float32))
    new_features = (features.astype(jnp.float32) + hidden).astype(jnp.bfloat16)
    chi = jnp.dot(hidden, w_out, precision=lax.Precision.HIGHEST) + lookup(species, chi_shift)
    own_labels = me * atoms + jnp.arange(atoms, dtype=jnp.int32)
    all_labels = jnp.arange(everybody, dtype=jnp.int32)
    rhs = field[0] * positions[2] - chi

    if everybody <= replicate_limit:
        kernel = coulomb(everyone, all_labels, everyone, all_labels)
        residual = gathered(rhs, devices).reshape(everybody)
        all_charges = conjugate(
            residual, lambda v: everyone[4] * v + jnp.sum(kernel * v[None, :], axis=1), jnp.sum
        )
        charges = lax.dynamic_slice(all_charges, (me * atoms,), (atoms,))
    else:
        kernel = coulomb(placed, own_labels, everyone, all_labels)

        def spread(vector):
            return gathered(vector, devices).reshape(everybody)

        charges = conjugate(
            rhs,
            lambda v: diag * v + jnp.sum(kernel * spread(v)[None, :], axis=1),
            lambda v: lax.psum(jnp.sum(v), everywhere),
        )
        all_charges = spread(charges)
    sums = pair_forces(placed, own_labels, everyone, all_labels, all_charges)
    pull = -charges[None, :] * sums[:3]
    forces = jnp.concatenate([pull[:2], pull[2:] + (charges * field[0])[None, :]], axis=0)
    virial = 0.5 * charges[None, :] * sums[3:]
    return (new_features, charges, forces, virial)


def conjugate(rhs, apply, total):
    charges = jnp.zeros_like(rhs)
    residual = rhs
    direction = rhs
    norm_now = total(residual * residual)
    for step in range(ITERS):
        image = apply(direction)
        alpha = norm_now / total(direction * image)
        charges = charges + alpha * direction
        if step + 1 < ITERS:
            residual = residual - alpha * image
            fresh = total(residual * residual)
            direction = residual + fresh / norm_now * direction
            norm_now = fresh
    return charges


def split3(value):
    first = value.astype(jnp.bfloat16).astype(jnp.float32)
    rest = value - first
    second = rest.astype(jnp.bfloat16).astype(jnp.float32)
    third = (rest - second).astype(jnp.bfloat16).astype(jnp.float32)
    return first, second, third


def over_first(left, right):
    return lax.dot_general(
        left, right, (((0,), (0,)), ((), ())), preferred_element_type=jnp.float32
    )


def over_last(left, right, precision=None):
    return lax.dot_general(
        left,
        right,
        (((1,), (1,)), ((), ())),
        precision=precision,
        preferred_element_type=jnp.float32,
    )


def silu(value):
    return value / (1.0 + jnp.exp(-value))


def silu_half(value):
    return (0.5 * value) * (1.0 + jnp.tanh(0.5 * value))


sine_series = [(-1.0) ** k * math.pi ** (2 * k + 1) / math.factorial(2 * k + 1) for k in range(7)]


def fetched(pairs, semaphores):
    copies = [
        pltpu.make_async_copy(source, target, semaphores.at[place])
        for place, (source, target) in enumerate(pairs)
    ]
    for copy in copies:
        copy.start()
    return copies


rhs_segment = 3


def pack_kernel(space_ref, features_ref, lists_ref, packed_ref, held_ref, semaphores):
    atoms, chans = features_ref.shape
    copies = fetched(
        [(lists_ref, held_ref), (features_ref, packed_ref.at[pl.ds(0, atoms)])], semaphores
    )
    copies[0].wait()
    _, lanes, width = held_ref.shape
    rows = []
    for place in range(lanes):
        row = held_ref[0, pl.ds(space_ref[0] ^ place, 1), :].astype(jnp.float32) + place * atoms
        parts = [jnp.zeros((1, width), jnp.float32)] * lanes
        parts[place] = row
        rows.append(jnp.concatenate(parts, axis=1))
    rows.append(jnp.zeros((packed_ref.shape[0] - atoms - lanes, chans), jnp.float32))
    packed_ref[atoms:, :] = jnp.concatenate(rows, axis=0).astype(jnp.bfloat16)
    copies[1].wait()


def edge_kernel(
    field_ref,
    space_ref,
    *refs,
):
    count = (len(refs) - 10) // 2
    far, near, semaphores = refs[:count], refs[count + 9 : -1], refs[-1]
    filter_ref, unit_ref, row_ref, slot_ref, local_ref, hit_ref = refs[count : count + 6]
    turned_ref, upward_ref, read_ref = refs[count + 6 : count + 9]
    vec_ref, first_ref, second_ref, send_ref, recv_ref, project_ref, update_ref = near[:7]
    species_ref, hardness_ref, width_ref, shift_ref, positions_ref, out_ref = near[7:]
    copies = fetched(list(zip(far, near)), semaphores)
    for copy in copies[:3]:
        copy.wait()
    edges = vec_ref.shape[1]
    orders = first_ref.shape[0]
    vec = vec_ref[...]
    east, north, up = vec[0:1], vec[1:2], vec[2:3]
    squared = east * east + north * north + up * up
    inverse = lax.rsqrt(squared)
    unit_ref[0:3, :] = vec * inverse
    ratio = squared * inverse * (1.0 / cutoff)
    envelope = (1.0 - ratio * ratio) * (1.0 - ratio * ratio) * (cutoff * inverse)
    order = lax.broadcasted_iota(jnp.int32, (orders, edges), 0).astype(jnp.float32) + 1.0
    turns = order * ratio
    whole = jnp.floor(turns + 0.5)
    part = turns - whole
    sign = 1.0 - 2.0 * (whole - 2.0 * jnp.floor(whole * 0.5))
    series = jnp.full_like(part, sine_series[-1])
    for coefficient in sine_series[-2::-1]:
        series = series * (part * part) + coefficient
    basis = series * part * (sign * envelope)
    b1, b2, b3 = split3(basis)
    w1, w2, w3 = split3(first_ref[...])
    mixed = over_first(
        jnp.concatenate([w1, w1, w2, w2, w1, w3], axis=0).astype(jnp.bfloat16),
        jnp.concatenate([b1, b2, b1, b2, b3, b1], axis=0).astype(jnp.bfloat16),
    )
    radial = silu_half(mixed).astype(jnp.bfloat16)
    filter_ref[...] = over_first(second_ref[...], radial)
    for copy in copies[3:]:
        copy.wait()
    species = species_ref[...]

    def table(ref):
        result = jnp.zeros(species.shape, jnp.float32)
        for kind in range(ref.shape[1]):
            result = result + jnp.where(species == kind, ref[:, kind : kind + 1], 0.0)
        return result

    positions = positions_ref[...]
    sigma = table(width_ref)
    atoms = species.shape[1]
    chans = row_ref.shape[1]
    diag = table(hardness_ref) + inverse_root_pi / sigma
    rhs = field_ref[0] * positions[2:3] - table(shift_ref)
    blank = jnp.zeros((2, atoms), jnp.float32)
    rows = [positions[0:1], blank, rhs, diag, sigma, positions[2:3], positions[1:2]]
    block = jnp.concatenate(
        [jnp.concatenate(rows, axis=0), jnp.zeros((8, chans - atoms), jnp.float32)], axis=1
    )
    block = pltpu.roll(block, 0, 1, stride=atoms, stride_axis=0)
    row_ref[...] = jnp.sum(block, axis=0, keepdims=True)
    lanes = local_ref.shape[0] // atoms
    slots = chans // lanes
    send = send_ref[...]
    own = send < atoms
    slot = jnp.where(own, -1, (send - atoms) ^ (space_ref[0] * slots))
    local = jnp.where(own, send, -1)

    def chosen(ref, index):
        hit = lax.broadcasted_iota(jnp.int32, ref.shape, 0) == index
        ref[...] = jnp.where(hit, 1.0, 0.0).astype(ref.dtype)

    chosen(slot_ref, slot)
    chosen(local_ref, local)
    chosen(hit_ref, recv_ref[...])
    turned_ref[...] = project_ref[...].astype(jnp.float32).T.astype(jnp.bfloat16)
    upward_ref[...] = update_ref[...].astype(jnp.float32).T.astype(jnp.bfloat16)
    read_ref[...] = jnp.broadcast_to(out_ref[...], (atoms, chans)).T


def node_kernel(
    own_ref,
    near_ref,
    side_ref,
    far_ref,
    filter_ref,
    unit_ref,
    row_ref,
    slot_ref,
    local_ref,
    hit_ref,
    turned_ref,
    upward_ref,
    read_ref,
    hidden_ref,
    block_ref,
):
    chans, atoms = hidden_ref.shape
    packed = (own_ref, near_ref, side_ref, far_ref)
    group = jnp.concatenate([ref[:atoms, :] for ref in packed], axis=0)
    chosen = jnp.zeros((1, chans), jnp.float32)
    for place, ref in enumerate(packed):
        tail = ref[atoms:, :].astype(jnp.float32)
        chosen = chosen + tail[place : place + 1]
    fill = jnp.where(
        lax.broadcasted_iota(jnp.int32, (len(packed) * atoms, chans), 0)
        == chosen.astype(jnp.int32),
        1.0,
        0.0,
    ).astype(jnp.bfloat16)
    sender = jnp.dot(fill, slot_ref[...], preferred_element_type=jnp.float32) + local_ref[...]
    projected = over_last(turned_ref[...], group).astype(jnp.bfloat16)
    picked = jnp.dot(projected, sender.astype(jnp.bfloat16), preferred_element_type=jnp.float32)
    scalar = picked[:chans] * filter_ref[:chans, :]
    carried = picked[chans:] * filter_ref[chans:, :]
    parts = [scalar] + [unit_ref[axis : axis + 1, :] * carried for axis in range(3)]
    message = jnp.concatenate([part.astype(jnp.bfloat16) for part in parts], axis=0)
    summed = over_last(message, hit_ref[...]) * message_scale
    square = jnp.zeros((chans, atoms), jnp.float32)
    for component in range(1, 4):
        part = summed[component * chans : (component + 1) * chans]
        square = square + part * part
    invariant = jnp.concatenate([summed[:chans], square], axis=0).astype(jnp.bfloat16)
    hidden = silu(jnp.dot(upward_ref[...], invariant, preferred_element_type=jnp.float32))
    chi = jnp.sum(hidden * read_ref[...], axis=0, keepdims=True)
    chi = jnp.concatenate([chi, jnp.zeros((1, chans - atoms), jnp.float32)], axis=1)
    row = row_ref[...] - pltpu.roll(chi, rhs_segment * atoms, 1)
    block_ref[...] = jnp.broadcast_to(row[None], block_ref.shape)
    hidden_ref[...] = hidden


def feature_kernel(packed_ref, hidden_ref, features_ref):
    atoms = features_ref.shape[0]
    old = packed_ref[...].astype(jnp.float32)[:atoms]
    features_ref[...] = (old + hidden_ref[...].T).astype(jnp.bfloat16)


def reciprocal(value):
    rough = pl.reciprocal(value, approx=True)
    return rough * (2.0 - value * rough)


def smeared(scaled):
    decay = jnp.exp2(scaled * scaled * -math.log2(math.e))
    turn = reciprocal(1.0 + 0.3275911 * scaled)
    series = 1.061405429 * turn - 1.453152027
    series = series * turn + 1.421413741
    series = series * turn - 0.284496736
    series = series * turn + 0.254829592
    return 1.0 - series * turn * decay, decay


def charge_kernel(
    place_ref,
    field_ref,
    all_ref,
    charges_ref,
    forces_ref,
    virial_ref,
    matrix_ref,
    side_ref,
    value_ref,
):
    blocks, _, lanes = all_ref.shape
    own = charges_ref.shape[1]
    count = blocks * own
    fit = lanes // own
    segment = lax.broadcasted_iota(jnp.int32, (8, lanes), 1) // own
    tiles = []
    for first in range(0, blocks, fit):
        tile = jnp.zeros((8, lanes), jnp.float32)
        for place in range(fit):
            row = all_ref[lax.rem(place_ref[0] + first + place, blocks)]
            row = pltpu.roll(jnp.broadcast_to(row, (8, lanes)), 0, 1, stride=own, stride_axis=0)
            row = pltpu.roll(row, place * own, 1) if place else row
            tile = jnp.where(segment == place, row, tile)
        tiles.append(tile)
    everyone = jnp.concatenate(tiles, axis=1)
    columns = everyone.T
    diag, rhs = everyone[4:5], everyone[5:6]
    rows = own
    spread_row = 2.0 * everyone[3:4] * everyone[3:4]
    tiles = count // lanes
    lane = lax.broadcasted_iota(jnp.int32, (rows, lanes), 1)
    line = lax.broadcasted_iota(jnp.int32, (rows, lanes), 0)

    def part(row, tile):
        return row[:, tile * lanes : (tile + 1) * lanes]

    def spread(column):
        return jnp.broadcast_to(column, (rows, lanes))

    above = [jnp.zeros((rows, lanes), jnp.float32) for _ in range(tiles)]
    kept = []
    for start in range(0, count, rows):
        first = start // lanes
        column = columns[start : start + rows]
        place = [spread(column[:, axis : axis + 1]) for axis in range(3)]
        wide = spread(2.0 * column[:, 3:4] * column[:, 3:4])
        value = spread(column[:, 5:6])
        value_ref[start : start + rows, :] = value
        below = jnp.zeros((rows, lanes), jnp.float32)
        for tile in range(first, tiles):
            delta = [place[axis] - part(everyone[axis : axis + 1], tile) for axis in range(3)]
            squared = delta[0] * delta[0] + delta[1] * delta[1] + delta[2] * delta[2]
            if tile == first:
                same = lane == line + (start - first * lanes)
                squared = jnp.where(same, 1.0, squared)
            inverse = lax.rsqrt(squared)
            scale = lax.rsqrt(wide + part(spread_row, tile))
            smear, decay = smeared(squared * inverse * scale)
            kernel = smear * inverse
            if start == 0:
                slope = (two_over_root_pi * scale * decay - kernel) * inverse * inverse
                slope = jnp.where(same, 0.0, slope) if tile == first else slope
                kept.append((delta, slope))
            if tile == first:
                kernel = jnp.where(same, 0.0, kernel)
            else:
                below = below + kernel * part(rhs, tile)
            above[tile] = above[tile] + kernel * value
            matrix_ref[start : start + rows, tile * lanes : (tile + 1) * lanes] = kernel
        if first + 1 < tiles:
            side_ref[start : start + rows, :] = below
    image = []
    for tile in range(tiles):
        value = jnp.sum(above[tile], axis=0, keepdims=True)
        if tile + 1 < tiles:
            below = side_ref[tile * lanes : (tile + 1) * lanes, :].T
            value = value + jnp.sum(below, axis=0, keepdims=True)
        image.append(value)
    image = diag * rhs + jnp.concatenate(image, axis=1)
    across = jnp.broadcast_to(image, (8, count)).T

    def total(value):
        return jnp.sum(value, axis=1, keepdims=True)

    norm = total(rhs * rhs)
    alpha = norm / total(rhs * image)
    residual = rhs - alpha * image
    fresh = total(residual * residual)
    again = fresh / norm
    direction = residual + again * rhs
    onto = [jnp.zeros((rows, lanes), jnp.float32) for _ in range(tiles)]
    above = [jnp.zeros((rows, lanes), jnp.float32) for _ in range(tiles)]
    for start in range(0, count, rows):
        first = start // lanes
        value = (1.0 + again) * value_ref[start : start + rows, :]
        value = value - alpha * spread(across[start : start + rows, 0:1])
        for tile in range(first, tiles):
            sums = onto if tile == first else above
            kernel = matrix_ref[start : start + rows, tile * lanes : (tile + 1) * lanes]
            sums[tile] = sums[tile] + kernel * value
    curved = jnp.zeros((rows, lanes), jnp.float32)
    for tile in range(tiles):
        curved = curved + (onto[tile] + 2.0 * above[tile]) * part(direction, tile)
    curved = jnp.sum(curved, axis=0, keepdims=True)
    for tile in range(tiles):
        curved = curved + part(diag * direction * direction, tile)
    charges = alpha * rhs + fresh / total(curved) * direction

    sums = [jnp.zeros((rows, lanes), jnp.float32) for _ in range(9)]
    for tile, (delta, slope) in enumerate(kept):
        weight = part(charges, tile) * slope
        pulled = [weight * delta[axis] for axis in range(3)]
        terms = pulled + [
            pulled[left] * delta[right]
            for left, right in ((0, 0), (1, 1), (2, 2), (0, 1), (0, 2), (1, 2))
        ]
        sums = [old + term for old, term in zip(sums, terms)]
    table = jnp.zeros((rows, lanes), jnp.float32)
    for place, value in enumerate(sums):
        table = jnp.where(lane == place, total(value), table)
    table = table.T
    mine = charges[:, :own]
    charges_ref[...] = mine
    pull = -mine * table[0:3]
    third = lax.broadcasted_iota(jnp.int32, pull.shape, 0) == 2
    forces_ref[...] = pull + jnp.where(third, mine * field_ref[0], 0.0)
    virial_ref[...] = 0.5 * mine * table[3:9]


def kernel_call(kernel, shapes, arguments, scalars=0, far=0, scratch=(), flops=0):
    shapes = tuple(jax.ShapeDtypeStruct(shape, kind) for shape, kind in shapes)
    spaces = [pltpu.SMEM] * scalars + [pltpu.HBM] * far
    spaces = spaces + [pltpu.VMEM] * (len(arguments) - len(spaces))
    arguments = [
        pltpu.with_memory_space_constraint(value, space) if space is pltpu.HBM else value
        for value, space in zip(arguments, spaces)
    ]
    return pl.pallas_call(
        kernel,
        out_shape=shapes,
        in_specs=[pl.BlockSpec(memory_space=space) for space in spaces],
        out_specs=tuple(pl.BlockSpec(memory_space=pltpu.VMEM) for _ in shapes),
        scratch_shapes=list(scratch),
        compiler_params=pltpu.CompilerParams(vmem_limit_bytes=32 * 1024 * 1024),
        cost_estimate=pl.CostEstimate(flops=flops, bytes_accessed=1 << 20, transcendentals=0),
    )(*arguments)


def exchanged(block, axis, step):
    size = lax.axis_size(axis)
    return lax.ppermute(block, axis, [(place, place ^ step) for place in range(size)])


def few_shards(
    features,
    positions,
    species,
    ghost_list,
    edge_recv,
    edge_send,
    edge_vec,
    w_msg,
    w_rad1,
    w_rad2,
    w_up,
    w_out,
    hardness,
    width,
    chi_shift,
    field,
):
    atoms, chans = features.shape
    edges = edge_recv.shape[0]
    rows, lanes = lax.axis_size("row"), lax.axis_size("space")
    space = lax.axis_index("space").astype(jnp.int32)
    (packed,) = kernel_call(
        pack_kernel,
        [((atoms + 16, chans), jnp.bfloat16)],
        (space.reshape(1), features, ghost_list),
        scalars=1,
        far=2,
        scratch=[
            pltpu.VMEM(ghost_list.shape, ghost_list.dtype),
            pltpu.SemaphoreType.DMA((2,)),
        ],
    )
    others = [exchanged(packed, "space", step) for step in range(1, lanes)]
    rest = (edge_vec, w_rad1, w_rad2, edge_send[None], edge_recv[None], w_msg, w_up)
    rest = rest + (species[None], hardness[None], width[None], chi_shift[None], positions)
    rest = rest + (w_out[None],)
    parts = kernel_call(
        edge_kernel,
        [
            ((2 * chans, edges), jnp.float32),
            ((8, edges), jnp.float32),
            ((1, chans), jnp.float32),
            ((chans, edges), jnp.bfloat16),
            ((lanes * atoms, edges), jnp.float32),
            ((atoms, edges), jnp.bfloat16),
            ((2 * chans, chans), jnp.bfloat16),
            ((chans, 2 * chans), jnp.bfloat16),
            ((chans, atoms), jnp.float32),
        ],
        (field, space.reshape(1), *rest),
        scalars=2,
        far=len(rest),
        scratch=[pltpu.VMEM(value.shape, value.dtype) for value in rest]
        + [pltpu.SemaphoreType.DMA((len(rest),))],
        flops=1 << 28,
    )
    devices = rows * lanes
    hidden, block = kernel_call(
        node_kernel,
        [((chans, atoms), jnp.float32), ((devices, 1, chans), jnp.float32)],
        (packed, *others, *parts),
        flops=1 << 28,
    )
    (new_features,) = kernel_call(
        feature_kernel, [((atoms, chans), jnp.bfloat16)], (packed, hidden), flops=1 << 20
    )
    block = lax.all_to_all(block, everywhere, 0, 0, tiled=True)
    place = lax.axis_index("row").astype(jnp.int32) * lanes + space
    everybody = rows * lanes * atoms
    charges, forces, virial = kernel_call(
        charge_kernel,
        [((count, atoms), jnp.float32) for count in (1, 3, 6)],
        (place.reshape(1), field, block),
        scalars=2,
        scratch=[
            pltpu.VMEM((everybody, everybody), jnp.float32),
            pltpu.VMEM((everybody, chans), jnp.float32),
            pltpu.VMEM((everybody, chans), jnp.float32),
        ],
        flops=1 << 28,
    )
    return (new_features, charges[0], forces, virial)


def solution(mesh):
    small = mesh.shape["space"] == 4 and mesh.shape["row"] == 8
    return jax.shard_map(
        few_shards if small else shards,
        mesh=mesh,
        in_specs=(
            P(("row", "space"), None),
            P(None, ("row", "space")),
            P(("row", "space")),
            P("row", "space", None),
            P(("row", "space")),
            P(("row", "space")),
            P(None, ("row", "space")),
            P(),
            P(),
            P(),
            P(),
            P(),
            P(),
            P(),
            P(),
            P(),
        ),
        out_specs=(
            P(("row", "space"), None),
            P(("row", "space")),
            P(None, ("row", "space")),
            P(None, ("row", "space")),
        ),
        check_vma=False,
    )
```

```python
import math

import jax
import jax.numpy as jnp
from jax import lax
from jax.experimental import pallas as pl
from jax.experimental.pallas import tpu as pltpu
from jax.sharding import PartitionSpec as P

ITERS = 2


cutoff = 6.0
message_scale = 0.125
two_over_root_pi = 2.0 / math.sqrt(math.pi)
inverse_root_pi = 1.0 / math.sqrt(math.pi)
replicate_limit = 1024
everywhere = ("row", "space")


def lookup(species, table):
    result = jnp.zeros(species.shape, jnp.float32)
    for kind in range(table.shape[0]):
        result = result + jnp.where(species == kind, table[kind], 0.0)
    return result


def pair_terms(target, target_labels, source, source_labels):
    delta = target[:3, :, None] - source[:3, None, :]
    squared = jnp.sum(delta * delta, axis=0)
    same = target_labels[:, None] == source_labels[None, :]
    squared = jnp.where(same, 1.0, squared)
    inverse = lax.rsqrt(squared)
    radius = squared * inverse
    spread = target[3][:, None] * target[3][:, None] + source[3][None, :] * source[3][None, :]
    scale = lax.rsqrt(2.0 * spread)
    scaled = radius * scale
    smear = lax.erf(scaled)
    return delta, same, inverse, scale, scaled, smear


def coulomb(target, target_labels, source, source_labels):
    _, same, inverse, _, _, smear = pair_terms(target, target_labels, source, source_labels)
    return jnp.where(same, 0.0, smear * inverse)


def pair_forces(target, target_labels, source, source_labels, source_charge):
    delta, same, inverse, scale, scaled, smear = pair_terms(
        target, target_labels, source, source_labels
    )
    slope = (
        two_over_root_pi * scale * jnp.exp(-scaled * scaled) * inverse - smear * inverse * inverse
    )
    weight = jnp.where(same, 0.0, source_charge[None, :] * slope * inverse)
    first = jnp.sum(weight[None] * delta, axis=2)
    pairs = ((0, 0), (1, 1), (2, 2), (0, 1), (0, 2), (1, 2))
    second = jnp.stack(
        [jnp.sum(weight * delta[left] * delta[right], axis=1) for left, right in pairs]
    )
    return jnp.concatenate([first, second], axis=0)


def edge_terms(receive, sender_rows, vectors, projected, w_rad1, w_rad2, atoms):
    length = jnp.sqrt(jnp.sum(vectors * vectors, axis=0))
    unit = vectors / length
    order = jnp.arange(1, w_rad1.shape[0] + 1, dtype=jnp.int32).astype(jnp.float32)[:, None]
    ratio = length / cutoff
    envelope = (1.0 - ratio * ratio) * (1.0 - ratio * ratio)
    basis = jnp.sin(order * math.pi * ratio) / ratio * envelope
    mixed = lax.dot_general(
        basis, w_rad1, (((0,), (0,)), ((), ())), precision=lax.Precision.HIGHEST
    )
    radial = jax.nn.silu(mixed).astype(jnp.bfloat16)
    filters = jnp.dot(radial, w_rad2, preferred_element_type=jnp.float32)
    picked = jnp.take(projected, sender_rows, axis=0).astype(jnp.float32) * filters
    chans = w_rad1.shape[1]
    scalar = picked[:, :chans]
    carried = picked[:, chans:]
    joined = [
        scalar,
        unit[0][:, None] * carried,
        unit[1][:, None] * carried,
        unit[2][:, None] * carried,
    ]
    message = jnp.concatenate(joined, axis=1).astype(jnp.bfloat16)
    onehot = (jnp.arange(atoms, dtype=jnp.int32)[:, None] == receive[None, :]).astype(jnp.bfloat16)
    return jnp.dot(onehot, message, preferred_element_type=jnp.float32)


def gathered(block, devices):
    copies = jnp.broadcast_to(block[None], (devices,) + block.shape)
    return lax.all_to_all(copies, everywhere, split_axis=0, concat_axis=0, tiled=True)


def shards(
    features,
    positions,
    species,
    ghost_list,
    edge_recv,
    edge_send,
    edge_vec,
    w_msg,
    w_rad1,
    w_rad2,
    w_up,
    w_out,
    hardness,
    width,
    chi_shift,
    field,
):
    atoms = features.shape[0]
    chans = features.shape[1]
    lanes = lax.axis_size("space")
    devices = lanes * lax.axis_size("row")
    everybody = devices * atoms
    me = lax.axis_index("row") * lanes + lax.axis_index("space")
    sigma = lookup(species, width)
    diag = lookup(species, hardness) + inverse_root_pi / sigma
    placed = jnp.concatenate([positions, sigma[None, :], diag[None, :]], axis=0)
    everyone = gathered(placed, devices).transpose(1, 0, 2).reshape(5, everybody)
    lists = ghost_list[0]
    outgoing = jnp.take(features, lists.reshape(-1), axis=0).reshape(lanes, lists.shape[1], chans)
    ghost_rows = jnp.einsum(
        "dkc,cf->dkf",
        lax.all_to_all(outgoing, "space", split_axis=0, concat_axis=0, tiled=True),
        w_msg,
        preferred_element_type=jnp.float32,
    ).astype(jnp.bfloat16)
    own_rows = jnp.dot(features, w_msg, preferred_element_type=jnp.float32).astype(jnp.bfloat16)
    projected = jnp.concatenate([own_rows, ghost_rows.reshape(-1, 2 * chans)], axis=0)
    summed = edge_terms(edge_recv, edge_send, edge_vec, projected, w_rad1, w_rad2, atoms)
    summed = summed * message_scale
    vector_part = summed[:, chans:].reshape(atoms, 3, chans)
    invariant = jnp.concatenate(
        [summed[:, :chans], jnp.sum(vector_part * vector_part, axis=1)], axis=1
    ).astype(jnp.bfloat16)
    hidden = jax.nn.silu(jnp.dot(invariant, w_up, preferred_element_type=jnp.float32))
    new_features = (features.astype(jnp.float32) + hidden).astype(jnp.bfloat16)
    chi = jnp.dot(hidden, w_out, precision=lax.Precision.HIGHEST) + lookup(species, chi_shift)
    own_labels = me * atoms + jnp.arange(atoms, dtype=jnp.int32)
    all_labels = jnp.arange(everybody, dtype=jnp.int32)
    rhs = field[0] * positions[2] - chi

    if everybody <= replicate_limit:
        kernel = coulomb(everyone, all_labels, everyone, all_labels)
        residual = gathered(rhs, devices).reshape(everybody)
        all_charges = conjugate(
            residual, lambda v: everyone[4] * v + jnp.sum(kernel * v[None, :], axis=1), jnp.sum
        )
        charges = lax.dynamic_slice(all_charges, (me * atoms,), (atoms,))
    else:
        kernel = coulomb(placed, own_labels, everyone, all_labels)

        def spread(vector):
            return gathered(vector, devices).reshape(everybody)

        charges = conjugate(
            rhs,
            lambda v: diag * v + jnp.sum(kernel * spread(v)[None, :], axis=1),
            lambda v: lax.psum(jnp.sum(v), everywhere),
        )
        all_charges = spread(charges)
    sums = pair_forces(placed, own_labels, everyone, all_labels, all_charges)
    pull = -charges[None, :] * sums[:3]
    forces = jnp.concatenate([pull[:2], pull[2:] + (charges * field[0])[None, :]], axis=0)
    virial = 0.5 * charges[None, :] * sums[3:]
    return (new_features, charges, forces, virial)


def conjugate(rhs, apply, total):
    charges = jnp.zeros_like(rhs)
    residual = rhs
    direction = rhs
    norm_now = total(residual * residual)
    for step in range(ITERS):
        image = apply(direction)
        alpha = norm_now / total(direction * image)
        charges = charges + alpha * direction
        if step + 1 < ITERS:
            residual = residual - alpha * image
            fresh = total(residual * residual)
            direction = residual + fresh / norm_now * direction
            norm_now = fresh
    return charges


def split3(value):
    first = value.astype(jnp.bfloat16).astype(jnp.float32)
    rest = value - first
    second = rest.astype(jnp.bfloat16).astype(jnp.float32)
    third = (rest - second).astype(jnp.bfloat16).astype(jnp.float32)
    return first, second, third


def over_first(left, right):
    return lax.dot_general(
        left, right, (((0,), (0,)), ((), ())), preferred_element_type=jnp.float32
    )


def over_last(left, right, precision=None):
    return lax.dot_general(
        left,
        right,
        (((1,), (1,)), ((), ())),
        precision=precision,
        preferred_element_type=jnp.float32,
    )


def silu(value):
    return value / (1.0 + jnp.exp(-value))


def silu_half(value):
    return (0.5 * value) * (1.0 + jnp.tanh(0.5 * value))


sine_series = [(-1.0) ** k * math.pi ** (2 * k + 1) / math.factorial(2 * k + 1) for k in range(7)]


def fetched(pairs, semaphores):
    copies = [
        pltpu.make_async_copy(source, target, semaphores.at[place])
        for place, (source, target) in enumerate(pairs)
    ]
    for copy in copies:
        copy.start()
    return copies


chi_segment = 3


def pack_kernel(space_ref, features_ref, lists_ref, packed_ref, held_ref, semaphores):
    atoms, chans = features_ref.shape
    copies = fetched(
        [(lists_ref, held_ref), (features_ref, packed_ref.at[pl.ds(0, atoms)])], semaphores
    )
    copies[0].wait()
    _, lanes, width = held_ref.shape
    rows = []
    for place in range(lanes):
        row = held_ref[0, pl.ds(space_ref[0] ^ place, 1), :].astype(jnp.float32) + place * atoms
        parts = [jnp.zeros((1, width), jnp.float32)] * lanes
        parts[place] = row
        rows.append(jnp.concatenate(parts, axis=1))
    rows.append(jnp.zeros((packed_ref.shape[0] - atoms - lanes, chans), jnp.float32))
    packed_ref[atoms:, :] = jnp.concatenate(rows, axis=0).astype(jnp.bfloat16)
    copies[1].wait()


def edge_kernel(
    space_ref,
    *refs,
):
    count = (len(refs) - 10) // 2
    far, near, semaphores = refs[:count], refs[count + 9 : -1], refs[-1]
    filter_ref, unit_ref, row_ref, slot_ref, local_ref, hit_ref = refs[count : count + 6]
    turned_ref, upward_ref, read_ref = refs[count + 6 : count + 9]
    vec_ref, first_ref, second_ref, send_ref, recv_ref, project_ref, update_ref = near[:7]
    species_ref, hardness_ref, width_ref, shift_ref, positions_ref, out_ref = near[7:]
    copies = fetched(list(zip(far, near)), semaphores)
    for copy in copies[:3]:
        copy.wait()
    edges = vec_ref.shape[1]
    orders = first_ref.shape[0]
    vec = vec_ref[...]
    east, north, up = vec[0:1], vec[1:2], vec[2:3]
    squared = east * east + north * north + up * up
    inverse = lax.rsqrt(squared)
    unit_ref[0:3, :] = vec * inverse
    ratio = squared * inverse * (1.0 / cutoff)
    envelope = (1.0 - ratio * ratio) * (1.0 - ratio * ratio) * (cutoff * inverse)
    order = lax.broadcasted_iota(jnp.int32, (orders, edges), 0).astype(jnp.float32) + 1.0
    turns = order * ratio
    whole = jnp.floor(turns + 0.5)
    part = turns - whole
    sign = 1.0 - 2.0 * (whole - 2.0 * jnp.floor(whole * 0.5))
    series = jnp.full_like(part, sine_series[-1])
    for coefficient in sine_series[-2::-1]:
        series = series * (part * part) + coefficient
    basis = series * part * (sign * envelope)
    b1, b2, b3 = split3(basis)
    w1, w2, w3 = split3(first_ref[...])
    mixed = over_first(
        jnp.concatenate([w1, w1, w2, w2, w1, w3], axis=0).astype(jnp.bfloat16),
        jnp.concatenate([b1, b2, b1, b2, b3, b1], axis=0).astype(jnp.bfloat16),
    )
    radial = silu_half(mixed).astype(jnp.bfloat16)
    filter_ref[...] = over_first(second_ref[...], radial)
    for copy in copies[3:]:
        copy.wait()
    species = species_ref[...]

    def table(ref):
        result = jnp.zeros(species.shape, jnp.float32)
        for kind in range(ref.shape[1]):
            result = result + jnp.where(species == kind, ref[:, kind : kind + 1], 0.0)
        return result

    positions = positions_ref[...]
    sigma = table(width_ref)
    atoms = species.shape[1]
    chans = row_ref.shape[1]
    diag = table(hardness_ref) + inverse_root_pi / sigma
    blank = jnp.zeros((2, atoms), jnp.float32)
    rows = [positions[0:1], blank, -table(shift_ref), diag, sigma, positions[2:3], positions[1:2]]
    block = jnp.concatenate(
        [jnp.concatenate(rows, axis=0), jnp.zeros((8, chans - atoms), jnp.float32)], axis=1
    )
    block = pltpu.roll(block, 0, 1, stride=atoms, stride_axis=0)
    row_ref[...] = jnp.sum(block, axis=0, keepdims=True)
    lanes = local_ref.shape[0] // atoms
    slots = chans // lanes
    send = send_ref[...]
    own = send < atoms
    slot = jnp.where(own, -1, (send - atoms) ^ (space_ref[0] * slots))
    local = jnp.where(own, send, -1)

    def chosen(ref, index):
        hit = lax.broadcasted_iota(jnp.int32, ref.shape, 0) == index
        ref[...] = jnp.where(hit, 1.0, 0.0).astype(ref.dtype)

    chosen(slot_ref, slot)
    chosen(local_ref, local)
    chosen(hit_ref, recv_ref[...])
    turned_ref[...] = project_ref[...].astype(jnp.float32).T.astype(jnp.bfloat16)
    upward_ref[...] = update_ref[...].astype(jnp.float32).T.astype(jnp.bfloat16)
    read_ref[...] = jnp.broadcast_to(out_ref[...], (atoms, chans)).T


def node_kernel(
    own_ref,
    near_ref,
    side_ref,
    far_ref,
    filter_ref,
    unit_ref,
    row_ref,
    slot_ref,
    local_ref,
    hit_ref,
    turned_ref,
    upward_ref,
    read_ref,
    hidden_ref,
    block_ref,
):
    chans, atoms = hidden_ref.shape
    packed = (own_ref, near_ref, side_ref, far_ref)
    group = jnp.concatenate([ref[:atoms, :] for ref in packed], axis=0)
    chosen = jnp.zeros((1, chans), jnp.float32)
    for place, ref in enumerate(packed):
        tail = ref[atoms:, :].astype(jnp.float32)
        chosen = chosen + tail[place : place + 1]
    fill = jnp.where(
        lax.broadcasted_iota(jnp.int32, (len(packed) * atoms, chans), 0)
        == chosen.astype(jnp.int32),
        1.0,
        0.0,
    ).astype(jnp.bfloat16)
    sender = jnp.dot(fill, slot_ref[...], preferred_element_type=jnp.float32) + local_ref[...]
    projected = over_last(turned_ref[...], group).astype(jnp.bfloat16)
    picked = jnp.dot(projected, sender.astype(jnp.bfloat16), preferred_element_type=jnp.float32)
    scalar = picked[:chans] * filter_ref[:chans, :]
    carried = picked[chans:] * filter_ref[chans:, :]
    parts = [scalar] + [unit_ref[axis : axis + 1, :] * carried for axis in range(3)]
    message = jnp.concatenate([part.astype(jnp.bfloat16) for part in parts], axis=0)
    summed = over_last(message, hit_ref[...]) * message_scale
    square = jnp.zeros((chans, atoms), jnp.float32)
    for component in range(1, 4):
        part = summed[component * chans : (component + 1) * chans]
        square = square + part * part
    invariant = jnp.concatenate([summed[:chans], square], axis=0).astype(jnp.bfloat16)
    hidden = silu(jnp.dot(upward_ref[...], invariant, preferred_element_type=jnp.float32))
    chi = jnp.sum(hidden * read_ref[...], axis=0, keepdims=True)
    chi = jnp.concatenate([chi, jnp.zeros((1, chans - atoms), jnp.float32)], axis=1)
    row = row_ref[...] - pltpu.roll(chi, chi_segment * atoms, 1)
    block_ref[...] = jnp.broadcast_to(row[None], block_ref.shape)
    hidden_ref[...] = hidden


def feature_kernel(packed_ref, hidden_ref, features_ref):
    atoms = features_ref.shape[0]
    old = packed_ref[...].astype(jnp.float32)[:atoms]
    features_ref[...] = (old + hidden_ref[...].T).astype(jnp.bfloat16)


def reciprocal(value):
    rough = pl.reciprocal(value, approx=True)
    return rough * (2.0 - value * rough)


def smeared(scaled):
    decay = jnp.exp2(scaled * scaled * -math.log2(math.e))
    turn = reciprocal(1.0 + 0.3275911 * scaled)
    series = 1.061405429 * turn - 1.453152027
    series = series * turn + 1.421413741
    series = series * turn - 0.284496736
    series = series * turn + 0.254829592
    return 1.0 - series * turn * decay, decay


def charge_kernel(
    place_ref,
    field_ref,
    all_ref,
    charges_ref,
    forces_ref,
    virial_ref,
    matrix_ref,
    side_ref,
    value_ref,
):
    blocks, _, lanes = all_ref.shape
    own = charges_ref.shape[1]
    count = blocks * own
    fit = lanes // own
    segment = lax.broadcasted_iota(jnp.int32, (8, lanes), 1) // own
    tiles = []
    for first in range(0, blocks, fit):
        tile = jnp.zeros((8, lanes), jnp.float32)
        for place in range(fit):
            row = all_ref[lax.rem(place_ref[0] + first + place, blocks)]
            row = pltpu.roll(jnp.broadcast_to(row, (8, lanes)), 0, 1, stride=own, stride_axis=0)
            row = pltpu.roll(row, place * own, 1) if place else row
            tile = jnp.where(segment == place, row, tile)
        tiles.append(tile)
    everyone = jnp.concatenate(tiles, axis=1)
    last = lax.broadcasted_iota(jnp.int32, everyone.shape, 0) == 5
    everyone = everyone + jnp.where(last, field_ref[0] * everyone[2:3], 0.0)
    columns = everyone.T
    diag, rhs = everyone[4:5], everyone[5:6]
    rows = own
    spread_row = 2.0 * everyone[3:4] * everyone[3:4]
    tiles = count // lanes
    lane = lax.broadcasted_iota(jnp.int32, (rows, lanes), 1)
    line = lax.broadcasted_iota(jnp.int32, (rows, lanes), 0)

    def part(row, tile):
        return row[:, tile * lanes : (tile + 1) * lanes]

    def spread(column):
        return jnp.broadcast_to(column, (rows, lanes))

    above = [jnp.zeros((rows, lanes), jnp.float32) for _ in range(tiles)]
    kept = []
    for start in range(0, count, rows):
        first = start // lanes
        column = columns[start : start + rows]
        place = [spread(column[:, axis : axis + 1]) for axis in range(3)]
        wide = spread(2.0 * column[:, 3:4] * column[:, 3:4])
        value = spread(column[:, 5:6])
        value_ref[start : start + rows, :] = value
        below = jnp.zeros((rows, lanes), jnp.float32)
        for tile in range(first, tiles):
            delta = [place[axis] - part(everyone[axis : axis + 1], tile) for axis in range(3)]
            squared = delta[0] * delta[0] + delta[1] * delta[1] + delta[2] * delta[2]
            if tile == first:
                same = lane == line + (start - first * lanes)
                squared = jnp.where(same, 1.0, squared)
            inverse = lax.rsqrt(squared)
            scale = lax.rsqrt(wide + part(spread_row, tile))
            smear, decay = smeared(squared * inverse * scale)
            kernel = smear * inverse
            if start == 0:
                slope = (two_over_root_pi * scale * decay - kernel) * inverse * inverse
                slope = jnp.where(same, 0.0, slope) if tile == first else slope
                kept.append((delta, slope))
            if tile == first:
                kernel = jnp.where(same, 0.0, kernel)
            else:
                below = below + kernel * part(rhs, tile)
            above[tile] = above[tile] + kernel * value
            matrix_ref[start : start + rows, tile * lanes : (tile + 1) * lanes] = kernel
        if first + 1 < tiles:
            side_ref[start : start + rows, :] = below
    image = []
    for tile in range(tiles):
        value = jnp.sum(above[tile], axis=0, keepdims=True)
        if tile + 1 < tiles:
            below = side_ref[tile * lanes : (tile + 1) * lanes, :].T
            value = value + jnp.sum(below, axis=0, keepdims=True)
        image.append(value)
    image = diag * rhs + jnp.concatenate(image, axis=1)
    across = jnp.broadcast_to(image, (8, count)).T

    def total(value):
        return jnp.sum(value, axis=1, keepdims=True)

    norm = total(rhs * rhs)
    alpha = norm / total(rhs * image)
    residual = rhs - alpha * image
    fresh = total(residual * residual)
    again = fresh / norm
    direction = residual + again * rhs
    onto = [jnp.zeros((rows, lanes), jnp.float32) for _ in range(tiles)]
    above = [jnp.zeros((rows, lanes), jnp.float32) for _ in range(tiles)]
    for start in range(0, count, rows):
        first = start // lanes
        value = (1.0 + again) * value_ref[start : start + rows, :]
        value = value - alpha * spread(across[start : start + rows, 0:1])
        for tile in range(first, tiles):
            sums = onto if tile == first else above
            kernel = matrix_ref[start : start + rows, tile * lanes : (tile + 1) * lanes]
            sums[tile] = sums[tile] + kernel * value
    curved = jnp.zeros((rows, lanes), jnp.float32)
    for tile in range(tiles):
        curved = curved + (onto[tile] + 2.0 * above[tile]) * part(direction, tile)
    curved = jnp.sum(curved, axis=0, keepdims=True)
    for tile in range(tiles):
        curved = curved + part(diag * direction * direction, tile)
    charges = alpha * rhs + fresh / total(curved) * direction

    sums = [jnp.zeros((rows, lanes), jnp.float32) for _ in range(9)]
    for tile, (delta, slope) in enumerate(kept):
        weight = part(charges, tile) * slope
        pulled = [weight * delta[axis] for axis in range(3)]
        terms = pulled + [
            pulled[left] * delta[right]
            for left, right in ((0, 0), (1, 1), (2, 2), (0, 1), (0, 2), (1, 2))
        ]
        sums = [old + term for old, term in zip(sums, terms)]
    table = jnp.zeros((rows, lanes), jnp.float32)
    for place, value in enumerate(sums):
        table = jnp.where(lane == place, total(value), table)
    table = table.T
    mine = charges[:, :own]
    charges_ref[...] = mine
    pull = -mine * table[0:3]
    third = lax.broadcasted_iota(jnp.int32, pull.shape, 0) == 2
    forces_ref[...] = pull + jnp.where(third, mine * field_ref[0], 0.0)
    virial_ref[...] = 0.5 * mine * table[3:9]


def kernel_call(kernel, shapes, arguments, scalars=0, far=0, scratch=(), flops=0):
    shapes = tuple(jax.ShapeDtypeStruct(shape, kind) for shape, kind in shapes)
    spaces = [pltpu.SMEM] * scalars + [pltpu.HBM] * far
    spaces = spaces + [pltpu.VMEM] * (len(arguments) - len(spaces))
    arguments = [
        pltpu.with_memory_space_constraint(value, space) if space is pltpu.HBM else value
        for value, space in zip(arguments, spaces)
    ]
    return pl.pallas_call(
        kernel,
        out_shape=shapes,
        in_specs=[pl.BlockSpec(memory_space=space) for space in spaces],
        out_specs=tuple(pl.BlockSpec(memory_space=pltpu.VMEM) for _ in shapes),
        scratch_shapes=list(scratch),
        compiler_params=pltpu.CompilerParams(vmem_limit_bytes=32 * 1024 * 1024),
        cost_estimate=pl.CostEstimate(flops=flops, bytes_accessed=1 << 20, transcendentals=0),
    )(*arguments)


def exchanged(block, axis, step):
    size = lax.axis_size(axis)
    return lax.ppermute(block, axis, [(place, place ^ step) for place in range(size)])


def few_shards(
    features,
    positions,
    species,
    ghost_list,
    edge_recv,
    edge_send,
    edge_vec,
    w_msg,
    w_rad1,
    w_rad2,
    w_up,
    w_out,
    hardness,
    width,
    chi_shift,
    field,
):
    atoms, chans = features.shape
    edges = edge_recv.shape[0]
    rows, lanes = lax.axis_size("row"), lax.axis_size("space")
    space = lax.axis_index("space").astype(jnp.int32)
    (packed,) = kernel_call(
        pack_kernel,
        [((atoms + 16, chans), jnp.bfloat16)],
        (space.reshape(1), features, ghost_list),
        scalars=1,
        far=2,
        scratch=[
            pltpu.VMEM(ghost_list.shape, ghost_list.dtype),
            pltpu.SemaphoreType.DMA((2,)),
        ],
    )
    others = [exchanged(packed, "space", step) for step in range(1, lanes)]
    rest = (edge_vec, w_rad1, w_rad2, edge_send[None], edge_recv[None], w_msg, w_up)
    rest = rest + (species[None], hardness[None], width[None], chi_shift[None], positions)
    rest = rest + (w_out[None],)
    parts = kernel_call(
        edge_kernel,
        [
            ((2 * chans, edges), jnp.float32),
            ((8, edges), jnp.float32),
            ((1, chans), jnp.float32),
            ((chans, edges), jnp.bfloat16),
            ((lanes * atoms, edges), jnp.float32),
            ((atoms, edges), jnp.bfloat16),
            ((2 * chans, chans), jnp.bfloat16),
            ((chans, 2 * chans), jnp.bfloat16),
            ((chans, atoms), jnp.float32),
        ],
        (space.reshape(1), *rest),
        scalars=1,
        far=len(rest),
        scratch=[pltpu.VMEM(value.shape, value.dtype) for value in rest]
        + [pltpu.SemaphoreType.DMA((len(rest),))],
        flops=1 << 28,
    )
    devices = rows * lanes
    hidden, block = kernel_call(
        node_kernel,
        [((chans, atoms), jnp.float32), ((devices, 1, chans), jnp.float32)],
        (packed, *others, *parts),
        flops=1 << 28,
    )
    (new_features,) = kernel_call(
        feature_kernel, [((atoms, chans), jnp.bfloat16)], (packed, hidden), flops=1 << 20
    )
    block = lax.all_to_all(block, everywhere, 0, 0, tiled=True)
    place = lax.axis_index("row").astype(jnp.int32) * lanes + space
    everybody = rows * lanes * atoms
    charges, forces, virial = kernel_call(
        charge_kernel,
        [((count, atoms), jnp.float32) for count in (1, 3, 6)],
        (place.reshape(1), field, block),
        scalars=2,
        scratch=[
            pltpu.VMEM((everybody, everybody), jnp.float32),
            pltpu.VMEM((everybody, chans), jnp.float32),
            pltpu.VMEM((everybody, chans), jnp.float32),
        ],
        flops=1 << 28,
    )
    return (new_features, charges[0], forces, virial)


def solution(mesh):
    small = mesh.shape["space"] == 4 and mesh.shape["row"] == 8
    return jax.shard_map(
        few_shards if small else shards,
        mesh=mesh,
        in_specs=(
            P(("row", "space"), None),
            P(None, ("row", "space")),
            P(("row", "space")),
            P("row", "space", None),
            P(("row", "space")),
            P(("row", "space")),
            P(None, ("row", "space")),
            P(),
            P(),
            P(),
            P(),
            P(),
            P(),
            P(),
            P(),
            P(),
        ),
        out_specs=(
            P(("row", "space"), None),
            P(("row", "space")),
            P(None, ("row", "space")),
            P(None, ("row", "space")),
        ),
        check_vma=False,
    )
```

```python
import math

import jax
import jax.numpy as jnp
from jax import lax
from jax.experimental import pallas as pl
from jax.experimental.pallas import tpu as pltpu
from jax.sharding import PartitionSpec as P

ITERS = 2


cutoff = 6.0
message_scale = 0.125
two_over_root_pi = 2.0 / math.sqrt(math.pi)
inverse_root_pi = 1.0 / math.sqrt(math.pi)
replicate_limit = 1024
everywhere = ("row", "space")


def lookup(species, table):
    result = jnp.zeros(species.shape, jnp.float32)
    for kind in range(table.shape[0]):
        result = result + jnp.where(species == kind, table[kind], 0.0)
    return result


def pair_terms(target, target_labels, source, source_labels):
    delta = target[:3, :, None] - source[:3, None, :]
    squared = jnp.sum(delta * delta, axis=0)
    same = target_labels[:, None] == source_labels[None, :]
    squared = jnp.where(same, 1.0, squared)
    inverse = lax.rsqrt(squared)
    radius = squared * inverse
    spread = target[3][:, None] * target[3][:, None] + source[3][None, :] * source[3][None, :]
    scale = lax.rsqrt(2.0 * spread)
    scaled = radius * scale
    smear = lax.erf(scaled)
    return delta, same, inverse, scale, scaled, smear


def coulomb(target, target_labels, source, source_labels):
    _, same, inverse, _, _, smear = pair_terms(target, target_labels, source, source_labels)
    return jnp.where(same, 0.0, smear * inverse)


def pair_forces(target, target_labels, source, source_labels, source_charge):
    delta, same, inverse, scale, scaled, smear = pair_terms(
        target, target_labels, source, source_labels
    )
    slope = (
        two_over_root_pi * scale * jnp.exp(-scaled * scaled) * inverse - smear * inverse * inverse
    )
    weight = jnp.where(same, 0.0, source_charge[None, :] * slope * inverse)
    first = jnp.sum(weight[None] * delta, axis=2)
    pairs = ((0, 0), (1, 1), (2, 2), (0, 1), (0, 2), (1, 2))
    second = jnp.stack(
        [jnp.sum(weight * delta[left] * delta[right], axis=1) for left, right in pairs]
    )
    return jnp.concatenate([first, second], axis=0)


def edge_terms(receive, sender_rows, vectors, projected, w_rad1, w_rad2, atoms):
    length = jnp.sqrt(jnp.sum(vectors * vectors, axis=0))
    unit = vectors / length
    order = jnp.arange(1, w_rad1.shape[0] + 1, dtype=jnp.int32).astype(jnp.float32)[:, None]
    ratio = length / cutoff
    envelope = (1.0 - ratio * ratio) * (1.0 - ratio * ratio)
    basis = jnp.sin(order * math.pi * ratio) / ratio * envelope
    mixed = lax.dot_general(
        basis, w_rad1, (((0,), (0,)), ((), ())), precision=lax.Precision.HIGHEST
    )
    radial = jax.nn.silu(mixed).astype(jnp.bfloat16)
    filters = jnp.dot(radial, w_rad2, preferred_element_type=jnp.float32)
    picked = jnp.take(projected, sender_rows, axis=0).astype(jnp.float32) * filters
    chans = w_rad1.shape[1]
    scalar = picked[:, :chans]
    carried = picked[:, chans:]
    joined = [
        scalar,
        unit[0][:, None] * carried,
        unit[1][:, None] * carried,
        unit[2][:, None] * carried,
    ]
    message = jnp.concatenate(joined, axis=1).astype(jnp.bfloat16)
    onehot = (jnp.arange(atoms, dtype=jnp.int32)[:, None] == receive[None, :]).astype(jnp.bfloat16)
    return jnp.dot(onehot, message, preferred_element_type=jnp.float32)


def gathered(block, devices):
    copies = jnp.broadcast_to(block[None], (devices,) + block.shape)
    return lax.all_to_all(copies, everywhere, split_axis=0, concat_axis=0, tiled=True)


def shards(
    features,
    positions,
    species,
    ghost_list,
    edge_recv,
    edge_send,
    edge_vec,
    w_msg,
    w_rad1,
    w_rad2,
    w_up,
    w_out,
    hardness,
    width,
    chi_shift,
    field,
):
    atoms = features.shape[0]
    chans = features.shape[1]
    lanes = lax.axis_size("space")
    devices = lanes * lax.axis_size("row")
    everybody = devices * atoms
    me = lax.axis_index("row") * lanes + lax.axis_index("space")
    sigma = lookup(species, width)
    diag = lookup(species, hardness) + inverse_root_pi / sigma
    placed = jnp.concatenate([positions, sigma[None, :], diag[None, :]], axis=0)
    everyone = gathered(placed, devices).transpose(1, 0, 2).reshape(5, everybody)
    lists = ghost_list[0]
    outgoing = jnp.take(features, lists.reshape(-1), axis=0).reshape(lanes, lists.shape[1], chans)
    ghost_rows = jnp.einsum(
        "dkc,cf->dkf",
        lax.all_to_all(outgoing, "space", split_axis=0, concat_axis=0, tiled=True),
        w_msg,
        preferred_element_type=jnp.float32,
    ).astype(jnp.bfloat16)
    own_rows = jnp.dot(features, w_msg, preferred_element_type=jnp.float32).astype(jnp.bfloat16)
    projected = jnp.concatenate([own_rows, ghost_rows.reshape(-1, 2 * chans)], axis=0)
    summed = edge_terms(edge_recv, edge_send, edge_vec, projected, w_rad1, w_rad2, atoms)
    summed = summed * message_scale
    vector_part = summed[:, chans:].reshape(atoms, 3, chans)
    invariant = jnp.concatenate(
        [summed[:, :chans], jnp.sum(vector_part * vector_part, axis=1)], axis=1
    ).astype(jnp.bfloat16)
    hidden = jax.nn.silu(jnp.dot(invariant, w_up, preferred_element_type=jnp.float32))
    new_features = (features.astype(jnp.float32) + hidden).astype(jnp.bfloat16)
    chi = jnp.dot(hidden, w_out, precision=lax.Precision.HIGHEST) + lookup(species, chi_shift)
    own_labels = me * atoms + jnp.arange(atoms, dtype=jnp.int32)
    all_labels = jnp.arange(everybody, dtype=jnp.int32)
    rhs = field[0] * positions[2] - chi

    if everybody <= replicate_limit:
        kernel = coulomb(everyone, all_labels, everyone, all_labels)
        residual = gathered(rhs, devices).reshape(everybody)
        all_charges = conjugate(
            residual, lambda v: everyone[4] * v + jnp.sum(kernel * v[None, :], axis=1), jnp.sum
        )
        charges = lax.dynamic_slice(all_charges, (me * atoms,), (atoms,))
    else:
        kernel = coulomb(placed, own_labels, everyone, all_labels)

        def spread(vector):
            return gathered(vector, devices).reshape(everybody)

        charges = conjugate(
            rhs,
            lambda v: diag * v + jnp.sum(kernel * spread(v)[None, :], axis=1),
            lambda v: lax.psum(jnp.sum(v), everywhere),
        )
        all_charges = spread(charges)
    sums = pair_forces(placed, own_labels, everyone, all_labels, all_charges)
    pull = -charges[None, :] * sums[:3]
    forces = jnp.concatenate([pull[:2], pull[2:] + (charges * field[0])[None, :]], axis=0)
    virial = 0.5 * charges[None, :] * sums[3:]
    return (new_features, charges, forces, virial)


def conjugate(rhs, apply, total):
    charges = jnp.zeros_like(rhs)
    residual = rhs
    direction = rhs
    norm_now = total(residual * residual)
    for step in range(ITERS):
        image = apply(direction)
        alpha = norm_now / total(direction * image)
        charges = charges + alpha * direction
        if step + 1 < ITERS:
            residual = residual - alpha * image
            fresh = total(residual * residual)
            direction = residual + fresh / norm_now * direction
            norm_now = fresh
    return charges


def split3(value):
    first = value.astype(jnp.bfloat16).astype(jnp.float32)
    rest = value - first
    second = rest.astype(jnp.bfloat16).astype(jnp.float32)
    third = (rest - second).astype(jnp.bfloat16).astype(jnp.float32)
    return first, second, third


def over_first(left, right):
    return lax.dot_general(
        left, right, (((0,), (0,)), ((), ())), preferred_element_type=jnp.float32
    )


def over_last(left, right, precision=None):
    return lax.dot_general(
        left,
        right,
        (((1,), (1,)), ((), ())),
        precision=precision,
        preferred_element_type=jnp.float32,
    )


def silu(value):
    return value / (1.0 + jnp.exp(-value))


def silu_half(value):
    return (0.5 * value) * (1.0 + jnp.tanh(0.5 * value))


sine_series = [(-1.0) ** k * math.pi ** (2 * k + 1) / math.factorial(2 * k + 1) for k in range(7)]


def fetched(pairs, semaphores):
    copies = [
        pltpu.make_async_copy(source, target, semaphores.at[place])
        for place, (source, target) in enumerate(pairs)
    ]
    for copy in copies:
        copy.start()
    return copies


chi_segment = 3


def pack_kernel(space_ref, features_ref, lists_ref, packed_ref, held_ref, semaphores):
    atoms, chans = features_ref.shape
    copies = fetched(
        [(lists_ref, held_ref), (features_ref, packed_ref.at[pl.ds(0, atoms)])], semaphores
    )
    copies[0].wait()
    _, lanes, width = held_ref.shape
    rows = []
    for place in range(lanes):
        row = held_ref[0, pl.ds(space_ref[0] ^ place, 1), :].astype(jnp.float32) + place * atoms
        parts = [jnp.zeros((1, width), jnp.float32)] * lanes
        parts[place] = row
        rows.append(jnp.concatenate(parts, axis=1))
    rows.append(jnp.zeros((packed_ref.shape[0] - atoms - lanes, chans), jnp.float32))
    packed_ref[atoms:, :] = jnp.concatenate(rows, axis=0).astype(jnp.bfloat16)
    copies[1].wait()


def edge_kernel(
    space_ref,
    *refs,
):
    count = (len(refs) - 10) // 2
    far, near, semaphores = refs[:count], refs[count + 9 : -1], refs[-1]
    filter_ref, unit_ref, row_ref, slot_ref, local_ref, hit_ref = refs[count : count + 6]
    turned_ref, upward_ref, read_ref = refs[count + 6 : count + 9]
    vec_ref, first_ref, second_ref, send_ref, recv_ref, project_ref, update_ref = near[:7]
    species_ref, hardness_ref, width_ref, shift_ref, positions_ref, out_ref = near[7:]
    copies = fetched(list(zip(far, near)), semaphores)
    for copy in copies[:3]:
        copy.wait()
    edges = vec_ref.shape[1]
    orders = first_ref.shape[0]
    vec = vec_ref[...]
    east, north, up = vec[0:1], vec[1:2], vec[2:3]
    squared = east * east + north * north + up * up
    inverse = lax.rsqrt(squared)
    unit_ref[0:3, :] = vec * inverse
    ratio = squared * inverse * (1.0 / cutoff)
    envelope = (1.0 - ratio * ratio) * (1.0 - ratio * ratio) * (cutoff * inverse)
    order = lax.broadcasted_iota(jnp.int32, (orders, edges), 0).astype(jnp.float32) + 1.0
    turns = order * ratio
    whole = jnp.floor(turns + 0.5)
    part = turns - whole
    sign = 1.0 - 2.0 * (whole - 2.0 * jnp.floor(whole * 0.5))
    series = jnp.full_like(part, sine_series[-1])
    for coefficient in sine_series[-2::-1]:
        series = series * (part * part) + coefficient
    basis = series * part * (sign * envelope)
    b1, b2, b3 = split3(basis)
    w1, w2, w3 = split3(first_ref[...])
    mixed = over_first(
        jnp.concatenate([w1, w1, w2, w2, w1, w3], axis=0).astype(jnp.bfloat16),
        jnp.concatenate([b1, b2, b1, b2, b3, b1], axis=0).astype(jnp.bfloat16),
    )
    radial = silu_half(mixed).astype(jnp.bfloat16)
    filter_ref[...] = over_first(second_ref[...], radial)
    for copy in copies[3:]:
        copy.wait()
    species = species_ref[...]

    def table(ref):
        result = jnp.zeros(species.shape, jnp.float32)
        for kind in range(ref.shape[1]):
            result = result + jnp.where(species == kind, ref[:, kind : kind + 1], 0.0)
        return result

    positions = positions_ref[...]
    sigma = table(width_ref)
    atoms = species.shape[1]
    chans = row_ref.shape[1]
    diag = table(hardness_ref) + inverse_root_pi / sigma
    blank = jnp.zeros((2, atoms), jnp.float32)
    rows = [positions[0:1], blank, -table(shift_ref), diag, sigma, positions[2:3], positions[1:2]]
    block = jnp.concatenate(
        [jnp.concatenate(rows, axis=0), jnp.zeros((8, chans - atoms), jnp.float32)], axis=1
    )
    block = pltpu.roll(block, 0, 1, stride=atoms, stride_axis=0)
    row_ref[...] = jnp.sum(block, axis=0, keepdims=True)
    lanes = local_ref.shape[0] // atoms
    slots = chans // lanes
    send = send_ref[...]
    own = send < atoms
    slot = jnp.where(own, -1, (send - atoms) ^ (space_ref[0] * slots))
    local = jnp.where(own, send, -1)

    def chosen(ref, index):
        hit = lax.broadcasted_iota(jnp.int32, ref.shape, 0) == index
        ref[...] = jnp.where(hit, 1.0, 0.0).astype(ref.dtype)

    chosen(slot_ref, slot)
    chosen(local_ref, local)
    chosen(hit_ref, recv_ref[...])
    turned_ref[...] = project_ref[...].astype(jnp.float32).T.astype(jnp.bfloat16)
    upward_ref[...] = update_ref[...].astype(jnp.float32).T.astype(jnp.bfloat16)
    read_ref[...] = jnp.broadcast_to(out_ref[...], (atoms, chans)).T


def node_kernel(
    own_ref,
    near_ref,
    side_ref,
    far_ref,
    filter_ref,
    unit_ref,
    row_ref,
    slot_ref,
    local_ref,
    hit_ref,
    turned_ref,
    upward_ref,
    read_ref,
    hidden_ref,
    block_ref,
):
    chans, atoms = hidden_ref.shape
    packed = (own_ref, near_ref, side_ref, far_ref)
    group = jnp.concatenate([ref[:atoms, :] for ref in packed], axis=0)
    chosen = jnp.zeros((1, chans), jnp.float32)
    for place, ref in enumerate(packed):
        tail = ref[atoms:, :].astype(jnp.float32)
        chosen = chosen + tail[place : place + 1]
    fill = jnp.where(
        lax.broadcasted_iota(jnp.int32, (len(packed) * atoms, chans), 0)
        == chosen.astype(jnp.int32),
        1.0,
        0.0,
    ).astype(jnp.bfloat16)
    sender = jnp.dot(fill, slot_ref[...], preferred_element_type=jnp.float32) + local_ref[...]
    projected = over_last(turned_ref[...], group).astype(jnp.bfloat16)
    picked = jnp.dot(projected, sender.astype(jnp.bfloat16), preferred_element_type=jnp.float32)
    scalar = picked[:chans] * filter_ref[:chans, :]
    carried = picked[chans:] * filter_ref[chans:, :]
    parts = [scalar] + [unit_ref[axis : axis + 1, :] * carried for axis in range(3)]
    message = jnp.concatenate([part.astype(jnp.bfloat16) for part in parts], axis=0)
    summed = over_last(message, hit_ref[...]) * message_scale
    square = jnp.zeros((chans, atoms), jnp.float32)
    for component in range(1, 4):
        part = summed[component * chans : (component + 1) * chans]
        square = square + part * part
    invariant = jnp.concatenate([summed[:chans], square], axis=0).astype(jnp.bfloat16)
    hidden = silu(jnp.dot(upward_ref[...], invariant, preferred_element_type=jnp.float32))
    chi = jnp.sum(hidden * read_ref[...], axis=0, keepdims=True)
    chi = jnp.concatenate([chi, jnp.zeros((1, chans - atoms), jnp.float32)], axis=1)
    row = row_ref[...] - pltpu.roll(chi, chi_segment * atoms, 1)
    block_ref[...] = jnp.broadcast_to(row[None], block_ref.shape)
    hidden_ref[...] = hidden


def feature_kernel(packed_ref, hidden_ref, features_ref):
    atoms = features_ref.shape[0]
    old = packed_ref[...].astype(jnp.float32)[:atoms]
    features_ref[...] = (old + hidden_ref[...].T).astype(jnp.bfloat16)


def reciprocal(value):
    rough = pl.reciprocal(value, approx=True)
    return rough * (2.0 - value * rough)


def smeared(scaled):
    decay = jnp.exp2(scaled * scaled * -math.log2(math.e))
    turn = reciprocal(1.0 + 0.3275911 * scaled)
    series = 1.061405429 * turn - 1.453152027
    series = series * turn + 1.421413741
    series = series * turn - 0.284496736
    series = series * turn + 0.254829592
    return 1.0 - series * turn * decay, decay


def charge_kernel(
    place_ref,
    field_ref,
    all_ref,
    charges_ref,
    forces_ref,
    virial_ref,
    matrix_ref,
    side_ref,
    value_ref,
):
    blocks, _, lanes = all_ref.shape
    own = charges_ref.shape[1]
    count = blocks * own
    fit = lanes // own
    segment = lax.broadcasted_iota(jnp.int32, (8, lanes), 1) // own
    tiles = []
    for first in range(0, blocks, fit):
        tile = jnp.zeros((8, lanes), jnp.float32)
        for place in range(fit):
            row = all_ref[lax.rem(place_ref[0] + first + place, blocks)]
            row = pltpu.roll(jnp.broadcast_to(row, (8, lanes)), 0, 1, stride=own, stride_axis=0)
            row = pltpu.roll(row, place * own, 1) if place else row
            tile = jnp.where(segment == place, row, tile)
        tiles.append(tile)
    everyone = jnp.concatenate(tiles, axis=1)
    last = lax.broadcasted_iota(jnp.int32, everyone.shape, 0) == 5
    everyone = everyone + jnp.where(last, field_ref[0] * everyone[2:3], 0.0)
    columns = everyone.T
    diag, rhs = everyone[4:5], everyone[5:6]
    rows = own
    spread_row = 2.0 * everyone[3:4] * everyone[3:4]
    tiles = count // lanes
    lane = lax.broadcasted_iota(jnp.int32, (rows, lanes), 1)
    line = lax.broadcasted_iota(jnp.int32, (rows, lanes), 0)

    def part(row, tile):
        return row[:, tile * lanes : (tile + 1) * lanes]

    def spread(column):
        return jnp.broadcast_to(column, (rows, lanes))

    above = [jnp.zeros((rows, lanes), jnp.float32) for _ in range(tiles)]
    kept = []
    for start in range(0, count, rows):
        first = start // lanes
        column = columns[start : start + rows]
        place = [spread(column[:, axis : axis + 1]) for axis in range(3)]
        wide = spread(2.0 * column[:, 3:4] * column[:, 3:4])
        value = spread(column[:, 5:6])
        value_ref[start : start + rows, :] = value
        below = jnp.zeros((rows, lanes), jnp.float32)
        for tile in range(first, tiles):
            delta = [place[axis] - part(everyone[axis : axis + 1], tile) for axis in range(3)]
            squared = delta[0] * delta[0] + delta[1] * delta[1] + delta[2] * delta[2]
            if tile == first:
                same = lane == line + (start - first * lanes)
                squared = jnp.where(same, 1.0, squared)
            inverse = lax.rsqrt(squared)
            scale = lax.rsqrt(wide + part(spread_row, tile))
            smear, decay = smeared(squared * inverse * scale)
            kernel = smear * inverse
            if start == 0:
                slope = (two_over_root_pi * scale * decay - kernel) * inverse * inverse
                slope = jnp.where(same, 0.0, slope) if tile == first else slope
                kept.append((delta, slope))
            if tile == first:
                kernel = jnp.where(same, 0.0, kernel)
            else:
                below = below + kernel * part(rhs, tile)
            above[tile] = above[tile] + kernel * value
            matrix_ref[start : start + rows, tile * lanes : (tile + 1) * lanes] = kernel
        if first + 1 < tiles:
            side_ref[start : start + rows, :] = below
    image = []
    for tile in range(tiles):
        value = jnp.sum(above[tile], axis=0, keepdims=True)
        if tile + 1 < tiles:
            below = side_ref[tile * lanes : (tile + 1) * lanes, :].T
            value = value + jnp.sum(below, axis=0, keepdims=True)
        image.append(value)
    image = diag * rhs + jnp.concatenate(image, axis=1)
    across = jnp.broadcast_to(image, (8, count)).T

    def total(value):
        return jnp.sum(value, axis=1, keepdims=True)

    norm = total(rhs * rhs)
    alpha = norm / total(rhs * image)
    residual = rhs - alpha * image
    fresh = total(residual * residual)
    again = fresh / norm
    direction = residual + again * rhs
    onto = [jnp.zeros((rows, lanes), jnp.float32) for _ in range(tiles)]
    above = [jnp.zeros((rows, lanes), jnp.float32) for _ in range(tiles)]
    for start in range(0, count, rows):
        first = start // lanes
        value = (1.0 + again) * value_ref[start : start + rows, :]
        value = value - alpha * spread(across[start : start + rows, 0:1])
        for tile in range(first, tiles):
            sums = onto if tile == first else above
            kernel = matrix_ref[start : start + rows, tile * lanes : (tile + 1) * lanes]
            sums[tile] = sums[tile] + kernel * value
    curved = jnp.zeros((rows, lanes), jnp.float32)
    for tile in range(tiles):
        curved = curved + (onto[tile] + 2.0 * above[tile]) * part(direction, tile)
    curved = jnp.sum(curved, axis=0, keepdims=True)
    for tile in range(tiles):
        curved = curved + part(diag * direction * direction, tile)
    charges = alpha * rhs + fresh / total(curved) * direction

    sums = [jnp.zeros((rows, lanes), jnp.float32) for _ in range(9)]
    for tile, (delta, slope) in enumerate(kept):
        weight = part(charges, tile) * slope
        pulled = [weight * delta[axis] for axis in range(3)]
        terms = pulled + [
            pulled[left] * delta[right]
            for left, right in ((0, 0), (1, 1), (2, 2), (0, 1), (0, 2), (1, 2))
        ]
        sums = [old + term for old, term in zip(sums, terms)]
    table = jnp.zeros((rows, lanes), jnp.float32)
    for place, value in enumerate(sums):
        table = jnp.where(lane == place, total(value), table)
    table = table.T
    mine = charges[:, :own]
    charges_ref[...] = mine
    pull = -mine * table[0:3]
    third = lax.broadcasted_iota(jnp.int32, pull.shape, 0) == 2
    forces_ref[...] = pull + jnp.where(third, mine * field_ref[0], 0.0)
    virial_ref[...] = 0.5 * mine * table[3:9]


def kernel_call(kernel, shapes, arguments, scalars=0, far=0, scratch=(), flops=0):
    shapes = tuple(
        jax.ShapeDtypeStruct(*shape) if isinstance(shape, tuple) else shape for shape in shapes
    )
    spaces = [pltpu.SMEM] * scalars + [pltpu.HBM] * far
    spaces = spaces + [pltpu.VMEM] * (len(arguments) - len(spaces))
    arguments = [
        pltpu.with_memory_space_constraint(value, space) if space is pltpu.HBM else value
        for value, space in zip(arguments, spaces)
    ]
    return pl.pallas_call(
        kernel,
        out_shape=shapes,
        in_specs=[pl.BlockSpec(memory_space=space) for space in spaces],
        out_specs=tuple(pl.BlockSpec(memory_space=pltpu.VMEM) for _ in shapes),
        scratch_shapes=list(scratch),
        compiler_params=pltpu.CompilerParams(vmem_limit_bytes=32 * 1024 * 1024),
        cost_estimate=pl.CostEstimate(flops=flops, bytes_accessed=1 << 20, transcendentals=0),
    )(*arguments)


def exchanged(block, axis, step):
    size = lax.axis_size(axis)
    return lax.ppermute(block, axis, [(place, place ^ step) for place in range(size)])


def few_shards(
    features,
    positions,
    species,
    ghost_list,
    edge_recv,
    edge_send,
    edge_vec,
    w_msg,
    w_rad1,
    w_rad2,
    w_up,
    w_out,
    hardness,
    width,
    chi_shift,
    field,
):
    atoms, chans = features.shape
    edges = edge_recv.shape[0]
    rows, lanes = lax.axis_size("row"), lax.axis_size("space")
    space = lax.axis_index("space").astype(jnp.int32)
    (packed,) = kernel_call(
        pack_kernel,
        [((atoms + 16, chans), jnp.bfloat16)],
        (space.reshape(1), features, ghost_list),
        scalars=1,
        far=2,
        scratch=[
            pltpu.VMEM(ghost_list.shape, ghost_list.dtype),
            pltpu.SemaphoreType.DMA((2,)),
        ],
    )
    others = [exchanged(packed, "space", step) for step in range(1, lanes)]
    rest = (edge_vec, w_rad1, w_rad2, edge_send[None], edge_recv[None], w_msg, w_up)
    rest = rest + (species[None], hardness[None], width[None], chi_shift[None], positions)
    rest = rest + (w_out[None],)
    parts = kernel_call(
        edge_kernel,
        [
            ((2 * chans, edges), jnp.float32),
            ((8, edges), jnp.float32),
            ((1, chans), jnp.float32),
            ((chans, edges), jnp.bfloat16),
            ((lanes * atoms, edges), jnp.float32),
            ((atoms, edges), jnp.bfloat16),
            ((2 * chans, chans), jnp.bfloat16),
            ((chans, 2 * chans), jnp.bfloat16),
            ((chans, atoms), jnp.float32),
        ],
        (space.reshape(1), *rest),
        scalars=1,
        far=len(rest),
        scratch=[pltpu.VMEM(value.shape, value.dtype) for value in rest]
        + [pltpu.SemaphoreType.DMA((len(rest),))],
        flops=1 << 28,
    )
    devices = rows * lanes
    hidden, block = kernel_call(
        node_kernel,
        [((chans, atoms), jnp.float32), pltpu.VMEM((devices, 1, chans), jnp.float32)],
        (packed, *others, *parts),
        flops=1 << 28,
    )
    (new_features,) = kernel_call(
        feature_kernel, [((atoms, chans), jnp.bfloat16)], (packed, hidden), flops=1 << 20
    )
    block = lax.all_to_all(block, everywhere, 0, 0, tiled=True)
    place = lax.axis_index("row").astype(jnp.int32) * lanes + space
    everybody = rows * lanes * atoms
    charges, forces, virial = kernel_call(
        charge_kernel,
        [((count, atoms), jnp.float32) for count in (1, 3, 6)],
        (place.reshape(1), field, block),
        scalars=2,
        scratch=[
            pltpu.VMEM((everybody, everybody), jnp.float32),
            pltpu.VMEM((everybody, chans), jnp.float32),
            pltpu.VMEM((everybody, chans), jnp.float32),
        ],
        flops=1 << 28,
    )
    return (new_features, charges[0], forces, virial)


def solution(mesh):
    small = mesh.shape["space"] == 4 and mesh.shape["row"] == 8
    return jax.shard_map(
        few_shards if small else shards,
        mesh=mesh,
        in_specs=(
            P(("row", "space"), None),
            P(None, ("row", "space")),
            P(("row", "space")),
            P("row", "space", None),
            P(("row", "space")),
            P(("row", "space")),
            P(None, ("row", "space")),
            P(),
            P(),
            P(),
            P(),
            P(),
            P(),
            P(),
            P(),
            P(),
        ),
        out_specs=(
            P(("row", "space"), None),
            P(("row", "space")),
            P(None, ("row", "space")),
            P(None, ("row", "space")),
        ),
        check_vma=False,
    )
```

```python
import math

import jax
import jax.numpy as jnp
from jax import lax
from jax.experimental import pallas as pl
from jax.experimental.pallas import tpu as pltpu
from jax.sharding import PartitionSpec as P

ITERS = 2


cutoff = 6.0
message_scale = 0.125
two_over_root_pi = 2.0 / math.sqrt(math.pi)
inverse_root_pi = 1.0 / math.sqrt(math.pi)
replicate_limit = 1024
everywhere = ("row", "space")


def lookup(species, table):
    result = jnp.zeros(species.shape, jnp.float32)
    for kind in range(table.shape[0]):
        result = result + jnp.where(species == kind, table[kind], 0.0)
    return result


def pair_terms(target, target_labels, source, source_labels):
    delta = target[:3, :, None] - source[:3, None, :]
    squared = jnp.sum(delta * delta, axis=0)
    same = target_labels[:, None] == source_labels[None, :]
    squared = jnp.where(same, 1.0, squared)
    inverse = lax.rsqrt(squared)
    radius = squared * inverse
    spread = target[3][:, None] * target[3][:, None] + source[3][None, :] * source[3][None, :]
    scale = lax.rsqrt(2.0 * spread)
    scaled = radius * scale
    smear = lax.erf(scaled)
    return delta, same, inverse, scale, scaled, smear


def coulomb(target, target_labels, source, source_labels):
    _, same, inverse, _, _, smear = pair_terms(target, target_labels, source, source_labels)
    return jnp.where(same, 0.0, smear * inverse)


def pair_forces(target, target_labels, source, source_labels, source_charge):
    delta, same, inverse, scale, scaled, smear = pair_terms(
        target, target_labels, source, source_labels
    )
    slope = (
        two_over_root_pi * scale * jnp.exp(-scaled * scaled) * inverse - smear * inverse * inverse
    )
    weight = jnp.where(same, 0.0, source_charge[None, :] * slope * inverse)
    first = jnp.sum(weight[None] * delta, axis=2)
    pairs = ((0, 0), (1, 1), (2, 2), (0, 1), (0, 2), (1, 2))
    second = jnp.stack(
        [jnp.sum(weight * delta[left] * delta[right], axis=1) for left, right in pairs]
    )
    return jnp.concatenate([first, second], axis=0)


def edge_terms(receive, sender_rows, vectors, projected, w_rad1, w_rad2, atoms):
    length = jnp.sqrt(jnp.sum(vectors * vectors, axis=0))
    unit = vectors / length
    order = jnp.arange(1, w_rad1.shape[0] + 1, dtype=jnp.int32).astype(jnp.float32)[:, None]
    ratio = length / cutoff
    envelope = (1.0 - ratio * ratio) * (1.0 - ratio * ratio)
    basis = jnp.sin(order * math.pi * ratio) / ratio * envelope
    mixed = lax.dot_general(
        basis, w_rad1, (((0,), (0,)), ((), ())), precision=lax.Precision.HIGHEST
    )
    radial = jax.nn.silu(mixed).astype(jnp.bfloat16)
    filters = jnp.dot(radial, w_rad2, preferred_element_type=jnp.float32)
    picked = jnp.take(projected, sender_rows, axis=0).astype(jnp.float32) * filters
    chans = w_rad1.shape[1]
    scalar = picked[:, :chans]
    carried = picked[:, chans:]
    joined = [
        scalar,
        unit[0][:, None] * carried,
        unit[1][:, None] * carried,
        unit[2][:, None] * carried,
    ]
    message = jnp.concatenate(joined, axis=1).astype(jnp.bfloat16)
    onehot = (jnp.arange(atoms, dtype=jnp.int32)[:, None] == receive[None, :]).astype(jnp.bfloat16)
    return jnp.dot(onehot, message, preferred_element_type=jnp.float32)


def gathered(block, devices):
    copies = jnp.broadcast_to(block[None], (devices,) + block.shape)
    return lax.all_to_all(copies, everywhere, split_axis=0, concat_axis=0, tiled=True)


def shards(
    features,
    positions,
    species,
    ghost_list,
    edge_recv,
    edge_send,
    edge_vec,
    w_msg,
    w_rad1,
    w_rad2,
    w_up,
    w_out,
    hardness,
    width,
    chi_shift,
    field,
):
    atoms = features.shape[0]
    chans = features.shape[1]
    lanes = lax.axis_size("space")
    devices = lanes * lax.axis_size("row")
    everybody = devices * atoms
    me = lax.axis_index("row") * lanes + lax.axis_index("space")
    sigma = lookup(species, width)
    diag = lookup(species, hardness) + inverse_root_pi / sigma
    placed = jnp.concatenate([positions, sigma[None, :], diag[None, :]], axis=0)
    everyone = gathered(placed, devices).transpose(1, 0, 2).reshape(5, everybody)
    lists = ghost_list[0]
    outgoing = jnp.take(features, lists.reshape(-1), axis=0).reshape(lanes, lists.shape[1], chans)
    ghost_rows = jnp.einsum(
        "dkc,cf->dkf",
        lax.all_to_all(outgoing, "space", split_axis=0, concat_axis=0, tiled=True),
        w_msg,
        preferred_element_type=jnp.float32,
    ).astype(jnp.bfloat16)
    own_rows = jnp.dot(features, w_msg, preferred_element_type=jnp.float32).astype(jnp.bfloat16)
    projected = jnp.concatenate([own_rows, ghost_rows.reshape(-1, 2 * chans)], axis=0)
    summed = edge_terms(edge_recv, edge_send, edge_vec, projected, w_rad1, w_rad2, atoms)
    summed = summed * message_scale
    vector_part = summed[:, chans:].reshape(atoms, 3, chans)
    invariant = jnp.concatenate(
        [summed[:, :chans], jnp.sum(vector_part * vector_part, axis=1)], axis=1
    ).astype(jnp.bfloat16)
    hidden = jax.nn.silu(jnp.dot(invariant, w_up, preferred_element_type=jnp.float32))
    new_features = (features.astype(jnp.float32) + hidden).astype(jnp.bfloat16)
    chi = jnp.dot(hidden, w_out, precision=lax.Precision.HIGHEST) + lookup(species, chi_shift)
    own_labels = me * atoms + jnp.arange(atoms, dtype=jnp.int32)
    all_labels = jnp.arange(everybody, dtype=jnp.int32)
    rhs = field[0] * positions[2] - chi

    if everybody <= replicate_limit:
        kernel = coulomb(everyone, all_labels, everyone, all_labels)
        residual = gathered(rhs, devices).reshape(everybody)
        all_charges = conjugate(
            residual, lambda v: everyone[4] * v + jnp.sum(kernel * v[None, :], axis=1), jnp.sum
        )
        charges = lax.dynamic_slice(all_charges, (me * atoms,), (atoms,))
    else:
        kernel = coulomb(placed, own_labels, everyone, all_labels)

        def spread(vector):
            return gathered(vector, devices).reshape(everybody)

        charges = conjugate(
            rhs,
            lambda v: diag * v + jnp.sum(kernel * spread(v)[None, :], axis=1),
            lambda v: lax.psum(jnp.sum(v), everywhere),
        )
        all_charges = spread(charges)
    sums = pair_forces(placed, own_labels, everyone, all_labels, all_charges)
    pull = -charges[None, :] * sums[:3]
    forces = jnp.concatenate([pull[:2], pull[2:] + (charges * field[0])[None, :]], axis=0)
    virial = 0.5 * charges[None, :] * sums[3:]
    return (new_features, charges, forces, virial)


def conjugate(rhs, apply, total):
    charges = jnp.zeros_like(rhs)
    residual = rhs
    direction = rhs
    norm_now = total(residual * residual)
    for step in range(ITERS):
        image = apply(direction)
        alpha = norm_now / total(direction * image)
        charges = charges + alpha * direction
        if step + 1 < ITERS:
            residual = residual - alpha * image
            fresh = total(residual * residual)
            direction = residual + fresh / norm_now * direction
            norm_now = fresh
    return charges


def split3(value):
    first = value.astype(jnp.bfloat16).astype(jnp.float32)
    rest = value - first
    second = rest.astype(jnp.bfloat16).astype(jnp.float32)
    third = (rest - second).astype(jnp.bfloat16).astype(jnp.float32)
    return first, second, third


def over_first(left, right):
    return lax.dot_general(
        left, right, (((0,), (0,)), ((), ())), preferred_element_type=jnp.float32
    )


def over_last(left, right, precision=None):
    return lax.dot_general(
        left,
        right,
        (((1,), (1,)), ((), ())),
        precision=precision,
        preferred_element_type=jnp.float32,
    )


def silu(value):
    return value / (1.0 + jnp.exp(-value))


def silu_half(value):
    return (0.5 * value) * (1.0 + jnp.tanh(0.5 * value))


sine_series = [(-1.0) ** k * math.pi ** (2 * k + 1) / math.factorial(2 * k + 1) for k in range(7)]


def fetched(pairs, semaphores):
    copies = [
        pltpu.make_async_copy(source, target, semaphores.at[place])
        for place, (source, target) in enumerate(pairs)
    ]
    for copy in copies:
        copy.start()
    return copies


chi_segment = 3


def pack_kernel(space_ref, features_ref, lists_ref, packed_ref, held_ref, semaphores):
    atoms, chans = features_ref.shape
    copies = fetched(
        [(lists_ref, held_ref), (features_ref, packed_ref.at[pl.ds(0, atoms)])], semaphores
    )
    copies[0].wait()
    _, lanes, width = held_ref.shape
    rows = []
    for place in range(lanes):
        row = held_ref[0, pl.ds(space_ref[0] ^ place, 1), :].astype(jnp.float32) + place * atoms
        parts = [jnp.zeros((1, width), jnp.float32)] * lanes
        parts[place] = row
        rows.append(jnp.concatenate(parts, axis=1))
    rows.append(jnp.zeros((packed_ref.shape[0] - atoms - lanes, chans), jnp.float32))
    packed_ref[atoms:, :] = jnp.concatenate(rows, axis=0).astype(jnp.bfloat16)
    copies[1].wait()


def edge_kernel(
    space_ref,
    *refs,
):
    count = (len(refs) - 10) // 2
    far, near, semaphores = refs[:count], refs[count + 9 : -1], refs[-1]
    filter_ref, unit_ref, row_ref, slot_ref, local_ref, hit_ref = refs[count : count + 6]
    turned_ref, upward_ref, read_ref = refs[count + 6 : count + 9]
    vec_ref, first_ref, second_ref, send_ref, recv_ref, project_ref, update_ref = near[:7]
    species_ref, hardness_ref, width_ref, shift_ref, positions_ref, out_ref = near[7:]
    copies = fetched(list(zip(far, near)), semaphores)
    for copy in copies[:3]:
        copy.wait()
    edges = vec_ref.shape[1]
    orders = first_ref.shape[0]
    vec = vec_ref[...]
    east, north, up = vec[0:1], vec[1:2], vec[2:3]
    squared = east * east + north * north + up * up
    inverse = lax.rsqrt(squared)
    unit_ref[0:3, :] = vec * inverse
    ratio = squared * inverse * (1.0 / cutoff)
    envelope = (1.0 - ratio * ratio) * (1.0 - ratio * ratio) * (cutoff * inverse)
    order = lax.broadcasted_iota(jnp.int32, (orders, edges), 0).astype(jnp.float32) + 1.0
    turns = order * ratio
    whole = jnp.floor(turns + 0.5)
    part = turns - whole
    sign = 1.0 - 2.0 * (whole - 2.0 * jnp.floor(whole * 0.5))
    series = jnp.full_like(part, sine_series[-1])
    for coefficient in sine_series[-2::-1]:
        series = series * (part * part) + coefficient
    basis = series * part * (sign * envelope)
    b1, b2, b3 = split3(basis)
    w1, w2, w3 = split3(first_ref[...])
    mixed = over_first(
        jnp.concatenate([w1, w1, w2, w2, w1, w3], axis=0).astype(jnp.bfloat16),
        jnp.concatenate([b1, b2, b1, b2, b3, b1], axis=0).astype(jnp.bfloat16),
    )
    radial = silu_half(mixed).astype(jnp.bfloat16)
    filter_ref[...] = over_first(second_ref[...], radial)
    for copy in copies[3:]:
        copy.wait()
    species = species_ref[...]

    def table(ref):
        result = jnp.zeros(species.shape, jnp.float32)
        for kind in range(ref.shape[1]):
            result = result + jnp.where(species == kind, ref[:, kind : kind + 1], 0.0)
        return result

    positions = positions_ref[...]
    sigma = table(width_ref)
    atoms = species.shape[1]
    chans = row_ref.shape[1]
    diag = table(hardness_ref) + inverse_root_pi / sigma
    blank = jnp.zeros((2, atoms), jnp.float32)
    rows = [positions[0:1], blank, -table(shift_ref), diag, sigma, positions[2:3], positions[1:2]]
    block = jnp.concatenate(
        [jnp.concatenate(rows, axis=0), jnp.zeros((8, chans - atoms), jnp.float32)], axis=1
    )
    block = pltpu.roll(block, 0, 1, stride=atoms, stride_axis=0)
    row_ref[...] = jnp.sum(block, axis=0, keepdims=True)
    lanes = local_ref.shape[0] // atoms
    slots = chans // lanes
    send = send_ref[...]
    own = send < atoms
    slot = jnp.where(own, -1, (send - atoms) ^ (space_ref[0] * slots))
    local = jnp.where(own, send, -1)

    def chosen(ref, index):
        hit = lax.broadcasted_iota(jnp.int32, ref.shape, 0) == index
        ref[...] = jnp.where(hit, 1.0, 0.0).astype(ref.dtype)

    chosen(slot_ref, slot)
    chosen(local_ref, local)
    chosen(hit_ref, recv_ref[...])
    turned_ref[...] = project_ref[...].astype(jnp.float32).T.astype(jnp.bfloat16)
    upward_ref[...] = update_ref[...].astype(jnp.float32).T.astype(jnp.bfloat16)
    read_ref[...] = jnp.broadcast_to(out_ref[...], (atoms, chans)).T


def node_kernel(
    own_ref,
    near_ref,
    side_ref,
    far_ref,
    filter_ref,
    unit_ref,
    row_ref,
    slot_ref,
    local_ref,
    hit_ref,
    turned_ref,
    upward_ref,
    read_ref,
    hidden_ref,
    block_ref,
):
    chans, atoms = hidden_ref.shape
    packed = (own_ref, near_ref, side_ref, far_ref)
    group = jnp.concatenate([ref[:atoms, :] for ref in packed], axis=0)
    chosen = jnp.zeros((1, chans), jnp.float32)
    for place, ref in enumerate(packed):
        tail = ref[atoms:, :].astype(jnp.float32)
        chosen = chosen + tail[place : place + 1]
    fill = jnp.where(
        lax.broadcasted_iota(jnp.int32, (len(packed) * atoms, chans), 0)
        == chosen.astype(jnp.int32),
        1.0,
        0.0,
    ).astype(jnp.bfloat16)
    sender = jnp.dot(fill, slot_ref[...], preferred_element_type=jnp.float32) + local_ref[...]
    projected = over_last(turned_ref[...], group).astype(jnp.bfloat16)
    picked = jnp.dot(projected, sender.astype(jnp.bfloat16), preferred_element_type=jnp.float32)
    scalar = picked[:chans] * filter_ref[:chans, :]
    carried = picked[chans:] * filter_ref[chans:, :]
    parts = [scalar] + [unit_ref[axis : axis + 1, :] * carried for axis in range(3)]
    message = jnp.concatenate([part.astype(jnp.bfloat16) for part in parts], axis=0)
    summed = over_last(message, hit_ref[...]) * message_scale
    square = jnp.zeros((chans, atoms), jnp.float32)
    for component in range(1, 4):
        part = summed[component * chans : (component + 1) * chans]
        square = square + part * part
    invariant = jnp.concatenate([summed[:chans], square], axis=0).astype(jnp.bfloat16)
    hidden = silu(jnp.dot(upward_ref[...], invariant, preferred_element_type=jnp.float32))
    chi = jnp.sum(hidden * read_ref[...], axis=0, keepdims=True)
    chi = jnp.concatenate([chi, jnp.zeros((1, chans - atoms), jnp.float32)], axis=1)
    row = row_ref[...] - pltpu.roll(chi, chi_segment * atoms, 1)
    block_ref[...] = jnp.broadcast_to(row[None], block_ref.shape)
    hidden_ref[...] = hidden


def feature_kernel(packed_ref, hidden_ref, features_ref):
    atoms = features_ref.shape[0]
    old = packed_ref[...].astype(jnp.float32)[:atoms]
    features_ref[...] = (old + hidden_ref[...].T).astype(jnp.bfloat16)


def reciprocal(value):
    rough = pl.reciprocal(value, approx=True)
    return rough * (2.0 - value * rough)


def smeared(scaled):
    decay = jnp.exp2(scaled * scaled * -math.log2(math.e))
    turn = reciprocal(1.0 + 0.3275911 * scaled)
    series = 1.061405429 * turn - 1.453152027
    series = series * turn + 1.421413741
    series = series * turn - 0.284496736
    series = series * turn + 0.254829592
    return 1.0 - series * turn * decay, decay


def charge_kernel(
    place_ref,
    field_ref,
    all_ref,
    charges_ref,
    forces_ref,
    virial_ref,
    matrix_ref,
    side_ref,
    value_ref,
):
    blocks, _, lanes = all_ref.shape
    own = charges_ref.shape[1]
    count = blocks * own
    fit = lanes // own
    segment = lax.broadcasted_iota(jnp.int32, (8, lanes), 1) // own
    tiles = []
    for first in range(0, blocks, fit):
        tile = jnp.zeros((8, lanes), jnp.float32)
        for place in range(fit):
            row = all_ref[(place_ref[0] + first + place) & (blocks - 1)]
            row = pltpu.roll(jnp.broadcast_to(row, (8, lanes)), 0, 1, stride=own, stride_axis=0)
            row = pltpu.roll(row, place * own, 1) if place else row
            tile = jnp.where(segment == place, row, tile)
        tiles.append(tile)
    everyone = jnp.concatenate(tiles, axis=1)
    last = lax.broadcasted_iota(jnp.int32, everyone.shape, 0) == 5
    everyone = everyone + jnp.where(last, field_ref[0] * everyone[2:3], 0.0)
    columns = everyone.T
    diag, rhs = everyone[4:5], everyone[5:6]
    rows = 8
    spread_row = 2.0 * everyone[3:4] * everyone[3:4]
    tiles = count // lanes
    lane = lax.broadcasted_iota(jnp.int32, (rows, lanes), 1)
    line = lax.broadcasted_iota(jnp.int32, (rows, lanes), 0)

    def part(row, tile):
        return row[:, tile * lanes : (tile + 1) * lanes]

    def spread(column):
        return jnp.broadcast_to(column, (rows, lanes))

    above = [jnp.zeros((rows, lanes), jnp.float32) for _ in range(tiles)]
    kept = []
    for start in range(0, count, rows):
        first = start // lanes
        if start < own:
            kept.append([])
        column = columns[start : start + rows]
        place = [spread(column[:, axis : axis + 1]) for axis in range(3)]
        wide = spread(2.0 * column[:, 3:4] * column[:, 3:4])
        value = spread(column[:, 5:6])
        value_ref[start : start + rows, :] = value
        below = jnp.zeros((rows, lanes), jnp.float32)
        for tile in range(first, tiles):
            delta = [place[axis] - part(everyone[axis : axis + 1], tile) for axis in range(3)]
            squared = delta[0] * delta[0] + delta[1] * delta[1] + delta[2] * delta[2]
            if tile == first:
                same = lane == line + (start - first * lanes)
                squared = jnp.where(same, 1.0, squared)
            inverse = lax.rsqrt(squared)
            scale = lax.rsqrt(wide + part(spread_row, tile))
            smear, decay = smeared(squared * inverse * scale)
            kernel = smear * inverse
            if start < own:
                slope = (two_over_root_pi * scale * decay - kernel) * inverse * inverse
                slope = jnp.where(same, 0.0, slope) if tile == first else slope
                kept[-1].append((delta, slope))
            if tile == first:
                kernel = jnp.where(same, 0.0, kernel)
            else:
                below = below + kernel * part(rhs, tile)
            above[tile] = above[tile] + kernel * value
            matrix_ref[start : start + rows, tile * lanes : (tile + 1) * lanes] = kernel
        if first + 1 < tiles:
            side_ref[start : start + rows, :] = below
    image = []
    for tile in range(tiles):
        value = jnp.sum(above[tile], axis=0, keepdims=True)
        if tile + 1 < tiles:
            below = side_ref[tile * lanes : (tile + 1) * lanes, :].T
            value = value + jnp.sum(below, axis=0, keepdims=True)
        image.append(value)
    image = diag * rhs + jnp.concatenate(image, axis=1)
    across = jnp.broadcast_to(image, (8, count)).T

    def total(value):
        return jnp.sum(value, axis=1, keepdims=True)

    norm = total(rhs * rhs)
    alpha = norm / total(rhs * image)
    residual = rhs - alpha * image
    fresh = total(residual * residual)
    again = fresh / norm
    direction = residual + again * rhs
    onto = [jnp.zeros((rows, lanes), jnp.float32) for _ in range(tiles)]
    above = [jnp.zeros((rows, lanes), jnp.float32) for _ in range(tiles)]
    for start in range(0, count, rows):
        first = start // lanes
        value = (1.0 + again) * value_ref[start : start + rows, :]
        value = value - alpha * spread(across[start : start + rows, 0:1])
        for tile in range(first, tiles):
            sums = onto if tile == first else above
            kernel = matrix_ref[start : start + rows, tile * lanes : (tile + 1) * lanes]
            sums[tile] = sums[tile] + kernel * value
    curved = jnp.zeros((rows, lanes), jnp.float32)
    for tile in range(tiles):
        curved = curved + (onto[tile] + 2.0 * above[tile]) * part(direction, tile)
    curved = jnp.sum(curved, axis=0, keepdims=True)
    for tile in range(tiles):
        curved = curved + part(diag * direction * direction, tile)
    charges = alpha * rhs + fresh / total(curved) * direction

    tables = []
    for chunk in kept:
        sums = [jnp.zeros((rows, lanes), jnp.float32) for _ in range(9)]
        for tile, (delta, slope) in enumerate(chunk):
            weight = part(charges, tile) * slope
            pulled = [weight * delta[axis] for axis in range(3)]
            terms = pulled + [
                pulled[left] * delta[right]
                for left, right in ((0, 0), (1, 1), (2, 2), (0, 1), (0, 2), (1, 2))
            ]
            sums = [old + term for old, term in zip(sums, terms)]
        table = jnp.zeros((rows, lanes), jnp.float32)
        for place, value in enumerate(sums):
            table = jnp.where(lane == place, total(value), table)
        tables.append(table)
    table = jnp.concatenate(tables, axis=0)
    table = table.T
    mine = charges[:, :own]
    charges_ref[...] = mine
    pull = -mine * table[0:3]
    third = lax.broadcasted_iota(jnp.int32, pull.shape, 0) == 2
    forces_ref[...] = pull + jnp.where(third, mine * field_ref[0], 0.0)
    virial_ref[...] = 0.5 * mine * table[3:9]


def kernel_call(kernel, shapes, arguments, scalars=0, far=0, scratch=(), flops=0):
    shapes = tuple(jax.ShapeDtypeStruct(shape, kind) for shape, kind in shapes)
    spaces = [pltpu.SMEM] * scalars + [pltpu.HBM] * far
    spaces = spaces + [pltpu.VMEM] * (len(arguments) - len(spaces))
    arguments = [
        pltpu.with_memory_space_constraint(value, space) if space is pltpu.HBM else value
        for value, space in zip(arguments, spaces)
    ]
    return pl.pallas_call(
        kernel,
        out_shape=shapes,
        in_specs=[pl.BlockSpec(memory_space=space) for space in spaces],
        out_specs=tuple(pl.BlockSpec(memory_space=pltpu.VMEM) for _ in shapes),
        scratch_shapes=list(scratch),
        compiler_params=pltpu.CompilerParams(vmem_limit_bytes=32 * 1024 * 1024),
        cost_estimate=pl.CostEstimate(flops=flops, bytes_accessed=1 << 20, transcendentals=0),
    )(*arguments)


def exchanged(block, axis, step):
    size = lax.axis_size(axis)
    return lax.ppermute(block, axis, [(place, place ^ step) for place in range(size)])


def few_shards(
    features,
    positions,
    species,
    ghost_list,
    edge_recv,
    edge_send,
    edge_vec,
    w_msg,
    w_rad1,
    w_rad2,
    w_up,
    w_out,
    hardness,
    width,
    chi_shift,
    field,
):
    atoms, chans = features.shape
    edges = edge_recv.shape[0]
    rows, lanes = lax.axis_size("row"), lax.axis_size("space")
    space = lax.axis_index("space").astype(jnp.int32)
    (packed,) = kernel_call(
        pack_kernel,
        [((atoms + 16, chans), jnp.bfloat16)],
        (space.reshape(1), features, ghost_list),
        scalars=1,
        far=2,
        scratch=[
            pltpu.VMEM(ghost_list.shape, ghost_list.dtype),
            pltpu.SemaphoreType.DMA((2,)),
        ],
    )
    others = [exchanged(packed, "space", step) for step in range(1, lanes)]
    rest = (edge_vec, w_rad1, w_rad2, edge_send[None], edge_recv[None], w_msg, w_up)
    rest = rest + (species[None], hardness[None], width[None], chi_shift[None], positions)
    rest = rest + (w_out[None],)
    parts = kernel_call(
        edge_kernel,
        [
            ((2 * chans, edges), jnp.float32),
            ((8, edges), jnp.float32),
            ((1, chans), jnp.float32),
            ((chans, edges), jnp.bfloat16),
            ((lanes * atoms, edges), jnp.float32),
            ((atoms, edges), jnp.bfloat16),
            ((2 * chans, chans), jnp.bfloat16),
            ((chans, 2 * chans), jnp.bfloat16),
            ((chans, atoms), jnp.float32),
        ],
        (space.reshape(1), *rest),
        scalars=1,
        far=len(rest),
        scratch=[pltpu.VMEM(value.shape, value.dtype) for value in rest]
        + [pltpu.SemaphoreType.DMA((len(rest),))],
        flops=1 << 28,
    )
    devices = rows * lanes
    hidden, block = kernel_call(
        node_kernel,
        [((chans, atoms), jnp.float32), ((devices, 1, chans), jnp.float32)],
        (packed, *others, *parts),
        flops=1 << 28,
    )
    (new_features,) = kernel_call(
        feature_kernel, [((atoms, chans), jnp.bfloat16)], (packed, hidden), flops=1 << 20
    )
    block = lax.all_to_all(block, everywhere, 0, 0, tiled=True)
    place = lax.axis_index("row").astype(jnp.int32) * lanes + space
    everybody = rows * lanes * atoms
    charges, forces, virial = kernel_call(
        charge_kernel,
        [((count, atoms), jnp.float32) for count in (1, 3, 6)],
        (place.reshape(1), field, block),
        scalars=2,
        scratch=[
            pltpu.VMEM((everybody, everybody), jnp.float32),
            pltpu.VMEM((everybody, chans), jnp.float32),
            pltpu.VMEM((everybody, chans), jnp.float32),
        ],
        flops=1 << 28,
    )
    return (new_features, charges[0], forces, virial)


def solution(mesh):
    small = mesh.shape["space"] == 4 and mesh.shape["row"] == 8
    return jax.shard_map(
        few_shards if small else shards,
        mesh=mesh,
        in_specs=(
            P(("row", "space"), None),
            P(None, ("row", "space")),
            P(("row", "space")),
            P("row", "space", None),
            P(("row", "space")),
            P(("row", "space")),
            P(None, ("row", "space")),
            P(),
            P(),
            P(),
            P(),
            P(),
            P(),
            P(),
            P(),
            P(),
        ),
        out_specs=(
            P(("row", "space"), None),
            P(("row", "space")),
            P(None, ("row", "space")),
            P(None, ("row", "space")),
        ),
        check_vma=False,
    )
```

```python
import math

import jax
import jax.numpy as jnp
from jax import lax
from jax.experimental import pallas as pl
from jax.experimental.pallas import tpu as pltpu
from jax.sharding import PartitionSpec as P

ITERS = 2


cutoff = 6.0
message_scale = 0.125
two_over_root_pi = 2.0 / math.sqrt(math.pi)
inverse_root_pi = 1.0 / math.sqrt(math.pi)
replicate_limit = 1024
everywhere = ("row", "space")


def lookup(species, table):
    result = jnp.zeros(species.shape, jnp.float32)
    for kind in range(table.shape[0]):
        result = result + jnp.where(species == kind, table[kind], 0.0)
    return result


def pair_terms(target, target_labels, source, source_labels):
    delta = target[:3, :, None] - source[:3, None, :]
    squared = jnp.sum(delta * delta, axis=0)
    same = target_labels[:, None] == source_labels[None, :]
    squared = jnp.where(same, 1.0, squared)
    inverse = lax.rsqrt(squared)
    radius = squared * inverse
    spread = target[3][:, None] * target[3][:, None] + source[3][None, :] * source[3][None, :]
    scale = lax.rsqrt(2.0 * spread)
    scaled = radius * scale
    smear = lax.erf(scaled)
    return delta, same, inverse, scale, scaled, smear


def coulomb(target, target_labels, source, source_labels):
    _, same, inverse, _, _, smear = pair_terms(target, target_labels, source, source_labels)
    return jnp.where(same, 0.0, smear * inverse)


def pair_forces(target, target_labels, source, source_labels, source_charge):
    delta, same, inverse, scale, scaled, smear = pair_terms(
        target, target_labels, source, source_labels
    )
    slope = (
        two_over_root_pi * scale * jnp.exp(-scaled * scaled) * inverse - smear * inverse * inverse
    )
    weight = jnp.where(same, 0.0, source_charge[None, :] * slope * inverse)
    first = jnp.sum(weight[None] * delta, axis=2)
    pairs = ((0, 0), (1, 1), (2, 2), (0, 1), (0, 2), (1, 2))
    second = jnp.stack(
        [jnp.sum(weight * delta[left] * delta[right], axis=1) for left, right in pairs]
    )
    return jnp.concatenate([first, second], axis=0)


def edge_terms(receive, sender_rows, vectors, projected, w_rad1, w_rad2, atoms):
    length = jnp.sqrt(jnp.sum(vectors * vectors, axis=0))
    unit = vectors / length
    order = jnp.arange(1, w_rad1.shape[0] + 1, dtype=jnp.int32).astype(jnp.float32)[:, None]
    ratio = length / cutoff
    envelope = (1.0 - ratio * ratio) * (1.0 - ratio * ratio)
    basis = jnp.sin(order * math.pi * ratio) / ratio * envelope
    mixed = lax.dot_general(
        basis, w_rad1, (((0,), (0,)), ((), ())), precision=lax.Precision.HIGHEST
    )
    radial = jax.nn.silu(mixed).astype(jnp.bfloat16)
    filters = jnp.dot(radial, w_rad2, preferred_element_type=jnp.float32)
    picked = jnp.take(projected, sender_rows, axis=0).astype(jnp.float32) * filters
    chans = w_rad1.shape[1]
    scalar = picked[:, :chans]
    carried = picked[:, chans:]
    joined = [
        scalar,
        unit[0][:, None] * carried,
        unit[1][:, None] * carried,
        unit[2][:, None] * carried,
    ]
    message = jnp.concatenate(joined, axis=1).astype(jnp.bfloat16)
    onehot = (jnp.arange(atoms, dtype=jnp.int32)[:, None] == receive[None, :]).astype(jnp.bfloat16)
    return jnp.dot(onehot, message, preferred_element_type=jnp.float32)


def gathered(block, devices):
    copies = jnp.broadcast_to(block[None], (devices,) + block.shape)
    return lax.all_to_all(copies, everywhere, split_axis=0, concat_axis=0, tiled=True)


def shards(
    features,
    positions,
    species,
    ghost_list,
    edge_recv,
    edge_send,
    edge_vec,
    w_msg,
    w_rad1,
    w_rad2,
    w_up,
    w_out,
    hardness,
    width,
    chi_shift,
    field,
):
    atoms = features.shape[0]
    chans = features.shape[1]
    lanes = lax.axis_size("space")
    devices = lanes * lax.axis_size("row")
    everybody = devices * atoms
    me = lax.axis_index("row") * lanes + lax.axis_index("space")
    sigma = lookup(species, width)
    diag = lookup(species, hardness) + inverse_root_pi / sigma
    placed = jnp.concatenate([positions, sigma[None, :], diag[None, :]], axis=0)
    everyone = gathered(placed, devices).transpose(1, 0, 2).reshape(5, everybody)
    lists = ghost_list[0]
    outgoing = jnp.take(features, lists.reshape(-1), axis=0).reshape(lanes, lists.shape[1], chans)
    ghost_rows = jnp.einsum(
        "dkc,cf->dkf",
        lax.all_to_all(outgoing, "space", split_axis=0, concat_axis=0, tiled=True),
        w_msg,
        preferred_element_type=jnp.float32,
    ).astype(jnp.bfloat16)
    own_rows = jnp.dot(features, w_msg, preferred_element_type=jnp.float32).astype(jnp.bfloat16)
    projected = jnp.concatenate([own_rows, ghost_rows.reshape(-1, 2 * chans)], axis=0)
    summed = edge_terms(edge_recv, edge_send, edge_vec, projected, w_rad1, w_rad2, atoms)
    summed = summed * message_scale
    vector_part = summed[:, chans:].reshape(atoms, 3, chans)
    invariant = jnp.concatenate(
        [summed[:, :chans], jnp.sum(vector_part * vector_part, axis=1)], axis=1
    ).astype(jnp.bfloat16)
    hidden = jax.nn.silu(jnp.dot(invariant, w_up, preferred_element_type=jnp.float32))
    new_features = (features.astype(jnp.float32) + hidden).astype(jnp.bfloat16)
    chi = jnp.dot(hidden, w_out, precision=lax.Precision.HIGHEST) + lookup(species, chi_shift)
    own_labels = me * atoms + jnp.arange(atoms, dtype=jnp.int32)
    all_labels = jnp.arange(everybody, dtype=jnp.int32)
    rhs = field[0] * positions[2] - chi

    if everybody <= replicate_limit:
        kernel = coulomb(everyone, all_labels, everyone, all_labels)
        residual = gathered(rhs, devices).reshape(everybody)
        all_charges = conjugate(
            residual, lambda v: everyone[4] * v + jnp.sum(kernel * v[None, :], axis=1), jnp.sum
        )
        charges = lax.dynamic_slice(all_charges, (me * atoms,), (atoms,))
    else:
        kernel = coulomb(placed, own_labels, everyone, all_labels)

        def spread(vector):
            return gathered(vector, devices).reshape(everybody)

        charges = conjugate(
            rhs,
            lambda v: diag * v + jnp.sum(kernel * spread(v)[None, :], axis=1),
            lambda v: lax.psum(jnp.sum(v), everywhere),
        )
        all_charges = spread(charges)
    sums = pair_forces(placed, own_labels, everyone, all_labels, all_charges)
    pull = -charges[None, :] * sums[:3]
    forces = jnp.concatenate([pull[:2], pull[2:] + (charges * field[0])[None, :]], axis=0)
    virial = 0.5 * charges[None, :] * sums[3:]
    return (new_features, charges, forces, virial)


def conjugate(rhs, apply, total):
    charges = jnp.zeros_like(rhs)
    residual = rhs
    direction = rhs
    norm_now = total(residual * residual)
    for step in range(ITERS):
        image = apply(direction)
        alpha = norm_now / total(direction * image)
        charges = charges + alpha * direction
        if step + 1 < ITERS:
            residual = residual - alpha * image
            fresh = total(residual * residual)
            direction = residual + fresh / norm_now * direction
            norm_now = fresh
    return charges


def split3(value):
    first = value.astype(jnp.bfloat16).astype(jnp.float32)
    rest = value - first
    second = rest.astype(jnp.bfloat16).astype(jnp.float32)
    third = (rest - second).astype(jnp.bfloat16).astype(jnp.float32)
    return first, second, third


def over_first(left, right):
    return lax.dot_general(
        left, right, (((0,), (0,)), ((), ())), preferred_element_type=jnp.float32
    )


def over_last(left, right, precision=None):
    return lax.dot_general(
        left,
        right,
        (((1,), (1,)), ((), ())),
        precision=precision,
        preferred_element_type=jnp.float32,
    )


def silu(value):
    return value / (1.0 + jnp.exp(-value))


def silu_half(value):
    return (0.5 * value) * (1.0 + jnp.tanh(0.5 * value))


sine_series = [(-1.0) ** k * math.pi ** (2 * k + 1) / math.factorial(2 * k + 1) for k in range(7)]


def fetched(pairs, semaphores):
    copies = [
        pltpu.make_async_copy(source, target, semaphores.at[place])
        for place, (source, target) in enumerate(pairs)
    ]
    for copy in copies:
        copy.start()
    return copies


chi_segment = 3


def pack_kernel(space_ref, features_ref, lists_ref, packed_ref, held_ref, semaphores):
    atoms, chans = features_ref.shape
    copies = fetched(
        [(lists_ref, held_ref), (features_ref, packed_ref.at[pl.ds(0, atoms)])], semaphores
    )
    copies[0].wait()
    _, lanes, width = held_ref.shape
    rows = []
    for place in range(lanes):
        row = held_ref[0, pl.ds(space_ref[0] ^ place, 1), :].astype(jnp.float32) + place * atoms
        parts = [jnp.zeros((1, width), jnp.float32)] * lanes
        parts[place] = row
        rows.append(jnp.concatenate(parts, axis=1))
    rows.append(jnp.zeros((packed_ref.shape[0] - atoms - lanes, chans), jnp.float32))
    packed_ref[atoms:, :] = jnp.concatenate(rows, axis=0).astype(jnp.bfloat16)
    copies[1].wait()


def edge_kernel(
    space_ref,
    *refs,
):
    count = (len(refs) - 10) // 2
    far, near, semaphores = refs[:count], refs[count + 9 : -1], refs[-1]
    filter_ref, unit_ref, row_ref, slot_ref, local_ref, hit_ref = refs[count : count + 6]
    turned_ref, upward_ref, read_ref = refs[count + 6 : count + 9]
    vec_ref, first_ref, second_ref, send_ref, recv_ref, project_ref, update_ref = near[:7]
    species_ref, hardness_ref, width_ref, shift_ref, positions_ref, out_ref = near[7:]
    copies = fetched(list(zip(far, near)), semaphores)
    for copy in copies[:3]:
        copy.wait()
    edges = vec_ref.shape[1]
    orders = first_ref.shape[0]
    vec = vec_ref[...]
    east, north, up = vec[0:1], vec[1:2], vec[2:3]
    squared = east * east + north * north + up * up
    inverse = lax.rsqrt(squared)
    unit_ref[0:3, :] = vec * inverse
    ratio = squared * inverse * (1.0 / cutoff)
    envelope = (1.0 - ratio * ratio) * (1.0 - ratio * ratio) * (cutoff * inverse)
    order = lax.broadcasted_iota(jnp.int32, (orders, edges), 0).astype(jnp.float32) + 1.0
    turns = order * ratio
    whole = jnp.floor(turns + 0.5)
    part = turns - whole
    sign = 1.0 - 2.0 * (whole - 2.0 * jnp.floor(whole * 0.5))
    series = jnp.full_like(part, sine_series[-1])
    for coefficient in sine_series[-2::-1]:
        series = series * (part * part) + coefficient
    basis = series * part * (sign * envelope)
    b1, b2, b3 = split3(basis)
    w1, w2, w3 = split3(first_ref[...])
    mixed = over_first(
        jnp.concatenate([w1, w1, w2, w2, w1, w3], axis=0).astype(jnp.bfloat16),
        jnp.concatenate([b1, b2, b1, b2, b3, b1], axis=0).astype(jnp.bfloat16),
    )
    radial = silu_half(mixed).astype(jnp.bfloat16)
    filter_ref[...] = over_first(second_ref[...], radial)
    for copy in copies[3:]:
        copy.wait()
    species = species_ref[...]

    def table(ref):
        result = jnp.zeros(species.shape, jnp.float32)
        for kind in range(ref.shape[1]):
            result = result + jnp.where(species == kind, ref[:, kind : kind + 1], 0.0)
        return result

    positions = positions_ref[...]
    sigma = table(width_ref)
    atoms = species.shape[1]
    chans = row_ref.shape[1]
    diag = table(hardness_ref) + inverse_root_pi / sigma
    blank = jnp.zeros((2, atoms), jnp.float32)
    rows = [positions[0:1], blank, -table(shift_ref), diag, sigma, positions[2:3], positions[1:2]]
    block = jnp.concatenate(
        [jnp.concatenate(rows, axis=0), jnp.zeros((8, chans - atoms), jnp.float32)], axis=1
    )
    block = pltpu.roll(block, 0, 1, stride=atoms, stride_axis=0)
    row_ref[...] = jnp.sum(block, axis=0, keepdims=True)
    lanes = local_ref.shape[0] // atoms
    slots = chans // lanes
    send = send_ref[...]
    own = send < atoms
    slot = jnp.where(own, -1, (send - atoms) ^ (space_ref[0] * slots))
    local = jnp.where(own, send, -1)

    def chosen(ref, index):
        hit = lax.broadcasted_iota(jnp.int32, ref.shape, 0) == index
        ref[...] = jnp.where(hit, 1.0, 0.0).astype(ref.dtype)

    chosen(slot_ref, slot)
    chosen(local_ref, local)
    chosen(hit_ref, recv_ref[...])
    turned_ref[...] = project_ref[...].astype(jnp.float32).T.astype(jnp.bfloat16)
    upward_ref[...] = update_ref[...].astype(jnp.float32).T.astype(jnp.bfloat16)
    read_ref[...] = jnp.broadcast_to(out_ref[...], (atoms, chans)).T


def node_kernel(
    own_ref,
    near_ref,
    side_ref,
    far_ref,
    filter_ref,
    unit_ref,
    row_ref,
    slot_ref,
    local_ref,
    hit_ref,
    turned_ref,
    upward_ref,
    read_ref,
    hidden_ref,
    block_ref,
):
    chans, atoms = hidden_ref.shape
    packed = (own_ref, near_ref, side_ref, far_ref)
    group = jnp.concatenate([ref[:atoms, :] for ref in packed], axis=0)
    chosen = jnp.zeros((1, chans), jnp.float32)
    for place, ref in enumerate(packed):
        tail = ref[atoms:, :].astype(jnp.float32)
        chosen = chosen + tail[place : place + 1]
    fill = jnp.where(
        lax.broadcasted_iota(jnp.int32, (len(packed) * atoms, chans), 0)
        == chosen.astype(jnp.int32),
        1.0,
        0.0,
    ).astype(jnp.bfloat16)
    sender = jnp.dot(fill, slot_ref[...], preferred_element_type=jnp.float32) + local_ref[...]
    projected = over_last(turned_ref[...], group).astype(jnp.bfloat16)
    picked = jnp.dot(projected, sender.astype(jnp.bfloat16), preferred_element_type=jnp.float32)
    scalar = picked[:chans] * filter_ref[:chans, :]
    carried = picked[chans:] * filter_ref[chans:, :]
    parts = [scalar] + [unit_ref[axis : axis + 1, :] * carried for axis in range(3)]
    message = jnp.concatenate([part.astype(jnp.bfloat16) for part in parts], axis=0)
    summed = over_last(message, hit_ref[...]) * message_scale
    square = jnp.zeros((chans, atoms), jnp.float32)
    for component in range(1, 4):
        part = summed[component * chans : (component + 1) * chans]
        square = square + part * part
    invariant = jnp.concatenate([summed[:chans], square], axis=0).astype(jnp.bfloat16)
    hidden = silu(jnp.dot(upward_ref[...], invariant, preferred_element_type=jnp.float32))
    chi = jnp.sum(hidden * read_ref[...], axis=0, keepdims=True)
    chi = jnp.concatenate([chi, jnp.zeros((1, chans - atoms), jnp.float32)], axis=1)
    row = row_ref[...] - pltpu.roll(chi, chi_segment * atoms, 1)
    block_ref[...] = jnp.broadcast_to(row[None], block_ref.shape)
    hidden_ref[...] = hidden


def feature_kernel(packed_ref, hidden_ref, features_ref):
    atoms = features_ref.shape[0]
    old = packed_ref[...].astype(jnp.float32)[:atoms]
    features_ref[...] = (old + hidden_ref[...].T).astype(jnp.bfloat16)


def reciprocal(value):
    rough = pl.reciprocal(value, approx=True)
    return rough * (2.0 - value * rough)


def smeared(scaled):
    decay = jnp.exp2(scaled * scaled * -math.log2(math.e))
    turn = reciprocal(1.0 + 0.3275911 * scaled)
    series = 1.061405429 * turn - 1.453152027
    series = series * turn + 1.421413741
    series = series * turn - 0.284496736
    series = series * turn + 0.254829592
    return 1.0 - series * turn * decay, decay


def charge_kernel(
    place_ref,
    field_ref,
    all_ref,
    charges_ref,
    forces_ref,
    virial_ref,
    matrix_ref,
    side_ref,
    value_ref,
):
    blocks, _, lanes = all_ref.shape
    own = charges_ref.shape[1]
    count = blocks * own
    fit = lanes // own
    segment = lax.broadcasted_iota(jnp.int32, (8, lanes), 1) // own
    tiles = []
    for first in range(0, blocks, fit):
        tile = jnp.zeros((8, lanes), jnp.float32)
        for place in range(fit):
            row = all_ref[(place_ref[0] + first + place) & (blocks - 1)]
            row = pltpu.roll(jnp.broadcast_to(row, (8, lanes)), 0, 1, stride=own, stride_axis=0)
            row = pltpu.roll(row, place * own, 1) if place else row
            tile = jnp.where(segment == place, row, tile)
        tiles.append(tile)
    everyone = jnp.concatenate(tiles, axis=1)
    last = lax.broadcasted_iota(jnp.int32, everyone.shape, 0) == 5
    everyone = everyone + jnp.where(last, field_ref[0] * everyone[2:3], 0.0)
    columns = everyone.T
    diag, rhs = everyone[4:5], everyone[5:6]
    spread_row = 2.0 * everyone[3:4] * everyone[3:4]
    tiles = count // lanes
    depth = own // 8
    shape = (depth, 8, lanes)
    lane = lax.broadcasted_iota(jnp.int32, shape, 2)
    line = lax.broadcasted_iota(jnp.int32, shape, 0) * 8 + lax.broadcasted_iota(jnp.int32, shape, 1)

    def part(row, tile):
        return row[:, tile * lanes : (tile + 1) * lanes]

    def down(row):
        return [jnp.broadcast_to(part(row, tile), (8, lanes))[None] for tile in range(tiles)]

    def along(column):
        return jnp.broadcast_to(column, (own, lanes)).reshape(shape)

    def total(value):
        return jnp.sum(value, axis=1, keepdims=True)

    axes = [down(everyone[axis : axis + 1]) for axis in range(3)]
    wide_row, rhs_row = down(spread_row), down(rhs)

    above = [jnp.zeros((8, lanes), jnp.float32) for _ in range(tiles)]
    kept = []
    for start in range(0, count, own):
        first = start // lanes
        column = columns[start : start + own]
        place = [along(column[:, axis : axis + 1]) for axis in range(3)]
        wide = along(2.0 * column[:, 3:4] * column[:, 3:4])
        value = along(column[:, 5:6])
        value_ref[start : start + own, :] = value.reshape(own, lanes)
        below = jnp.zeros(shape, jnp.float32)
        for tile in range(first, tiles):
            delta = [place[axis] - axes[axis][tile] for axis in range(3)]
            squared = delta[0] * delta[0] + delta[1] * delta[1] + delta[2] * delta[2]
            if tile == first:
                same = lane == line + (start - first * lanes)
                squared = jnp.where(same, 1.0, squared)
            inverse = lax.rsqrt(squared)
            scale = lax.rsqrt(wide + wide_row[tile])
            smear, decay = smeared(squared * inverse * scale)
            kernel = smear * inverse
            if start == 0:
                slope = (two_over_root_pi * scale * decay - kernel) * inverse * inverse
                slope = jnp.where(same, 0.0, slope) if tile == first else slope
                kept.append((delta, slope))
            if tile == first:
                kernel = jnp.where(same, 0.0, kernel)
            else:
                below = below + kernel * rhs_row[tile]
            above[tile] = above[tile] + jnp.sum(kernel * value, axis=0)
            matrix_ref[start : start + own, tile * lanes : (tile + 1) * lanes] = kernel.reshape(
                own, lanes
            )
        if first + 1 < tiles:
            side_ref[start : start + own, :] = below.reshape(own, lanes)
    image = []
    for tile in range(tiles):
        value = jnp.sum(above[tile], axis=0, keepdims=True)
        if tile + 1 < tiles:
            below = side_ref[tile * lanes : (tile + 1) * lanes, :].T
            value = value + jnp.sum(below, axis=0, keepdims=True)
        image.append(value)
    image = diag * rhs + jnp.concatenate(image, axis=1)
    across = jnp.broadcast_to(image, (8, count)).T
    norm = total(rhs * rhs)
    alpha = norm / total(rhs * image)
    residual = rhs - alpha * image
    fresh = total(residual * residual)
    again = fresh / norm
    direction = residual + again * rhs
    onto = [jnp.zeros((8, lanes), jnp.float32) for _ in range(tiles)]
    above = [jnp.zeros((8, lanes), jnp.float32) for _ in range(tiles)]
    for start in range(0, count, own):
        first = start // lanes
        value = (1.0 + again) * value_ref[start : start + own, :]
        value = value - alpha * jnp.broadcast_to(across[start : start + own, 0:1], (own, lanes))
        value = value.reshape(shape)
        for tile in range(first, tiles):
            sums = onto if tile == first else above
            kernel = matrix_ref[start : start + own, tile * lanes : (tile + 1) * lanes]
            sums[tile] = sums[tile] + jnp.sum(kernel.reshape(shape) * value, axis=0)
    curved = jnp.zeros((8, lanes), jnp.float32)
    for tile in range(tiles):
        curved = curved + (onto[tile] + 2.0 * above[tile]) * part(direction, tile)
    curved = jnp.sum(curved, axis=0, keepdims=True)
    for tile in range(tiles):
        curved = curved + part(diag * direction * direction, tile)
    charges = alpha * rhs + fresh / total(curved) * direction

    sums = [jnp.zeros(shape, jnp.float32) for _ in range(9)]
    charge_row = down(charges)
    for tile, (delta, slope) in enumerate(kept):
        weight = charge_row[tile] * slope
        pulled = [weight * delta[axis] for axis in range(3)]
        terms = pulled + [
            pulled[left] * delta[right]
            for left, right in ((0, 0), (1, 1), (2, 2), (0, 1), (0, 2), (1, 2))
        ]
        sums = [old + term for old, term in zip(sums, terms)]
    table = jnp.zeros((own, lanes), jnp.float32)
    lane = lane.reshape(own, lanes)
    for place, value in enumerate(sums):
        table = jnp.where(lane == place, total(value.reshape(own, lanes)), table)
    table = table.T
    mine = charges[:, :own]
    charges_ref[...] = mine
    pull = -mine * table[0:3]
    third = lax.broadcasted_iota(jnp.int32, pull.shape, 0) == 2
    forces_ref[...] = pull + jnp.where(third, mine * field_ref[0], 0.0)
    virial_ref[...] = 0.5 * mine * table[3:9]


def kernel_call(kernel, shapes, arguments, scalars=0, far=0, scratch=(), flops=0):
    shapes = tuple(jax.ShapeDtypeStruct(shape, kind) for shape, kind in shapes)
    spaces = [pltpu.SMEM] * scalars + [pltpu.HBM] * far
    spaces = spaces + [pltpu.VMEM] * (len(arguments) - len(spaces))
    arguments = [
        pltpu.with_memory_space_constraint(value, space) if space is pltpu.HBM else value
        for value, space in zip(arguments, spaces)
    ]
    return pl.pallas_call(
        kernel,
        out_shape=shapes,
        in_specs=[pl.BlockSpec(memory_space=space) for space in spaces],
        out_specs=tuple(pl.BlockSpec(memory_space=pltpu.VMEM) for _ in shapes),
        scratch_shapes=list(scratch),
        compiler_params=pltpu.CompilerParams(vmem_limit_bytes=32 * 1024 * 1024),
        cost_estimate=pl.CostEstimate(flops=flops, bytes_accessed=1 << 20, transcendentals=0),
    )(*arguments)


def exchanged(block, axis, step):
    size = lax.axis_size(axis)
    return lax.ppermute(block, axis, [(place, place ^ step) for place in range(size)])


def few_shards(
    features,
    positions,
    species,
    ghost_list,
    edge_recv,
    edge_send,
    edge_vec,
    w_msg,
    w_rad1,
    w_rad2,
    w_up,
    w_out,
    hardness,
    width,
    chi_shift,
    field,
):
    atoms, chans = features.shape
    edges = edge_recv.shape[0]
    rows, lanes = lax.axis_size("row"), lax.axis_size("space")
    space = lax.axis_index("space").astype(jnp.int32)
    (packed,) = kernel_call(
        pack_kernel,
        [((atoms + 16, chans), jnp.bfloat16)],
        (space.reshape(1), features, ghost_list),
        scalars=1,
        far=2,
        scratch=[
            pltpu.VMEM(ghost_list.shape, ghost_list.dtype),
            pltpu.SemaphoreType.DMA((2,)),
        ],
    )
    others = [exchanged(packed, "space", step) for step in range(1, lanes)]
    rest = (edge_vec, w_rad1, w_rad2, edge_send[None], edge_recv[None], w_msg, w_up)
    rest = rest + (species[None], hardness[None], width[None], chi_shift[None], positions)
    rest = rest + (w_out[None],)
    parts = kernel_call(
        edge_kernel,
        [
            ((2 * chans, edges), jnp.float32),
            ((8, edges), jnp.float32),
            ((1, chans), jnp.float32),
            ((chans, edges), jnp.bfloat16),
            ((lanes * atoms, edges), jnp.float32),
            ((atoms, edges), jnp.bfloat16),
            ((2 * chans, chans), jnp.bfloat16),
            ((chans, 2 * chans), jnp.bfloat16),
            ((chans, atoms), jnp.float32),
        ],
        (space.reshape(1), *rest),
        scalars=1,
        far=len(rest),
        scratch=[pltpu.VMEM(value.shape, value.dtype) for value in rest]
        + [pltpu.SemaphoreType.DMA((len(rest),))],
        flops=1 << 28,
    )
    devices = rows * lanes
    hidden, block = kernel_call(
        node_kernel,
        [((chans, atoms), jnp.float32), ((devices, 1, chans), jnp.float32)],
        (packed, *others, *parts),
        flops=1 << 28,
    )
    (new_features,) = kernel_call(
        feature_kernel, [((atoms, chans), jnp.bfloat16)], (packed, hidden), flops=1 << 20
    )
    block = lax.all_to_all(block, everywhere, 0, 0, tiled=True)
    place = lax.axis_index("row").astype(jnp.int32) * lanes + space
    everybody = rows * lanes * atoms
    charges, forces, virial = kernel_call(
        charge_kernel,
        [((count, atoms), jnp.float32) for count in (1, 3, 6)],
        (place.reshape(1), field, block),
        scalars=2,
        scratch=[
            pltpu.VMEM((everybody, everybody), jnp.float32),
            pltpu.VMEM((everybody, chans), jnp.float32),
            pltpu.VMEM((everybody, chans), jnp.float32),
        ],
        flops=1 << 28,
    )
    return (new_features, charges[0], forces, virial)


def solution(mesh):
    small = mesh.shape["space"] == 4 and mesh.shape["row"] == 8
    return jax.shard_map(
        few_shards if small else shards,
        mesh=mesh,
        in_specs=(
            P(("row", "space"), None),
            P(None, ("row", "space")),
            P(("row", "space")),
            P("row", "space", None),
            P(("row", "space")),
            P(("row", "space")),
            P(None, ("row", "space")),
            P(),
            P(),
            P(),
            P(),
            P(),
            P(),
            P(),
            P(),
            P(),
        ),
        out_specs=(
            P(("row", "space"), None),
            P(("row", "space")),
            P(None, ("row", "space")),
            P(None, ("row", "space")),
        ),
        check_vma=False,
    )
```

```python
import math

import jax
import jax.numpy as jnp
from jax import lax
from jax.experimental import pallas as pl
from jax.experimental.pallas import tpu as pltpu
from jax.sharding import PartitionSpec as P

ITERS = 2


cutoff = 6.0
message_scale = 0.125
two_over_root_pi = 2.0 / math.sqrt(math.pi)
inverse_root_pi = 1.0 / math.sqrt(math.pi)
replicate_limit = 1024
everywhere = ("row", "space")


def lookup(species, table):
    result = jnp.zeros(species.shape, jnp.float32)
    for kind in range(table.shape[0]):
        result = result + jnp.where(species == kind, table[kind], 0.0)
    return result


def pair_terms(target, target_labels, source, source_labels):
    delta = target[:3, :, None] - source[:3, None, :]
    squared = jnp.sum(delta * delta, axis=0)
    same = target_labels[:, None] == source_labels[None, :]
    squared = jnp.where(same, 1.0, squared)
    inverse = lax.rsqrt(squared)
    radius = squared * inverse
    spread = target[3][:, None] * target[3][:, None] + source[3][None, :] * source[3][None, :]
    scale = lax.rsqrt(2.0 * spread)
    scaled = radius * scale
    smear = lax.erf(scaled)
    return delta, same, inverse, scale, scaled, smear


def coulomb(target, target_labels, source, source_labels):
    _, same, inverse, _, _, smear = pair_terms(target, target_labels, source, source_labels)
    return jnp.where(same, 0.0, smear * inverse)


def pair_forces(target, target_labels, source, source_labels, source_charge):
    delta, same, inverse, scale, scaled, smear = pair_terms(
        target, target_labels, source, source_labels
    )
    slope = (
        two_over_root_pi * scale * jnp.exp(-scaled * scaled) * inverse - smear * inverse * inverse
    )
    weight = jnp.where(same, 0.0, source_charge[None, :] * slope * inverse)
    first = jnp.sum(weight[None] * delta, axis=2)
    pairs = ((0, 0), (1, 1), (2, 2), (0, 1), (0, 2), (1, 2))
    second = jnp.stack(
        [jnp.sum(weight * delta[left] * delta[right], axis=1) for left, right in pairs]
    )
    return jnp.concatenate([first, second], axis=0)


def edge_terms(receive, sender_rows, vectors, projected, w_rad1, w_rad2, atoms):
    length = jnp.sqrt(jnp.sum(vectors * vectors, axis=0))
    unit = vectors / length
    order = jnp.arange(1, w_rad1.shape[0] + 1, dtype=jnp.int32).astype(jnp.float32)[:, None]
    ratio = length / cutoff
    envelope = (1.0 - ratio * ratio) * (1.0 - ratio * ratio)
    basis = jnp.sin(order * math.pi * ratio) / ratio * envelope
    mixed = lax.dot_general(
        basis, w_rad1, (((0,), (0,)), ((), ())), precision=lax.Precision.HIGHEST
    )
    radial = jax.nn.silu(mixed).astype(jnp.bfloat16)
    filters = jnp.dot(radial, w_rad2, preferred_element_type=jnp.float32)
    picked = jnp.take(projected, sender_rows, axis=0).astype(jnp.float32) * filters
    chans = w_rad1.shape[1]
    scalar = picked[:, :chans]
    carried = picked[:, chans:]
    joined = [
        scalar,
        unit[0][:, None] * carried,
        unit[1][:, None] * carried,
        unit[2][:, None] * carried,
    ]
    message = jnp.concatenate(joined, axis=1).astype(jnp.bfloat16)
    onehot = (jnp.arange(atoms, dtype=jnp.int32)[:, None] == receive[None, :]).astype(jnp.bfloat16)
    return jnp.dot(onehot, message, preferred_element_type=jnp.float32)


def gathered(block, devices):
    copies = jnp.broadcast_to(block[None], (devices,) + block.shape)
    return lax.all_to_all(copies, everywhere, split_axis=0, concat_axis=0, tiled=True)


def shards(
    features,
    positions,
    species,
    ghost_list,
    edge_recv,
    edge_send,
    edge_vec,
    w_msg,
    w_rad1,
    w_rad2,
    w_up,
    w_out,
    hardness,
    width,
    chi_shift,
    field,
):
    atoms = features.shape[0]
    chans = features.shape[1]
    lanes = lax.axis_size("space")
    devices = lanes * lax.axis_size("row")
    everybody = devices * atoms
    me = lax.axis_index("row") * lanes + lax.axis_index("space")
    sigma = lookup(species, width)
    diag = lookup(species, hardness) + inverse_root_pi / sigma
    placed = jnp.concatenate([positions, sigma[None, :], diag[None, :]], axis=0)
    everyone = gathered(placed, devices).transpose(1, 0, 2).reshape(5, everybody)
    lists = ghost_list[0]
    outgoing = jnp.take(features, lists.reshape(-1), axis=0).reshape(lanes, lists.shape[1], chans)
    ghost_rows = jnp.einsum(
        "dkc,cf->dkf",
        lax.all_to_all(outgoing, "space", split_axis=0, concat_axis=0, tiled=True),
        w_msg,
        preferred_element_type=jnp.float32,
    ).astype(jnp.bfloat16)
    own_rows = jnp.dot(features, w_msg, preferred_element_type=jnp.float32).astype(jnp.bfloat16)
    projected = jnp.concatenate([own_rows, ghost_rows.reshape(-1, 2 * chans)], axis=0)
    summed = edge_terms(edge_recv, edge_send, edge_vec, projected, w_rad1, w_rad2, atoms)
    summed = summed * message_scale
    vector_part = summed[:, chans:].reshape(atoms, 3, chans)
    invariant = jnp.concatenate(
        [summed[:, :chans], jnp.sum(vector_part * vector_part, axis=1)], axis=1
    ).astype(jnp.bfloat16)
    hidden = jax.nn.silu(jnp.dot(invariant, w_up, preferred_element_type=jnp.float32))
    new_features = (features.astype(jnp.float32) + hidden).astype(jnp.bfloat16)
    chi = jnp.dot(hidden, w_out, precision=lax.Precision.HIGHEST) + lookup(species, chi_shift)
    own_labels = me * atoms + jnp.arange(atoms, dtype=jnp.int32)
    all_labels = jnp.arange(everybody, dtype=jnp.int32)
    rhs = field[0] * positions[2] - chi

    if everybody <= replicate_limit:
        kernel = coulomb(everyone, all_labels, everyone, all_labels)
        residual = gathered(rhs, devices).reshape(everybody)
        all_charges = conjugate(
            residual, lambda v: everyone[4] * v + jnp.sum(kernel * v[None, :], axis=1), jnp.sum
        )
        charges = lax.dynamic_slice(all_charges, (me * atoms,), (atoms,))
    else:
        kernel = coulomb(placed, own_labels, everyone, all_labels)

        def spread(vector):
            return gathered(vector, devices).reshape(everybody)

        charges = conjugate(
            rhs,
            lambda v: diag * v + jnp.sum(kernel * spread(v)[None, :], axis=1),
            lambda v: lax.psum(jnp.sum(v), everywhere),
        )
        all_charges = spread(charges)
    sums = pair_forces(placed, own_labels, everyone, all_labels, all_charges)
    pull = -charges[None, :] * sums[:3]
    forces = jnp.concatenate([pull[:2], pull[2:] + (charges * field[0])[None, :]], axis=0)
    virial = 0.5 * charges[None, :] * sums[3:]
    return (new_features, charges, forces, virial)


def conjugate(rhs, apply, total):
    charges = jnp.zeros_like(rhs)
    residual = rhs
    direction = rhs
    norm_now = total(residual * residual)
    for step in range(ITERS):
        image = apply(direction)
        alpha = norm_now / total(direction * image)
        charges = charges + alpha * direction
        if step + 1 < ITERS:
            residual = residual - alpha * image
            fresh = total(residual * residual)
            direction = residual + fresh / norm_now * direction
            norm_now = fresh
    return charges


def split3(value):
    first = value.astype(jnp.bfloat16).astype(jnp.float32)
    rest = value - first
    second = rest.astype(jnp.bfloat16).astype(jnp.float32)
    third = (rest - second).astype(jnp.bfloat16).astype(jnp.float32)
    return first, second, third


def over_first(left, right):
    return lax.dot_general(
        left, right, (((0,), (0,)), ((), ())), preferred_element_type=jnp.float32
    )


def over_last(left, right, precision=None):
    return lax.dot_general(
        left,
        right,
        (((1,), (1,)), ((), ())),
        precision=precision,
        preferred_element_type=jnp.float32,
    )


def silu(value):
    return value / (1.0 + jnp.exp(-value))


def silu_half(value):
    return (0.5 * value) * (1.0 + jnp.tanh(0.5 * value))


sine_series = [(-1.0) ** k * math.pi ** (2 * k + 1) / math.factorial(2 * k + 1) for k in range(7)]


def fetched(pairs, semaphores):
    copies = [
        pltpu.make_async_copy(source, target, semaphores.at[place])
        for place, (source, target) in enumerate(pairs)
    ]
    for copy in copies:
        copy.start()
    return copies


chi_segment = 3


def pack_kernel(space_ref, features_ref, lists_ref, packed_ref, held_ref, semaphores):
    atoms, chans = features_ref.shape
    copies = fetched(
        [(lists_ref, held_ref), (features_ref, packed_ref.at[pl.ds(0, atoms)])], semaphores
    )
    copies[0].wait()
    _, lanes, width = held_ref.shape
    rows = []
    for place in range(lanes):
        row = held_ref[0, pl.ds(space_ref[0] ^ place, 1), :].astype(jnp.float32) + place * atoms
        parts = [jnp.zeros((1, width), jnp.float32)] * lanes
        parts[place] = row
        rows.append(jnp.concatenate(parts, axis=1))
    rows.append(jnp.zeros((packed_ref.shape[0] - atoms - lanes, chans), jnp.float32))
    packed_ref[atoms:, :] = jnp.concatenate(rows, axis=0).astype(jnp.bfloat16)
    copies[1].wait()


def edge_kernel(
    space_ref,
    *refs,
):
    count = (len(refs) - 10) // 2
    far, near, semaphores = refs[:count], refs[count + 9 : -1], refs[-1]
    filter_ref, unit_ref, row_ref, slot_ref, local_ref, hit_ref = refs[count : count + 6]
    turned_ref, upward_ref, read_ref = refs[count + 6 : count + 9]
    vec_ref, first_ref, second_ref, send_ref, recv_ref, project_ref, update_ref = near[:7]
    species_ref, hardness_ref, width_ref, shift_ref, positions_ref, out_ref = near[7:]
    copies = fetched(list(zip(far, near)), semaphores)
    for copy in copies[:3]:
        copy.wait()
    edges = vec_ref.shape[1]
    orders = first_ref.shape[0]
    vec = vec_ref[...]
    east, north, up = vec[0:1], vec[1:2], vec[2:3]
    squared = east * east + north * north + up * up
    inverse = lax.rsqrt(squared)
    unit_ref[0:3, :] = vec * inverse
    ratio = squared * inverse * (1.0 / cutoff)
    envelope = (1.0 - ratio * ratio) * (1.0 - ratio * ratio) * (cutoff * inverse)
    order = lax.broadcasted_iota(jnp.int32, (orders, edges), 0).astype(jnp.float32) + 1.0
    turns = order * ratio
    whole = jnp.floor(turns + 0.5)
    part = turns - whole
    sign = 1.0 - 2.0 * (whole - 2.0 * jnp.floor(whole * 0.5))
    series = jnp.full_like(part, sine_series[-1])
    for coefficient in sine_series[-2::-1]:
        series = series * (part * part) + coefficient
    basis = series * part * (sign * envelope)
    b1, b2, b3 = split3(basis)
    w1, w2, w3 = split3(first_ref[...])
    mixed = over_first(
        jnp.concatenate([w1, w1, w2, w2, w1, w3], axis=0).astype(jnp.bfloat16),
        jnp.concatenate([b1, b2, b1, b2, b3, b1], axis=0).astype(jnp.bfloat16),
    )
    radial = silu_half(mixed).astype(jnp.bfloat16)
    filter_ref[...] = over_first(second_ref[...], radial)
    for copy in copies[3:]:
        copy.wait()
    species = species_ref[...]

    def table(ref):
        result = jnp.zeros(species.shape, jnp.float32)
        for kind in range(ref.shape[1]):
            result = result + jnp.where(species == kind, ref[:, kind : kind + 1], 0.0)
        return result

    positions = positions_ref[...]
    sigma = table(width_ref)
    atoms = species.shape[1]
    chans = row_ref.shape[1]
    diag = table(hardness_ref) + inverse_root_pi / sigma
    blank = jnp.zeros((2, atoms), jnp.float32)
    rows = [positions[0:1], blank, -table(shift_ref), diag, sigma, positions[2:3], positions[1:2]]
    block = jnp.concatenate(
        [jnp.concatenate(rows, axis=0), jnp.zeros((8, chans - atoms), jnp.float32)], axis=1
    )
    block = pltpu.roll(block, 0, 1, stride=atoms, stride_axis=0)
    row_ref[...] = jnp.sum(block, axis=0, keepdims=True)
    lanes = local_ref.shape[0] // atoms
    slots = chans // lanes
    send = send_ref[...]
    own = send < atoms
    slot = jnp.where(own, -1, (send - atoms) ^ (space_ref[0] * slots))
    local = jnp.where(own, send, -1)

    def chosen(ref, index):
        hit = lax.broadcasted_iota(jnp.int32, ref.shape, 0) == index
        ref[...] = jnp.where(hit, 1.0, 0.0).astype(ref.dtype)

    chosen(slot_ref, slot)
    chosen(local_ref, local)
    chosen(hit_ref, recv_ref[...])
    turned_ref[...] = project_ref[...].astype(jnp.float32).T.astype(jnp.bfloat16)
    upward_ref[...] = update_ref[...].astype(jnp.float32).T.astype(jnp.bfloat16)
    read_ref[...] = jnp.broadcast_to(out_ref[...], (atoms, chans)).T


def node_kernel(
    own_ref,
    near_ref,
    side_ref,
    far_ref,
    filter_ref,
    unit_ref,
    row_ref,
    slot_ref,
    local_ref,
    hit_ref,
    turned_ref,
    upward_ref,
    read_ref,
    hidden_ref,
    block_ref,
):
    chans, atoms = hidden_ref.shape
    packed = (own_ref, near_ref, side_ref, far_ref)
    group = jnp.concatenate([ref[:atoms, :] for ref in packed], axis=0)
    chosen = jnp.zeros((1, chans), jnp.float32)
    for place, ref in enumerate(packed):
        tail = ref[atoms:, :].astype(jnp.float32)
        chosen = chosen + tail[place : place + 1]
    fill = jnp.where(
        lax.broadcasted_iota(jnp.int32, (len(packed) * atoms, chans), 0)
        == chosen.astype(jnp.int32),
        1.0,
        0.0,
    ).astype(jnp.bfloat16)
    sender = jnp.dot(fill, slot_ref[...], preferred_element_type=jnp.float32) + local_ref[...]
    projected = over_last(turned_ref[...], group).astype(jnp.bfloat16)
    picked = jnp.dot(projected, sender.astype(jnp.bfloat16), preferred_element_type=jnp.float32)
    scalar = picked[:chans] * filter_ref[:chans, :]
    carried = picked[chans:] * filter_ref[chans:, :]
    parts = [scalar] + [unit_ref[axis : axis + 1, :] * carried for axis in range(3)]
    message = jnp.concatenate([part.astype(jnp.bfloat16) for part in parts], axis=0)
    summed = over_last(message, hit_ref[...]) * message_scale
    square = jnp.zeros((chans, atoms), jnp.float32)
    for component in range(1, 4):
        part = summed[component * chans : (component + 1) * chans]
        square = square + part * part
    invariant = jnp.concatenate([summed[:chans], square], axis=0).astype(jnp.bfloat16)
    hidden = silu(jnp.dot(upward_ref[...], invariant, preferred_element_type=jnp.float32))
    chi = jnp.sum(hidden * read_ref[...], axis=0, keepdims=True)
    chi = jnp.concatenate([chi, jnp.zeros((1, chans - atoms), jnp.float32)], axis=1)
    row = row_ref[...] - pltpu.roll(chi, chi_segment * atoms, 1)
    block_ref[...] = jnp.broadcast_to(row[None], block_ref.shape)
    hidden_ref[...] = hidden


def feature_kernel(packed_ref, hidden_ref, features_ref):
    atoms = features_ref.shape[0]
    old = packed_ref[...].astype(jnp.float32)[:atoms]
    features_ref[...] = (old + hidden_ref[...].T).astype(jnp.bfloat16)


def reciprocal(value):
    rough = pl.reciprocal(value, approx=True)
    return rough * (2.0 - value * rough)


def smeared(scaled):
    decay = jnp.exp2(scaled * scaled * -math.log2(math.e))
    turn = reciprocal(1.0 + 0.3275911 * scaled)
    series = 1.061405429 * turn - 1.453152027
    series = series * turn + 1.421413741
    series = series * turn - 0.284496736
    series = series * turn + 0.254829592
    return 1.0 - series * turn * decay, decay


def charge_kernel(
    place_ref,
    field_ref,
    all_ref,
    charges_ref,
    forces_ref,
    virial_ref,
    matrix_ref,
    side_ref,
    value_ref,
):
    blocks, _, lanes = all_ref.shape
    own = charges_ref.shape[1]
    count = blocks * own
    fit = lanes // own
    segment = lax.broadcasted_iota(jnp.int32, (8, lanes), 1) // own
    tiles = []
    for first in range(0, blocks, fit):
        tile = jnp.zeros((8, lanes), jnp.float32)
        for place in range(fit):
            row = all_ref[(place_ref[0] + first + place) & (blocks - 1)]
            row = pltpu.roll(jnp.broadcast_to(row, (8, lanes)), 0, 1, stride=own, stride_axis=0)
            row = pltpu.roll(row, place * own, 1) if place else row
            tile = jnp.where(segment == place, row, tile)
        tiles.append(tile)
    everyone = jnp.concatenate(tiles, axis=1)
    last = lax.broadcasted_iota(jnp.int32, everyone.shape, 0) == 5
    everyone = everyone + jnp.where(last, field_ref[0] * everyone[2:3], 0.0)
    columns = everyone.T
    diag, rhs = everyone[4:5], everyone[5:6]
    spread_row = 2.0 * everyone[3:4] * everyone[3:4]
    tiles = count // lanes
    rows = 32
    shape = (rows // 8, 8, lanes)
    lane = lax.broadcasted_iota(jnp.int32, shape, 2)
    line = lax.broadcasted_iota(jnp.int32, shape, 0) * 8 + lax.broadcasted_iota(jnp.int32, shape, 1)

    def part(row, tile):
        return row[:, tile * lanes : (tile + 1) * lanes]

    def down(row):
        return [jnp.broadcast_to(part(row, tile), (8, lanes))[None] for tile in range(tiles)]

    def along(column):
        return jnp.broadcast_to(column, (rows, lanes)).reshape(shape)

    def total(value):
        return jnp.sum(value, axis=1, keepdims=True)

    axes = [down(everyone[axis : axis + 1]) for axis in range(3)]
    wide_row, rhs_row = down(spread_row), down(rhs)

    above = [jnp.zeros((8, lanes), jnp.float32) for _ in range(tiles)]
    kept = []
    for start in range(0, count, rows):
        first = start // lanes
        column = columns[start : start + rows]
        place = [along(column[:, axis : axis + 1]) for axis in range(3)]
        wide = along(2.0 * column[:, 3:4] * column[:, 3:4])
        value = along(column[:, 5:6])
        value_ref[start : start + rows, :] = value.reshape(rows, lanes)
        below = jnp.zeros(shape, jnp.float32)
        for tile in range(first, tiles):
            delta = [place[axis] - axes[axis][tile] for axis in range(3)]
            squared = delta[0] * delta[0] + delta[1] * delta[1] + delta[2] * delta[2]
            if tile == first:
                same = lane == line + (start - first * lanes)
                squared = jnp.where(same, 1.0, squared)
            inverse = lax.rsqrt(squared)
            scale = lax.rsqrt(wide + wide_row[tile])
            smear, decay = smeared(squared * inverse * scale)
            kernel = smear * inverse
            if start == 0:
                slope = (two_over_root_pi * scale * decay - kernel) * inverse * inverse
                slope = jnp.where(same, 0.0, slope) if tile == first else slope
                kept.append(([value[: own // 8] for value in delta], slope[: own // 8]))
            if tile == first:
                kernel = jnp.where(same, 0.0, kernel)
            else:
                below = below + kernel * rhs_row[tile]
            above[tile] = above[tile] + jnp.sum(kernel * value, axis=0)
            matrix_ref[start : start + rows, tile * lanes : (tile + 1) * lanes] = kernel.reshape(
                rows, lanes
            )
        if first + 1 < tiles:
            side_ref[start : start + rows, :] = below.reshape(rows, lanes)
    image = []
    for tile in range(tiles):
        value = jnp.sum(above[tile], axis=0, keepdims=True)
        if tile + 1 < tiles:
            below = side_ref[tile * lanes : (tile + 1) * lanes, :].T
            value = value + jnp.sum(below, axis=0, keepdims=True)
        image.append(value)
    image = diag * rhs + jnp.concatenate(image, axis=1)
    across = jnp.broadcast_to(image, (8, count)).T
    norm = total(rhs * rhs)
    alpha = norm / total(rhs * image)
    residual = rhs - alpha * image
    fresh = total(residual * residual)
    again = fresh / norm
    direction = residual + again * rhs
    onto = [jnp.zeros((8, lanes), jnp.float32) for _ in range(tiles)]
    above = [jnp.zeros((8, lanes), jnp.float32) for _ in range(tiles)]
    for start in range(0, count, rows):
        first = start // lanes
        value = (1.0 + again) * value_ref[start : start + rows, :]
        value = value - alpha * jnp.broadcast_to(across[start : start + rows, 0:1], (rows, lanes))
        value = value.reshape(shape)
        for tile in range(first, tiles):
            sums = onto if tile == first else above
            kernel = matrix_ref[start : start + rows, tile * lanes : (tile + 1) * lanes]
            sums[tile] = sums[tile] + jnp.sum(kernel.reshape(shape) * value, axis=0)
    curved = jnp.zeros((8, lanes), jnp.float32)
    for tile in range(tiles):
        curved = curved + (onto[tile] + 2.0 * above[tile]) * part(direction, tile)
    curved = jnp.sum(curved, axis=0, keepdims=True)
    for tile in range(tiles):
        curved = curved + part(diag * direction * direction, tile)
    charges = alpha * rhs + fresh / total(curved) * direction

    sums = [jnp.zeros((own // 8, 8, lanes), jnp.float32) for _ in range(9)]
    charge_row = down(charges)
    for tile, (delta, slope) in enumerate(kept):
        weight = charge_row[tile] * slope
        pulled = [weight * delta[axis] for axis in range(3)]
        terms = pulled + [
            pulled[left] * delta[right]
            for left, right in ((0, 0), (1, 1), (2, 2), (0, 1), (0, 2), (1, 2))
        ]
        sums = [old + term for old, term in zip(sums, terms)]
    table = jnp.zeros((own, lanes), jnp.float32)
    lane = lax.broadcasted_iota(jnp.int32, (own, lanes), 1)
    for place, value in enumerate(sums):
        table = jnp.where(lane == place, total(value.reshape(own, lanes)), table)
    table = table.T
    mine = charges[:, :own]
    charges_ref[...] = mine
    pull = -mine * table[0:3]
    third = lax.broadcasted_iota(jnp.int32, pull.shape, 0) == 2
    forces_ref[...] = pull + jnp.where(third, mine * field_ref[0], 0.0)
    virial_ref[...] = 0.5 * mine * table[3:9]


def kernel_call(kernel, shapes, arguments, scalars=0, far=0, scratch=(), flops=0):
    shapes = tuple(jax.ShapeDtypeStruct(shape, kind) for shape, kind in shapes)
    spaces = [pltpu.SMEM] * scalars + [pltpu.HBM] * far
    spaces = spaces + [pltpu.VMEM] * (len(arguments) - len(spaces))
    arguments = [
        pltpu.with_memory_space_constraint(value, space) if space is pltpu.HBM else value
        for value, space in zip(arguments, spaces)
    ]
    return pl.pallas_call(
        kernel,
        out_shape=shapes,
        in_specs=[pl.BlockSpec(memory_space=space) for space in spaces],
        out_specs=tuple(pl.BlockSpec(memory_space=pltpu.VMEM) for _ in shapes),
        scratch_shapes=list(scratch),
        compiler_params=pltpu.CompilerParams(vmem_limit_bytes=32 * 1024 * 1024),
        cost_estimate=pl.CostEstimate(flops=flops, bytes_accessed=1 << 20, transcendentals=0),
    )(*arguments)


def exchanged(block, axis, step):
    size = lax.axis_size(axis)
    return lax.ppermute(block, axis, [(place, place ^ step) for place in range(size)])


def few_shards(
    features,
    positions,
    species,
    ghost_list,
    edge_recv,
    edge_send,
    edge_vec,
    w_msg,
    w_rad1,
    w_rad2,
    w_up,
    w_out,
    hardness,
    width,
    chi_shift,
    field,
):
    atoms, chans = features.shape
    edges = edge_recv.shape[0]
    rows, lanes = lax.axis_size("row"), lax.axis_size("space")
    space = lax.axis_index("space").astype(jnp.int32)
    (packed,) = kernel_call(
        pack_kernel,
        [((atoms + 16, chans), jnp.bfloat16)],
        (space.reshape(1), features, ghost_list),
        scalars=1,
        far=2,
        scratch=[
            pltpu.VMEM(ghost_list.shape, ghost_list.dtype),
            pltpu.SemaphoreType.DMA((2,)),
        ],
    )
    others = [exchanged(packed, "space", step) for step in range(1, lanes)]
    rest = (edge_vec, w_rad1, w_rad2, edge_send[None], edge_recv[None], w_msg, w_up)
    rest = rest + (species[None], hardness[None], width[None], chi_shift[None], positions)
    rest = rest + (w_out[None],)
    parts = kernel_call(
        edge_kernel,
        [
            ((2 * chans, edges), jnp.float32),
            ((8, edges), jnp.float32),
            ((1, chans), jnp.float32),
            ((chans, edges), jnp.bfloat16),
            ((lanes * atoms, edges), jnp.float32),
            ((atoms, edges), jnp.bfloat16),
            ((2 * chans, chans), jnp.bfloat16),
            ((chans, 2 * chans), jnp.bfloat16),
            ((chans, atoms), jnp.float32),
        ],
        (space.reshape(1), *rest),
        scalars=1,
        far=len(rest),
        scratch=[pltpu.VMEM(value.shape, value.dtype) for value in rest]
        + [pltpu.SemaphoreType.DMA((len(rest),))],
        flops=1 << 28,
    )
    devices = rows * lanes
    hidden, block = kernel_call(
        node_kernel,
        [((chans, atoms), jnp.float32), ((devices, 1, chans), jnp.float32)],
        (packed, *others, *parts),
        flops=1 << 28,
    )
    (new_features,) = kernel_call(
        feature_kernel, [((atoms, chans), jnp.bfloat16)], (packed, hidden), flops=1 << 20
    )
    block = lax.all_to_all(block, everywhere, 0, 0, tiled=True)
    place = lax.axis_index("row").astype(jnp.int32) * lanes + space
    everybody = rows * lanes * atoms
    charges, forces, virial = kernel_call(
        charge_kernel,
        [((count, atoms), jnp.float32) for count in (1, 3, 6)],
        (place.reshape(1), field, block),
        scalars=2,
        scratch=[
            pltpu.VMEM((everybody, everybody), jnp.float32),
            pltpu.VMEM((everybody, chans), jnp.float32),
            pltpu.VMEM((everybody, chans), jnp.float32),
        ],
        flops=1 << 28,
    )
    return (new_features, charges[0], forces, virial)


def solution(mesh):
    small = mesh.shape["space"] == 4 and mesh.shape["row"] == 8
    return jax.shard_map(
        few_shards if small else shards,
        mesh=mesh,
        in_specs=(
            P(("row", "space"), None),
            P(None, ("row", "space")),
            P(("row", "space")),
            P("row", "space", None),
            P(("row", "space")),
            P(("row", "space")),
            P(None, ("row", "space")),
            P(),
            P(),
            P(),
            P(),
            P(),
            P(),
            P(),
            P(),
            P(),
        ),
        out_specs=(
            P(("row", "space"), None),
            P(("row", "space")),
            P(None, ("row", "space")),
            P(None, ("row", "space")),
        ),
        check_vma=False,
    )
```

```python
import math

import jax
import jax.numpy as jnp
from jax import lax
from jax.experimental import pallas as pl
from jax.experimental.pallas import tpu as pltpu
from jax.sharding import PartitionSpec as P

ITERS = 2


cutoff = 6.0
message_scale = 0.125
two_over_root_pi = 2.0 / math.sqrt(math.pi)
inverse_root_pi = 1.0 / math.sqrt(math.pi)
replicate_limit = 1024
everywhere = ("row", "space")


def lookup(species, table):
    result = jnp.zeros(species.shape, jnp.float32)
    for kind in range(table.shape[0]):
        result = result + jnp.where(species == kind, table[kind], 0.0)
    return result


def pair_terms(target, target_labels, source, source_labels):
    delta = target[:3, :, None] - source[:3, None, :]
    squared = jnp.sum(delta * delta, axis=0)
    same = target_labels[:, None] == source_labels[None, :]
    squared = jnp.where(same, 1.0, squared)
    inverse = lax.rsqrt(squared)
    radius = squared * inverse
    spread = target[3][:, None] * target[3][:, None] + source[3][None, :] * source[3][None, :]
    scale = lax.rsqrt(2.0 * spread)
    scaled = radius * scale
    smear = lax.erf(scaled)
    return delta, same, inverse, scale, scaled, smear


def coulomb(target, target_labels, source, source_labels):
    _, same, inverse, _, _, smear = pair_terms(target, target_labels, source, source_labels)
    return jnp.where(same, 0.0, smear * inverse)


def pair_forces(target, target_labels, source, source_labels, source_charge):
    delta, same, inverse, scale, scaled, smear = pair_terms(
        target, target_labels, source, source_labels
    )
    slope = (
        two_over_root_pi * scale * jnp.exp(-scaled * scaled) * inverse - smear * inverse * inverse
    )
    weight = jnp.where(same, 0.0, source_charge[None, :] * slope * inverse)
    first = jnp.sum(weight[None] * delta, axis=2)
    pairs = ((0, 0), (1, 1), (2, 2), (0, 1), (0, 2), (1, 2))
    second = jnp.stack(
        [jnp.sum(weight * delta[left] * delta[right], axis=1) for left, right in pairs]
    )
    return jnp.concatenate([first, second], axis=0)


def edge_terms(receive, sender_rows, vectors, projected, w_rad1, w_rad2, atoms):
    length = jnp.sqrt(jnp.sum(vectors * vectors, axis=0))
    unit = vectors / length
    order = jnp.arange(1, w_rad1.shape[0] + 1, dtype=jnp.int32).astype(jnp.float32)[:, None]
    ratio = length / cutoff
    envelope = (1.0 - ratio * ratio) * (1.0 - ratio * ratio)
    basis = jnp.sin(order * math.pi * ratio) / ratio * envelope
    mixed = lax.dot_general(
        basis, w_rad1, (((0,), (0,)), ((), ())), precision=lax.Precision.HIGHEST
    )
    radial = jax.nn.silu(mixed).astype(jnp.bfloat16)
    filters = jnp.dot(radial, w_rad2, preferred_element_type=jnp.float32)
    picked = jnp.take(projected, sender_rows, axis=0).astype(jnp.float32) * filters
    chans = w_rad1.shape[1]
    scalar = picked[:, :chans]
    carried = picked[:, chans:]
    joined = [
        scalar,
        unit[0][:, None] * carried,
        unit[1][:, None] * carried,
        unit[2][:, None] * carried,
    ]
    message = jnp.concatenate(joined, axis=1).astype(jnp.bfloat16)
    onehot = (jnp.arange(atoms, dtype=jnp.int32)[:, None] == receive[None, :]).astype(jnp.bfloat16)
    return jnp.dot(onehot, message, preferred_element_type=jnp.float32)


def gathered(block, devices):
    copies = jnp.broadcast_to(block[None], (devices,) + block.shape)
    return lax.all_to_all(copies, everywhere, split_axis=0, concat_axis=0, tiled=True)


def shards(
    features,
    positions,
    species,
    ghost_list,
    edge_recv,
    edge_send,
    edge_vec,
    w_msg,
    w_rad1,
    w_rad2,
    w_up,
    w_out,
    hardness,
    width,
    chi_shift,
    field,
):
    atoms = features.shape[0]
    chans = features.shape[1]
    lanes = lax.axis_size("space")
    devices = lanes * lax.axis_size("row")
    everybody = devices * atoms
    me = lax.axis_index("row") * lanes + lax.axis_index("space")
    sigma = lookup(species, width)
    diag = lookup(species, hardness) + inverse_root_pi / sigma
    placed = jnp.concatenate([positions, sigma[None, :], diag[None, :]], axis=0)
    everyone = gathered(placed, devices).transpose(1, 0, 2).reshape(5, everybody)
    lists = ghost_list[0]
    outgoing = jnp.take(features, lists.reshape(-1), axis=0).reshape(lanes, lists.shape[1], chans)
    ghost_rows = jnp.einsum(
        "dkc,cf->dkf",
        lax.all_to_all(outgoing, "space", split_axis=0, concat_axis=0, tiled=True),
        w_msg,
        preferred_element_type=jnp.float32,
    ).astype(jnp.bfloat16)
    own_rows = jnp.dot(features, w_msg, preferred_element_type=jnp.float32).astype(jnp.bfloat16)
    projected = jnp.concatenate([own_rows, ghost_rows.reshape(-1, 2 * chans)], axis=0)
    summed = edge_terms(edge_recv, edge_send, edge_vec, projected, w_rad1, w_rad2, atoms)
    summed = summed * message_scale
    vector_part = summed[:, chans:].reshape(atoms, 3, chans)
    invariant = jnp.concatenate(
        [summed[:, :chans], jnp.sum(vector_part * vector_part, axis=1)], axis=1
    ).astype(jnp.bfloat16)
    hidden = jax.nn.silu(jnp.dot(invariant, w_up, preferred_element_type=jnp.float32))
    new_features = (features.astype(jnp.float32) + hidden).astype(jnp.bfloat16)
    chi = jnp.dot(hidden, w_out, precision=lax.Precision.HIGHEST) + lookup(species, chi_shift)
    own_labels = me * atoms + jnp.arange(atoms, dtype=jnp.int32)
    all_labels = jnp.arange(everybody, dtype=jnp.int32)
    rhs = field[0] * positions[2] - chi

    if everybody <= replicate_limit:
        kernel = coulomb(everyone, all_labels, everyone, all_labels)
        residual = gathered(rhs, devices).reshape(everybody)
        all_charges = conjugate(
            residual, lambda v: everyone[4] * v + jnp.sum(kernel * v[None, :], axis=1), jnp.sum
        )
        charges = lax.dynamic_slice(all_charges, (me * atoms,), (atoms,))
    else:
        kernel = coulomb(placed, own_labels, everyone, all_labels)

        def spread(vector):
            return gathered(vector, devices).reshape(everybody)

        charges = conjugate(
            rhs,
            lambda v: diag * v + jnp.sum(kernel * spread(v)[None, :], axis=1),
            lambda v: lax.psum(jnp.sum(v), everywhere),
        )
        all_charges = spread(charges)
    sums = pair_forces(placed, own_labels, everyone, all_labels, all_charges)
    pull = -charges[None, :] * sums[:3]
    forces = jnp.concatenate([pull[:2], pull[2:] + (charges * field[0])[None, :]], axis=0)
    virial = 0.5 * charges[None, :] * sums[3:]
    return (new_features, charges, forces, virial)


def conjugate(rhs, apply, total):
    charges = jnp.zeros_like(rhs)
    residual = rhs
    direction = rhs
    norm_now = total(residual * residual)
    for step in range(ITERS):
        image = apply(direction)
        alpha = norm_now / total(direction * image)
        charges = charges + alpha * direction
        if step + 1 < ITERS:
            residual = residual - alpha * image
            fresh = total(residual * residual)
            direction = residual + fresh / norm_now * direction
            norm_now = fresh
    return charges


def split3(value):
    first = value.astype(jnp.bfloat16).astype(jnp.float32)
    rest = value - first
    second = rest.astype(jnp.bfloat16).astype(jnp.float32)
    third = (rest - second).astype(jnp.bfloat16).astype(jnp.float32)
    return first, second, third


def over_first(left, right):
    return lax.dot_general(
        left, right, (((0,), (0,)), ((), ())), preferred_element_type=jnp.float32
    )


def over_last(left, right, precision=None):
    return lax.dot_general(
        left,
        right,
        (((1,), (1,)), ((), ())),
        precision=precision,
        preferred_element_type=jnp.float32,
    )


def silu(value):
    return value / (1.0 + jnp.exp(-value))


def silu_half(value):
    return (0.5 * value) * (1.0 + jnp.tanh(0.5 * value))


sine_series = [(-1.0) ** k * math.pi ** (2 * k + 1) / math.factorial(2 * k + 1) for k in range(7)]


def fetched(pairs, semaphores):
    copies = [
        pltpu.make_async_copy(source, target, semaphores.at[place])
        for place, (source, target) in enumerate(pairs)
    ]
    for copy in copies:
        copy.start()
    return copies


chi_segment = 3


def pack_kernel(space_ref, features_ref, lists_ref, packed_ref, held_ref, semaphores):
    atoms, chans = features_ref.shape
    copies = fetched(
        [(lists_ref, held_ref), (features_ref, packed_ref.at[pl.ds(0, atoms)])], semaphores
    )
    copies[0].wait()
    _, lanes, width = held_ref.shape
    rows = []
    for place in range(lanes):
        row = held_ref[0, pl.ds(space_ref[0] ^ place, 1), :].astype(jnp.float32) + place * atoms
        parts = [jnp.zeros((1, width), jnp.float32)] * lanes
        parts[place] = row
        rows.append(jnp.concatenate(parts, axis=1))
    rows.append(jnp.zeros((packed_ref.shape[0] - atoms - lanes, chans), jnp.float32))
    packed_ref[atoms:, :] = jnp.concatenate(rows, axis=0).astype(jnp.bfloat16)
    copies[1].wait()


def edge_kernel(
    space_ref,
    *refs,
):
    count = (len(refs) - 10) // 2
    far, near, semaphores = refs[:count], refs[count + 9 : -1], refs[-1]
    filter_ref, unit_ref, row_ref, slot_ref, local_ref, hit_ref = refs[count : count + 6]
    turned_ref, upward_ref, read_ref = refs[count + 6 : count + 9]
    vec_ref, first_ref, second_ref, send_ref, recv_ref, project_ref, update_ref = near[:7]
    species_ref, hardness_ref, width_ref, shift_ref, positions_ref, out_ref = near[7:]
    copies = fetched(list(zip(far, near)), semaphores)
    for copy in copies[:3]:
        copy.wait()
    edges = vec_ref.shape[1]
    orders = first_ref.shape[0]
    vec = vec_ref[...]
    east, north, up = vec[0:1], vec[1:2], vec[2:3]
    squared = east * east + north * north + up * up
    inverse = lax.rsqrt(squared)
    unit_ref[0:3, :] = vec * inverse
    ratio = squared * inverse * (1.0 / cutoff)
    envelope = (1.0 - ratio * ratio) * (1.0 - ratio * ratio) * (cutoff * inverse)
    order = lax.broadcasted_iota(jnp.int32, (orders, edges), 0).astype(jnp.float32) + 1.0
    turns = order * ratio
    whole = jnp.floor(turns + 0.5)
    part = turns - whole
    sign = 1.0 - 2.0 * (whole - 2.0 * jnp.floor(whole * 0.5))
    series = jnp.full_like(part, sine_series[-1])
    for coefficient in sine_series[-2::-1]:
        series = series * (part * part) + coefficient
    basis = series * part * (sign * envelope)
    b1, b2, b3 = split3(basis)
    w1, w2, w3 = split3(first_ref[...])
    mixed = over_first(
        jnp.concatenate([w1, w1, w2, w2, w1, w3], axis=0).astype(jnp.bfloat16),
        jnp.concatenate([b1, b2, b1, b2, b3, b1], axis=0).astype(jnp.bfloat16),
    )
    radial = silu_half(mixed).astype(jnp.bfloat16)
    filter_ref[...] = over_first(second_ref[...], radial)
    for copy in copies[3:]:
        copy.wait()
    species = species_ref[...]

    def table(ref):
        result = jnp.zeros(species.shape, jnp.float32)
        for kind in range(ref.shape[1]):
            result = result + jnp.where(species == kind, ref[:, kind : kind + 1], 0.0)
        return result

    positions = positions_ref[...]
    sigma = table(width_ref)
    atoms = species.shape[1]
    chans = row_ref.shape[1]
    diag = table(hardness_ref) + inverse_root_pi / sigma
    blank = jnp.zeros((2, atoms), jnp.float32)
    rows = [positions[0:1], blank, -table(shift_ref), diag, sigma, positions[2:3], positions[1:2]]
    block = jnp.concatenate(
        [jnp.concatenate(rows, axis=0), jnp.zeros((8, chans - atoms), jnp.float32)], axis=1
    )
    block = pltpu.roll(block, 0, 1, stride=atoms, stride_axis=0)
    row_ref[...] = jnp.sum(block, axis=0, keepdims=True)
    lanes = local_ref.shape[0] // atoms
    slots = chans // lanes
    send = send_ref[...]
    own = send < atoms
    slot = jnp.where(own, -1, (send - atoms) ^ (space_ref[0] * slots))
    local = jnp.where(own, send, -1)

    def chosen(ref, index):
        hit = lax.broadcasted_iota(jnp.int32, ref.shape, 0) == index
        ref[...] = jnp.where(hit, 1.0, 0.0).astype(ref.dtype)

    chosen(slot_ref, slot)
    chosen(local_ref, local)
    chosen(hit_ref, recv_ref[...])
    turned_ref[...] = project_ref[...].astype(jnp.float32).T.astype(jnp.bfloat16)
    upward_ref[...] = update_ref[...].astype(jnp.float32).T.astype(jnp.bfloat16)
    read_ref[...] = jnp.broadcast_to(out_ref[...], (atoms, chans)).T


def node_kernel(
    own_ref,
    near_ref,
    side_ref,
    far_ref,
    filter_ref,
    unit_ref,
    row_ref,
    slot_ref,
    local_ref,
    hit_ref,
    turned_ref,
    upward_ref,
    read_ref,
    hidden_ref,
    block_ref,
):
    chans, atoms = hidden_ref.shape
    packed = (own_ref, near_ref, side_ref, far_ref)
    group = jnp.concatenate([ref[:atoms, :] for ref in packed], axis=0)
    chosen = jnp.zeros((1, chans), jnp.float32)
    for place, ref in enumerate(packed):
        tail = ref[atoms:, :].astype(jnp.float32)
        chosen = chosen + tail[place : place + 1]
    fill = jnp.where(
        lax.broadcasted_iota(jnp.int32, (len(packed) * atoms, chans), 0)
        == chosen.astype(jnp.int32),
        1.0,
        0.0,
    ).astype(jnp.bfloat16)
    sender = jnp.dot(fill, slot_ref[...], preferred_element_type=jnp.float32) + local_ref[...]
    projected = over_last(turned_ref[...], group).astype(jnp.bfloat16)
    picked = jnp.dot(projected, sender.astype(jnp.bfloat16), preferred_element_type=jnp.float32)
    scalar = picked[:chans] * filter_ref[:chans, :]
    carried = picked[chans:] * filter_ref[chans:, :]
    parts = [scalar] + [unit_ref[axis : axis + 1, :] * carried for axis in range(3)]
    message = jnp.concatenate([part.astype(jnp.bfloat16) for part in parts], axis=0)
    summed = over_last(message, hit_ref[...]) * message_scale
    square = jnp.zeros((chans, atoms), jnp.float32)
    for component in range(1, 4):
        part = summed[component * chans : (component + 1) * chans]
        square = square + part * part
    invariant = jnp.concatenate([summed[:chans], square], axis=0).astype(jnp.bfloat16)
    hidden = silu(jnp.dot(upward_ref[...], invariant, preferred_element_type=jnp.float32))
    chi = jnp.sum(hidden * read_ref[...], axis=0, keepdims=True)
    chi = jnp.concatenate([chi, jnp.zeros((1, chans - atoms), jnp.float32)], axis=1)
    row = row_ref[...] - pltpu.roll(chi, chi_segment * atoms, 1)
    block_ref[...] = jnp.broadcast_to(row[None], block_ref.shape)
    hidden_ref[...] = hidden


def feature_kernel(packed_ref, hidden_ref, features_ref):
    atoms = features_ref.shape[0]
    old = packed_ref[...].astype(jnp.float32)[:atoms]
    features_ref[...] = (old + hidden_ref[...].T).astype(jnp.bfloat16)


def reciprocal(value):
    rough = pl.reciprocal(value, approx=True)
    return rough * (2.0 - value * rough)


def smeared(scaled):
    decay = jnp.exp2(scaled * scaled * -math.log2(math.e))
    turn = reciprocal(1.0 + 0.3275911 * scaled)
    series = 1.061405429 * turn - 1.453152027
    series = series * turn + 1.421413741
    series = series * turn - 0.284496736
    series = series * turn + 0.254829592
    return 1.0 - series * turn * decay, decay


def charge_kernel(
    place_ref,
    field_ref,
    all_ref,
    charges_ref,
    forces_ref,
    virial_ref,
    matrix_ref,
    side_ref,
    value_ref,
):
    blocks, _, lanes = all_ref.shape
    own = charges_ref.shape[1]
    count = blocks * own
    fit = lanes // own
    segment = lax.broadcasted_iota(jnp.int32, (8, lanes), 1) // own
    tiles = []
    for first in range(0, blocks, fit):
        tile = jnp.zeros((8, lanes), jnp.float32)
        for place in range(fit):
            row = all_ref[(place_ref[0] + first + place) & (blocks - 1)]
            row = pltpu.roll(jnp.broadcast_to(row, (8, lanes)), 0, 1, stride=own, stride_axis=0)
            row = pltpu.roll(row, place * own, 1) if place else row
            tile = jnp.where(segment == place, row, tile)
        tiles.append(tile)
    everyone = jnp.concatenate(tiles, axis=1)
    last = lax.broadcasted_iota(jnp.int32, everyone.shape, 0) == 5
    everyone = everyone + jnp.where(last, field_ref[0] * everyone[2:3], 0.0)
    columns = everyone.T
    diag, rhs = everyone[4:5], everyone[5:6]
    spread_row = 2.0 * everyone[3:4] * everyone[3:4]
    tiles = count // lanes
    rows = 32
    shape = (rows // 8, 8, lanes)
    lane = lax.broadcasted_iota(jnp.int32, shape, 2)
    line = lax.broadcasted_iota(jnp.int32, shape, 0) * 8 + lax.broadcasted_iota(jnp.int32, shape, 1)

    def part(row, tile):
        return row[:, tile * lanes : (tile + 1) * lanes]

    def down(row, tile):
        return jnp.broadcast_to(part(row, tile), (8, lanes))[None]

    def along(column):
        return jnp.broadcast_to(column, (rows, lanes)).reshape(shape)

    def total(value):
        return jnp.sum(value, axis=1, keepdims=True)

    def held(ref, start):
        return ref[start : start + rows, :].reshape(shape)

    def hold(ref, start, value):
        ref[start : start + rows, :] = value.reshape(rows, lanes)

    kept, image, summed = [], [], []
    for tile in range(tiles):
        axes = [down(everyone[axis : axis + 1], tile) for axis in range(3)]
        wide_row, rhs_row = down(spread_row, tile), down(rhs, tile)
        above = jnp.zeros((8, lanes), jnp.float32)
        for start in range(0, (tile + 1) * lanes, rows):
            onto = start >= tile * lanes
            if onto:
                column = columns[start : start + rows]
                values = [along(column[:, axis : axis + 1]) for axis in range(3)]
                values.append(along(2.0 * column[:, 3:4] * column[:, 3:4]))
                values.append(along(column[:, 5:6]))
                for place, value in enumerate(values):
                    hold(value_ref.at[place], start, value)
            else:
                values = [held(value_ref.at[place], start) for place in range(5)]
            delta = [values[axis] - axes[axis] for axis in range(3)]
            squared = delta[0] * delta[0] + delta[1] * delta[1] + delta[2] * delta[2]
            if onto:
                same = lane == line + (start - tile * lanes)
                squared = jnp.where(same, 1.0, squared)
            inverse = lax.rsqrt(squared)
            scale = lax.rsqrt(values[3] + wide_row)
            smear, decay = smeared(squared * inverse * scale)
            kernel = smear * inverse
            if start == 0:
                few = own // 8
                slope = two_over_root_pi * scale[:few] * decay[:few] - kernel[:few]
                slope = slope * inverse[:few] * inverse[:few]
                slope = jnp.where(same[:few], 0.0, slope) if onto else slope
                kept.append(([value[:few] for value in delta], slope))
            if onto:
                kernel = jnp.where(same, 0.0, kernel)
            else:
                below = kernel * rhs_row
                if start // lanes + 1 < tile:
                    below = below + held(side_ref, start)
                hold(side_ref, start, below)
            above = above + jnp.sum(kernel * values[4], axis=0)
            hold(matrix_ref.at[tile], start, kernel)
        image.append(jnp.sum(above, axis=0, keepdims=True))
    for tile in range(tiles - 1):
        below = side_ref[tile * lanes : (tile + 1) * lanes, :].T
        image[tile] = image[tile] + jnp.sum(below, axis=0, keepdims=True)
    image = diag * rhs + jnp.concatenate(image, axis=1)
    across = jnp.broadcast_to(image, (8, count)).T
    norm = total(rhs * rhs)
    alpha = norm / total(rhs * image)
    residual = rhs - alpha * image
    fresh = total(residual * residual)
    again = fresh / norm
    direction = residual + again * rhs
    curved = jnp.zeros((8, lanes), jnp.float32)
    for tile in range(tiles):
        sums = [jnp.zeros((8, lanes), jnp.float32) for _ in range(2)]
        for start in range(0, (tile + 1) * lanes, rows):
            onto = start >= tile * lanes
            if onto:
                value = (1.0 + again) * held(value_ref.at[4], start)
                value = value - alpha * along(across[start : start + rows, 0:1])
                hold(value_ref.at[0], start, value)
            else:
                value = held(value_ref.at[0], start)
            add = jnp.sum(held(matrix_ref.at[tile], start) * value, axis=0)
            sums[onto] = sums[onto] + add
        curved = curved + (2.0 * sums[0] + sums[1]) * part(direction, tile)
    curved = jnp.sum(curved, axis=0, keepdims=True)
    for tile in range(tiles):
        curved = curved + part(diag * direction * direction, tile)
    charges = alpha * rhs + fresh / total(curved) * direction

    sums = [jnp.zeros((own // 8, 8, lanes), jnp.float32) for _ in range(9)]
    for tile, (delta, slope) in enumerate(kept):
        weight = down(charges, tile) * slope
        pulled = [weight * delta[axis] for axis in range(3)]
        terms = pulled + [
            pulled[left] * delta[right]
            for left, right in ((0, 0), (1, 1), (2, 2), (0, 1), (0, 2), (1, 2))
        ]
        sums = [old + term for old, term in zip(sums, terms)]
    table = jnp.zeros((own, lanes), jnp.float32)
    lane = lax.broadcasted_iota(jnp.int32, (own, lanes), 1)
    for place, value in enumerate(sums):
        table = jnp.where(lane == place, total(value.reshape(own, lanes)), table)
    table = table.T
    mine = charges[:, :own]
    charges_ref[...] = mine
    pull = -mine * table[0:3]
    third = lax.broadcasted_iota(jnp.int32, pull.shape, 0) == 2
    forces_ref[...] = pull + jnp.where(third, mine * field_ref[0], 0.0)
    virial_ref[...] = 0.5 * mine * table[3:9]


def kernel_call(kernel, shapes, arguments, scalars=0, far=0, scratch=(), flops=0):
    shapes = tuple(jax.ShapeDtypeStruct(shape, kind) for shape, kind in shapes)
    spaces = [pltpu.SMEM] * scalars + [pltpu.HBM] * far
    spaces = spaces + [pltpu.VMEM] * (len(arguments) - len(spaces))
    arguments = [
        pltpu.with_memory_space_constraint(value, space) if space is pltpu.HBM else value
        for value, space in zip(arguments, spaces)
    ]
    return pl.pallas_call(
        kernel,
        out_shape=shapes,
        in_specs=[pl.BlockSpec(memory_space=space) for space in spaces],
        out_specs=tuple(pl.BlockSpec(memory_space=pltpu.VMEM) for _ in shapes),
        scratch_shapes=list(scratch),
        compiler_params=pltpu.CompilerParams(vmem_limit_bytes=32 * 1024 * 1024),
        cost_estimate=pl.CostEstimate(flops=flops, bytes_accessed=1 << 20, transcendentals=0),
    )(*arguments)


def exchanged(block, axis, step):
    size = lax.axis_size(axis)
    return lax.ppermute(block, axis, [(place, place ^ step) for place in range(size)])


def few_shards(
    features,
    positions,
    species,
    ghost_list,
    edge_recv,
    edge_send,
    edge_vec,
    w_msg,
    w_rad1,
    w_rad2,
    w_up,
    w_out,
    hardness,
    width,
    chi_shift,
    field,
):
    atoms, chans = features.shape
    edges = edge_recv.shape[0]
    rows, lanes = lax.axis_size("row"), lax.axis_size("space")
    space = lax.axis_index("space").astype(jnp.int32)
    (packed,) = kernel_call(
        pack_kernel,
        [((atoms + 16, chans), jnp.bfloat16)],
        (space.reshape(1), features, ghost_list),
        scalars=1,
        far=2,
        scratch=[
            pltpu.VMEM(ghost_list.shape, ghost_list.dtype),
            pltpu.SemaphoreType.DMA((2,)),
        ],
    )
    others = [exchanged(packed, "space", step) for step in range(1, lanes)]
    rest = (edge_vec, w_rad1, w_rad2, edge_send[None], edge_recv[None], w_msg, w_up)
    rest = rest + (species[None], hardness[None], width[None], chi_shift[None], positions)
    rest = rest + (w_out[None],)
    parts = kernel_call(
        edge_kernel,
        [
            ((2 * chans, edges), jnp.float32),
            ((8, edges), jnp.float32),
            ((1, chans), jnp.float32),
            ((chans, edges), jnp.bfloat16),
            ((lanes * atoms, edges), jnp.float32),
            ((atoms, edges), jnp.bfloat16),
            ((2 * chans, chans), jnp.bfloat16),
            ((chans, 2 * chans), jnp.bfloat16),
            ((chans, atoms), jnp.float32),
        ],
        (space.reshape(1), *rest),
        scalars=1,
        far=len(rest),
        scratch=[pltpu.VMEM(value.shape, value.dtype) for value in rest]
        + [pltpu.SemaphoreType.DMA((len(rest),))],
        flops=1 << 28,
    )
    devices = rows * lanes
    hidden, block = kernel_call(
        node_kernel,
        [((chans, atoms), jnp.float32), ((devices, 1, chans), jnp.float32)],
        (packed, *others, *parts),
        flops=1 << 28,
    )
    (new_features,) = kernel_call(
        feature_kernel, [((atoms, chans), jnp.bfloat16)], (packed, hidden), flops=1 << 20
    )
    block = lax.all_to_all(block, everywhere, 0, 0, tiled=True)
    place = lax.axis_index("row").astype(jnp.int32) * lanes + space
    everybody = rows * lanes * atoms
    charges, forces, virial = kernel_call(
        charge_kernel,
        [((count, atoms), jnp.float32) for count in (1, 3, 6)],
        (place.reshape(1), field, block),
        scalars=2,
        scratch=[
            pltpu.VMEM((everybody // chans, everybody, chans), jnp.float32),
            pltpu.VMEM((everybody, chans), jnp.float32),
            pltpu.VMEM((5, everybody, chans), jnp.float32),
        ],
        flops=1 << 28,
    )
    return (new_features, charges[0], forces, virial)


def solution(mesh):
    small = mesh.shape["space"] == 4 and mesh.shape["row"] == 8
    return jax.shard_map(
        few_shards if small else shards,
        mesh=mesh,
        in_specs=(
            P(("row", "space"), None),
            P(None, ("row", "space")),
            P(("row", "space")),
            P("row", "space", None),
            P(("row", "space")),
            P(("row", "space")),
            P(None, ("row", "space")),
            P(),
            P(),
            P(),
            P(),
            P(),
            P(),
            P(),
            P(),
            P(),
        ),
        out_specs=(
            P(("row", "space"), None),
            P(("row", "space")),
            P(None, ("row", "space")),
            P(None, ("row", "space")),
        ),
        check_vma=False,
    )
```

```python
import math

import jax
import jax.numpy as jnp
from jax import lax
from jax.experimental import pallas as pl
from jax.experimental.pallas import tpu as pltpu
from jax.sharding import PartitionSpec as P

ITERS = 2


cutoff = 6.0
message_scale = 0.125
two_over_root_pi = 2.0 / math.sqrt(math.pi)
inverse_root_pi = 1.0 / math.sqrt(math.pi)
replicate_limit = 1024
everywhere = ("row", "space")


def lookup(species, table):
    result = jnp.zeros(species.shape, jnp.float32)
    for kind in range(table.shape[0]):
        result = result + jnp.where(species == kind, table[kind], 0.0)
    return result


def pair_terms(target, target_labels, source, source_labels):
    delta = target[:3, :, None] - source[:3, None, :]
    squared = jnp.sum(delta * delta, axis=0)
    same = target_labels[:, None] == source_labels[None, :]
    squared = jnp.where(same, 1.0, squared)
    inverse = lax.rsqrt(squared)
    radius = squared * inverse
    spread = target[3][:, None] * target[3][:, None] + source[3][None, :] * source[3][None, :]
    scale = lax.rsqrt(2.0 * spread)
    scaled = radius * scale
    smear = lax.erf(scaled)
    return delta, same, inverse, scale, scaled, smear


def coulomb(target, target_labels, source, source_labels):
    _, same, inverse, _, _, smear = pair_terms(target, target_labels, source, source_labels)
    return jnp.where(same, 0.0, smear * inverse)


def pair_forces(target, target_labels, source, source_labels, source_charge):
    delta, same, inverse, scale, scaled, smear = pair_terms(
        target, target_labels, source, source_labels
    )
    slope = (
        two_over_root_pi * scale * jnp.exp(-scaled * scaled) * inverse - smear * inverse * inverse
    )
    weight = jnp.where(same, 0.0, source_charge[None, :] * slope * inverse)
    first = jnp.sum(weight[None] * delta, axis=2)
    pairs = ((0, 0), (1, 1), (2, 2), (0, 1), (0, 2), (1, 2))
    second = jnp.stack(
        [jnp.sum(weight * delta[left] * delta[right], axis=1) for left, right in pairs]
    )
    return jnp.concatenate([first, second], axis=0)


def edge_terms(receive, sender_rows, vectors, projected, w_rad1, w_rad2, atoms):
    length = jnp.sqrt(jnp.sum(vectors * vectors, axis=0))
    unit = vectors / length
    order = jnp.arange(1, w_rad1.shape[0] + 1, dtype=jnp.int32).astype(jnp.float32)[:, None]
    ratio = length / cutoff
    envelope = (1.0 - ratio * ratio) * (1.0 - ratio * ratio)
    basis = jnp.sin(order * math.pi * ratio) / ratio * envelope
    mixed = lax.dot_general(
        basis, w_rad1, (((0,), (0,)), ((), ())), precision=lax.Precision.HIGHEST
    )
    radial = jax.nn.silu(mixed).astype(jnp.bfloat16)
    filters = jnp.dot(radial, w_rad2, preferred_element_type=jnp.float32)
    picked = jnp.take(projected, sender_rows, axis=0).astype(jnp.float32) * filters
    chans = w_rad1.shape[1]
    scalar = picked[:, :chans]
    carried = picked[:, chans:]
    joined = [
        scalar,
        unit[0][:, None] * carried,
        unit[1][:, None] * carried,
        unit[2][:, None] * carried,
    ]
    message = jnp.concatenate(joined, axis=1).astype(jnp.bfloat16)
    onehot = (jnp.arange(atoms, dtype=jnp.int32)[:, None] == receive[None, :]).astype(jnp.bfloat16)
    return jnp.dot(onehot, message, preferred_element_type=jnp.float32)


def gathered(block, devices):
    copies = jnp.broadcast_to(block[None], (devices,) + block.shape)
    return lax.all_to_all(copies, everywhere, split_axis=0, concat_axis=0, tiled=True)


def shards(
    features,
    positions,
    species,
    ghost_list,
    edge_recv,
    edge_send,
    edge_vec,
    w_msg,
    w_rad1,
    w_rad2,
    w_up,
    w_out,
    hardness,
    width,
    chi_shift,
    field,
):
    atoms = features.shape[0]
    chans = features.shape[1]
    lanes = lax.axis_size("space")
    devices = lanes * lax.axis_size("row")
    everybody = devices * atoms
    me = lax.axis_index("row") * lanes + lax.axis_index("space")
    sigma = lookup(species, width)
    diag = lookup(species, hardness) + inverse_root_pi / sigma
    placed = jnp.concatenate([positions, sigma[None, :], diag[None, :]], axis=0)
    everyone = gathered(placed, devices).transpose(1, 0, 2).reshape(5, everybody)
    lists = ghost_list[0]
    outgoing = jnp.take(features, lists.reshape(-1), axis=0).reshape(lanes, lists.shape[1], chans)
    ghost_rows = jnp.einsum(
        "dkc,cf->dkf",
        lax.all_to_all(outgoing, "space", split_axis=0, concat_axis=0, tiled=True),
        w_msg,
        preferred_element_type=jnp.float32,
    ).astype(jnp.bfloat16)
    own_rows = jnp.dot(features, w_msg, preferred_element_type=jnp.float32).astype(jnp.bfloat16)
    projected = jnp.concatenate([own_rows, ghost_rows.reshape(-1, 2 * chans)], axis=0)
    summed = edge_terms(edge_recv, edge_send, edge_vec, projected, w_rad1, w_rad2, atoms)
    summed = summed * message_scale
    vector_part = summed[:, chans:].reshape(atoms, 3, chans)
    invariant = jnp.concatenate(
        [summed[:, :chans], jnp.sum(vector_part * vector_part, axis=1)], axis=1
    ).astype(jnp.bfloat16)
    hidden = jax.nn.silu(jnp.dot(invariant, w_up, preferred_element_type=jnp.float32))
    new_features = (features.astype(jnp.float32) + hidden).astype(jnp.bfloat16)
    chi = jnp.dot(hidden, w_out, precision=lax.Precision.HIGHEST) + lookup(species, chi_shift)
    own_labels = me * atoms + jnp.arange(atoms, dtype=jnp.int32)
    all_labels = jnp.arange(everybody, dtype=jnp.int32)
    rhs = field[0] * positions[2] - chi

    if everybody <= replicate_limit:
        kernel = coulomb(everyone, all_labels, everyone, all_labels)
        residual = gathered(rhs, devices).reshape(everybody)
        all_charges = conjugate(
            residual, lambda v: everyone[4] * v + jnp.sum(kernel * v[None, :], axis=1), jnp.sum
        )
        charges = lax.dynamic_slice(all_charges, (me * atoms,), (atoms,))
    else:
        kernel = coulomb(placed, own_labels, everyone, all_labels)

        def spread(vector):
            return gathered(vector, devices).reshape(everybody)

        charges = conjugate(
            rhs,
            lambda v: diag * v + jnp.sum(kernel * spread(v)[None, :], axis=1),
            lambda v: lax.psum(jnp.sum(v), everywhere),
        )
        all_charges = spread(charges)
    sums = pair_forces(placed, own_labels, everyone, all_labels, all_charges)
    pull = -charges[None, :] * sums[:3]
    forces = jnp.concatenate([pull[:2], pull[2:] + (charges * field[0])[None, :]], axis=0)
    virial = 0.5 * charges[None, :] * sums[3:]
    return (new_features, charges, forces, virial)


def conjugate(rhs, apply, total):
    charges = jnp.zeros_like(rhs)
    residual = rhs
    direction = rhs
    norm_now = total(residual * residual)
    for step in range(ITERS):
        image = apply(direction)
        alpha = norm_now / total(direction * image)
        charges = charges + alpha * direction
        if step + 1 < ITERS:
            residual = residual - alpha * image
            fresh = total(residual * residual)
            direction = residual + fresh / norm_now * direction
            norm_now = fresh
    return charges


def split3(value):
    first = value.astype(jnp.bfloat16).astype(jnp.float32)
    rest = value - first
    second = rest.astype(jnp.bfloat16).astype(jnp.float32)
    third = (rest - second).astype(jnp.bfloat16).astype(jnp.float32)
    return first, second, third


def over_first(left, right):
    return lax.dot_general(
        left, right, (((0,), (0,)), ((), ())), preferred_element_type=jnp.float32
    )


def over_last(left, right, precision=None):
    return lax.dot_general(
        left,
        right,
        (((1,), (1,)), ((), ())),
        precision=precision,
        preferred_element_type=jnp.float32,
    )


def silu(value):
    return value / (1.0 + jnp.exp(-value))


def silu_half(value):
    return (0.5 * value) * (1.0 + jnp.tanh(0.5 * value))


sine_series = [(-1.0) ** k * math.pi ** (2 * k + 1) / math.factorial(2 * k + 1) for k in range(7)]


def fetched(pairs, semaphores):
    copies = [
        pltpu.make_async_copy(source, target, semaphores.at[place])
        for place, (source, target) in enumerate(pairs)
    ]
    for copy in copies:
        copy.start()
    return copies


chi_segment = 3


def pack_kernel(space_ref, features_ref, lists_ref, packed_ref, held_ref, semaphores):
    atoms, chans = features_ref.shape
    copies = fetched(
        [(lists_ref, held_ref), (features_ref, packed_ref.at[pl.ds(0, atoms)])], semaphores
    )
    copies[0].wait()
    _, lanes, width = held_ref.shape
    rows = []
    for place in range(lanes):
        row = held_ref[0, pl.ds(space_ref[0] ^ place, 1), :].astype(jnp.float32) + place * atoms
        parts = [jnp.zeros((1, width), jnp.float32)] * lanes
        parts[place] = row
        rows.append(jnp.concatenate(parts, axis=1))
    rows.append(jnp.zeros((packed_ref.shape[0] - atoms - lanes, chans), jnp.float32))
    packed_ref[atoms:, :] = jnp.concatenate(rows, axis=0).astype(jnp.bfloat16)
    copies[1].wait()


def edge_kernel(
    space_ref,
    *refs,
):
    count = (len(refs) - 12) // 2
    far, near, semaphores = refs[:count], refs[count + 11 : -1], refs[-1]
    vec_ref, first_ref, filter_ref, unit_ref, row_ref, slot_ref = refs[count : count + 6]
    local_ref, hit_ref, turned_ref, upward_ref, read_ref = refs[count + 6 : count + 11]
    second_ref, send_ref, recv_ref, project_ref, update_ref = near[:5]
    species_ref, hardness_ref, width_ref, shift_ref, positions_ref, out_ref = near[5:]
    copies = fetched(list(zip(far, near)), semaphores)
    edges = vec_ref.shape[1]
    orders = first_ref.shape[0]
    vec = vec_ref[...]
    east, north, up = vec[0:1], vec[1:2], vec[2:3]
    squared = east * east + north * north + up * up
    inverse = lax.rsqrt(squared)
    unit_ref[0:3, :] = vec * inverse
    ratio = squared * inverse * (1.0 / cutoff)
    envelope = (1.0 - ratio * ratio) * (1.0 - ratio * ratio) * (cutoff * inverse)
    order = lax.broadcasted_iota(jnp.int32, (orders, edges), 0).astype(jnp.float32) + 1.0
    turns = order * ratio
    whole = jnp.floor(turns + 0.5)
    part = turns - whole
    sign = 1.0 - 2.0 * (whole - 2.0 * jnp.floor(whole * 0.5))
    series = jnp.full_like(part, sine_series[-1])
    for coefficient in sine_series[-2::-1]:
        series = series * (part * part) + coefficient
    basis = series * part * (sign * envelope)
    b1, b2, b3 = split3(basis)
    w1, w2, w3 = split3(first_ref[...])
    mixed = over_first(
        jnp.concatenate([w1, w1, w2, w2, w1, w3], axis=0).astype(jnp.bfloat16),
        jnp.concatenate([b1, b2, b1, b2, b3, b1], axis=0).astype(jnp.bfloat16),
    )
    radial = silu_half(mixed).astype(jnp.bfloat16)
    copies[0].wait()
    filter_ref[...] = over_first(second_ref[...], radial)
    for copy in copies[1:]:
        copy.wait()
    species = species_ref[...]

    def table(ref):
        result = jnp.zeros(species.shape, jnp.float32)
        for kind in range(ref.shape[1]):
            result = result + jnp.where(species == kind, ref[:, kind : kind + 1], 0.0)
        return result

    positions = positions_ref[...]
    sigma = table(width_ref)
    atoms = species.shape[1]
    chans = row_ref.shape[1]
    diag = table(hardness_ref) + inverse_root_pi / sigma
    blank = jnp.zeros((2, atoms), jnp.float32)
    rows = [positions[0:1], blank, -table(shift_ref), diag, sigma, positions[2:3], positions[1:2]]
    block = jnp.concatenate(
        [jnp.concatenate(rows, axis=0), jnp.zeros((8, chans - atoms), jnp.float32)], axis=1
    )
    block = pltpu.roll(block, 0, 1, stride=atoms, stride_axis=0)
    row_ref[...] = jnp.sum(block, axis=0, keepdims=True)
    lanes = local_ref.shape[0] // atoms
    slots = chans // lanes
    send = send_ref[...]
    own = send < atoms
    slot = jnp.where(own, -1, (send - atoms) ^ (space_ref[0] * slots))
    local = jnp.where(own, send, -1)

    def chosen(ref, index):
        hit = lax.broadcasted_iota(jnp.int32, ref.shape, 0) == index
        ref[...] = jnp.where(hit, 1.0, 0.0).astype(ref.dtype)

    chosen(slot_ref, slot)
    chosen(local_ref, local)
    chosen(hit_ref, recv_ref[...])
    turned_ref[...] = project_ref[...].astype(jnp.float32).T.astype(jnp.bfloat16)
    upward_ref[...] = update_ref[...].astype(jnp.float32).T.astype(jnp.bfloat16)
    read_ref[...] = jnp.broadcast_to(out_ref[...], (atoms, chans)).T


def node_kernel(
    own_ref,
    near_ref,
    side_ref,
    far_ref,
    filter_ref,
    unit_ref,
    row_ref,
    slot_ref,
    local_ref,
    hit_ref,
    turned_ref,
    upward_ref,
    read_ref,
    hidden_ref,
    block_ref,
):
    chans, atoms = hidden_ref.shape
    packed = (own_ref, near_ref, side_ref, far_ref)
    group = jnp.concatenate([ref[:atoms, :] for ref in packed], axis=0)
    chosen = jnp.zeros((1, chans), jnp.float32)
    for place, ref in enumerate(packed):
        tail = ref[atoms:, :].astype(jnp.float32)
        chosen = chosen + tail[place : place + 1]
    fill = jnp.where(
        lax.broadcasted_iota(jnp.int32, (len(packed) * atoms, chans), 0)
        == chosen.astype(jnp.int32),
        1.0,
        0.0,
    ).astype(jnp.bfloat16)
    sender = jnp.dot(fill, slot_ref[...], preferred_element_type=jnp.float32) + local_ref[...]
    projected = over_last(turned_ref[...], group).astype(jnp.bfloat16)
    picked = jnp.dot(projected, sender.astype(jnp.bfloat16), preferred_element_type=jnp.float32)
    scalar = picked[:chans] * filter_ref[:chans, :]
    carried = picked[chans:] * filter_ref[chans:, :]
    parts = [scalar] + [unit_ref[axis : axis + 1, :] * carried for axis in range(3)]
    message = jnp.concatenate([part.astype(jnp.bfloat16) for part in parts], axis=0)
    summed = over_last(message, hit_ref[...]) * message_scale
    square = jnp.zeros((chans, atoms), jnp.float32)
    for component in range(1, 4):
        part = summed[component * chans : (component + 1) * chans]
        square = square + part * part
    invariant = jnp.concatenate([summed[:chans], square], axis=0).astype(jnp.bfloat16)
    hidden = silu(jnp.dot(upward_ref[...], invariant, preferred_element_type=jnp.float32))
    chi = jnp.sum(hidden * read_ref[...], axis=0, keepdims=True)
    chi = jnp.concatenate([chi, jnp.zeros((1, chans - atoms), jnp.float32)], axis=1)
    row = row_ref[...] - pltpu.roll(chi, chi_segment * atoms, 1)
    block_ref[...] = jnp.broadcast_to(row[None], block_ref.shape)
    hidden_ref[...] = hidden


def feature_kernel(packed_ref, hidden_ref, features_ref):
    atoms = features_ref.shape[0]
    old = packed_ref[...].astype(jnp.float32)[:atoms]
    features_ref[...] = (old + hidden_ref[...].T).astype(jnp.bfloat16)


def reciprocal(value):
    rough = pl.reciprocal(value, approx=True)
    return rough * (2.0 - value * rough)


def smeared(scaled):
    decay = jnp.exp2(scaled * scaled * -math.log2(math.e))
    turn = reciprocal(1.0 + 0.3275911 * scaled)
    series = 1.061405429 * turn - 1.453152027
    series = series * turn + 1.421413741
    series = series * turn - 0.284496736
    series = series * turn + 0.254829592
    return 1.0 - series * turn * decay, decay


def charge_kernel(
    place_ref,
    field_ref,
    all_ref,
    charges_ref,
    forces_ref,
    virial_ref,
    matrix_ref,
    side_ref,
    value_ref,
):
    blocks, _, lanes = all_ref.shape
    own = charges_ref.shape[1]
    count = blocks * own
    fit = lanes // own
    segment = lax.broadcasted_iota(jnp.int32, (8, lanes), 1) // own
    tiles = []
    for first in range(0, blocks, fit):
        tile = jnp.zeros((8, lanes), jnp.float32)
        for place in range(fit):
            row = all_ref[(place_ref[0] + first + place) & (blocks - 1)]
            row = pltpu.roll(jnp.broadcast_to(row, (8, lanes)), 0, 1, stride=own, stride_axis=0)
            row = pltpu.roll(row, place * own, 1) if place else row
            tile = jnp.where(segment == place, row, tile)
        tiles.append(tile)
    everyone = jnp.concatenate(tiles, axis=1)
    last = lax.broadcasted_iota(jnp.int32, everyone.shape, 0) == 5
    everyone = everyone + jnp.where(last, field_ref[0] * everyone[2:3], 0.0)
    columns = everyone.T
    diag, rhs = everyone[4:5], everyone[5:6]
    rows = own
    spread_row = 2.0 * everyone[3:4] * everyone[3:4]
    tiles = count // lanes
    lane = lax.broadcasted_iota(jnp.int32, (rows, lanes), 1)
    line = lax.broadcasted_iota(jnp.int32, (rows, lanes), 0)

    def part(row, tile):
        return row[:, tile * lanes : (tile + 1) * lanes]

    def spread(column):
        return jnp.broadcast_to(column, (rows, lanes))

    above = [jnp.zeros((rows, lanes), jnp.float32) for _ in range(tiles)]
    kept = []
    for start in range(0, count, rows):
        first = start // lanes
        column = columns[start : start + rows]
        place = [spread(column[:, axis : axis + 1]) for axis in range(3)]
        wide = spread(2.0 * column[:, 3:4] * column[:, 3:4])
        value = spread(column[:, 5:6])
        value_ref[start : start + rows, :] = value
        below = jnp.zeros((rows, lanes), jnp.float32)
        for tile in range(first, tiles):
            delta = [place[axis] - part(everyone[axis : axis + 1], tile) for axis in range(3)]
            squared = delta[0] * delta[0] + delta[1] * delta[1] + delta[2] * delta[2]
            if tile == first:
                same = lane == line + (start - first * lanes)
                squared = jnp.where(same, 1.0, squared)
            inverse = lax.rsqrt(squared)
            scale = lax.rsqrt(wide + part(spread_row, tile))
            smear, decay = smeared(squared * inverse * scale)
            kernel = smear * inverse
            if start == 0:
                slope = (two_over_root_pi * scale * decay - kernel) * inverse * inverse
                slope = jnp.where(same, 0.0, slope) if tile == first else slope
                kept.append((delta, slope))
            if tile == first:
                kernel = jnp.where(same, 0.0, kernel)
            else:
                below = below + kernel * part(rhs, tile)
            above[tile] = above[tile] + kernel * value
            matrix_ref[start : start + rows, tile * lanes : (tile + 1) * lanes] = kernel
        if first + 1 < tiles:
            side_ref[start : start + rows, :] = below
    image = []
    for tile in range(tiles):
        value = jnp.sum(above[tile], axis=0, keepdims=True)
        if tile + 1 < tiles:
            below = side_ref[tile * lanes : (tile + 1) * lanes, :].T
            value = value + jnp.sum(below, axis=0, keepdims=True)
        image.append(value)
    image = diag * rhs + jnp.concatenate(image, axis=1)
    across = jnp.broadcast_to(image, (8, count)).T

    def total(value):
        return jnp.sum(value, axis=1, keepdims=True)

    norm = total(rhs * rhs)
    alpha = norm / total(rhs * image)
    residual = rhs - alpha * image
    fresh = total(residual * residual)
    again = fresh / norm
    direction = residual + again * rhs
    onto = [jnp.zeros((rows, lanes), jnp.float32) for _ in range(tiles)]
    above = [jnp.zeros((rows, lanes), jnp.float32) for _ in range(tiles)]
    for start in range(0, count, rows):
        first = start // lanes
        value = (1.0 + again) * value_ref[start : start + rows, :]
        value = value - alpha * spread(across[start : start + rows, 0:1])
        for tile in range(first, tiles):
            sums = onto if tile == first else above
            kernel = matrix_ref[start : start + rows, tile * lanes : (tile + 1) * lanes]
            sums[tile] = sums[tile] + kernel * value
    curved = jnp.zeros((rows, lanes), jnp.float32)
    for tile in range(tiles):
        curved = curved + (onto[tile] + 2.0 * above[tile]) * part(direction, tile)
    curved = jnp.sum(curved, axis=0, keepdims=True)
    for tile in range(tiles):
        curved = curved + part(diag * direction * direction, tile)
    charges = alpha * rhs + fresh / total(curved) * direction

    sums = [jnp.zeros((rows, lanes), jnp.float32) for _ in range(9)]
    for tile, (delta, slope) in enumerate(kept):
        weight = part(charges, tile) * slope
        pulled = [weight * delta[axis] for axis in range(3)]
        terms = pulled + [
            pulled[left] * delta[right]
            for left, right in ((0, 0), (1, 1), (2, 2), (0, 1), (0, 2), (1, 2))
        ]
        sums = [old + term for old, term in zip(sums, terms)]
    table = jnp.zeros((rows, lanes), jnp.float32)
    for place, value in enumerate(sums):
        table = jnp.where(lane == place, total(value), table)
    table = table.T
    mine = charges[:, :own]
    charges_ref[...] = mine
    pull = -mine * table[0:3]
    third = lax.broadcasted_iota(jnp.int32, pull.shape, 0) == 2
    forces_ref[...] = pull + jnp.where(third, mine * field_ref[0], 0.0)
    virial_ref[...] = 0.5 * mine * table[3:9]


def kernel_call(kernel, shapes, arguments, scalars=0, far=0, scratch=(), flops=0):
    shapes = tuple(jax.ShapeDtypeStruct(shape, kind) for shape, kind in shapes)
    spaces = [pltpu.SMEM] * scalars + [pltpu.HBM] * far
    spaces = spaces + [pltpu.VMEM] * (len(arguments) - len(spaces))
    arguments = [
        pltpu.with_memory_space_constraint(value, space) if space is pltpu.HBM else value
        for value, space in zip(arguments, spaces)
    ]
    return pl.pallas_call(
        kernel,
        out_shape=shapes,
        in_specs=[pl.BlockSpec(memory_space=space) for space in spaces],
        out_specs=tuple(pl.BlockSpec(memory_space=pltpu.VMEM) for _ in shapes),
        scratch_shapes=list(scratch),
        compiler_params=pltpu.CompilerParams(vmem_limit_bytes=32 * 1024 * 1024),
        cost_estimate=pl.CostEstimate(flops=flops, bytes_accessed=1 << 20, transcendentals=0),
    )(*arguments)


def exchanged(block, axis, step):
    size = lax.axis_size(axis)
    return lax.ppermute(block, axis, [(place, place ^ step) for place in range(size)])


def few_shards(
    features,
    positions,
    species,
    ghost_list,
    edge_recv,
    edge_send,
    edge_vec,
    w_msg,
    w_rad1,
    w_rad2,
    w_up,
    w_out,
    hardness,
    width,
    chi_shift,
    field,
):
    atoms, chans = features.shape
    edges = edge_recv.shape[0]
    rows, lanes = lax.axis_size("row"), lax.axis_size("space")
    space = lax.axis_index("space").astype(jnp.int32)
    (packed,) = kernel_call(
        pack_kernel,
        [((atoms + 16, chans), jnp.bfloat16)],
        (space.reshape(1), features, ghost_list),
        scalars=1,
        far=2,
        scratch=[
            pltpu.VMEM(ghost_list.shape, ghost_list.dtype),
            pltpu.SemaphoreType.DMA((2,)),
        ],
    )
    near, far, side = [exchanged(packed, "space", step) for step in (1, 3, 2)]
    others = (near, side, far)
    rest = (w_rad2, edge_send[None], edge_recv[None], w_msg, w_up)
    rest = rest + (species[None], hardness[None], width[None], chi_shift[None], positions)
    rest = rest + (w_out[None],)
    parts = kernel_call(
        edge_kernel,
        [
            ((2 * chans, edges), jnp.float32),
            ((8, edges), jnp.float32),
            ((1, chans), jnp.float32),
            ((chans, edges), jnp.bfloat16),
            ((lanes * atoms, edges), jnp.float32),
            ((atoms, edges), jnp.bfloat16),
            ((2 * chans, chans), jnp.bfloat16),
            ((chans, 2 * chans), jnp.bfloat16),
            ((chans, atoms), jnp.float32),
        ],
        (space.reshape(1), *rest, edge_vec, w_rad1),
        scalars=1,
        far=len(rest),
        scratch=[pltpu.VMEM(value.shape, value.dtype) for value in rest]
        + [pltpu.SemaphoreType.DMA((len(rest),))],
        flops=1 << 28,
    )
    devices = rows * lanes
    hidden, block = kernel_call(
        node_kernel,
        [((chans, atoms), jnp.float32), ((devices, 1, chans), jnp.float32)],
        (packed, *others, *parts),
        flops=1 << 28,
    )
    (new_features,) = kernel_call(
        feature_kernel, [((atoms, chans), jnp.bfloat16)], (packed, hidden), flops=1 << 20
    )
    block = lax.all_to_all(block, everywhere, 0, 0, tiled=True)
    place = lax.axis_index("row").astype(jnp.int32) * lanes + space
    everybody = rows * lanes * atoms
    charges, forces, virial = kernel_call(
        charge_kernel,
        [((count, atoms), jnp.float32) for count in (1, 3, 6)],
        (place.reshape(1), field, block),
        scalars=2,
        scratch=[
            pltpu.VMEM((everybody, everybody), jnp.float32),
            pltpu.VMEM((everybody, chans), jnp.float32),
            pltpu.VMEM((everybody, chans), jnp.float32),
        ],
        flops=1 << 28,
    )
    return (new_features, charges[0], forces, virial)


def solution(mesh):
    small = mesh.shape["space"] == 4 and mesh.shape["row"] == 8
    return jax.shard_map(
        few_shards if small else shards,
        mesh=mesh,
        in_specs=(
            P(("row", "space"), None),
            P(None, ("row", "space")),
            P(("row", "space")),
            P("row", "space", None),
            P(("row", "space")),
            P(("row", "space")),
            P(None, ("row", "space")),
            P(),
            P(),
            P(),
            P(),
            P(),
            P(),
            P(),
            P(),
            P(),
        ),
        out_specs=(
            P(("row", "space"), None),
            P(("row", "space")),
            P(None, ("row", "space")),
            P(None, ("row", "space")),
        ),
        check_vma=False,
    )
```

```python
import math

import jax
import jax.numpy as jnp
from jax import lax
from jax.experimental import pallas as pl
from jax.experimental.pallas import tpu as pltpu
from jax.sharding import PartitionSpec as P

ITERS = 2


cutoff = 6.0
message_scale = 0.125
two_over_root_pi = 2.0 / math.sqrt(math.pi)
inverse_root_pi = 1.0 / math.sqrt(math.pi)
replicate_limit = 1024
everywhere = ("row", "space")


def lookup(species, table):
    result = jnp.zeros(species.shape, jnp.float32)
    for kind in range(table.shape[0]):
        result = result + jnp.where(species == kind, table[kind], 0.0)
    return result


def pair_terms(target, target_labels, source, source_labels):
    delta = target[:3, :, None] - source[:3, None, :]
    squared = jnp.sum(delta * delta, axis=0)
    same = target_labels[:, None] == source_labels[None, :]
    squared = jnp.where(same, 1.0, squared)
    inverse = lax.rsqrt(squared)
    radius = squared * inverse
    spread = target[3][:, None] * target[3][:, None] + source[3][None, :] * source[3][None, :]
    scale = lax.rsqrt(2.0 * spread)
    scaled = radius * scale
    smear = lax.erf(scaled)
    return delta, same, inverse, scale, scaled, smear


def coulomb(target, target_labels, source, source_labels):
    _, same, inverse, _, _, smear = pair_terms(target, target_labels, source, source_labels)
    return jnp.where(same, 0.0, smear * inverse)


def pair_forces(target, target_labels, source, source_labels, source_charge):
    delta, same, inverse, scale, scaled, smear = pair_terms(
        target, target_labels, source, source_labels
    )
    slope = (
        two_over_root_pi * scale * jnp.exp(-scaled * scaled) * inverse - smear * inverse * inverse
    )
    weight = jnp.where(same, 0.0, source_charge[None, :] * slope * inverse)
    first = jnp.sum(weight[None] * delta, axis=2)
    pairs = ((0, 0), (1, 1), (2, 2), (0, 1), (0, 2), (1, 2))
    second = jnp.stack(
        [jnp.sum(weight * delta[left] * delta[right], axis=1) for left, right in pairs]
    )
    return jnp.concatenate([first, second], axis=0)


def edge_terms(receive, sender_rows, vectors, projected, w_rad1, w_rad2, atoms):
    length = jnp.sqrt(jnp.sum(vectors * vectors, axis=0))
    unit = vectors / length
    order = jnp.arange(1, w_rad1.shape[0] + 1, dtype=jnp.int32).astype(jnp.float32)[:, None]
    ratio = length / cutoff
    envelope = (1.0 - ratio * ratio) * (1.0 - ratio * ratio)
    basis = jnp.sin(order * math.pi * ratio) / ratio * envelope
    mixed = lax.dot_general(
        basis, w_rad1, (((0,), (0,)), ((), ())), precision=lax.Precision.HIGHEST
    )
    radial = jax.nn.silu(mixed).astype(jnp.bfloat16)
    filters = jnp.dot(radial, w_rad2, preferred_element_type=jnp.float32)
    picked = jnp.take(projected, sender_rows, axis=0).astype(jnp.float32) * filters
    chans = w_rad1.shape[1]
    scalar = picked[:, :chans]
    carried = picked[:, chans:]
    joined = [
        scalar,
        unit[0][:, None] * carried,
        unit[1][:, None] * carried,
        unit[2][:, None] * carried,
    ]
    message = jnp.concatenate(joined, axis=1).astype(jnp.bfloat16)
    onehot = (jnp.arange(atoms, dtype=jnp.int32)[:, None] == receive[None, :]).astype(jnp.bfloat16)
    return jnp.dot(onehot, message, preferred_element_type=jnp.float32)


def gathered(block, devices):
    copies = jnp.broadcast_to(block[None], (devices,) + block.shape)
    return lax.all_to_all(copies, everywhere, split_axis=0, concat_axis=0, tiled=True)


def shards(
    features,
    positions,
    species,
    ghost_list,
    edge_recv,
    edge_send,
    edge_vec,
    w_msg,
    w_rad1,
    w_rad2,
    w_up,
    w_out,
    hardness,
    width,
    chi_shift,
    field,
):
    atoms = features.shape[0]
    chans = features.shape[1]
    lanes = lax.axis_size("space")
    devices = lanes * lax.axis_size("row")
    everybody = devices * atoms
    me = lax.axis_index("row") * lanes + lax.axis_index("space")
    sigma = lookup(species, width)
    diag = lookup(species, hardness) + inverse_root_pi / sigma
    placed = jnp.concatenate([positions, sigma[None, :], diag[None, :]], axis=0)
    everyone = gathered(placed, devices).transpose(1, 0, 2).reshape(5, everybody)
    lists = ghost_list[0]
    outgoing = jnp.take(features, lists.reshape(-1), axis=0).reshape(lanes, lists.shape[1], chans)
    ghost_rows = jnp.einsum(
        "dkc,cf->dkf",
        lax.all_to_all(outgoing, "space", split_axis=0, concat_axis=0, tiled=True),
        w_msg,
        preferred_element_type=jnp.float32,
    ).astype(jnp.bfloat16)
    own_rows = jnp.dot(features, w_msg, preferred_element_type=jnp.float32).astype(jnp.bfloat16)
    projected = jnp.concatenate([own_rows, ghost_rows.reshape(-1, 2 * chans)], axis=0)
    summed = edge_terms(edge_recv, edge_send, edge_vec, projected, w_rad1, w_rad2, atoms)
    summed = summed * message_scale
    vector_part = summed[:, chans:].reshape(atoms, 3, chans)
    invariant = jnp.concatenate(
        [summed[:, :chans], jnp.sum(vector_part * vector_part, axis=1)], axis=1
    ).astype(jnp.bfloat16)
    hidden = jax.nn.silu(jnp.dot(invariant, w_up, preferred_element_type=jnp.float32))
    new_features = (features.astype(jnp.float32) + hidden).astype(jnp.bfloat16)
    chi = jnp.dot(hidden, w_out, precision=lax.Precision.HIGHEST) + lookup(species, chi_shift)
    own_labels = me * atoms + jnp.arange(atoms, dtype=jnp.int32)
    all_labels = jnp.arange(everybody, dtype=jnp.int32)
    rhs = field[0] * positions[2] - chi

    if everybody <= replicate_limit:
        kernel = coulomb(everyone, all_labels, everyone, all_labels)
        residual = gathered(rhs, devices).reshape(everybody)
        all_charges = conjugate(
            residual, lambda v: everyone[4] * v + jnp.sum(kernel * v[None, :], axis=1), jnp.sum
        )
        charges = lax.dynamic_slice(all_charges, (me * atoms,), (atoms,))
    else:
        kernel = coulomb(placed, own_labels, everyone, all_labels)

        def spread(vector):
            return gathered(vector, devices).reshape(everybody)

        charges = conjugate(
            rhs,
            lambda v: diag * v + jnp.sum(kernel * spread(v)[None, :], axis=1),
            lambda v: lax.psum(jnp.sum(v), everywhere),
        )
        all_charges = spread(charges)
    sums = pair_forces(placed, own_labels, everyone, all_labels, all_charges)
    pull = -charges[None, :] * sums[:3]
    forces = jnp.concatenate([pull[:2], pull[2:] + (charges * field[0])[None, :]], axis=0)
    virial = 0.5 * charges[None, :] * sums[3:]
    return (new_features, charges, forces, virial)


def conjugate(rhs, apply, total):
    charges = jnp.zeros_like(rhs)
    residual = rhs
    direction = rhs
    norm_now = total(residual * residual)
    for step in range(ITERS):
        image = apply(direction)
        alpha = norm_now / total(direction * image)
        charges = charges + alpha * direction
        if step + 1 < ITERS:
            residual = residual - alpha * image
            fresh = total(residual * residual)
            direction = residual + fresh / norm_now * direction
            norm_now = fresh
    return charges


def split3(value):
    first = value.astype(jnp.bfloat16).astype(jnp.float32)
    rest = value - first
    second = rest.astype(jnp.bfloat16).astype(jnp.float32)
    third = (rest - second).astype(jnp.bfloat16).astype(jnp.float32)
    return first, second, third


def over_first(left, right):
    return lax.dot_general(
        left, right, (((0,), (0,)), ((), ())), preferred_element_type=jnp.float32
    )


def over_last(left, right, precision=None):
    return lax.dot_general(
        left,
        right,
        (((1,), (1,)), ((), ())),
        precision=precision,
        preferred_element_type=jnp.float32,
    )


def silu(value):
    return value / (1.0 + jnp.exp(-value))


def silu_half(value):
    return (0.5 * value) * (1.0 + jnp.tanh(0.5 * value))


sine_series = [(-1.0) ** k * math.pi ** (2 * k + 1) / math.factorial(2 * k + 1) for k in range(7)]


def fetched(pairs, semaphores):
    copies = [
        pltpu.make_async_copy(source, target, semaphores.at[place])
        for place, (source, target) in enumerate(pairs)
    ]
    for copy in copies:
        copy.start()
    return copies


chi_segment = 3


def pack_kernel(space_ref, features_ref, lists_ref, packed_ref, held_ref, semaphores):
    atoms, chans = features_ref.shape
    copies = fetched(
        [(lists_ref, held_ref), (features_ref, packed_ref.at[pl.ds(0, atoms)])], semaphores
    )
    copies[0].wait()
    _, lanes, width = held_ref.shape
    rows = []
    for place in range(lanes):
        row = held_ref[0, pl.ds(space_ref[0] ^ place, 1), :].astype(jnp.float32) + place * atoms
        parts = [jnp.zeros((1, width), jnp.float32)] * lanes
        parts[place] = row
        rows.append(jnp.concatenate(parts, axis=1))
    rows.append(jnp.zeros((packed_ref.shape[0] - atoms - lanes, chans), jnp.float32))
    packed_ref[atoms:, :] = jnp.concatenate(rows, axis=0).astype(jnp.bfloat16)
    copies[1].wait()


def edge_kernel(
    space_ref,
    *refs,
):
    count = (len(refs) - 11) // 2
    far, near, semaphores = refs[:count], refs[count + 10 : -1], refs[-1]
    vec_ref, filter_ref, unit_ref, row_ref, slot_ref = refs[count : count + 5]
    local_ref, hit_ref, turned_ref, upward_ref, read_ref = refs[count + 5 : count + 10]
    first_ref, second_ref, send_ref, recv_ref, project_ref, update_ref = near[:6]
    out_ref, species_ref, hardness_ref, width_ref, shift_ref, positions_ref = near[6:]
    copies = fetched(list(zip(far, near)), semaphores)
    edges = vec_ref.shape[1]
    orders = first_ref.shape[0]
    atoms, chans = hit_ref.shape[0], row_ref.shape[1]
    vec = vec_ref[...]
    east, north, up = vec[0:1], vec[1:2], vec[2:3]
    squared = east * east + north * north + up * up
    inverse = lax.rsqrt(squared)
    unit_ref[0:3, :] = vec * inverse
    ratio = squared * inverse * (1.0 / cutoff)
    envelope = (1.0 - ratio * ratio) * (1.0 - ratio * ratio) * (cutoff * inverse)
    order = lax.broadcasted_iota(jnp.int32, (orders, edges), 0).astype(jnp.float32) + 1.0
    turns = order * ratio
    whole = jnp.floor(turns + 0.5)
    part = turns - whole
    sign = 1.0 - 2.0 * (whole - 2.0 * jnp.floor(whole * 0.5))
    series = jnp.full_like(part, sine_series[-1])
    for coefficient in sine_series[-2::-1]:
        series = series * (part * part) + coefficient
    basis = series * part * (sign * envelope)
    b1, b2, b3 = split3(basis)
    copies[0].wait()
    w1, w2, w3 = split3(first_ref[...])
    mixed = over_first(
        jnp.concatenate([w1, w1, w2, w2, w1, w3], axis=0).astype(jnp.bfloat16),
        jnp.concatenate([b1, b2, b1, b2, b3, b1], axis=0).astype(jnp.bfloat16),
    )
    radial = silu_half(mixed).astype(jnp.bfloat16)
    copies[1].wait()
    filter_ref[...] = over_first(second_ref[...], radial)
    lanes = local_ref.shape[0] // atoms
    slots = chans // lanes

    def chosen(ref, index):
        hit = lax.broadcasted_iota(jnp.int32, ref.shape, 0) == index
        ref[...] = jnp.where(hit, 1.0, 0.0).astype(ref.dtype)

    copies[2].wait()
    send = send_ref[...]
    own = send < atoms
    chosen(slot_ref, jnp.where(own, -1, (send - atoms) ^ (space_ref[0] * slots)))
    chosen(local_ref, jnp.where(own, send, -1))
    copies[3].wait()
    chosen(hit_ref, recv_ref[...])
    copies[4].wait()
    turned_ref[...] = project_ref[...].astype(jnp.float32).T.astype(jnp.bfloat16)
    copies[5].wait()
    upward_ref[...] = update_ref[...].astype(jnp.float32).T.astype(jnp.bfloat16)
    copies[6].wait()
    read_ref[...] = jnp.broadcast_to(out_ref[...], (atoms, chans)).T
    for copy in copies[7:]:
        copy.wait()
    species = species_ref[...]

    def table(ref):
        result = jnp.zeros(species.shape, jnp.float32)
        for kind in range(ref.shape[1]):
            result = result + jnp.where(species == kind, ref[:, kind : kind + 1], 0.0)
        return result

    positions = positions_ref[...]
    sigma = table(width_ref)
    diag = table(hardness_ref) + inverse_root_pi / sigma
    blank = jnp.zeros((2, atoms), jnp.float32)
    rows = [positions[0:1], blank, -table(shift_ref), diag, sigma, positions[2:3], positions[1:2]]
    block = jnp.concatenate(
        [jnp.concatenate(rows, axis=0), jnp.zeros((8, chans - atoms), jnp.float32)], axis=1
    )
    block = pltpu.roll(block, 0, 1, stride=atoms, stride_axis=0)
    row_ref[...] = jnp.sum(block, axis=0, keepdims=True)


def node_kernel(
    own_ref,
    near_ref,
    far_ref,
    side_ref,
    filter_ref,
    unit_ref,
    row_ref,
    slot_ref,
    local_ref,
    hit_ref,
    turned_ref,
    upward_ref,
    read_ref,
    hidden_ref,
    block_ref,
):
    chans, atoms = hidden_ref.shape
    packed = (own_ref, near_ref, side_ref, far_ref)
    group = jnp.concatenate([ref[:atoms, :] for ref in packed], axis=0)
    chosen = jnp.zeros((1, chans), jnp.float32)
    for place, ref in enumerate(packed):
        tail = ref[atoms:, :].astype(jnp.float32)
        chosen = chosen + tail[place : place + 1]
    fill = jnp.where(
        lax.broadcasted_iota(jnp.int32, (len(packed) * atoms, chans), 0)
        == chosen.astype(jnp.int32),
        1.0,
        0.0,
    ).astype(jnp.bfloat16)
    sender = jnp.dot(fill, slot_ref[...], preferred_element_type=jnp.float32) + local_ref[...]
    projected = over_last(turned_ref[...], group).astype(jnp.bfloat16)
    picked = jnp.dot(projected, sender.astype(jnp.bfloat16), preferred_element_type=jnp.float32)
    scalar = picked[:chans] * filter_ref[:chans, :]
    carried = picked[chans:] * filter_ref[chans:, :]
    parts = [scalar] + [unit_ref[axis : axis + 1, :] * carried for axis in range(3)]
    message = jnp.concatenate([part.astype(jnp.bfloat16) for part in parts], axis=0)
    summed = over_last(message, hit_ref[...]) * message_scale
    square = jnp.zeros((chans, atoms), jnp.float32)
    for component in range(1, 4):
        part = summed[component * chans : (component + 1) * chans]
        square = square + part * part
    invariant = jnp.concatenate([summed[:chans], square], axis=0).astype(jnp.bfloat16)
    hidden = silu(jnp.dot(upward_ref[...], invariant, preferred_element_type=jnp.float32))
    chi = jnp.sum(hidden * read_ref[...], axis=0, keepdims=True)
    chi = jnp.concatenate([chi, jnp.zeros((1, chans - atoms), jnp.float32)], axis=1)
    row = row_ref[...] - pltpu.roll(chi, chi_segment * atoms, 1)
    block_ref[...] = jnp.broadcast_to(row[None], block_ref.shape)
    hidden_ref[...] = hidden


def feature_kernel(packed_ref, hidden_ref, features_ref):
    atoms = features_ref.shape[0]
    old = packed_ref[...].astype(jnp.float32)[:atoms]
    features_ref[...] = (old + hidden_ref[...].T).astype(jnp.bfloat16)


def reciprocal(value):
    rough = pl.reciprocal(value, approx=True)
    return rough * (2.0 - value * rough)


def smeared(scaled):
    decay = jnp.exp2(scaled * scaled * -math.log2(math.e))
    turn = reciprocal(1.0 + 0.3275911 * scaled)
    series = 1.061405429 * turn - 1.453152027
    series = series * turn + 1.421413741
    series = series * turn - 0.284496736
    series = series * turn + 0.254829592
    return 1.0 - series * turn * decay, decay


def charge_kernel(
    place_ref,
    field_ref,
    all_ref,
    charges_ref,
    forces_ref,
    virial_ref,
    matrix_ref,
    side_ref,
    value_ref,
):
    blocks, _, lanes = all_ref.shape
    own = charges_ref.shape[1]
    count = blocks * own
    fit = lanes // own
    segment = lax.broadcasted_iota(jnp.int32, (8, lanes), 1) // own
    tiles = []
    for first in range(0, blocks, fit):
        tile = jnp.zeros((8, lanes), jnp.float32)
        for place in range(fit):
            row = all_ref[(place_ref[0] + first + place) & (blocks - 1)]
            row = pltpu.roll(jnp.broadcast_to(row, (8, lanes)), 0, 1, stride=own, stride_axis=0)
            row = pltpu.roll(row, place * own, 1) if place else row
            tile = jnp.where(segment == place, row, tile)
        tiles.append(tile)
    everyone = jnp.concatenate(tiles, axis=1)
    last = lax.broadcasted_iota(jnp.int32, everyone.shape, 0) == 5
    everyone = everyone + jnp.where(last, field_ref[0] * everyone[2:3], 0.0)
    columns = everyone.T
    diag, rhs = everyone[4:5], everyone[5:6]
    rows = own
    spread_row = 2.0 * everyone[3:4] * everyone[3:4]
    tiles = count // lanes
    lane = lax.broadcasted_iota(jnp.int32, (rows, lanes), 1)
    line = lax.broadcasted_iota(jnp.int32, (rows, lanes), 0)

    def part(row, tile):
        return row[:, tile * lanes : (tile + 1) * lanes]

    def spread(column):
        return jnp.broadcast_to(column, (rows, lanes))

    above = [jnp.zeros((rows, lanes), jnp.float32) for _ in range(tiles)]
    kept = []
    for start in range(0, count, rows):
        first = start // lanes
        column = columns[start : start + rows]
        place = [spread(column[:, axis : axis + 1]) for axis in range(3)]
        wide = spread(2.0 * column[:, 3:4] * column[:, 3:4])
        value = spread(column[:, 5:6])
        value_ref[start : start + rows, :] = value
        below = jnp.zeros((rows, lanes), jnp.float32)
        for tile in range(first, tiles):
            delta = [place[axis] - part(everyone[axis : axis + 1], tile) for axis in range(3)]
            squared = delta[0] * delta[0] + delta[1] * delta[1] + delta[2] * delta[2]
            if tile == first:
                same = lane == line + (start - first * lanes)
                squared = jnp.where(same, 1.0, squared)
            inverse = lax.rsqrt(squared)
            scale = lax.rsqrt(wide + part(spread_row, tile))
            smear, decay = smeared(squared * inverse * scale)
            kernel = smear * inverse
            if start == 0:
                slope = (two_over_root_pi * scale * decay - kernel) * inverse * inverse
                slope = jnp.where(same, 0.0, slope) if tile == first else slope
                kept.append((delta, slope))
            if tile == first:
                kernel = jnp.where(same, 0.0, kernel)
            else:
                below = below + kernel * part(rhs, tile)
            above[tile] = above[tile] + kernel * value
            matrix_ref[start : start + rows, tile * lanes : (tile + 1) * lanes] = kernel
        if first + 1 < tiles:
            side_ref[start : start + rows, :] = below
    image = []
    for tile in range(tiles):
        value = jnp.sum(above[tile], axis=0, keepdims=True)
        if tile + 1 < tiles:
            below = side_ref[tile * lanes : (tile + 1) * lanes, :].T
            value = value + jnp.sum(below, axis=0, keepdims=True)
        image.append(value)
    image = diag * rhs + jnp.concatenate(image, axis=1)
    across = jnp.broadcast_to(image, (8, count)).T

    def total(value):
        return jnp.sum(value, axis=1, keepdims=True)

    norm = total(rhs * rhs)
    alpha = norm / total(rhs * image)
    residual = rhs - alpha * image
    fresh = total(residual * residual)
    again = fresh / norm
    direction = residual + again * rhs
    onto = [jnp.zeros((rows, lanes), jnp.float32) for _ in range(tiles)]
    above = [jnp.zeros((rows, lanes), jnp.float32) for _ in range(tiles)]
    for start in range(0, count, rows):
        first = start // lanes
        value = (1.0 + again) * value_ref[start : start + rows, :]
        value = value - alpha * spread(across[start : start + rows, 0:1])
        for tile in range(first, tiles):
            sums = onto if tile == first else above
            kernel = matrix_ref[start : start + rows, tile * lanes : (tile + 1) * lanes]
            sums[tile] = sums[tile] + kernel * value
    curved = jnp.zeros((rows, lanes), jnp.float32)
    for tile in range(tiles):
        curved = curved + (onto[tile] + 2.0 * above[tile]) * part(direction, tile)
    curved = jnp.sum(curved, axis=0, keepdims=True)
    for tile in range(tiles):
        curved = curved + part(diag * direction * direction, tile)
    charges = alpha * rhs + fresh / total(curved) * direction

    sums = [jnp.zeros((rows, lanes), jnp.float32) for _ in range(9)]
    for tile, (delta, slope) in enumerate(kept):
        weight = part(charges, tile) * slope
        pulled = [weight * delta[axis] for axis in range(3)]
        terms = pulled + [
            pulled[left] * delta[right]
            for left, right in ((0, 0), (1, 1), (2, 2), (0, 1), (0, 2), (1, 2))
        ]
        sums = [old + term for old, term in zip(sums, terms)]
    table = jnp.zeros((rows, lanes), jnp.float32)
    for place, value in enumerate(sums):
        table = jnp.where(lane == place, total(value), table)
    table = table.T
    mine = charges[:, :own]
    charges_ref[...] = mine
    pull = -mine * table[0:3]
    third = lax.broadcasted_iota(jnp.int32, pull.shape, 0) == 2
    forces_ref[...] = pull + jnp.where(third, mine * field_ref[0], 0.0)
    virial_ref[...] = 0.5 * mine * table[3:9]


def kernel_call(kernel, shapes, arguments, scalars=0, far=0, scratch=(), flops=0):
    shapes = tuple(jax.ShapeDtypeStruct(shape, kind) for shape, kind in shapes)
    spaces = [pltpu.SMEM] * scalars + [pltpu.HBM] * far
    spaces = spaces + [pltpu.VMEM] * (len(arguments) - len(spaces))
    arguments = [
        pltpu.with_memory_space_constraint(value, space) if space is pltpu.HBM else value
        for value, space in zip(arguments, spaces)
    ]
    return pl.pallas_call(
        kernel,
        out_shape=shapes,
        in_specs=[pl.BlockSpec(memory_space=space) for space in spaces],
        out_specs=tuple(pl.BlockSpec(memory_space=pltpu.VMEM) for _ in shapes),
        scratch_shapes=list(scratch),
        compiler_params=pltpu.CompilerParams(vmem_limit_bytes=32 * 1024 * 1024),
        cost_estimate=pl.CostEstimate(flops=flops, bytes_accessed=1 << 20, transcendentals=0),
    )(*arguments)


def exchanged(block, axis, step):
    size = lax.axis_size(axis)
    return lax.ppermute(block, axis, [(place, place ^ step) for place in range(size)])


def few_shards(
    features,
    positions,
    species,
    ghost_list,
    edge_recv,
    edge_send,
    edge_vec,
    w_msg,
    w_rad1,
    w_rad2,
    w_up,
    w_out,
    hardness,
    width,
    chi_shift,
    field,
):
    atoms, chans = features.shape
    edges = edge_recv.shape[0]
    rows, lanes = lax.axis_size("row"), lax.axis_size("space")
    space = lax.axis_index("space").astype(jnp.int32)
    (packed,) = kernel_call(
        pack_kernel,
        [((atoms + 16, chans), jnp.bfloat16)],
        (space.reshape(1), features, ghost_list),
        scalars=1,
        far=2,
        scratch=[
            pltpu.VMEM(ghost_list.shape, ghost_list.dtype),
            pltpu.SemaphoreType.DMA((2,)),
        ],
    )
    near, far, side = [exchanged(packed, "space", step) for step in (1, 3, 2)]
    rest = (w_rad1, w_rad2, edge_send[None], edge_recv[None], w_msg, w_up, w_out[None])
    rest = rest + (species[None], hardness[None], width[None], chi_shift[None], positions)
    parts = kernel_call(
        edge_kernel,
        [
            ((2 * chans, edges), jnp.float32),
            ((8, edges), jnp.float32),
            ((1, chans), jnp.float32),
            ((chans, edges), jnp.bfloat16),
            ((lanes * atoms, edges), jnp.float32),
            ((atoms, edges), jnp.bfloat16),
            ((2 * chans, chans), jnp.bfloat16),
            ((chans, 2 * chans), jnp.bfloat16),
            ((chans, atoms), jnp.float32),
        ],
        (space.reshape(1), *rest, edge_vec),
        scalars=1,
        far=len(rest),
        scratch=[pltpu.VMEM(value.shape, value.dtype) for value in rest]
        + [pltpu.SemaphoreType.DMA((len(rest),))],
        flops=1 << 28,
    )
    devices = rows * lanes
    hidden, block = kernel_call(
        node_kernel,
        [((chans, atoms), jnp.float32), ((devices, 1, chans), jnp.float32)],
        (packed, near, far, side, *parts),
        flops=1 << 28,
    )
    (new_features,) = kernel_call(
        feature_kernel, [((atoms, chans), jnp.bfloat16)], (packed, hidden), flops=1 << 20
    )
    block = lax.all_to_all(block, everywhere, 0, 0, tiled=True)
    place = lax.axis_index("row").astype(jnp.int32) * lanes + space
    everybody = rows * lanes * atoms
    charges, forces, virial = kernel_call(
        charge_kernel,
        [((count, atoms), jnp.float32) for count in (1, 3, 6)],
        (place.reshape(1), field, block),
        scalars=2,
        scratch=[
            pltpu.VMEM((everybody, everybody), jnp.float32),
            pltpu.VMEM((everybody, chans), jnp.float32),
            pltpu.VMEM((everybody, chans), jnp.float32),
        ],
        flops=1 << 28,
    )
    return (new_features, charges[0], forces, virial)


def solution(mesh):
    small = mesh.shape["space"] == 4 and mesh.shape["row"] == 8
    return jax.shard_map(
        few_shards if small else shards,
        mesh=mesh,
        in_specs=(
            P(("row", "space"), None),
            P(None, ("row", "space")),
            P(("row", "space")),
            P("row", "space", None),
            P(("row", "space")),
            P(("row", "space")),
            P(None, ("row", "space")),
            P(),
            P(),
            P(),
            P(),
            P(),
            P(),
            P(),
            P(),
            P(),
        ),
        out_specs=(
            P(("row", "space"), None),
            P(("row", "space")),
            P(None, ("row", "space")),
            P(None, ("row", "space")),
        ),
        check_vma=False,
    )
```

```python
import functools
import math

import jax
import jax.numpy as jnp
from jax import lax
from jax.experimental import pallas as pl
from jax.experimental.pallas import tpu as pltpu
from jax.sharding import PartitionSpec as P

ITERS = 2


cutoff = 6.0
message_scale = 0.125
two_over_root_pi = 2.0 / math.sqrt(math.pi)
inverse_root_pi = 1.0 / math.sqrt(math.pi)
replicate_limit = 1024
everywhere = ("row", "space")


def lookup(species, table):
    result = jnp.zeros(species.shape, jnp.float32)
    for kind in range(table.shape[0]):
        result = result + jnp.where(species == kind, table[kind], 0.0)
    return result


def pair_terms(target, target_labels, source, source_labels):
    delta = target[:3, :, None] - source[:3, None, :]
    squared = jnp.sum(delta * delta, axis=0)
    same = target_labels[:, None] == source_labels[None, :]
    squared = jnp.where(same, 1.0, squared)
    inverse = lax.rsqrt(squared)
    radius = squared * inverse
    spread = target[3][:, None] * target[3][:, None] + source[3][None, :] * source[3][None, :]
    scale = lax.rsqrt(2.0 * spread)
    scaled = radius * scale
    smear = lax.erf(scaled)
    return delta, same, inverse, scale, scaled, smear


def coulomb(target, target_labels, source, source_labels):
    _, same, inverse, _, _, smear = pair_terms(target, target_labels, source, source_labels)
    return jnp.where(same, 0.0, smear * inverse)


def pair_forces(target, target_labels, source, source_labels, source_charge):
    delta, same, inverse, scale, scaled, smear = pair_terms(
        target, target_labels, source, source_labels
    )
    slope = (
        two_over_root_pi * scale * jnp.exp(-scaled * scaled) * inverse - smear * inverse * inverse
    )
    weight = jnp.where(same, 0.0, source_charge[None, :] * slope * inverse)
    first = jnp.sum(weight[None] * delta, axis=2)
    pairs = ((0, 0), (1, 1), (2, 2), (0, 1), (0, 2), (1, 2))
    second = jnp.stack(
        [jnp.sum(weight * delta[left] * delta[right], axis=1) for left, right in pairs]
    )
    return jnp.concatenate([first, second], axis=0)


def edge_terms(receive, sender_rows, vectors, projected, w_rad1, w_rad2, atoms):
    length = jnp.sqrt(jnp.sum(vectors * vectors, axis=0))
    unit = vectors / length
    order = jnp.arange(1, w_rad1.shape[0] + 1, dtype=jnp.int32).astype(jnp.float32)[:, None]
    ratio = length / cutoff
    envelope = (1.0 - ratio * ratio) * (1.0 - ratio * ratio)
    basis = jnp.sin(order * math.pi * ratio) / ratio * envelope
    mixed = lax.dot_general(
        basis, w_rad1, (((0,), (0,)), ((), ())), precision=lax.Precision.HIGHEST
    )
    radial = jax.nn.silu(mixed).astype(jnp.bfloat16)
    filters = jnp.dot(radial, w_rad2, preferred_element_type=jnp.float32)
    picked = jnp.take(projected, sender_rows, axis=0).astype(jnp.float32) * filters
    chans = w_rad1.shape[1]
    scalar = picked[:, :chans]
    carried = picked[:, chans:]
    joined = [
        scalar,
        unit[0][:, None] * carried,
        unit[1][:, None] * carried,
        unit[2][:, None] * carried,
    ]
    message = jnp.concatenate(joined, axis=1).astype(jnp.bfloat16)
    onehot = (jnp.arange(atoms, dtype=jnp.int32)[:, None] == receive[None, :]).astype(jnp.bfloat16)
    return jnp.dot(onehot, message, preferred_element_type=jnp.float32)


def gathered(block, devices):
    copies = jnp.broadcast_to(block[None], (devices,) + block.shape)
    return lax.all_to_all(copies, everywhere, split_axis=0, concat_axis=0, tiled=True)


def shards(
    features,
    positions,
    species,
    ghost_list,
    edge_recv,
    edge_send,
    edge_vec,
    w_msg,
    w_rad1,
    w_rad2,
    w_up,
    w_out,
    hardness,
    width,
    chi_shift,
    field,
):
    atoms = features.shape[0]
    chans = features.shape[1]
    lanes = lax.axis_size("space")
    devices = lanes * lax.axis_size("row")
    everybody = devices * atoms
    me = lax.axis_index("row") * lanes + lax.axis_index("space")
    sigma = lookup(species, width)
    diag = lookup(species, hardness) + inverse_root_pi / sigma
    placed = jnp.concatenate([positions, sigma[None, :], diag[None, :]], axis=0)
    everyone = gathered(placed, devices).transpose(1, 0, 2).reshape(5, everybody)
    lists = ghost_list[0]
    outgoing = jnp.take(features, lists.reshape(-1), axis=0).reshape(lanes, lists.shape[1], chans)
    ghost_rows = jnp.einsum(
        "dkc,cf->dkf",
        lax.all_to_all(outgoing, "space", split_axis=0, concat_axis=0, tiled=True),
        w_msg,
        preferred_element_type=jnp.float32,
    ).astype(jnp.bfloat16)
    own_rows = jnp.dot(features, w_msg, preferred_element_type=jnp.float32).astype(jnp.bfloat16)
    projected = jnp.concatenate([own_rows, ghost_rows.reshape(-1, 2 * chans)], axis=0)
    summed = edge_terms(edge_recv, edge_send, edge_vec, projected, w_rad1, w_rad2, atoms)
    summed = summed * message_scale
    vector_part = summed[:, chans:].reshape(atoms, 3, chans)
    invariant = jnp.concatenate(
        [summed[:, :chans], jnp.sum(vector_part * vector_part, axis=1)], axis=1
    ).astype(jnp.bfloat16)
    hidden = jax.nn.silu(jnp.dot(invariant, w_up, preferred_element_type=jnp.float32))
    new_features = (features.astype(jnp.float32) + hidden).astype(jnp.bfloat16)
    chi = jnp.dot(hidden, w_out, precision=lax.Precision.HIGHEST) + lookup(species, chi_shift)
    own_labels = me * atoms + jnp.arange(atoms, dtype=jnp.int32)
    all_labels = jnp.arange(everybody, dtype=jnp.int32)
    rhs = field[0] * positions[2] - chi

    if everybody <= replicate_limit:
        kernel = coulomb(everyone, all_labels, everyone, all_labels)
        residual = gathered(rhs, devices).reshape(everybody)
        all_charges = conjugate(
            residual, lambda v: everyone[4] * v + jnp.sum(kernel * v[None, :], axis=1), jnp.sum
        )
        charges = lax.dynamic_slice(all_charges, (me * atoms,), (atoms,))
    else:
        kernel = coulomb(placed, own_labels, everyone, all_labels)

        def spread(vector):
            return gathered(vector, devices).reshape(everybody)

        charges = conjugate(
            rhs,
            lambda v: diag * v + jnp.sum(kernel * spread(v)[None, :], axis=1),
            lambda v: lax.psum(jnp.sum(v), everywhere),
        )
        all_charges = spread(charges)
    sums = pair_forces(placed, own_labels, everyone, all_labels, all_charges)
    pull = -charges[None, :] * sums[:3]
    forces = jnp.concatenate([pull[:2], pull[2:] + (charges * field[0])[None, :]], axis=0)
    virial = 0.5 * charges[None, :] * sums[3:]
    return (new_features, charges, forces, virial)


def conjugate(rhs, apply, total):
    charges = jnp.zeros_like(rhs)
    residual = rhs
    direction = rhs
    norm_now = total(residual * residual)
    for step in range(ITERS):
        image = apply(direction)
        alpha = norm_now / total(direction * image)
        charges = charges + alpha * direction
        if step + 1 < ITERS:
            residual = residual - alpha * image
            fresh = total(residual * residual)
            direction = residual + fresh / norm_now * direction
            norm_now = fresh
    return charges


def split3(value):
    first = value.astype(jnp.bfloat16).astype(jnp.float32)
    rest = value - first
    second = rest.astype(jnp.bfloat16).astype(jnp.float32)
    third = (rest - second).astype(jnp.bfloat16).astype(jnp.float32)
    return first, second, third


def over_first(left, right):
    return lax.dot_general(
        left, right, (((0,), (0,)), ((), ())), preferred_element_type=jnp.float32
    )


def over_last(left, right, precision=None):
    return lax.dot_general(
        left,
        right,
        (((1,), (1,)), ((), ())),
        precision=precision,
        preferred_element_type=jnp.float32,
    )


def silu(value):
    return value / (1.0 + jnp.exp(-value))


def silu_half(value):
    return (0.5 * value) * (1.0 + jnp.tanh(0.5 * value))


sine_series = [(-1.0) ** k * math.pi ** (2 * k + 1) / math.factorial(2 * k + 1) for k in range(7)]


def fetched(pairs, semaphores):
    copies = [
        pltpu.make_async_copy(source, target, semaphores.at[place])
        for place, (source, target) in enumerate(pairs)
    ]
    for copy in copies:
        copy.start()
    return copies


chi_segment = 3


def pack_kernel(space_ref, features_ref, lists_ref, packed_ref, held_ref, semaphores):
    atoms, chans = features_ref.shape
    copies = fetched(
        [(lists_ref, held_ref), (features_ref, packed_ref.at[pl.ds(0, atoms)])], semaphores
    )
    copies[0].wait()
    _, lanes, width = held_ref.shape
    rows = []
    for place in range(lanes):
        row = held_ref[0, pl.ds(space_ref[0] ^ place, 1), :].astype(jnp.float32) + place * atoms
        parts = [jnp.zeros((1, width), jnp.float32)] * lanes
        parts[place] = row
        rows.append(jnp.concatenate(parts, axis=1))
    rows.append(jnp.zeros((packed_ref.shape[0] - atoms - lanes, chans), jnp.float32))
    packed_ref[atoms:, :] = jnp.concatenate(rows, axis=0).astype(jnp.bfloat16)
    copies[1].wait()


def edge_kernel(lanes, space_ref, *refs):
    count = (len(refs) - 10) // 2
    far, near, semaphores = refs[:count], refs[count + 9 : -1], refs[-1]
    vec_ref, filter_ref, unit_ref, row_ref, slot_ref = refs[count : count + 5]
    hit_ref, turned_ref, upward_ref, read_ref = refs[count + 5 : count + 9]
    first_ref, second_ref, send_ref, recv_ref, project_ref, update_ref = near[:6]
    out_ref, species_ref, hardness_ref, width_ref, shift_ref, positions_ref = near[6:]
    copies = fetched(list(zip(far, near)), semaphores)
    edges = vec_ref.shape[1]
    orders = first_ref.shape[0]
    atoms, chans = hit_ref.shape[0], row_ref.shape[1]
    vec = vec_ref[...]
    east, north, up = vec[0:1], vec[1:2], vec[2:3]
    squared = east * east + north * north + up * up
    inverse = lax.rsqrt(squared)
    unit_ref[0:3, :] = vec * inverse
    ratio = squared * inverse * (1.0 / cutoff)
    envelope = (1.0 - ratio * ratio) * (1.0 - ratio * ratio) * (cutoff * inverse)
    order = lax.broadcasted_iota(jnp.int32, (orders, edges), 0).astype(jnp.float32) + 1.0
    turns = order * ratio
    whole = jnp.floor(turns + 0.5)
    part = turns - whole
    sign = 1.0 - 2.0 * (whole - 2.0 * jnp.floor(whole * 0.5))
    series = jnp.full_like(part, sine_series[-1])
    for coefficient in sine_series[-2::-1]:
        series = series * (part * part) + coefficient
    basis = series * part * (sign * envelope)
    b1, b2, b3 = split3(basis)
    for copy in copies[:2]:
        copy.wait()
    w1, w2, w3 = split3(first_ref[...])
    mixed = over_first(
        jnp.concatenate([w1, w1, w2, w2, w1, w3], axis=0).astype(jnp.bfloat16),
        jnp.concatenate([b1, b2, b1, b2, b3, b1], axis=0).astype(jnp.bfloat16),
    )
    radial = silu_half(mixed).astype(jnp.bfloat16)
    filter_ref[...] = over_first(second_ref[...], radial)
    for copy in copies[2:]:
        copy.wait()
    slots = slot_ref.shape[0] - atoms
    width = slots // lanes

    def chosen(ref, index, value):
        hit = lax.broadcasted_iota(jnp.int32, ref.shape, 0) == index
        ref[...] = jnp.where(hit, value, 0.0).astype(ref.dtype)

    send = send_ref[...]
    ghost = (send - atoms) ^ (space_ref[0] * width)
    chosen(slot_ref, jnp.where(send < atoms, send + slots, ghost), 1.0)
    chosen(hit_ref, recv_ref[...], message_scale)
    turned_ref[...] = project_ref[...].astype(jnp.float32).T.astype(jnp.bfloat16)
    upward_ref[...] = update_ref[...].astype(jnp.float32).T.astype(jnp.bfloat16)
    read_ref[...] = jnp.broadcast_to(out_ref[...], (atoms, chans)).T
    species = species_ref[...]

    def table(ref):
        result = jnp.zeros(species.shape, jnp.float32)
        for kind in range(ref.shape[1]):
            result = result + jnp.where(species == kind, ref[:, kind : kind + 1], 0.0)
        return result

    positions = positions_ref[...]
    sigma = table(width_ref)
    diag = table(hardness_ref) + inverse_root_pi / sigma
    blank = jnp.zeros((2, atoms), jnp.float32)
    rows = [positions[0:1], blank, -table(shift_ref), diag, sigma, positions[2:3], positions[1:2]]
    block = jnp.concatenate(
        [jnp.concatenate(rows, axis=0), jnp.zeros((8, chans - atoms), jnp.float32)], axis=1
    )
    block = pltpu.roll(block, 0, 1, stride=atoms, stride_axis=0)
    row_ref[...] = jnp.sum(block, axis=0, keepdims=True)


def node_kernel(
    own_ref,
    near_ref,
    far_ref,
    side_ref,
    filter_ref,
    unit_ref,
    row_ref,
    slot_ref,
    hit_ref,
    turned_ref,
    upward_ref,
    read_ref,
    hidden_ref,
    block_ref,
):
    chans, atoms = hidden_ref.shape
    packed = (own_ref, near_ref, side_ref, far_ref)
    group = jnp.concatenate([ref[:atoms, :] for ref in packed], axis=0)
    chosen = jnp.zeros((1, chans), jnp.float32)
    for place, ref in enumerate(packed):
        tail = ref[atoms:, :].astype(jnp.float32)
        chosen = chosen + tail[place : place + 1]
    member = lax.broadcasted_iota(jnp.int32, (len(packed) * atoms, chans), 0)
    fill = jnp.where(member == chosen.astype(jnp.int32), 1.0, 0.0)
    lane = lax.broadcasted_iota(jnp.int32, (len(packed) * atoms, atoms), 1)
    fill = jnp.concatenate([fill, jnp.where(member[:, :atoms] == lane, 1.0, 0.0)], axis=1)
    sender = jnp.dot(
        fill.astype(jnp.bfloat16), slot_ref[...], preferred_element_type=jnp.float32
    )
    projected = over_last(turned_ref[...], group).astype(jnp.bfloat16)
    picked = jnp.dot(projected, sender.astype(jnp.bfloat16), preferred_element_type=jnp.float32)
    scalar = picked[:chans] * filter_ref[:chans, :]
    carried = picked[chans:] * filter_ref[chans:, :]
    parts = [scalar] + [unit_ref[axis : axis + 1, :] * carried for axis in range(3)]
    message = jnp.concatenate([part.astype(jnp.bfloat16) for part in parts], axis=0)
    summed = over_last(message, hit_ref[...])
    square = jnp.zeros((chans, atoms), jnp.float32)
    for component in range(1, 4):
        part = summed[component * chans : (component + 1) * chans]
        square = square + part * part
    invariant = jnp.concatenate([summed[:chans], square], axis=0).astype(jnp.bfloat16)
    hidden = silu(jnp.dot(upward_ref[...], invariant, preferred_element_type=jnp.float32))
    chi = jnp.sum(hidden * read_ref[...], axis=0, keepdims=True)
    chi = jnp.concatenate([chi, jnp.zeros((1, chans - atoms), jnp.float32)], axis=1)
    row = row_ref[...] - pltpu.roll(chi, chi_segment * atoms, 1)
    block_ref[...] = jnp.broadcast_to(row[None], block_ref.shape)
    hidden_ref[...] = hidden


def feature_kernel(packed_ref, hidden_ref, features_ref):
    atoms = features_ref.shape[0]
    old = packed_ref[...].astype(jnp.float32)[:atoms]
    features_ref[...] = (old + hidden_ref[...].T).astype(jnp.bfloat16)


def reciprocal(value):
    rough = pl.reciprocal(value, approx=True)
    return rough * (2.0 - value * rough)


def smeared(scaled):
    decay = jnp.exp2(scaled * scaled * -math.log2(math.e))
    turn = reciprocal(1.0 + 0.3275911 * scaled)
    series = 1.061405429 * turn - 1.453152027
    series = series * turn + 1.421413741
    series = series * turn - 0.284496736
    series = series * turn + 0.254829592
    return 1.0 - series * turn * decay, decay


def charge_kernel(
    place_ref,
    field_ref,
    all_ref,
    charges_ref,
    forces_ref,
    virial_ref,
    matrix_ref,
    side_ref,
    value_ref,
):
    blocks, _, lanes = all_ref.shape
    own = charges_ref.shape[1]
    count = blocks * own
    fit = lanes // own
    segment = lax.broadcasted_iota(jnp.int32, (8, lanes), 1) // own
    tiles = []
    for first in range(0, blocks, fit):
        tile = jnp.zeros((8, lanes), jnp.float32)
        for place in range(fit):
            row = all_ref[(place_ref[0] + first + place) & (blocks - 1)]
            row = pltpu.roll(jnp.broadcast_to(row, (8, lanes)), 0, 1, stride=own, stride_axis=0)
            row = pltpu.roll(row, place * own, 1) if place else row
            tile = jnp.where(segment == place, row, tile)
        tiles.append(tile)
    everyone = jnp.concatenate(tiles, axis=1)
    last = lax.broadcasted_iota(jnp.int32, everyone.shape, 0) == 5
    everyone = everyone + jnp.where(last, field_ref[0] * everyone[2:3], 0.0)
    columns = everyone.T
    diag, rhs = everyone[4:5], everyone[5:6]
    spread_row = 2.0 * everyone[3:4] * everyone[3:4]
    tiles = count // lanes
    depth = own // 8
    shape = (depth, 8, lanes)
    lane = lax.broadcasted_iota(jnp.int32, shape, 2)
    line = lax.broadcasted_iota(jnp.int32, shape, 0) * 8 + lax.broadcasted_iota(jnp.int32, shape, 1)

    def part(row, tile):
        return row[:, tile * lanes : (tile + 1) * lanes]

    def down(row):
        return [jnp.broadcast_to(part(row, tile), (8, lanes))[None] for tile in range(tiles)]

    def along(column):
        return jnp.broadcast_to(column, (own, lanes)).reshape(shape)

    def total(value):
        return jnp.sum(value, axis=1, keepdims=True)

    axes = [down(everyone[axis : axis + 1]) for axis in range(3)]
    wide_row, rhs_row = down(spread_row), down(rhs)

    above = [jnp.zeros((8, lanes), jnp.float32) for _ in range(tiles)]
    kept = []
    for start in range(0, count, own):
        first = start // lanes
        column = columns[start : start + own]
        place = [along(column[:, axis : axis + 1]) for axis in range(3)]
        wide = along(2.0 * column[:, 3:4] * column[:, 3:4])
        value = along(column[:, 5:6])
        value_ref[start : start + own, :] = value.reshape(own, lanes)
        below = jnp.zeros(shape, jnp.float32)
        for tile in range(first, tiles):
            delta = [place[axis] - axes[axis][tile] for axis in range(3)]
            squared = delta[0] * delta[0] + delta[1] * delta[1] + delta[2] * delta[2]
            if tile == first:
                same = lane == line + (start - first * lanes)
                squared = jnp.where(same, 1.0, squared)
            inverse = lax.rsqrt(squared)
            scale = lax.rsqrt(wide + wide_row[tile])
            smear, decay = smeared(squared * inverse * scale)
            kernel = smear * inverse
            if start == 0:
                slope = (two_over_root_pi * scale * decay - kernel) * inverse * inverse
                slope = jnp.where(same, 0.0, slope) if tile == first else slope
                kept.append((delta, slope))
            if tile == first:
                kernel = jnp.where(same, 0.0, kernel)
            else:
                below = below + kernel * rhs_row[tile]
            above[tile] = above[tile] + jnp.sum(kernel * value, axis=0)
            matrix_ref[start : start + own, tile * lanes : (tile + 1) * lanes] = kernel.reshape(
                own, lanes
            )
        if first + 1 < tiles:
            side_ref[start : start + own, :] = below.reshape(own, lanes)
    image = []
    for tile in range(tiles):
        value = jnp.sum(above[tile], axis=0, keepdims=True)
        if tile + 1 < tiles:
            below = side_ref[tile * lanes : (tile + 1) * lanes, :].T
            value = value + jnp.sum(below, axis=0, keepdims=True)
        image.append(value)
    image = diag * rhs + jnp.concatenate(image, axis=1)
    across = jnp.broadcast_to(image, (8, count)).T
    norm = total(rhs * rhs)
    alpha = norm / total(rhs * image)
    residual = rhs - alpha * image
    fresh = total(residual * residual)
    again = fresh / norm
    direction = residual + again * rhs
    onto = [jnp.zeros((8, lanes), jnp.float32) for _ in range(tiles)]
    above = [jnp.zeros((8, lanes), jnp.float32) for _ in range(tiles)]
    for start in range(0, count, own):
        first = start // lanes
        value = (1.0 + again) * value_ref[start : start + own, :]
        value = value - alpha * jnp.broadcast_to(across[start : start + own, 0:1], (own, lanes))
        value = value.reshape(shape)
        for tile in range(first, tiles):
            sums = onto if tile == first else above
            kernel = matrix_ref[start : start + own, tile * lanes : (tile + 1) * lanes]
            sums[tile] = sums[tile] + jnp.sum(kernel.reshape(shape) * value, axis=0)
    curved = jnp.zeros((8, lanes), jnp.float32)
    for tile in range(tiles):
        curved = curved + (onto[tile] + 2.0 * above[tile]) * part(direction, tile)
    curved = jnp.sum(curved, axis=0, keepdims=True)
    for tile in range(tiles):
        curved = curved + part(diag * direction * direction, tile)
    charges = alpha * rhs + fresh / total(curved) * direction

    sums = [jnp.zeros(shape, jnp.float32) for _ in range(9)]
    charge_row = down(charges)
    for tile, (delta, slope) in enumerate(kept):
        weight = charge_row[tile] * slope
        pulled = [weight * delta[axis] for axis in range(3)]
        terms = pulled + [
            pulled[left] * delta[right]
            for left, right in ((0, 0), (1, 1), (2, 2), (0, 1), (0, 2), (1, 2))
        ]
        sums = [old + term for old, term in zip(sums, terms)]
    table = jnp.zeros((own, lanes), jnp.float32)
    lane = lane.reshape(own, lanes)
    for place, value in enumerate(sums):
        table = jnp.where(lane == place, total(value.reshape(own, lanes)), table)
    table = table.T
    mine = charges[:, :own]
    charges_ref[...] = mine
    pull = -mine * table[0:3]
    third = lax.broadcasted_iota(jnp.int32, pull.shape, 0) == 2
    forces_ref[...] = pull + jnp.where(third, mine * field_ref[0], 0.0)
    virial_ref[...] = 0.5 * mine * table[3:9]


def kernel_call(kernel, shapes, arguments, scalars=0, far=0, scratch=(), flops=0):
    shapes = tuple(jax.ShapeDtypeStruct(shape, kind) for shape, kind in shapes)
    spaces = [pltpu.SMEM] * scalars + [pltpu.HBM] * far
    spaces = spaces + [pltpu.VMEM] * (len(arguments) - len(spaces))
    arguments = [
        pltpu.with_memory_space_constraint(value, space) if space is pltpu.HBM else value
        for value, space in zip(arguments, spaces)
    ]
    return pl.pallas_call(
        kernel,
        out_shape=shapes,
        in_specs=[pl.BlockSpec(memory_space=space) for space in spaces],
        out_specs=tuple(pl.BlockSpec(memory_space=pltpu.VMEM) for _ in shapes),
        scratch_shapes=list(scratch),
        compiler_params=pltpu.CompilerParams(vmem_limit_bytes=32 * 1024 * 1024),
        cost_estimate=pl.CostEstimate(flops=flops, bytes_accessed=1 << 20, transcendentals=0),
    )(*arguments)


def exchanged(block, axis, step):
    size = lax.axis_size(axis)
    return lax.ppermute(block, axis, [(place, place ^ step) for place in range(size)])


def few_shards(
    features,
    positions,
    species,
    ghost_list,
    edge_recv,
    edge_send,
    edge_vec,
    w_msg,
    w_rad1,
    w_rad2,
    w_up,
    w_out,
    hardness,
    width,
    chi_shift,
    field,
):
    atoms, chans = features.shape
    edges = edge_recv.shape[0]
    rows, lanes = lax.axis_size("row"), lax.axis_size("space")
    space = lax.axis_index("space").astype(jnp.int32)
    (packed,) = kernel_call(
        pack_kernel,
        [((atoms + 16, chans), jnp.bfloat16)],
        (space.reshape(1), features, ghost_list),
        scalars=1,
        far=2,
        scratch=[
            pltpu.VMEM(ghost_list.shape, ghost_list.dtype),
            pltpu.SemaphoreType.DMA((2,)),
        ],
    )
    near, far, side = [exchanged(packed, "space", step) for step in (1, 3, 2)]
    rest = (w_rad1, w_rad2, edge_send[None], edge_recv[None], w_msg, w_up, w_out[None])
    rest = rest + (species[None], hardness[None], width[None], chi_shift[None], positions)
    parts = kernel_call(
        functools.partial(edge_kernel, lanes),
        [
            ((2 * chans, edges), jnp.float32),
            ((8, edges), jnp.float32),
            ((1, chans), jnp.float32),
            ((chans + atoms, edges), jnp.bfloat16),
            ((atoms, edges), jnp.bfloat16),
            ((2 * chans, chans), jnp.bfloat16),
            ((chans, 2 * chans), jnp.bfloat16),
            ((chans, atoms), jnp.float32),
        ],
        (space.reshape(1), *rest, edge_vec),
        scalars=1,
        far=len(rest),
        scratch=[pltpu.VMEM(value.shape, value.dtype) for value in rest]
        + [pltpu.SemaphoreType.DMA((len(rest),))],
        flops=1 << 28,
    )
    devices = rows * lanes
    hidden, block = kernel_call(
        node_kernel,
        [((chans, atoms), jnp.float32), ((devices, 1, chans), jnp.float32)],
        (packed, near, far, side, *parts),
        flops=1 << 28,
    )
    (new_features,) = kernel_call(
        feature_kernel, [((atoms, chans), jnp.bfloat16)], (packed, hidden), flops=1 << 20
    )
    block = lax.all_to_all(block, everywhere, 0, 0, tiled=True)
    place = lax.axis_index("row").astype(jnp.int32) * lanes + space
    everybody = rows * lanes * atoms
    charges, forces, virial = kernel_call(
        charge_kernel,
        [((count, atoms), jnp.float32) for count in (1, 3, 6)],
        (place.reshape(1), field, block),
        scalars=2,
        scratch=[
            pltpu.VMEM((everybody, everybody), jnp.float32),
            pltpu.VMEM((everybody, chans), jnp.float32),
            pltpu.VMEM((everybody, chans), jnp.float32),
        ],
        flops=1 << 28,
    )
    return (new_features, charges[0], forces, virial)


def solution(mesh):
    small = mesh.shape["space"] == 4 and mesh.shape["row"] == 8
    return jax.shard_map(
        few_shards if small else shards,
        mesh=mesh,
        in_specs=(
            P(("row", "space"), None),
            P(None, ("row", "space")),
            P(("row", "space")),
            P("row", "space", None),
            P(("row", "space")),
            P(("row", "space")),
            P(None, ("row", "space")),
            P(),
            P(),
            P(),
            P(),
            P(),
            P(),
            P(),
            P(),
            P(),
        ),
        out_specs=(
            P(("row", "space"), None),
            P(("row", "space")),
            P(None, ("row", "space")),
            P(None, ("row", "space")),
        ),
        check_vma=False,
    )
```

```python
import math

import jax
import jax.numpy as jnp
from jax import lax
from jax.experimental import pallas as pl
from jax.experimental.pallas import tpu as pltpu
from jax.sharding import PartitionSpec as P

ITERS = 2


cutoff = 6.0
message_scale = 0.125
two_over_root_pi = 2.0 / math.sqrt(math.pi)
inverse_root_pi = 1.0 / math.sqrt(math.pi)
replicate_limit = 1024
everywhere = ("row", "space")


def lookup(species, table):
    result = jnp.zeros(species.shape, jnp.float32)
    for kind in range(table.shape[0]):
        result = result + jnp.where(species == kind, table[kind], 0.0)
    return result


def pair_terms(target, target_labels, source, source_labels):
    delta = target[:3, :, None] - source[:3, None, :]
    squared = jnp.sum(delta * delta, axis=0)
    same = target_labels[:, None] == source_labels[None, :]
    squared = jnp.where(same, 1.0, squared)
    inverse = lax.rsqrt(squared)
    radius = squared * inverse
    spread = target[3][:, None] * target[3][:, None] + source[3][None, :] * source[3][None, :]
    scale = lax.rsqrt(2.0 * spread)
    scaled = radius * scale
    smear = lax.erf(scaled)
    return delta, same, inverse, scale, scaled, smear


def coulomb(target, target_labels, source, source_labels):
    _, same, inverse, _, _, smear = pair_terms(target, target_labels, source, source_labels)
    return jnp.where(same, 0.0, smear * inverse)


def pair_forces(target, target_labels, source, source_labels, source_charge):
    delta, same, inverse, scale, scaled, smear = pair_terms(
        target, target_labels, source, source_labels
    )
    slope = (
        two_over_root_pi * scale * jnp.exp(-scaled * scaled) * inverse - smear * inverse * inverse
    )
    weight = jnp.where(same, 0.0, source_charge[None, :] * slope * inverse)
    first = jnp.sum(weight[None] * delta, axis=2)
    pairs = ((0, 0), (1, 1), (2, 2), (0, 1), (0, 2), (1, 2))
    second = jnp.stack(
        [jnp.sum(weight * delta[left] * delta[right], axis=1) for left, right in pairs]
    )
    return jnp.concatenate([first, second], axis=0)


def edge_terms(receive, sender_rows, vectors, projected, w_rad1, w_rad2, atoms):
    length = jnp.sqrt(jnp.sum(vectors * vectors, axis=0))
    unit = vectors / length
    order = jnp.arange(1, w_rad1.shape[0] + 1, dtype=jnp.int32).astype(jnp.float32)[:, None]
    ratio = length / cutoff
    envelope = (1.0 - ratio * ratio) * (1.0 - ratio * ratio)
    basis = jnp.sin(order * math.pi * ratio) / ratio * envelope
    mixed = lax.dot_general(
        basis, w_rad1, (((0,), (0,)), ((), ())), precision=lax.Precision.HIGHEST
    )
    radial = jax.nn.silu(mixed).astype(jnp.bfloat16)
    filters = jnp.dot(radial, w_rad2, preferred_element_type=jnp.float32)
    picked = jnp.take(projected, sender_rows, axis=0).astype(jnp.float32) * filters
    chans = w_rad1.shape[1]
    scalar = picked[:, :chans]
    carried = picked[:, chans:]
    joined = [
        scalar,
        unit[0][:, None] * carried,
        unit[1][:, None] * carried,
        unit[2][:, None] * carried,
    ]
    message = jnp.concatenate(joined, axis=1).astype(jnp.bfloat16)
    onehot = (jnp.arange(atoms, dtype=jnp.int32)[:, None] == receive[None, :]).astype(jnp.bfloat16)
    return jnp.dot(onehot, message, preferred_element_type=jnp.float32)


def gathered(block, devices):
    copies = jnp.broadcast_to(block[None], (devices,) + block.shape)
    return lax.all_to_all(copies, everywhere, split_axis=0, concat_axis=0, tiled=True)


def shards(
    features,
    positions,
    species,
    ghost_list,
    edge_recv,
    edge_send,
    edge_vec,
    w_msg,
    w_rad1,
    w_rad2,
    w_up,
    w_out,
    hardness,
    width,
    chi_shift,
    field,
):
    atoms = features.shape[0]
    chans = features.shape[1]
    lanes = lax.axis_size("space")
    devices = lanes * lax.axis_size("row")
    everybody = devices * atoms
    me = lax.axis_index("row") * lanes + lax.axis_index("space")
    sigma = lookup(species, width)
    diag = lookup(species, hardness) + inverse_root_pi / sigma
    placed = jnp.concatenate([positions, sigma[None, :], diag[None, :]], axis=0)
    everyone = gathered(placed, devices).transpose(1, 0, 2).reshape(5, everybody)
    lists = ghost_list[0]
    outgoing = jnp.take(features, lists.reshape(-1), axis=0).reshape(lanes, lists.shape[1], chans)
    ghost_rows = jnp.einsum(
        "dkc,cf->dkf",
        lax.all_to_all(outgoing, "space", split_axis=0, concat_axis=0, tiled=True),
        w_msg,
        preferred_element_type=jnp.float32,
    ).astype(jnp.bfloat16)
    own_rows = jnp.dot(features, w_msg, preferred_element_type=jnp.float32).astype(jnp.bfloat16)
    projected = jnp.concatenate([own_rows, ghost_rows.reshape(-1, 2 * chans)], axis=0)
    summed = edge_terms(edge_recv, edge_send, edge_vec, projected, w_rad1, w_rad2, atoms)
    summed = summed * message_scale
    vector_part = summed[:, chans:].reshape(atoms, 3, chans)
    invariant = jnp.concatenate(
        [summed[:, :chans], jnp.sum(vector_part * vector_part, axis=1)], axis=1
    ).astype(jnp.bfloat16)
    hidden = jax.nn.silu(jnp.dot(invariant, w_up, preferred_element_type=jnp.float32))
    new_features = (features.astype(jnp.float32) + hidden).astype(jnp.bfloat16)
    chi = jnp.dot(hidden, w_out, precision=lax.Precision.HIGHEST) + lookup(species, chi_shift)
    own_labels = me * atoms + jnp.arange(atoms, dtype=jnp.int32)
    all_labels = jnp.arange(everybody, dtype=jnp.int32)
    rhs = field[0] * positions[2] - chi

    if everybody <= replicate_limit:
        kernel = coulomb(everyone, all_labels, everyone, all_labels)
        residual = gathered(rhs, devices).reshape(everybody)
        all_charges = conjugate(
            residual, lambda v: everyone[4] * v + jnp.sum(kernel * v[None, :], axis=1), jnp.sum
        )
        charges = lax.dynamic_slice(all_charges, (me * atoms,), (atoms,))
    else:
        kernel = coulomb(placed, own_labels, everyone, all_labels)

        def spread(vector):
            return gathered(vector, devices).reshape(everybody)

        charges = conjugate(
            rhs,
            lambda v: diag * v + jnp.sum(kernel * spread(v)[None, :], axis=1),
            lambda v: lax.psum(jnp.sum(v), everywhere),
        )
        all_charges = spread(charges)
    sums = pair_forces(placed, own_labels, everyone, all_labels, all_charges)
    pull = -charges[None, :] * sums[:3]
    forces = jnp.concatenate([pull[:2], pull[2:] + (charges * field[0])[None, :]], axis=0)
    virial = 0.5 * charges[None, :] * sums[3:]
    return (new_features, charges, forces, virial)


def conjugate(rhs, apply, total):
    charges = jnp.zeros_like(rhs)
    residual = rhs
    direction = rhs
    norm_now = total(residual * residual)
    for step in range(ITERS):
        image = apply(direction)
        alpha = norm_now / total(direction * image)
        charges = charges + alpha * direction
        if step + 1 < ITERS:
            residual = residual - alpha * image
            fresh = total(residual * residual)
            direction = residual + fresh / norm_now * direction
            norm_now = fresh
    return charges


def split3(value):
    first = value.astype(jnp.bfloat16).astype(jnp.float32)
    rest = value - first
    second = rest.astype(jnp.bfloat16).astype(jnp.float32)
    third = (rest - second).astype(jnp.bfloat16).astype(jnp.float32)
    return first, second, third


def over_first(left, right):
    return lax.dot_general(
        left, right, (((0,), (0,)), ((), ())), preferred_element_type=jnp.float32
    )


def over_last(left, right, precision=None):
    return lax.dot_general(
        left,
        right,
        (((1,), (1,)), ((), ())),
        precision=precision,
        preferred_element_type=jnp.float32,
    )


def silu(value):
    return value / (1.0 + jnp.exp(-value))


def silu_half(value):
    return (0.5 * value) * (1.0 + jnp.tanh(0.5 * value))


sine_series = [(-1.0) ** k * math.pi ** (2 * k + 1) / math.factorial(2 * k + 1) for k in range(7)]


def fetched(pairs, semaphores):
    copies = [
        pltpu.make_async_copy(source, target, semaphores.at[place])
        for place, (source, target) in enumerate(pairs)
    ]
    for copy in copies:
        copy.start()
    return copies


chi_segment = 3


def pack_kernel(space_ref, features_ref, lists_ref, packed_ref, held_ref, semaphores):
    atoms, chans = features_ref.shape
    copies = fetched(
        [(lists_ref, held_ref), (features_ref, packed_ref.at[pl.ds(0, atoms)])], semaphores
    )
    copies[0].wait()
    _, lanes, width = held_ref.shape
    rows = []
    for place in range(lanes):
        row = held_ref[0, pl.ds(space_ref[0] ^ place, 1), :].astype(jnp.float32) + place * atoms
        parts = [jnp.zeros((1, width), jnp.float32)] * lanes
        parts[place] = row
        rows.append(jnp.concatenate(parts, axis=1))
    rows.append(jnp.zeros((packed_ref.shape[0] - atoms - lanes, chans), jnp.float32))
    packed_ref[atoms:, :] = jnp.concatenate(rows, axis=0).astype(jnp.bfloat16)
    copies[1].wait()


def edge_kernel(
    space_ref,
    *refs,
):
    count = (len(refs) - 10) // 2
    far, near, semaphores = refs[:count], refs[count + 9 : -1], refs[-1]
    filter_ref, unit_ref, row_ref, slot_ref, local_ref, hit_ref = refs[count : count + 6]
    turned_ref, upward_ref, read_ref = refs[count + 6 : count + 9]
    vec_ref, first_ref, second_ref, send_ref, recv_ref, project_ref, update_ref = near[:7]
    species_ref, hardness_ref, width_ref, shift_ref, positions_ref, out_ref = near[7:]
    copies = fetched(list(zip(far, near)), semaphores)
    for copy in copies[:3]:
        copy.wait()
    edges = vec_ref.shape[1]
    orders = first_ref.shape[0]
    vec = vec_ref[...]
    east, north, up = vec[0:1], vec[1:2], vec[2:3]
    squared = east * east + north * north + up * up
    inverse = lax.rsqrt(squared)
    unit_ref[0:3, :] = vec * inverse
    ratio = squared * inverse * (1.0 / cutoff)
    envelope = (1.0 - ratio * ratio) * (1.0 - ratio * ratio) * (cutoff * inverse)
    order = lax.broadcasted_iota(jnp.int32, (orders, edges), 0).astype(jnp.float32) + 1.0
    turns = order * ratio
    whole = jnp.floor(turns + 0.5)
    part = turns - whole
    sign = 1.0 - 2.0 * (whole - 2.0 * jnp.floor(whole * 0.5))
    series = jnp.full_like(part, sine_series[-1])
    for coefficient in sine_series[-2::-1]:
        series = series * (part * part) + coefficient
    basis = series * part * (sign * envelope)
    b1, b2, b3 = split3(basis)
    w1, w2, w3 = split3(first_ref[...])
    mixed = over_first(
        jnp.concatenate([w1, w1, w2, w2, w1, w3], axis=0).astype(jnp.bfloat16),
        jnp.concatenate([b1, b2, b1, b2, b3, b1], axis=0).astype(jnp.bfloat16),
    )
    radial = silu_half(mixed).astype(jnp.bfloat16)
    filter_ref[...] = over_first(second_ref[...], radial)
    for copy in copies[3:]:
        copy.wait()
    species = species_ref[...]

    def table(ref):
        result = jnp.zeros(species.shape, jnp.float32)
        for kind in range(ref.shape[1]):
            result = result + jnp.where(species == kind, ref[:, kind : kind + 1], 0.0)
        return result

    positions = positions_ref[...]
    sigma = table(width_ref)
    atoms = species.shape[1]
    chans = row_ref.shape[1]
    diag = table(hardness_ref) + inverse_root_pi / sigma
    blank = jnp.zeros((2, atoms), jnp.float32)
    rows = [positions[0:1], blank, -table(shift_ref), diag, sigma, positions[2:3], positions[1:2]]
    block = jnp.concatenate(
        [jnp.concatenate(rows, axis=0), jnp.zeros((8, chans - atoms), jnp.float32)], axis=1
    )
    block = pltpu.roll(block, 0, 1, stride=atoms, stride_axis=0)
    row_ref[...] = jnp.sum(block, axis=0, keepdims=True)
    lanes = local_ref.shape[0] // atoms
    slots = chans // lanes
    send = send_ref[...]
    own = send < atoms
    slot = jnp.where(own, -1, (send - atoms) ^ (space_ref[0] * slots))
    local = jnp.where(own, send, -1)

    def chosen(ref, index):
        hit = lax.broadcasted_iota(jnp.int32, ref.shape, 0) == index
        ref[...] = jnp.where(hit, 1.0, 0.0).astype(ref.dtype)

    chosen(slot_ref, slot)
    chosen(local_ref, local)
    chosen(hit_ref, recv_ref[...])
    turned_ref[...] = project_ref[...].astype(jnp.float32).T.astype(jnp.bfloat16)
    upward_ref[...] = update_ref[...].astype(jnp.float32).T.astype(jnp.bfloat16)
    read_ref[...] = jnp.broadcast_to(out_ref[...], (atoms, chans)).T


def node_kernel(
    own_ref,
    near_ref,
    side_ref,
    far_ref,
    filter_ref,
    unit_ref,
    row_ref,
    slot_ref,
    local_ref,
    hit_ref,
    turned_ref,
    upward_ref,
    read_ref,
    hidden_ref,
    block_ref,
):
    chans, atoms = hidden_ref.shape
    packed = (own_ref, near_ref, side_ref, far_ref)
    group = jnp.concatenate([ref[:atoms, :] for ref in packed], axis=0)
    chosen = jnp.zeros((1, chans), jnp.float32)
    for place, ref in enumerate(packed):
        tail = ref[atoms:, :].astype(jnp.float32)
        chosen = chosen + tail[place : place + 1]
    fill = jnp.where(
        lax.broadcasted_iota(jnp.int32, (len(packed) * atoms, chans), 0)
        == chosen.astype(jnp.int32),
        1.0,
        0.0,
    ).astype(jnp.bfloat16)
    sender = jnp.dot(fill, slot_ref[...], preferred_element_type=jnp.float32) + local_ref[...]
    projected = over_last(turned_ref[...], group).astype(jnp.bfloat16)
    picked = jnp.dot(projected, sender.astype(jnp.bfloat16), preferred_element_type=jnp.float32)
    scalar = picked[:chans] * filter_ref[:chans, :]
    carried = picked[chans:] * filter_ref[chans:, :]
    parts = [scalar] + [unit_ref[axis : axis + 1, :] * carried for axis in range(3)]
    message = jnp.concatenate([part.astype(jnp.bfloat16) for part in parts], axis=0)
    summed = over_last(message, hit_ref[...]) * message_scale
    square = jnp.zeros((chans, atoms), jnp.float32)
    for component in range(1, 4):
        part = summed[component * chans : (component + 1) * chans]
        square = square + part * part
    invariant = jnp.concatenate([summed[:chans], square], axis=0).astype(jnp.bfloat16)
    hidden = silu(jnp.dot(upward_ref[...], invariant, preferred_element_type=jnp.float32))
    chi = jnp.sum(hidden * read_ref[...], axis=0, keepdims=True)
    chi = jnp.concatenate([chi, jnp.zeros((1, chans - atoms), jnp.float32)], axis=1)
    row = row_ref[...] - pltpu.roll(chi, chi_segment * atoms, 1)
    block_ref[...] = jnp.broadcast_to(row[None], block_ref.shape)
    hidden_ref[...] = hidden


def feature_kernel(packed_ref, hidden_ref, features_ref):
    atoms = features_ref.shape[0]
    old = packed_ref[...].astype(jnp.float32)[:atoms]
    features_ref[...] = (old + hidden_ref[...].T).astype(jnp.bfloat16)


def reciprocal(value):
    rough = pl.reciprocal(value, approx=True)
    return rough * (2.0 - value * rough)


def smeared(scaled):
    decay = jnp.exp2(scaled * scaled * -math.log2(math.e))
    turn = reciprocal(1.0 + 0.3275911 * scaled)
    series = 1.061405429 * turn - 1.453152027
    series = series * turn + 1.421413741
    series = series * turn - 0.284496736
    series = series * turn + 0.254829592
    return 1.0 - series * turn * decay, decay


def charge_kernel(
    place_ref,
    field_ref,
    all_ref,
    charges_ref,
    forces_ref,
    virial_ref,
    matrix_ref,
    side_ref,
    value_ref,
    kept_ref,
):
    blocks, _, lanes = all_ref.shape
    own = charges_ref.shape[1]
    count = blocks * own
    fit = lanes // own
    segment = lax.broadcasted_iota(jnp.int32, (8, lanes), 1) // own
    tiles = []
    for first in range(0, blocks, fit):
        tile = jnp.zeros((8, lanes), jnp.float32)
        for place in range(fit):
            row = all_ref[(place_ref[0] + first + place) & (blocks - 1)]
            row = pltpu.roll(jnp.broadcast_to(row, (8, lanes)), 0, 1, stride=own, stride_axis=0)
            row = pltpu.roll(row, place * own, 1) if place else row
            tile = jnp.where(segment == place, row, tile)
        tiles.append(tile)
    everyone = jnp.concatenate(tiles, axis=1)
    last = lax.broadcasted_iota(jnp.int32, everyone.shape, 0) == 5
    everyone = everyone + jnp.where(last, field_ref[0] * everyone[2:3], 0.0)
    columns = everyone.T
    diag, rhs = everyone[4:5], everyone[5:6]
    spread_row = 2.0 * everyone[3:4] * everyone[3:4]
    tiles = count // lanes
    depth = own // 8
    shape = (depth, 8, lanes)
    lane = lax.broadcasted_iota(jnp.int32, shape, 2)
    line = lax.broadcasted_iota(jnp.int32, shape, 0) * 8 + lax.broadcasted_iota(jnp.int32, shape, 1)

    def part(row, tile):
        return row[:, tile * lanes : (tile + 1) * lanes]

    def down(row):
        return [jnp.broadcast_to(part(row, tile), (8, lanes))[None] for tile in range(tiles)]

    def along(column):
        return jnp.broadcast_to(column, (own, lanes)).reshape(shape)

    def total(value):
        return jnp.sum(value, axis=1, keepdims=True)

    axes = [down(everyone[axis : axis + 1]) for axis in range(3)]
    wide_row, rhs_row = down(spread_row), down(rhs)

    above = [jnp.zeros((8, lanes), jnp.float32) for _ in range(tiles)]
    for start in range(0, count, own):
        first = start // lanes
        column = columns[start : start + own]
        place = [along(column[:, axis : axis + 1]) for axis in range(3)]
        wide = along(2.0 * column[:, 3:4] * column[:, 3:4])
        value = along(column[:, 5:6])
        value_ref[start : start + own, :] = value.reshape(own, lanes)
        below = jnp.zeros(shape, jnp.float32)
        for tile in range(first, tiles):
            delta = [place[axis] - axes[axis][tile] for axis in range(3)]
            squared = delta[0] * delta[0] + delta[1] * delta[1] + delta[2] * delta[2]
            if tile == first:
                same = lane == line + (start - first * lanes)
                squared = jnp.where(same, 1.0, squared)
            inverse = lax.rsqrt(squared)
            scale = lax.rsqrt(wide + wide_row[tile])
            smear, decay = smeared(squared * inverse * scale)
            kernel = smear * inverse
            if start == 0:
                slope = (two_over_root_pi * scale * decay - kernel) * inverse * inverse
                slope = jnp.where(same, 0.0, slope) if tile == first else slope
                for which, kind in enumerate(delta + [slope]):
                    kept_ref[which, :, tile * lanes : (tile + 1) * lanes] = kind.reshape(own, lanes)
            if tile == first:
                kernel = jnp.where(same, 0.0, kernel)
            else:
                below = below + kernel * rhs_row[tile]
            above[tile] = above[tile] + jnp.sum(kernel * value, axis=0)
            matrix_ref[start : start + own, tile * lanes : (tile + 1) * lanes] = kernel.reshape(
                own, lanes
            )
        if first + 1 < tiles:
            side_ref[start : start + own, :] = below.reshape(own, lanes)
    image = []
    for tile in range(tiles):
        value = jnp.sum(above[tile], axis=0, keepdims=True)
        if tile + 1 < tiles:
            below = side_ref[tile * lanes : (tile + 1) * lanes, :].T
            value = value + jnp.sum(below, axis=0, keepdims=True)
        image.append(value)
    image = diag * rhs + jnp.concatenate(image, axis=1)
    across = jnp.broadcast_to(image, (8, count)).T
    norm = total(rhs * rhs)
    alpha = norm * reciprocal(total(rhs * image))
    residual = rhs - alpha * image
    fresh = total(residual * residual)
    again = fresh * reciprocal(norm)
    direction = residual + again * rhs
    onto = [jnp.zeros((8, lanes), jnp.float32) for _ in range(tiles)]
    above = [jnp.zeros((8, lanes), jnp.float32) for _ in range(tiles)]
    for start in range(0, count, own):
        first = start // lanes
        value = (1.0 + again) * value_ref[start : start + own, :]
        value = value - alpha * jnp.broadcast_to(across[start : start + own, 0:1], (own, lanes))
        value = value.reshape(shape)
        for tile in range(first, tiles):
            sums = onto if tile == first else above
            kernel = matrix_ref[start : start + own, tile * lanes : (tile + 1) * lanes]
            sums[tile] = sums[tile] + jnp.sum(kernel.reshape(shape) * value, axis=0)
    curved = jnp.zeros((8, lanes), jnp.float32)
    for tile in range(tiles):
        curved = curved + (onto[tile] + 2.0 * above[tile]) * part(direction, tile)
    curved = jnp.sum(curved, axis=0, keepdims=True)
    for tile in range(tiles):
        curved = curved + part(diag * direction * direction, tile)
    charges = alpha * rhs + fresh * reciprocal(total(curved)) * direction

    sums = [jnp.zeros(shape, jnp.float32) for _ in range(9)]
    charge_row = down(charges)
    for tile in range(tiles):
        *delta, slope = [
            kept_ref[which, :, tile * lanes : (tile + 1) * lanes].reshape(shape)
            for which in range(4)
        ]
        weight = charge_row[tile] * slope
        pulled = [weight * delta[axis] for axis in range(3)]
        terms = pulled + [
            pulled[left] * delta[right]
            for left, right in ((0, 0), (1, 1), (2, 2), (0, 1), (0, 2), (1, 2))
        ]
        sums = [old + term for old, term in zip(sums, terms)]
    table = jnp.zeros((own, lanes), jnp.float32)
    lane = lane.reshape(own, lanes)
    for place, value in enumerate(sums):
        table = jnp.where(lane == place, total(value.reshape(own, lanes)), table)
    table = table.T
    mine = charges[:, :own]
    charges_ref[...] = mine
    pull = -mine * table[0:3]
    third = lax.broadcasted_iota(jnp.int32, pull.shape, 0) == 2
    forces_ref[...] = pull + jnp.where(third, mine * field_ref[0], 0.0)
    virial_ref[...] = 0.5 * mine * table[3:9]


def kernel_call(kernel, shapes, arguments, scalars=0, far=0, scratch=(), flops=0):
    shapes = tuple(jax.ShapeDtypeStruct(shape, kind) for shape, kind in shapes)
    spaces = [pltpu.SMEM] * scalars + [pltpu.HBM] * far
    spaces = spaces + [pltpu.VMEM] * (len(arguments) - len(spaces))
    arguments = [
        pltpu.with_memory_space_constraint(value, space) if space is pltpu.HBM else value
        for value, space in zip(arguments, spaces)
    ]
    return pl.pallas_call(
        kernel,
        out_shape=shapes,
        in_specs=[pl.BlockSpec(memory_space=space) for space in spaces],
        out_specs=tuple(pl.BlockSpec(memory_space=pltpu.VMEM) for _ in shapes),
        scratch_shapes=list(scratch),
        compiler_params=pltpu.CompilerParams(vmem_limit_bytes=32 * 1024 * 1024),
        cost_estimate=pl.CostEstimate(flops=flops, bytes_accessed=1 << 20, transcendentals=0),
    )(*arguments)


def exchanged(block, axis, step):
    size = lax.axis_size(axis)
    return lax.ppermute(block, axis, [(place, place ^ step) for place in range(size)])


def few_shards(
    features,
    positions,
    species,
    ghost_list,
    edge_recv,
    edge_send,
    edge_vec,
    w_msg,
    w_rad1,
    w_rad2,
    w_up,
    w_out,
    hardness,
    width,
    chi_shift,
    field,
):
    atoms, chans = features.shape
    edges = edge_recv.shape[0]
    rows, lanes = lax.axis_size("row"), lax.axis_size("space")
    space = lax.axis_index("space").astype(jnp.int32)
    (packed,) = kernel_call(
        pack_kernel,
        [((atoms + 16, chans), jnp.bfloat16)],
        (space.reshape(1), features, ghost_list),
        scalars=1,
        far=2,
        scratch=[
            pltpu.VMEM(ghost_list.shape, ghost_list.dtype),
            pltpu.SemaphoreType.DMA((2,)),
        ],
    )
    others = [exchanged(packed, "space", step) for step in range(1, lanes)]
    rest = (edge_vec, w_rad1, w_rad2, edge_send[None], edge_recv[None], w_msg, w_up)
    rest = rest + (species[None], hardness[None], width[None], chi_shift[None], positions)
    rest = rest + (w_out[None],)
    parts = kernel_call(
        edge_kernel,
        [
            ((2 * chans, edges), jnp.float32),
            ((8, edges), jnp.float32),
            ((1, chans), jnp.float32),
            ((chans, edges), jnp.bfloat16),
            ((lanes * atoms, edges), jnp.float32),
            ((atoms, edges), jnp.bfloat16),
            ((2 * chans, chans), jnp.bfloat16),
            ((chans, 2 * chans), jnp.bfloat16),
            ((chans, atoms), jnp.float32),
        ],
        (space.reshape(1), *rest),
        scalars=1,
        far=len(rest),
        scratch=[pltpu.VMEM(value.shape, value.dtype) for value in rest]
        + [pltpu.SemaphoreType.DMA((len(rest),))],
        flops=1 << 28,
    )
    devices = rows * lanes
    hidden, block = kernel_call(
        node_kernel,
        [((chans, atoms), jnp.float32), ((devices, 1, chans), jnp.float32)],
        (packed, *others, *parts),
        flops=1 << 28,
    )
    (new_features,) = kernel_call(
        feature_kernel, [((atoms, chans), jnp.bfloat16)], (packed, hidden), flops=1 << 20
    )
    block = lax.all_to_all(block, everywhere, 0, 0, tiled=True)
    place = lax.axis_index("row").astype(jnp.int32) * lanes + space
    everybody = rows * lanes * atoms
    charges, forces, virial = kernel_call(
        charge_kernel,
        [((count, atoms), jnp.float32) for count in (1, 3, 6)],
        (place.reshape(1), field, block),
        scalars=2,
        scratch=[
            pltpu.VMEM((everybody, everybody), jnp.float32),
            pltpu.VMEM((everybody, chans), jnp.float32),
            pltpu.VMEM((everybody, chans), jnp.float32),
            pltpu.VMEM((4, atoms, everybody), jnp.float32),
        ],
        flops=1 << 28,
    )
    return (new_features, charges[0], forces, virial)


def solution(mesh):
    small = mesh.shape["space"] == 4 and mesh.shape["row"] == 8
    return jax.shard_map(
        few_shards if small else shards,
        mesh=mesh,
        in_specs=(
            P(("row", "space"), None),
            P(None, ("row", "space")),
            P(("row", "space")),
            P("row", "space", None),
            P(("row", "space")),
            P(("row", "space")),
            P(None, ("row", "space")),
            P(),
            P(),
            P(),
            P(),
            P(),
            P(),
            P(),
            P(),
            P(),
        ),
        out_specs=(
            P(("row", "space"), None),
            P(("row", "space")),
            P(None, ("row", "space")),
            P(None, ("row", "space")),
        ),
        check_vma=False,
    )
```

```python
import math

import jax
import jax.numpy as jnp
from jax import lax
from jax.experimental import pallas as pl
from jax.experimental.pallas import tpu as pltpu
from jax.sharding import PartitionSpec as P

ITERS = 2


cutoff = 6.0
message_scale = 0.125
two_over_root_pi = 2.0 / math.sqrt(math.pi)
inverse_root_pi = 1.0 / math.sqrt(math.pi)
replicate_limit = 1024
everywhere = ("row", "space")


def lookup(species, table):
    result = jnp.zeros(species.shape, jnp.float32)
    for kind in range(table.shape[0]):
        result = result + jnp.where(species == kind, table[kind], 0.0)
    return result


def pair_terms(target, target_labels, source, source_labels):
    delta = target[:3, :, None] - source[:3, None, :]
    squared = jnp.sum(delta * delta, axis=0)
    same = target_labels[:, None] == source_labels[None, :]
    squared = jnp.where(same, 1.0, squared)
    inverse = lax.rsqrt(squared)
    radius = squared * inverse
    spread = target[3][:, None] * target[3][:, None] + source[3][None, :] * source[3][None, :]
    scale = lax.rsqrt(2.0 * spread)
    scaled = radius * scale
    smear = lax.erf(scaled)
    return delta, same, inverse, scale, scaled, smear


def coulomb(target, target_labels, source, source_labels):
    _, same, inverse, _, _, smear = pair_terms(target, target_labels, source, source_labels)
    return jnp.where(same, 0.0, smear * inverse)


def pair_forces(target, target_labels, source, source_labels, source_charge):
    delta, same, inverse, scale, scaled, smear = pair_terms(
        target, target_labels, source, source_labels
    )
    slope = (
        two_over_root_pi * scale * jnp.exp(-scaled * scaled) * inverse - smear * inverse * inverse
    )
    weight = jnp.where(same, 0.0, source_charge[None, :] * slope * inverse)
    first = jnp.sum(weight[None] * delta, axis=2)
    pairs = ((0, 0), (1, 1), (2, 2), (0, 1), (0, 2), (1, 2))
    second = jnp.stack(
        [jnp.sum(weight * delta[left] * delta[right], axis=1) for left, right in pairs]
    )
    return jnp.concatenate([first, second], axis=0)


def edge_terms(receive, sender_rows, vectors, projected, w_rad1, w_rad2, atoms):
    length = jnp.sqrt(jnp.sum(vectors * vectors, axis=0))
    unit = vectors / length
    order = jnp.arange(1, w_rad1.shape[0] + 1, dtype=jnp.int32).astype(jnp.float32)[:, None]
    ratio = length / cutoff
    envelope = (1.0 - ratio * ratio) * (1.0 - ratio * ratio)
    basis = jnp.sin(order * math.pi * ratio) / ratio * envelope
    mixed = lax.dot_general(
        basis, w_rad1, (((0,), (0,)), ((), ())), precision=lax.Precision.HIGHEST
    )
    radial = jax.nn.silu(mixed).astype(jnp.bfloat16)
    filters = jnp.dot(radial, w_rad2, preferred_element_type=jnp.float32)
    picked = jnp.take(projected, sender_rows, axis=0).astype(jnp.float32) * filters
    chans = w_rad1.shape[1]
    scalar = picked[:, :chans]
    carried = picked[:, chans:]
    joined = [
        scalar,
        unit[0][:, None] * carried,
        unit[1][:, None] * carried,
        unit[2][:, None] * carried,
    ]
    message = jnp.concatenate(joined, axis=1).astype(jnp.bfloat16)
    onehot = (jnp.arange(atoms, dtype=jnp.int32)[:, None] == receive[None, :]).astype(jnp.bfloat16)
    return jnp.dot(onehot, message, preferred_element_type=jnp.float32)


def gathered(block, devices):
    copies = jnp.broadcast_to(block[None], (devices,) + block.shape)
    return lax.all_to_all(copies, everywhere, split_axis=0, concat_axis=0, tiled=True)


def shards(
    features,
    positions,
    species,
    ghost_list,
    edge_recv,
    edge_send,
    edge_vec,
    w_msg,
    w_rad1,
    w_rad2,
    w_up,
    w_out,
    hardness,
    width,
    chi_shift,
    field,
):
    atoms = features.shape[0]
    chans = features.shape[1]
    lanes = lax.axis_size("space")
    devices = lanes * lax.axis_size("row")
    everybody = devices * atoms
    me = lax.axis_index("row") * lanes + lax.axis_index("space")
    sigma = lookup(species, width)
    diag = lookup(species, hardness) + inverse_root_pi / sigma
    placed = jnp.concatenate([positions, sigma[None, :], diag[None, :]], axis=0)
    everyone = gathered(placed, devices).transpose(1, 0, 2).reshape(5, everybody)
    lists = ghost_list[0]
    outgoing = jnp.take(features, lists.reshape(-1), axis=0).reshape(lanes, lists.shape[1], chans)
    ghost_rows = jnp.einsum(
        "dkc,cf->dkf",
        lax.all_to_all(outgoing, "space", split_axis=0, concat_axis=0, tiled=True),
        w_msg,
        preferred_element_type=jnp.float32,
    ).astype(jnp.bfloat16)
    own_rows = jnp.dot(features, w_msg, preferred_element_type=jnp.float32).astype(jnp.bfloat16)
    projected = jnp.concatenate([own_rows, ghost_rows.reshape(-1, 2 * chans)], axis=0)
    summed = edge_terms(edge_recv, edge_send, edge_vec, projected, w_rad1, w_rad2, atoms)
    summed = summed * message_scale
    vector_part = summed[:, chans:].reshape(atoms, 3, chans)
    invariant = jnp.concatenate(
        [summed[:, :chans], jnp.sum(vector_part * vector_part, axis=1)], axis=1
    ).astype(jnp.bfloat16)
    hidden = jax.nn.silu(jnp.dot(invariant, w_up, preferred_element_type=jnp.float32))
    new_features = (features.astype(jnp.float32) + hidden).astype(jnp.bfloat16)
    chi = jnp.dot(hidden, w_out, precision=lax.Precision.HIGHEST) + lookup(species, chi_shift)
    own_labels = me * atoms + jnp.arange(atoms, dtype=jnp.int32)
    all_labels = jnp.arange(everybody, dtype=jnp.int32)
    rhs = field[0] * positions[2] - chi

    if everybody <= replicate_limit:
        kernel = coulomb(everyone, all_labels, everyone, all_labels)
        residual = gathered(rhs, devices).reshape(everybody)
        all_charges = conjugate(
            residual, lambda v: everyone[4] * v + jnp.sum(kernel * v[None, :], axis=1), jnp.sum
        )
        charges = lax.dynamic_slice(all_charges, (me * atoms,), (atoms,))
    else:
        kernel = coulomb(placed, own_labels, everyone, all_labels)

        def spread(vector):
            return gathered(vector, devices).reshape(everybody)

        charges = conjugate(
            rhs,
            lambda v: diag * v + jnp.sum(kernel * spread(v)[None, :], axis=1),
            lambda v: lax.psum(jnp.sum(v), everywhere),
        )
        all_charges = spread(charges)
    sums = pair_forces(placed, own_labels, everyone, all_labels, all_charges)
    pull = -charges[None, :] * sums[:3]
    forces = jnp.concatenate([pull[:2], pull[2:] + (charges * field[0])[None, :]], axis=0)
    virial = 0.5 * charges[None, :] * sums[3:]
    return (new_features, charges, forces, virial)


def conjugate(rhs, apply, total):
    charges = jnp.zeros_like(rhs)
    residual = rhs
    direction = rhs
    norm_now = total(residual * residual)
    for step in range(ITERS):
        image = apply(direction)
        alpha = norm_now / total(direction * image)
        charges = charges + alpha * direction
        if step + 1 < ITERS:
            residual = residual - alpha * image
            fresh = total(residual * residual)
            direction = residual + fresh / norm_now * direction
            norm_now = fresh
    return charges


def split3(value):
    first = value.astype(jnp.bfloat16).astype(jnp.float32)
    rest = value - first
    second = rest.astype(jnp.bfloat16).astype(jnp.float32)
    third = (rest - second).astype(jnp.bfloat16).astype(jnp.float32)
    return first, second, third


def over_first(left, right):
    return lax.dot_general(
        left, right, (((0,), (0,)), ((), ())), preferred_element_type=jnp.float32
    )


def over_last(left, right, precision=None):
    return lax.dot_general(
        left,
        right,
        (((1,), (1,)), ((), ())),
        precision=precision,
        preferred_element_type=jnp.float32,
    )


def silu(value):
    return value / (1.0 + jnp.exp(-value))


def silu_half(value):
    return (0.5 * value) * (1.0 + jnp.tanh(0.5 * value))


sine_series = [(-1.0) ** k * math.pi ** (2 * k + 1) / math.factorial(2 * k + 1) for k in range(7)]


def fetched(pairs, semaphores):
    copies = [
        pltpu.make_async_copy(source, target, semaphores.at[place])
        for place, (source, target) in enumerate(pairs)
    ]
    for copy in copies:
        copy.start()
    return copies


chi_segment = 3


def pack_kernel(space_ref, features_ref, lists_ref, packed_ref, held_ref, semaphores):
    atoms, chans = features_ref.shape
    copies = fetched(
        [(lists_ref, held_ref), (features_ref, packed_ref.at[pl.ds(0, atoms)])], semaphores
    )
    copies[0].wait()
    _, lanes, width = held_ref.shape
    rows = []
    for place in range(lanes):
        row = held_ref[0, pl.ds(space_ref[0] ^ place, 1), :].astype(jnp.float32) + place * atoms
        parts = [jnp.zeros((1, width), jnp.float32)] * lanes
        parts[place] = row
        rows.append(jnp.concatenate(parts, axis=1))
    rows.append(jnp.zeros((packed_ref.shape[0] - atoms - lanes, chans), jnp.float32))
    packed_ref[atoms:, :] = jnp.concatenate(rows, axis=0).astype(jnp.bfloat16)
    copies[1].wait()


def edge_kernel(
    space_ref,
    *refs,
):
    count = (len(refs) - 8) // 2
    far, near, semaphores = refs[:count], refs[count + 9 : -1], refs[-1]
    filter_ref, unit_ref, row_ref, slot_ref, local_ref, hit_ref = refs[count : count + 6]
    turned_ref, update_ref, out_ref = refs[count + 6 : count + 9]
    vec_ref, first_ref, second_ref, send_ref, recv_ref, project_ref = near[:6]
    species_ref, hardness_ref, width_ref, shift_ref, positions_ref = near[6:]
    copies = fetched(list(zip(far, near + (update_ref, out_ref))), semaphores)
    for copy in copies[:3]:
        copy.wait()
    edges = vec_ref.shape[1]
    orders = first_ref.shape[0]
    vec = vec_ref[...]
    east, north, up = vec[0:1], vec[1:2], vec[2:3]
    squared = east * east + north * north + up * up
    inverse = lax.rsqrt(squared)
    unit_ref[0:3, :] = vec * inverse
    ratio = squared * inverse * (1.0 / cutoff)
    envelope = (1.0 - ratio * ratio) * (1.0 - ratio * ratio) * (cutoff * inverse)
    order = lax.broadcasted_iota(jnp.int32, (orders, edges), 0).astype(jnp.float32) + 1.0
    turns = order * ratio
    whole = jnp.floor(turns + 0.5)
    part = turns - whole
    sign = 1.0 - 2.0 * (whole - 2.0 * jnp.floor(whole * 0.5))
    series = jnp.full_like(part, sine_series[-1])
    for coefficient in sine_series[-2::-1]:
        series = series * (part * part) + coefficient
    basis = series * part * (sign * envelope)
    b1, b2, b3 = split3(basis)
    w1, w2, w3 = split3(first_ref[...])
    mixed = over_first(
        jnp.concatenate([w1, w1, w2, w2, w1, w3], axis=0).astype(jnp.bfloat16),
        jnp.concatenate([b1, b2, b1, b2, b3, b1], axis=0).astype(jnp.bfloat16),
    )
    radial = silu_half(mixed).astype(jnp.bfloat16)
    filter_ref[...] = over_first(second_ref[...], radial)
    for copy in copies[3:]:
        copy.wait()
    species = species_ref[...]

    def table(ref):
        result = jnp.zeros(species.shape, jnp.float32)
        for kind in range(ref.shape[1]):
            result = result + jnp.where(species == kind, ref[:, kind : kind + 1], 0.0)
        return result

    positions = positions_ref[...]
    sigma = table(width_ref)
    atoms = species.shape[1]
    chans = row_ref.shape[1]
    diag = table(hardness_ref) + inverse_root_pi / sigma
    blank = jnp.zeros((2, atoms), jnp.float32)
    rows = [positions[0:1], blank, -table(shift_ref), diag, sigma, positions[2:3], positions[1:2]]
    block = jnp.concatenate(
        [jnp.concatenate(rows, axis=0), jnp.zeros((8, chans - atoms), jnp.float32)], axis=1
    )
    block = pltpu.roll(block, 0, 1, stride=atoms, stride_axis=0)
    row_ref[...] = jnp.sum(block, axis=0, keepdims=True)
    lanes = local_ref.shape[0] // atoms
    slots = chans // lanes
    send = send_ref[...]
    own = send < atoms
    slot = jnp.where(own, -1, (send - atoms) ^ (space_ref[0] * slots))
    local = jnp.where(own, send, -1)

    def chosen(ref, index):
        hit = lax.broadcasted_iota(jnp.int32, ref.shape, 0) == index
        ref[...] = jnp.where(hit, 1.0, 0.0).astype(ref.dtype)

    chosen(slot_ref, slot)
    chosen(local_ref, local)
    chosen(hit_ref, recv_ref[...])
    turned_ref[...] = project_ref[...].astype(jnp.float32).T.astype(jnp.bfloat16)


def node_kernel(
    own_ref,
    near_ref,
    side_ref,
    far_ref,
    filter_ref,
    unit_ref,
    row_ref,
    slot_ref,
    local_ref,
    hit_ref,
    turned_ref,
    update_ref,
    out_ref,
    hidden_ref,
    block_ref,
):
    atoms, chans = hidden_ref.shape
    packed = (own_ref, near_ref, side_ref, far_ref)
    group = jnp.concatenate([ref[:atoms, :] for ref in packed], axis=0)
    chosen = jnp.zeros((1, chans), jnp.float32)
    for place, ref in enumerate(packed):
        tail = ref[atoms:, :].astype(jnp.float32)
        chosen = chosen + tail[place : place + 1]
    fill = jnp.where(
        lax.broadcasted_iota(jnp.int32, (len(packed) * atoms, chans), 0)
        == chosen.astype(jnp.int32),
        1.0,
        0.0,
    ).astype(jnp.bfloat16)
    sender = jnp.dot(fill, slot_ref[...], preferred_element_type=jnp.float32) + local_ref[...]
    projected = over_last(turned_ref[...], group).astype(jnp.bfloat16)
    picked = jnp.dot(projected, sender.astype(jnp.bfloat16), preferred_element_type=jnp.float32)
    scalar = picked[:chans] * filter_ref[:chans, :]
    carried = picked[chans:] * filter_ref[chans:, :]
    parts = [scalar] + [unit_ref[axis : axis + 1, :] * carried for axis in range(3)]
    message = jnp.concatenate([part.astype(jnp.bfloat16) for part in parts], axis=0)
    summed = over_last(hit_ref[...], message) * message_scale
    square = jnp.zeros((atoms, chans), jnp.float32)
    for component in range(1, 4):
        part = summed[:, component * chans : (component + 1) * chans]
        square = square + part * part
    invariant = jnp.concatenate([summed[:, :chans], square], axis=1).astype(jnp.bfloat16)
    hidden = silu(jnp.dot(invariant, update_ref[...], preferred_element_type=jnp.float32))
    chi = jnp.sum(hidden * out_ref[...], axis=1, keepdims=True)
    lane = lax.broadcasted_iota(jnp.int32, (atoms, chans), 1)
    atom = lax.broadcasted_iota(jnp.int32, (atoms, chans), 0)
    chi = jnp.where(lane == atom + chi_segment * atoms, chi, 0.0)
    row = row_ref[...] - jnp.sum(chi, axis=0, keepdims=True)
    block_ref[...] = jnp.broadcast_to(row[None], block_ref.shape)
    hidden_ref[...] = hidden


def feature_kernel(packed_ref, hidden_ref, features_ref):
    atoms = features_ref.shape[0]
    old = packed_ref[...].astype(jnp.float32)[:atoms]
    features_ref[...] = (old + hidden_ref[...]).astype(jnp.bfloat16)


def reciprocal(value):
    rough = pl.reciprocal(value, approx=True)
    return rough * (2.0 - value * rough)


def smeared(scaled):
    decay = jnp.exp2(scaled * scaled * -math.log2(math.e))
    turn = reciprocal(1.0 + 0.3275911 * scaled)
    series = 1.061405429 * turn - 1.453152027
    series = series * turn + 1.421413741
    series = series * turn - 0.284496736
    series = series * turn + 0.254829592
    return 1.0 - series * turn * decay, decay


def charge_kernel(
    place_ref,
    field_ref,
    all_ref,
    charges_ref,
    forces_ref,
    virial_ref,
    matrix_ref,
    side_ref,
    value_ref,
    kept_ref,
):
    blocks, _, lanes = all_ref.shape
    own = charges_ref.shape[1]
    count = blocks * own
    fit = lanes // own
    segment = lax.broadcasted_iota(jnp.int32, (8, lanes), 1) // own
    tiles = []
    for first in range(0, blocks, fit):
        tile = jnp.zeros((8, lanes), jnp.float32)
        for place in range(fit):
            row = all_ref[(place_ref[0] + first + place) & (blocks - 1)]
            row = pltpu.roll(jnp.broadcast_to(row, (8, lanes)), 0, 1, stride=own, stride_axis=0)
            row = pltpu.roll(row, place * own, 1) if place else row
            tile = jnp.where(segment == place, row, tile)
        tiles.append(tile)
    everyone = jnp.concatenate(tiles, axis=1)
    last = lax.broadcasted_iota(jnp.int32, everyone.shape, 0) == 5
    everyone = everyone + jnp.where(last, field_ref[0] * everyone[2:3], 0.0)
    columns = everyone.T
    diag, rhs = everyone[4:5], everyone[5:6]
    spread_row = 2.0 * everyone[3:4] * everyone[3:4]
    tiles = count // lanes
    depth = own // 8
    shape = (depth, 8, lanes)
    lane = lax.broadcasted_iota(jnp.int32, shape, 2)
    line = lax.broadcasted_iota(jnp.int32, shape, 0) * 8 + lax.broadcasted_iota(jnp.int32, shape, 1)

    def part(row, tile):
        return row[:, tile * lanes : (tile + 1) * lanes]

    def down(row):
        return [jnp.broadcast_to(part(row, tile), (8, lanes))[None] for tile in range(tiles)]

    def along(column):
        return jnp.broadcast_to(column, (own, lanes)).reshape(shape)

    def total(value):
        return jnp.sum(value, axis=1, keepdims=True)

    axes = [down(everyone[axis : axis + 1]) for axis in range(3)]
    wide_row, rhs_row = down(spread_row), down(rhs)

    above = [jnp.zeros((8, lanes), jnp.float32) for _ in range(tiles)]
    for start in range(0, count, own):
        first = start // lanes
        column = columns[start : start + own]
        place = [along(column[:, axis : axis + 1]) for axis in range(3)]
        wide = along(2.0 * column[:, 3:4] * column[:, 3:4])
        value = along(column[:, 5:6])
        value_ref[start : start + own, :] = value.reshape(own, lanes)
        below = jnp.zeros(shape, jnp.float32)
        for tile in range(first, tiles):
            delta = [place[axis] - axes[axis][tile] for axis in range(3)]
            squared = delta[0] * delta[0] + delta[1] * delta[1] + delta[2] * delta[2]
            if tile == first:
                same = lane == line + (start - first * lanes)
                squared = jnp.where(same, 1.0, squared)
            inverse = lax.rsqrt(squared)
            scale = lax.rsqrt(wide + wide_row[tile])
            smear, decay = smeared(squared * inverse * scale)
            kernel = smear * inverse
            if start == 0:
                slope = (two_over_root_pi * scale * decay - kernel) * inverse * inverse
                slope = jnp.where(same, 0.0, slope) if tile == first else slope
                for which, kind in enumerate(delta + [slope]):
                    kept_ref[which, :, tile * lanes : (tile + 1) * lanes] = kind.reshape(own, lanes)
            if tile == first:
                kernel = jnp.where(same, 0.0, kernel)
            else:
                below = below + kernel * rhs_row[tile]
            above[tile] = above[tile] + jnp.sum(kernel * value, axis=0)
            matrix_ref[start : start + own, tile * lanes : (tile + 1) * lanes] = kernel.reshape(
                own, lanes
            )
        if first + 1 < tiles:
            side_ref[start : start + own, :] = below.reshape(own, lanes)
    image = []
    for tile in range(tiles):
        value = jnp.sum(above[tile], axis=0, keepdims=True)
        if tile + 1 < tiles:
            below = side_ref[tile * lanes : (tile + 1) * lanes, :].T
            value = value + jnp.sum(below, axis=0, keepdims=True)
        image.append(value)
    image = diag * rhs + jnp.concatenate(image, axis=1)
    across = jnp.broadcast_to(image, (8, count)).T
    norm = total(rhs * rhs)
    alpha = norm * reciprocal(total(rhs * image))
    residual = rhs - alpha * image
    fresh = total(residual * residual)
    again = fresh * reciprocal(norm)
    direction = residual + again * rhs
    onto = [jnp.zeros((8, lanes), jnp.float32) for _ in range(tiles)]
    above = [jnp.zeros((8, lanes), jnp.float32) for _ in range(tiles)]
    for start in range(0, count, own):
        first = start // lanes
        value = (1.0 + again) * value_ref[start : start + own, :]
        value = value - alpha * jnp.broadcast_to(across[start : start + own, 0:1], (own, lanes))
        value = value.reshape(shape)
        for tile in range(first, tiles):
            sums = onto if tile == first else above
            kernel = matrix_ref[start : start + own, tile * lanes : (tile + 1) * lanes]
            sums[tile] = sums[tile] + jnp.sum(kernel.reshape(shape) * value, axis=0)
    curved = jnp.zeros((8, lanes), jnp.float32)
    for tile in range(tiles):
        curved = curved + (onto[tile] + 2.0 * above[tile]) * part(direction, tile)
    curved = jnp.sum(curved, axis=0, keepdims=True)
    for tile in range(tiles):
        curved = curved + part(diag * direction * direction, tile)
    charges = alpha * rhs + fresh * reciprocal(total(curved)) * direction

    sums = [jnp.zeros(shape, jnp.float32) for _ in range(9)]
    charge_row = down(charges)
    for tile in range(tiles):
        *delta, slope = [
            kept_ref[which, :, tile * lanes : (tile + 1) * lanes].reshape(shape)
            for which in range(4)
        ]
        weight = charge_row[tile] * slope
        pulled = [weight * delta[axis] for axis in range(3)]
        terms = pulled + [
            pulled[left] * delta[right]
            for left, right in ((0, 0), (1, 1), (2, 2), (0, 1), (0, 2), (1, 2))
        ]
        sums = [old + term for old, term in zip(sums, terms)]
    table = jnp.zeros((own, lanes), jnp.float32)
    lane = lane.reshape(own, lanes)
    for place, value in enumerate(sums):
        table = jnp.where(lane == place, total(value.reshape(own, lanes)), table)
    table = table.T
    mine = charges[:, :own]
    charges_ref[...] = mine
    pull = -mine * table[0:3]
    third = lax.broadcasted_iota(jnp.int32, pull.shape, 0) == 2
    forces_ref[...] = pull + jnp.where(third, mine * field_ref[0], 0.0)
    virial_ref[...] = 0.5 * mine * table[3:9]


def kernel_call(kernel, shapes, arguments, scalars=0, far=0, scratch=(), flops=0):
    shapes = tuple(jax.ShapeDtypeStruct(shape, kind) for shape, kind in shapes)
    spaces = [pltpu.SMEM] * scalars + [pltpu.HBM] * far
    spaces = spaces + [pltpu.VMEM] * (len(arguments) - len(spaces))
    arguments = [
        pltpu.with_memory_space_constraint(value, space) if space is pltpu.HBM else value
        for value, space in zip(arguments, spaces)
    ]
    return pl.pallas_call(
        kernel,
        out_shape=shapes,
        in_specs=[pl.BlockSpec(memory_space=space) for space in spaces],
        out_specs=tuple(pl.BlockSpec(memory_space=pltpu.VMEM) for _ in shapes),
        scratch_shapes=list(scratch),
        compiler_params=pltpu.CompilerParams(vmem_limit_bytes=32 * 1024 * 1024),
        cost_estimate=pl.CostEstimate(flops=flops, bytes_accessed=1 << 20, transcendentals=0),
    )(*arguments)


def exchanged(block, axis, step):
    size = lax.axis_size(axis)
    return lax.ppermute(block, axis, [(place, place ^ step) for place in range(size)])


def few_shards(
    features,
    positions,
    species,
    ghost_list,
    edge_recv,
    edge_send,
    edge_vec,
    w_msg,
    w_rad1,
    w_rad2,
    w_up,
    w_out,
    hardness,
    width,
    chi_shift,
    field,
):
    atoms, chans = features.shape
    edges = edge_recv.shape[0]
    rows, lanes = lax.axis_size("row"), lax.axis_size("space")
    space = lax.axis_index("space").astype(jnp.int32)
    (packed,) = kernel_call(
        pack_kernel,
        [((atoms + 16, chans), jnp.bfloat16)],
        (space.reshape(1), features, ghost_list),
        scalars=1,
        far=2,
        scratch=[
            pltpu.VMEM(ghost_list.shape, ghost_list.dtype),
            pltpu.SemaphoreType.DMA((2,)),
        ],
    )
    others = [exchanged(packed, "space", step) for step in range(1, lanes)]
    rest = (edge_vec, w_rad1, w_rad2, edge_send[None], edge_recv[None], w_msg)
    rest = rest + (species[None], hardness[None], width[None], chi_shift[None], positions)
    kept = (w_up, w_out[None])
    parts = kernel_call(
        edge_kernel,
        [
            ((2 * chans, edges), jnp.float32),
            ((8, edges), jnp.float32),
            ((1, chans), jnp.float32),
            ((chans, edges), jnp.bfloat16),
            ((lanes * atoms, edges), jnp.float32),
            ((atoms, edges), jnp.bfloat16),
            ((2 * chans, chans), jnp.bfloat16),
            (w_up.shape, w_up.dtype),
            ((1, chans), jnp.float32),
        ],
        (space.reshape(1), *rest, *kept),
        scalars=1,
        far=len(rest + kept),
        scratch=[pltpu.VMEM(value.shape, value.dtype) for value in rest]
        + [pltpu.SemaphoreType.DMA((len(rest + kept),))],
        flops=1 << 28,
    )
    devices = rows * lanes
    hidden, block = kernel_call(
        node_kernel,
        [((atoms, chans), jnp.float32), ((devices, 1, chans), jnp.float32)],
        (packed, *others, *parts),
        flops=1 << 28,
    )
    (new_features,) = kernel_call(
        feature_kernel, [((atoms, chans), jnp.bfloat16)], (packed, hidden), flops=1 << 20
    )
    block = lax.all_to_all(block, everywhere, 0, 0, tiled=True)
    place = lax.axis_index("row").astype(jnp.int32) * lanes + space
    everybody = rows * lanes * atoms
    charges, forces, virial = kernel_call(
        charge_kernel,
        [((count, atoms), jnp.float32) for count in (1, 3, 6)],
        (place.reshape(1), field, block),
        scalars=2,
        scratch=[
            pltpu.VMEM((everybody, everybody), jnp.float32),
            pltpu.VMEM((everybody, chans), jnp.float32),
            pltpu.VMEM((everybody, chans), jnp.float32),
            pltpu.VMEM((4, atoms, everybody), jnp.float32),
        ],
        flops=1 << 28,
    )
    return (new_features, charges[0], forces, virial)


def solution(mesh):
    small = mesh.shape["space"] == 4 and mesh.shape["row"] == 8
    return jax.shard_map(
        few_shards if small else shards,
        mesh=mesh,
        in_specs=(
            P(("row", "space"), None),
            P(None, ("row", "space")),
            P(("row", "space")),
            P("row", "space", None),
            P(("row", "space")),
            P(("row", "space")),
            P(None, ("row", "space")),
            P(),
            P(),
            P(),
            P(),
            P(),
            P(),
            P(),
            P(),
            P(),
        ),
        out_specs=(
            P(("row", "space"), None),
            P(("row", "space")),
            P(None, ("row", "space")),
            P(None, ("row", "space")),
        ),
        check_vma=False,
    )
```

```python
import functools
import math

import jax
import jax.numpy as jnp
from jax import lax
from jax.experimental import pallas as pl
from jax.experimental.pallas import tpu as pltpu
from jax.sharding import PartitionSpec as P

ITERS = 2


cutoff = 6.0
message_scale = 0.125
two_over_root_pi = 2.0 / math.sqrt(math.pi)
inverse_root_pi = 1.0 / math.sqrt(math.pi)
replicate_limit = 1024
everywhere = ("row", "space")


def lookup(species, table):
    result = jnp.zeros(species.shape, jnp.float32)
    for kind in range(table.shape[0]):
        result = result + jnp.where(species == kind, table[kind], 0.0)
    return result


def pair_terms(target, target_labels, source, source_labels):
    delta = target[:3, :, None] - source[:3, None, :]
    squared = jnp.sum(delta * delta, axis=0)
    same = target_labels[:, None] == source_labels[None, :]
    squared = jnp.where(same, 1.0, squared)
    inverse = lax.rsqrt(squared)
    radius = squared * inverse
    spread = target[3][:, None] * target[3][:, None] + source[3][None, :] * source[3][None, :]
    scale = lax.rsqrt(2.0 * spread)
    scaled = radius * scale
    smear = lax.erf(scaled)
    return delta, same, inverse, scale, scaled, smear


def coulomb(target, target_labels, source, source_labels):
    _, same, inverse, _, _, smear = pair_terms(target, target_labels, source, source_labels)
    return jnp.where(same, 0.0, smear * inverse)


def pair_forces(target, target_labels, source, source_labels, source_charge):
    delta, same, inverse, scale, scaled, smear = pair_terms(
        target, target_labels, source, source_labels
    )
    slope = (
        two_over_root_pi * scale * jnp.exp(-scaled * scaled) * inverse - smear * inverse * inverse
    )
    weight = jnp.where(same, 0.0, source_charge[None, :] * slope * inverse)
    first = jnp.sum(weight[None] * delta, axis=2)
    pairs = ((0, 0), (1, 1), (2, 2), (0, 1), (0, 2), (1, 2))
    second = jnp.stack(
        [jnp.sum(weight * delta[left] * delta[right], axis=1) for left, right in pairs]
    )
    return jnp.concatenate([first, second], axis=0)


def edge_terms(receive, sender_rows, vectors, projected, w_rad1, w_rad2, atoms):
    length = jnp.sqrt(jnp.sum(vectors * vectors, axis=0))
    unit = vectors / length
    order = jnp.arange(1, w_rad1.shape[0] + 1, dtype=jnp.int32).astype(jnp.float32)[:, None]
    ratio = length / cutoff
    envelope = (1.0 - ratio * ratio) * (1.0 - ratio * ratio)
    basis = jnp.sin(order * math.pi * ratio) / ratio * envelope
    mixed = lax.dot_general(
        basis, w_rad1, (((0,), (0,)), ((), ())), precision=lax.Precision.HIGHEST
    )
    radial = jax.nn.silu(mixed).astype(jnp.bfloat16)
    filters = jnp.dot(radial, w_rad2, preferred_element_type=jnp.float32)
    picked = jnp.take(projected, sender_rows, axis=0).astype(jnp.float32) * filters
    chans = w_rad1.shape[1]
    scalar = picked[:, :chans]
    carried = picked[:, chans:]
    joined = [
        scalar,
        unit[0][:, None] * carried,
        unit[1][:, None] * carried,
        unit[2][:, None] * carried,
    ]
    message = jnp.concatenate(joined, axis=1).astype(jnp.bfloat16)
    onehot = (jnp.arange(atoms, dtype=jnp.int32)[:, None] == receive[None, :]).astype(jnp.bfloat16)
    return jnp.dot(onehot, message, preferred_element_type=jnp.float32)


def gathered(block, devices):
    copies = jnp.broadcast_to(block[None], (devices,) + block.shape)
    return lax.all_to_all(copies, everywhere, split_axis=0, concat_axis=0, tiled=True)


def shards(
    features,
    positions,
    species,
    ghost_list,
    edge_recv,
    edge_send,
    edge_vec,
    w_msg,
    w_rad1,
    w_rad2,
    w_up,
    w_out,
    hardness,
    width,
    chi_shift,
    field,
):
    atoms = features.shape[0]
    chans = features.shape[1]
    lanes = lax.axis_size("space")
    devices = lanes * lax.axis_size("row")
    everybody = devices * atoms
    me = lax.axis_index("row") * lanes + lax.axis_index("space")
    sigma = lookup(species, width)
    diag = lookup(species, hardness) + inverse_root_pi / sigma
    placed = jnp.concatenate([positions, sigma[None, :], diag[None, :]], axis=0)
    everyone = gathered(placed, devices).transpose(1, 0, 2).reshape(5, everybody)
    lists = ghost_list[0]
    outgoing = jnp.take(features, lists.reshape(-1), axis=0).reshape(lanes, lists.shape[1], chans)
    ghost_rows = jnp.einsum(
        "dkc,cf->dkf",
        lax.all_to_all(outgoing, "space", split_axis=0, concat_axis=0, tiled=True),
        w_msg,
        preferred_element_type=jnp.float32,
    ).astype(jnp.bfloat16)
    own_rows = jnp.dot(features, w_msg, preferred_element_type=jnp.float32).astype(jnp.bfloat16)
    projected = jnp.concatenate([own_rows, ghost_rows.reshape(-1, 2 * chans)], axis=0)
    summed = edge_terms(edge_recv, edge_send, edge_vec, projected, w_rad1, w_rad2, atoms)
    summed = summed * message_scale
    vector_part = summed[:, chans:].reshape(atoms, 3, chans)
    invariant = jnp.concatenate(
        [summed[:, :chans], jnp.sum(vector_part * vector_part, axis=1)], axis=1
    ).astype(jnp.bfloat16)
    hidden = jax.nn.silu(jnp.dot(invariant, w_up, preferred_element_type=jnp.float32))
    new_features = (features.astype(jnp.float32) + hidden).astype(jnp.bfloat16)
    chi = jnp.dot(hidden, w_out, precision=lax.Precision.HIGHEST) + lookup(species, chi_shift)
    own_labels = me * atoms + jnp.arange(atoms, dtype=jnp.int32)
    all_labels = jnp.arange(everybody, dtype=jnp.int32)
    rhs = field[0] * positions[2] - chi

    if everybody <= replicate_limit:
        kernel = coulomb(everyone, all_labels, everyone, all_labels)
        residual = gathered(rhs, devices).reshape(everybody)
        all_charges = conjugate(
            residual, lambda v: everyone[4] * v + jnp.sum(kernel * v[None, :], axis=1), jnp.sum
        )
        charges = lax.dynamic_slice(all_charges, (me * atoms,), (atoms,))
    else:
        kernel = coulomb(placed, own_labels, everyone, all_labels)

        def spread(vector):
            return gathered(vector, devices).reshape(everybody)

        charges = conjugate(
            rhs,
            lambda v: diag * v + jnp.sum(kernel * spread(v)[None, :], axis=1),
            lambda v: lax.psum(jnp.sum(v), everywhere),
        )
        all_charges = spread(charges)
    sums = pair_forces(placed, own_labels, everyone, all_labels, all_charges)
    pull = -charges[None, :] * sums[:3]
    forces = jnp.concatenate([pull[:2], pull[2:] + (charges * field[0])[None, :]], axis=0)
    virial = 0.5 * charges[None, :] * sums[3:]
    return (new_features, charges, forces, virial)


def conjugate(rhs, apply, total):
    charges = jnp.zeros_like(rhs)
    residual = rhs
    direction = rhs
    norm_now = total(residual * residual)
    for step in range(ITERS):
        image = apply(direction)
        alpha = norm_now / total(direction * image)
        charges = charges + alpha * direction
        if step + 1 < ITERS:
            residual = residual - alpha * image
            fresh = total(residual * residual)
            direction = residual + fresh / norm_now * direction
            norm_now = fresh
    return charges


def split3(value):
    first = value.astype(jnp.bfloat16).astype(jnp.float32)
    rest = value - first
    second = rest.astype(jnp.bfloat16).astype(jnp.float32)
    third = (rest - second).astype(jnp.bfloat16).astype(jnp.float32)
    return first, second, third


def over_first(left, right):
    return lax.dot_general(
        left, right, (((0,), (0,)), ((), ())), preferred_element_type=jnp.float32
    )


def over_last(left, right, precision=None):
    return lax.dot_general(
        left,
        right,
        (((1,), (1,)), ((), ())),
        precision=precision,
        preferred_element_type=jnp.float32,
    )


def silu(value):
    return value / (1.0 + jnp.exp(-value))


def silu_half(value):
    return (0.5 * value) * (1.0 + jnp.tanh(0.5 * value))


sine_series = [(-1.0) ** k * math.pi ** (2 * k + 1) / math.factorial(2 * k + 1) for k in range(7)]


def fetched(pairs, semaphores):
    copies = [
        pltpu.make_async_copy(source, target, semaphores.at[place])
        for place, (source, target) in enumerate(pairs)
    ]
    for copy in copies:
        copy.start()
    return copies


chi_segment = 3


def pack_kernel(space_ref, features_ref, lists_ref, packed_ref, held_ref, semaphores):
    atoms, chans = features_ref.shape
    copies = fetched(
        [(lists_ref, held_ref), (features_ref, packed_ref.at[pl.ds(0, atoms)])], semaphores
    )
    copies[0].wait()
    _, lanes, width = held_ref.shape
    rows = []
    for place in range(lanes):
        row = held_ref[0, pl.ds(space_ref[0] ^ place, 1), :].astype(jnp.float32) + place * atoms
        parts = [jnp.zeros((1, width), jnp.float32)] * lanes
        parts[place] = row
        rows.append(jnp.concatenate(parts, axis=1))
    rows.append(jnp.zeros((packed_ref.shape[0] - atoms - lanes, chans), jnp.float32))
    packed_ref[atoms:, :] = jnp.concatenate(rows, axis=0).astype(jnp.bfloat16)
    copies[1].wait()


def edge_kernel(lanes, space_ref, *refs):
    count = (len(refs) - 7) // 2
    far, near, semaphores = refs[:count], refs[count + 8 : -1], refs[-1]
    filter_ref, unit_ref, row_ref, slot_ref, hit_ref = refs[count : count + 5]
    turned_ref, update_ref, out_ref = refs[count + 5 : count + 8]
    vec_ref, first_ref, second_ref, send_ref, recv_ref, project_ref = near[:6]
    species_ref, hardness_ref, width_ref, shift_ref, positions_ref = near[6:]
    copies = fetched(list(zip(far, near + (update_ref, out_ref))), semaphores)
    for copy in copies[:3]:
        copy.wait()
    edges = vec_ref.shape[1]
    orders = first_ref.shape[0]
    vec = vec_ref[...]
    east, north, up = vec[0:1], vec[1:2], vec[2:3]
    squared = east * east + north * north + up * up
    inverse = lax.rsqrt(squared)
    unit_ref[0:3, :] = vec * inverse
    ratio = squared * inverse * (1.0 / cutoff)
    envelope = (1.0 - ratio * ratio) * (1.0 - ratio * ratio) * (cutoff * inverse)
    order = lax.broadcasted_iota(jnp.int32, (orders, edges), 0).astype(jnp.float32) + 1.0
    turns = order * ratio
    whole = jnp.floor(turns + 0.5)
    part = turns - whole
    sign = 1.0 - 2.0 * (whole - 2.0 * jnp.floor(whole * 0.5))
    series = jnp.full_like(part, sine_series[-1])
    for coefficient in sine_series[-2::-1]:
        series = series * (part * part) + coefficient
    basis = series * part * (sign * envelope)
    b1, b2, b3 = split3(basis)
    w1, w2, w3 = split3(first_ref[...])
    mixed = over_first(
        jnp.concatenate([w1, w1, w2, w2, w1, w3], axis=0).astype(jnp.bfloat16),
        jnp.concatenate([b1, b2, b1, b2, b3, b1], axis=0).astype(jnp.bfloat16),
    )
    radial = silu_half(mixed).astype(jnp.bfloat16)
    filter_ref[...] = over_first(second_ref[...], radial)
    for copy in copies[3:]:
        copy.wait()
    species = species_ref[...]

    def table(ref):
        result = jnp.zeros(species.shape, jnp.float32)
        for kind in range(ref.shape[1]):
            result = result + jnp.where(species == kind, ref[:, kind : kind + 1], 0.0)
        return result

    positions = positions_ref[...]
    sigma = table(width_ref)
    atoms = species.shape[1]
    chans = row_ref.shape[1]
    diag = table(hardness_ref) + inverse_root_pi / sigma
    blank = jnp.zeros((2, atoms), jnp.float32)
    rows = [positions[0:1], blank, -table(shift_ref), diag, sigma, positions[2:3], positions[1:2]]
    block = jnp.concatenate(
        [jnp.concatenate(rows, axis=0), jnp.zeros((8, chans - atoms), jnp.float32)], axis=1
    )
    block = pltpu.roll(block, 0, 1, stride=atoms, stride_axis=0)
    row_ref[...] = jnp.sum(block, axis=0, keepdims=True)
    slots = slot_ref.shape[0] - atoms
    width = slots // lanes
    send = send_ref[...]
    ghost = (send - atoms) ^ (space_ref[0] * width)

    def chosen(ref, index, value):
        hit = lax.broadcasted_iota(jnp.int32, ref.shape, 0) == index
        ref[...] = jnp.where(hit, value, 0.0).astype(ref.dtype)

    chosen(slot_ref, jnp.where(send < atoms, send + slots, ghost), 1.0)
    chosen(hit_ref, recv_ref[...], message_scale)
    turned_ref[...] = project_ref[...].astype(jnp.float32).T.astype(jnp.bfloat16)


def node_kernel(
    own_ref,
    near_ref,
    side_ref,
    far_ref,
    filter_ref,
    unit_ref,
    row_ref,
    slot_ref,
    hit_ref,
    turned_ref,
    update_ref,
    out_ref,
    hidden_ref,
    block_ref,
):
    atoms, chans = hidden_ref.shape
    packed = (own_ref, near_ref, side_ref, far_ref)
    group = jnp.concatenate([ref[:atoms, :] for ref in packed], axis=0)
    chosen = jnp.zeros((1, chans), jnp.float32)
    for place, ref in enumerate(packed):
        tail = ref[atoms:, :].astype(jnp.float32)
        chosen = chosen + tail[place : place + 1]
    member = lax.broadcasted_iota(jnp.int32, (len(packed) * atoms, chans), 0)
    fill = jnp.where(member == chosen.astype(jnp.int32), 1.0, 0.0)
    lane = lax.broadcasted_iota(jnp.int32, (len(packed) * atoms, atoms), 1)
    fill = jnp.concatenate([fill, jnp.where(member[:, :atoms] == lane, 1.0, 0.0)], axis=1)
    sender = jnp.dot(
        fill.astype(jnp.bfloat16), slot_ref[...], preferred_element_type=jnp.float32
    )
    projected = over_last(turned_ref[...], group).astype(jnp.bfloat16)
    picked = jnp.dot(projected, sender.astype(jnp.bfloat16), preferred_element_type=jnp.float32)
    scalar = picked[:chans] * filter_ref[:chans, :]
    carried = picked[chans:] * filter_ref[chans:, :]
    parts = [scalar] + [unit_ref[axis : axis + 1, :] * carried for axis in range(3)]
    message = jnp.concatenate([part.astype(jnp.bfloat16) for part in parts], axis=0)
    summed = over_last(hit_ref[...], message)
    square = jnp.zeros((atoms, chans), jnp.float32)
    for component in range(1, 4):
        part = summed[:, component * chans : (component + 1) * chans]
        square = square + part * part
    invariant = jnp.concatenate([summed[:, :chans], square], axis=1).astype(jnp.bfloat16)
    hidden = silu(jnp.dot(invariant, update_ref[...], preferred_element_type=jnp.float32))
    chi = jnp.sum(hidden * out_ref[...], axis=1, keepdims=True)
    lane = lax.broadcasted_iota(jnp.int32, (atoms, chans), 1)
    atom = lax.broadcasted_iota(jnp.int32, (atoms, chans), 0)
    chi = jnp.where(lane == atom + chi_segment * atoms, chi, 0.0)
    row = row_ref[...] - jnp.sum(chi, axis=0, keepdims=True)
    block_ref[...] = jnp.broadcast_to(row[None], block_ref.shape)
    hidden_ref[...] = hidden


def feature_kernel(packed_ref, hidden_ref, features_ref):
    atoms = features_ref.shape[0]
    old = packed_ref[...].astype(jnp.float32)[:atoms]
    features_ref[...] = (old + hidden_ref[...]).astype(jnp.bfloat16)


def reciprocal(value):
    rough = pl.reciprocal(value, approx=True)
    return rough * (2.0 - value * rough)


def smeared(scaled):
    decay = jnp.exp2(scaled * scaled * -math.log2(math.e))
    turn = reciprocal(1.0 + 0.3275911 * scaled)
    series = 1.061405429 * turn - 1.453152027
    series = series * turn + 1.421413741
    series = series * turn - 0.284496736
    series = series * turn + 0.254829592
    return 1.0 - series * turn * decay, decay


def charge_kernel(
    place_ref,
    field_ref,
    all_ref,
    charges_ref,
    forces_ref,
    virial_ref,
    matrix_ref,
    side_ref,
    value_ref,
    kept_ref,
):
    blocks, _, lanes = all_ref.shape
    own = charges_ref.shape[1]
    count = blocks * own
    fit = lanes // own
    segment = lax.broadcasted_iota(jnp.int32, (8, lanes), 1) // own
    tiles = []
    for first in range(0, blocks, fit):
        tile = jnp.zeros((8, lanes), jnp.float32)
        for place in range(fit):
            row = all_ref[(place_ref[0] + first + place) & (blocks - 1)]
            row = pltpu.roll(jnp.broadcast_to(row, (8, lanes)), 0, 1, stride=own, stride_axis=0)
            row = pltpu.roll(row, place * own, 1) if place else row
            tile = jnp.where(segment == place, row, tile)
        tiles.append(tile)
    everyone = jnp.concatenate(tiles, axis=1)
    last = lax.broadcasted_iota(jnp.int32, everyone.shape, 0) == 5
    everyone = everyone + jnp.where(last, field_ref[0] * everyone[2:3], 0.0)
    columns = everyone.T
    diag, rhs = everyone[4:5], everyone[5:6]
    spread_row = 2.0 * everyone[3:4] * everyone[3:4]
    tiles = count // lanes
    depth = own // 8
    shape = (depth, 8, lanes)
    lane = lax.broadcasted_iota(jnp.int32, shape, 2)
    line = lax.broadcasted_iota(jnp.int32, shape, 0) * 8 + lax.broadcasted_iota(jnp.int32, shape, 1)

    def part(row, tile):
        return row[:, tile * lanes : (tile + 1) * lanes]

    def down(row):
        return [jnp.broadcast_to(part(row, tile), (8, lanes))[None] for tile in range(tiles)]

    def along(column):
        return jnp.broadcast_to(column, (own, lanes)).reshape(shape)

    def total(value):
        return jnp.sum(value, axis=1, keepdims=True)

    axes = [down(everyone[axis : axis + 1]) for axis in range(3)]
    wide_row, rhs_row = down(spread_row), down(rhs)

    above = [jnp.zeros((8, lanes), jnp.float32) for _ in range(tiles)]
    for start in range(0, count, own):
        first = start // lanes
        column = columns[start : start + own]
        place = [along(column[:, axis : axis + 1]) for axis in range(3)]
        wide = along(2.0 * column[:, 3:4] * column[:, 3:4])
        value = along(column[:, 5:6])
        value_ref[start : start + own, :] = value.reshape(own, lanes)
        below = jnp.zeros(shape, jnp.float32)
        for tile in range(first, tiles):
            delta = [place[axis] - axes[axis][tile] for axis in range(3)]
            squared = delta[0] * delta[0] + delta[1] * delta[1] + delta[2] * delta[2]
            if tile == first:
                same = lane == line + (start - first * lanes)
                squared = jnp.where(same, 1.0, squared)
            inverse = lax.rsqrt(squared)
            scale = lax.rsqrt(wide + wide_row[tile])
            smear, decay = smeared(squared * inverse * scale)
            kernel = smear * inverse
            if start == 0:
                slope = (two_over_root_pi * scale * decay - kernel) * inverse * inverse
                slope = jnp.where(same, 0.0, slope) if tile == first else slope
                for which, kind in enumerate(delta + [slope]):
                    kept_ref[which, :, tile * lanes : (tile + 1) * lanes] = kind.reshape(own, lanes)
            if tile == first:
                kernel = jnp.where(same, 0.0, kernel)
            else:
                below = below + kernel * rhs_row[tile]
            above[tile] = above[tile] + jnp.sum(kernel * value, axis=0)
            matrix_ref[start : start + own, tile * lanes : (tile + 1) * lanes] = kernel.reshape(
                own, lanes
            )
        if first + 1 < tiles:
            side_ref[start : start + own, :] = below.reshape(own, lanes)
    image = []
    for tile in range(tiles):
        value = jnp.sum(above[tile], axis=0, keepdims=True)
        if tile + 1 < tiles:
            below = side_ref[tile * lanes : (tile + 1) * lanes, :].T
            value = value + jnp.sum(below, axis=0, keepdims=True)
        image.append(value)
    image = diag * rhs + jnp.concatenate(image, axis=1)
    across = jnp.broadcast_to(image, (8, count)).T
    norm = total(rhs * rhs)
    alpha = norm * reciprocal(total(rhs * image))
    residual = rhs - alpha * image
    fresh = total(residual * residual)
    again = fresh * reciprocal(norm)
    direction = residual + again * rhs
    onto = [jnp.zeros((8, lanes), jnp.float32) for _ in range(tiles)]
    above = [jnp.zeros((8, lanes), jnp.float32) for _ in range(tiles)]
    for start in range(0, count, own):
        first = start // lanes
        value = (1.0 + again) * value_ref[start : start + own, :]
        value = value - alpha * jnp.broadcast_to(across[start : start + own, 0:1], (own, lanes))
        value = value.reshape(shape)
        for tile in range(first, tiles):
            sums = onto if tile == first else above
            kernel = matrix_ref[start : start + own, tile * lanes : (tile + 1) * lanes]
            sums[tile] = sums[tile] + jnp.sum(kernel.reshape(shape) * value, axis=0)
    curved = jnp.zeros((8, lanes), jnp.float32)
    for tile in range(tiles):
        curved = curved + (onto[tile] + 2.0 * above[tile]) * part(direction, tile)
    curved = jnp.sum(curved, axis=0, keepdims=True)
    for tile in range(tiles):
        curved = curved + part(diag * direction * direction, tile)
    charges = alpha * rhs + fresh * reciprocal(total(curved)) * direction

    sums = [jnp.zeros(shape, jnp.float32) for _ in range(9)]
    charge_row = down(charges)
    for tile in range(tiles):
        *delta, slope = [
            kept_ref[which, :, tile * lanes : (tile + 1) * lanes].reshape(shape)
            for which in range(4)
        ]
        weight = charge_row[tile] * slope
        pulled = [weight * delta[axis] for axis in range(3)]
        terms = pulled + [
            pulled[left] * delta[right]
            for left, right in ((0, 0), (1, 1), (2, 2), (0, 1), (0, 2), (1, 2))
        ]
        sums = [old + term for old, term in zip(sums, terms)]
    table = jnp.zeros((own, lanes), jnp.float32)
    lane = lane.reshape(own, lanes)
    for place, value in enumerate(sums):
        table = jnp.where(lane == place, total(value.reshape(own, lanes)), table)
    table = table.T
    mine = charges[:, :own]
    charges_ref[...] = mine
    pull = -mine * table[0:3]
    third = lax.broadcasted_iota(jnp.int32, pull.shape, 0) == 2
    forces_ref[...] = pull + jnp.where(third, mine * field_ref[0], 0.0)
    virial_ref[...] = 0.5 * mine * table[3:9]


def kernel_call(kernel, shapes, arguments, scalars=0, far=0, scratch=(), flops=0):
    shapes = tuple(jax.ShapeDtypeStruct(shape, kind) for shape, kind in shapes)
    spaces = [pltpu.SMEM] * scalars + [pltpu.HBM] * far
    spaces = spaces + [pltpu.VMEM] * (len(arguments) - len(spaces))
    arguments = [
        pltpu.with_memory_space_constraint(value, space) if space is pltpu.HBM else value
        for value, space in zip(arguments, spaces)
    ]
    return pl.pallas_call(
        kernel,
        out_shape=shapes,
        in_specs=[pl.BlockSpec(memory_space=space) for space in spaces],
        out_specs=tuple(pl.BlockSpec(memory_space=pltpu.VMEM) for _ in shapes),
        scratch_shapes=list(scratch),
        compiler_params=pltpu.CompilerParams(vmem_limit_bytes=32 * 1024 * 1024),
        cost_estimate=pl.CostEstimate(flops=flops, bytes_accessed=1 << 20, transcendentals=0),
    )(*arguments)


def exchanged(block, axis, step):
    size = lax.axis_size(axis)
    return lax.ppermute(block, axis, [(place, place ^ step) for place in range(size)])


def few_shards(
    features,
    positions,
    species,
    ghost_list,
    edge_recv,
    edge_send,
    edge_vec,
    w_msg,
    w_rad1,
    w_rad2,
    w_up,
    w_out,
    hardness,
    width,
    chi_shift,
    field,
):
    atoms, chans = features.shape
    edges = edge_recv.shape[0]
    rows, lanes = lax.axis_size("row"), lax.axis_size("space")
    space = lax.axis_index("space").astype(jnp.int32)
    (packed,) = kernel_call(
        pack_kernel,
        [((atoms + 8, chans), jnp.bfloat16)],
        (space.reshape(1), features, ghost_list),
        scalars=1,
        far=2,
        scratch=[
            pltpu.VMEM(ghost_list.shape, ghost_list.dtype),
            pltpu.SemaphoreType.DMA((2,)),
        ],
    )
    others = [exchanged(packed, "space", step) for step in range(1, lanes)]
    rest = (edge_vec, w_rad1, w_rad2, edge_send[None], edge_recv[None], w_msg)
    rest = rest + (species[None], hardness[None], width[None], chi_shift[None], positions)
    kept = (w_up, w_out[None])
    parts = kernel_call(
        functools.partial(edge_kernel, lanes),
        [
            ((2 * chans, edges), jnp.float32),
            ((8, edges), jnp.float32),
            ((1, chans), jnp.float32),
            ((chans + atoms, edges), jnp.bfloat16),
            ((atoms, edges), jnp.bfloat16),
            ((2 * chans, chans), jnp.bfloat16),
            (w_up.shape, w_up.dtype),
            ((1, chans), jnp.float32),
        ],
        (space.reshape(1), *rest, *kept),
        scalars=1,
        far=len(rest + kept),
        scratch=[pltpu.VMEM(value.shape, value.dtype) for value in rest]
        + [pltpu.SemaphoreType.DMA((len(rest + kept),))],
        flops=1 << 28,
    )
    devices = rows * lanes
    hidden, block = kernel_call(
        node_kernel,
        [((atoms, chans), jnp.float32), ((devices, 1, chans), jnp.float32)],
        (packed, *others, *parts),
        flops=1 << 28,
    )
    (new_features,) = kernel_call(
        feature_kernel, [((atoms, chans), jnp.bfloat16)], (packed, hidden), flops=1 << 20
    )
    block = lax.all_to_all(block, everywhere, 0, 0, tiled=True)
    place = lax.axis_index("row").astype(jnp.int32) * lanes + space
    everybody = rows * lanes * atoms
    charges, forces, virial = kernel_call(
        charge_kernel,
        [((count, atoms), jnp.float32) for count in (1, 3, 6)],
        (place.reshape(1), field, block),
        scalars=2,
        scratch=[
            pltpu.VMEM((everybody, everybody), jnp.float32),
            pltpu.VMEM((everybody, chans), jnp.float32),
            pltpu.VMEM((everybody, chans), jnp.float32),
            pltpu.VMEM((4, atoms, everybody), jnp.float32),
        ],
        flops=1 << 28,
    )
    return (new_features, charges[0], forces, virial)


def solution(mesh):
    small = mesh.shape["space"] == 4 and mesh.shape["row"] == 8
    return jax.shard_map(
        few_shards if small else shards,
        mesh=mesh,
        in_specs=(
            P(("row", "space"), None),
            P(None, ("row", "space")),
            P(("row", "space")),
            P("row", "space", None),
            P(("row", "space")),
            P(("row", "space")),
            P(None, ("row", "space")),
            P(),
            P(),
            P(),
            P(),
            P(),
            P(),
            P(),
            P(),
            P(),
        ),
        out_specs=(
            P(("row", "space"), None),
            P(("row", "space")),
            P(None, ("row", "space")),
            P(None, ("row", "space")),
        ),
        check_vma=False,
    )
```

```python
import functools
import math

import jax
import jax.numpy as jnp
from jax import lax
from jax.experimental import pallas as pl
from jax.experimental.pallas import tpu as pltpu
from jax.sharding import PartitionSpec as P

ITERS = 2


cutoff = 6.0
message_scale = 0.125
two_over_root_pi = 2.0 / math.sqrt(math.pi)
inverse_root_pi = 1.0 / math.sqrt(math.pi)
replicate_limit = 1024
everywhere = ("row", "space")


def lookup(species, table):
    result = jnp.zeros(species.shape, jnp.float32)
    for kind in range(table.shape[0]):
        result = result + jnp.where(species == kind, table[kind], 0.0)
    return result


def pair_terms(target, target_labels, source, source_labels):
    delta = target[:3, :, None] - source[:3, None, :]
    squared = jnp.sum(delta * delta, axis=0)
    same = target_labels[:, None] == source_labels[None, :]
    squared = jnp.where(same, 1.0, squared)
    inverse = lax.rsqrt(squared)
    radius = squared * inverse
    spread = target[3][:, None] * target[3][:, None] + source[3][None, :] * source[3][None, :]
    scale = lax.rsqrt(2.0 * spread)
    scaled = radius * scale
    smear = lax.erf(scaled)
    return delta, same, inverse, scale, scaled, smear


def coulomb(target, target_labels, source, source_labels):
    _, same, inverse, _, _, smear = pair_terms(target, target_labels, source, source_labels)
    return jnp.where(same, 0.0, smear * inverse)


def pair_forces(target, target_labels, source, source_labels, source_charge):
    delta, same, inverse, scale, scaled, smear = pair_terms(
        target, target_labels, source, source_labels
    )
    slope = (
        two_over_root_pi * scale * jnp.exp(-scaled * scaled) * inverse - smear * inverse * inverse
    )
    weight = jnp.where(same, 0.0, source_charge[None, :] * slope * inverse)
    first = jnp.sum(weight[None] * delta, axis=2)
    pairs = ((0, 0), (1, 1), (2, 2), (0, 1), (0, 2), (1, 2))
    second = jnp.stack(
        [jnp.sum(weight * delta[left] * delta[right], axis=1) for left, right in pairs]
    )
    return jnp.concatenate([first, second], axis=0)


def edge_terms(receive, sender_rows, vectors, projected, w_rad1, w_rad2, atoms):
    length = jnp.sqrt(jnp.sum(vectors * vectors, axis=0))
    unit = vectors / length
    order = jnp.arange(1, w_rad1.shape[0] + 1, dtype=jnp.int32).astype(jnp.float32)[:, None]
    ratio = length / cutoff
    envelope = (1.0 - ratio * ratio) * (1.0 - ratio * ratio)
    basis = jnp.sin(order * math.pi * ratio) / ratio * envelope
    mixed = lax.dot_general(
        basis, w_rad1, (((0,), (0,)), ((), ())), precision=lax.Precision.HIGHEST
    )
    radial = jax.nn.silu(mixed).astype(jnp.bfloat16)
    filters = jnp.dot(radial, w_rad2, preferred_element_type=jnp.float32)
    picked = jnp.take(projected, sender_rows, axis=0).astype(jnp.float32) * filters
    chans = w_rad1.shape[1]
    scalar = picked[:, :chans]
    carried = picked[:, chans:]
    joined = [
        scalar,
        unit[0][:, None] * carried,
        unit[1][:, None] * carried,
        unit[2][:, None] * carried,
    ]
    message = jnp.concatenate(joined, axis=1).astype(jnp.bfloat16)
    onehot = (jnp.arange(atoms, dtype=jnp.int32)[:, None] == receive[None, :]).astype(jnp.bfloat16)
    return jnp.dot(onehot, message, preferred_element_type=jnp.float32)


def gathered(block, devices):
    copies = jnp.broadcast_to(block[None], (devices,) + block.shape)
    return lax.all_to_all(copies, everywhere, split_axis=0, concat_axis=0, tiled=True)


def shards(
    features,
    positions,
    species,
    ghost_list,
    edge_recv,
    edge_send,
    edge_vec,
    w_msg,
    w_rad1,
    w_rad2,
    w_up,
    w_out,
    hardness,
    width,
    chi_shift,
    field,
):
    atoms = features.shape[0]
    chans = features.shape[1]
    lanes = lax.axis_size("space")
    devices = lanes * lax.axis_size("row")
    everybody = devices * atoms
    me = lax.axis_index("row") * lanes + lax.axis_index("space")
    sigma = lookup(species, width)
    diag = lookup(species, hardness) + inverse_root_pi / sigma
    placed = jnp.concatenate([positions, sigma[None, :], diag[None, :]], axis=0)
    everyone = gathered(placed, devices).transpose(1, 0, 2).reshape(5, everybody)
    lists = ghost_list[0]
    outgoing = jnp.take(features, lists.reshape(-1), axis=0).reshape(lanes, lists.shape[1], chans)
    ghost_rows = jnp.einsum(
        "dkc,cf->dkf",
        lax.all_to_all(outgoing, "space", split_axis=0, concat_axis=0, tiled=True),
        w_msg,
        preferred_element_type=jnp.float32,
    ).astype(jnp.bfloat16)
    own_rows = jnp.dot(features, w_msg, preferred_element_type=jnp.float32).astype(jnp.bfloat16)
    projected = jnp.concatenate([own_rows, ghost_rows.reshape(-1, 2 * chans)], axis=0)
    summed = edge_terms(edge_recv, edge_send, edge_vec, projected, w_rad1, w_rad2, atoms)
    summed = summed * message_scale
    vector_part = summed[:, chans:].reshape(atoms, 3, chans)
    invariant = jnp.concatenate(
        [summed[:, :chans], jnp.sum(vector_part * vector_part, axis=1)], axis=1
    ).astype(jnp.bfloat16)
    hidden = jax.nn.silu(jnp.dot(invariant, w_up, preferred_element_type=jnp.float32))
    new_features = (features.astype(jnp.float32) + hidden).astype(jnp.bfloat16)
    chi = jnp.dot(hidden, w_out, precision=lax.Precision.HIGHEST) + lookup(species, chi_shift)
    own_labels = me * atoms + jnp.arange(atoms, dtype=jnp.int32)
    all_labels = jnp.arange(everybody, dtype=jnp.int32)
    rhs = field[0] * positions[2] - chi

    if everybody <= replicate_limit:
        kernel = coulomb(everyone, all_labels, everyone, all_labels)
        residual = gathered(rhs, devices).reshape(everybody)
        all_charges = conjugate(
            residual, lambda v: everyone[4] * v + jnp.sum(kernel * v[None, :], axis=1), jnp.sum
        )
        charges = lax.dynamic_slice(all_charges, (me * atoms,), (atoms,))
    else:
        kernel = coulomb(placed, own_labels, everyone, all_labels)

        def spread(vector):
            return gathered(vector, devices).reshape(everybody)

        charges = conjugate(
            rhs,
            lambda v: diag * v + jnp.sum(kernel * spread(v)[None, :], axis=1),
            lambda v: lax.psum(jnp.sum(v), everywhere),
        )
        all_charges = spread(charges)
    sums = pair_forces(placed, own_labels, everyone, all_labels, all_charges)
    pull = -charges[None, :] * sums[:3]
    forces = jnp.concatenate([pull[:2], pull[2:] + (charges * field[0])[None, :]], axis=0)
    virial = 0.5 * charges[None, :] * sums[3:]
    return (new_features, charges, forces, virial)


def conjugate(rhs, apply, total):
    charges = jnp.zeros_like(rhs)
    residual = rhs
    direction = rhs
    norm_now = total(residual * residual)
    for step in range(ITERS):
        image = apply(direction)
        alpha = norm_now / total(direction * image)
        charges = charges + alpha * direction
        if step + 1 < ITERS:
            residual = residual - alpha * image
            fresh = total(residual * residual)
            direction = residual + fresh / norm_now * direction
            norm_now = fresh
    return charges


def split3(value):
    first = value.astype(jnp.bfloat16).astype(jnp.float32)
    rest = value - first
    second = rest.astype(jnp.bfloat16).astype(jnp.float32)
    third = (rest - second).astype(jnp.bfloat16).astype(jnp.float32)
    return first, second, third


def over_first(left, right):
    return lax.dot_general(
        left, right, (((0,), (0,)), ((), ())), preferred_element_type=jnp.float32
    )


def over_last(left, right, precision=None):
    return lax.dot_general(
        left,
        right,
        (((1,), (1,)), ((), ())),
        precision=precision,
        preferred_element_type=jnp.float32,
    )


def silu(value):
    return value / (1.0 + jnp.exp(-value))


def silu_half(value):
    return (0.5 * value) * (1.0 + jnp.tanh(0.5 * value))


sine_series = [(-1.0) ** k * math.pi ** (2 * k + 1) / math.factorial(2 * k + 1) for k in range(7)]


def fetched(pairs, semaphores):
    copies = [
        pltpu.make_async_copy(source, target, semaphores.at[place])
        for place, (source, target) in enumerate(pairs)
    ]
    for copy in copies:
        copy.start()
    return copies


chi_segment = 3


def pack_kernel(space_ref, features_ref, lists_ref, packed_ref, held_ref, semaphores):
    atoms, chans = features_ref.shape
    copies = fetched(
        [(lists_ref, held_ref), (features_ref, packed_ref.at[pl.ds(0, atoms)])], semaphores
    )
    copies[0].wait()
    _, lanes, width = held_ref.shape
    rows = []
    for place in range(lanes):
        row = held_ref[0, pl.ds(space_ref[0] ^ place, 1), :].astype(jnp.float32) + place * atoms
        parts = [jnp.zeros((1, width), jnp.float32)] * lanes
        parts[place] = row
        rows.append(jnp.concatenate(parts, axis=1))
    rows.append(jnp.zeros((packed_ref.shape[0] - atoms - lanes, chans), jnp.float32))
    packed_ref[atoms:, :] = jnp.concatenate(rows, axis=0).astype(jnp.bfloat16)
    copies[1].wait()


def edge_kernel(lanes, space_ref, *refs):
    count = (len(refs) - 7) // 2
    far, near, semaphores = refs[:count], refs[count + 8 : -1], refs[-1]
    filter_ref, unit_ref, row_ref, slot_ref, hit_ref = refs[count : count + 5]
    turned_ref, update_ref, out_ref = refs[count + 5 : count + 8]
    vec_ref, first_ref, second_ref, send_ref, recv_ref, project_ref = near[:6]
    species_ref, hardness_ref, width_ref, shift_ref, positions_ref = near[6:]
    copies = fetched(list(zip(far, near + (update_ref, out_ref))), semaphores)
    for copy in copies[:3]:
        copy.wait()
    edges = vec_ref.shape[1]
    orders = first_ref.shape[0]
    vec = vec_ref[...]
    east, north, up = vec[0:1], vec[1:2], vec[2:3]
    squared = east * east + north * north + up * up
    inverse = lax.rsqrt(squared)
    unit_ref[0:3, :] = vec * inverse
    ratio = squared * inverse * (1.0 / cutoff)
    envelope = (1.0 - ratio * ratio) * (1.0 - ratio * ratio) * (cutoff * inverse)
    order = lax.broadcasted_iota(jnp.int32, (orders, edges), 0).astype(jnp.float32) + 1.0
    turns = order * ratio
    whole = jnp.floor(turns + 0.5)
    part = turns - whole
    sign = 1.0 - 2.0 * (whole - 2.0 * jnp.floor(whole * 0.5))
    series = jnp.full_like(part, sine_series[-1])
    for coefficient in sine_series[-2::-1]:
        series = series * (part * part) + coefficient
    basis = series * part * (sign * envelope)
    b1, b2, b3 = split3(basis)
    w1, w2, w3 = split3(first_ref[...])
    mixed = over_first(
        jnp.concatenate([w1, w1, w2, w2, w1, w3], axis=0).astype(jnp.bfloat16),
        jnp.concatenate([b1, b2, b1, b2, b3, b1], axis=0).astype(jnp.bfloat16),
    )
    radial = silu_half(mixed).astype(jnp.bfloat16)
    filter_ref[...] = over_first(second_ref[...], radial)
    for copy in copies[3:]:
        copy.wait()
    species = species_ref[...]

    def table(ref):
        result = jnp.zeros(species.shape, jnp.float32)
        for kind in range(ref.shape[1]):
            result = result + jnp.where(species == kind, ref[:, kind : kind + 1], 0.0)
        return result

    positions = positions_ref[...]
    sigma = table(width_ref)
    atoms = species.shape[1]
    chans = row_ref.shape[1]
    diag = table(hardness_ref) + inverse_root_pi / sigma
    blank = jnp.zeros((2, atoms), jnp.float32)
    rows = [positions[0:1], blank, -table(shift_ref), diag, sigma, positions[2:3], positions[1:2]]
    block = jnp.concatenate(
        [jnp.concatenate(rows, axis=0), jnp.zeros((8, chans - atoms), jnp.float32)], axis=1
    )
    block = pltpu.roll(block, 0, 1, stride=atoms, stride_axis=0)
    row_ref[...] = jnp.sum(block, axis=0, keepdims=True)
    slots = slot_ref.shape[0] - atoms
    width = slots // lanes
    send = send_ref[...]
    ghost = (send - atoms) ^ (space_ref[0] * width)

    def chosen(ref, index, value):
        hit = lax.broadcasted_iota(jnp.int32, ref.shape, 0) == index
        ref[...] = jnp.where(hit, value, 0.0).astype(ref.dtype)

    chosen(slot_ref, jnp.where(send < atoms, send + slots, ghost), 1.0)
    chosen(hit_ref, recv_ref[...], message_scale)
    turned_ref[...] = project_ref[...].astype(jnp.float32).T.astype(jnp.bfloat16)


def node_kernel(
    own_ref,
    near_ref,
    side_ref,
    far_ref,
    filter_ref,
    unit_ref,
    row_ref,
    slot_ref,
    hit_ref,
    turned_ref,
    update_ref,
    out_ref,
    hidden_ref,
    block_ref,
):
    atoms, chans = hidden_ref.shape
    packed = (own_ref, near_ref, side_ref, far_ref)
    group = jnp.concatenate([ref[:atoms, :] for ref in packed], axis=0)
    chosen = jnp.zeros((1, chans), jnp.float32)
    for place, ref in enumerate(packed):
        tail = ref[atoms:, :].astype(jnp.float32)
        chosen = chosen + tail[place : place + 1]
    member = lax.broadcasted_iota(jnp.int32, (len(packed) * atoms, chans), 0)
    fill = jnp.where(member == chosen.astype(jnp.int32), 1.0, 0.0)
    lane = lax.broadcasted_iota(jnp.int32, (len(packed) * atoms, atoms), 1)
    fill = jnp.concatenate([fill, jnp.where(member[:, :atoms] == lane, 1.0, 0.0)], axis=1)
    sender = jnp.dot(
        fill.astype(jnp.bfloat16), slot_ref[...], preferred_element_type=jnp.float32
    )
    projected = over_last(turned_ref[...], group).astype(jnp.bfloat16)
    picked = jnp.dot(projected, sender.astype(jnp.bfloat16), preferred_element_type=jnp.float32)
    scalar = picked[:chans] * filter_ref[:chans, :]
    carried = picked[chans:] * filter_ref[chans:, :]
    parts = [scalar] + [unit_ref[axis : axis + 1, :] * carried for axis in range(3)]
    message = jnp.concatenate([part.astype(jnp.bfloat16) for part in parts], axis=0)
    summed = over_last(hit_ref[...], message)
    square = jnp.zeros((atoms, chans), jnp.float32)
    for component in range(1, 4):
        part = summed[:, component * chans : (component + 1) * chans]
        square = square + part * part
    invariant = jnp.concatenate([summed[:, :chans], square], axis=1).astype(jnp.bfloat16)
    hidden = silu(jnp.dot(invariant, update_ref[...], preferred_element_type=jnp.float32))
    chi = jnp.sum(hidden * out_ref[...], axis=1, keepdims=True)
    lane = lax.broadcasted_iota(jnp.int32, (atoms, chans), 1)
    atom = lax.broadcasted_iota(jnp.int32, (atoms, chans), 0)
    chi = jnp.where(lane == atom + chi_segment * atoms, chi, 0.0)
    row = row_ref[...] - jnp.sum(chi, axis=0, keepdims=True)
    block_ref[...] = jnp.broadcast_to(row[None], block_ref.shape)
    hidden_ref[...] = hidden


def feature_kernel(packed_ref, hidden_ref, features_ref):
    atoms = features_ref.shape[0]
    old = packed_ref[...].astype(jnp.float32)[:atoms]
    features_ref[...] = (old + hidden_ref[...]).astype(jnp.bfloat16)


def reciprocal(value):
    rough = pl.reciprocal(value, approx=True)
    return rough * (2.0 - value * rough)


def smeared(scaled):
    decay = jnp.exp2(scaled * scaled * -math.log2(math.e))
    turn = reciprocal(1.0 + 0.3275911 * scaled)
    series = 1.061405429 * turn - 1.453152027
    series = series * turn + 1.421413741
    series = series * turn - 0.284496736
    series = series * turn + 0.254829592
    return 1.0 - series * turn * decay, decay


def charge_kernel(
    place_ref,
    field_ref,
    all_ref,
    charges_ref,
    forces_ref,
    virial_ref,
    matrix_ref,
    side_ref,
    value_ref,
    kept_ref,
):
    blocks, _, lanes = all_ref.shape
    own = charges_ref.shape[1]
    count = blocks * own
    fit = lanes // own
    segment = lax.broadcasted_iota(jnp.int32, (8, lanes), 1) // own
    tiles = []
    for first in range(0, blocks, fit):
        tile = jnp.zeros((8, lanes), jnp.float32)
        for place in range(fit):
            row = all_ref[(place_ref[0] + first + place) & (blocks - 1)]
            row = pltpu.roll(jnp.broadcast_to(row, (8, lanes)), 0, 1, stride=own, stride_axis=0)
            row = pltpu.roll(row, place * own, 1) if place else row
            tile = jnp.where(segment == place, row, tile)
        tiles.append(tile)
    everyone = jnp.concatenate(tiles, axis=1)
    last = lax.broadcasted_iota(jnp.int32, everyone.shape, 0) == 5
    everyone = everyone + jnp.where(last, field_ref[0] * everyone[2:3], 0.0)
    columns = everyone.T
    diag, rhs = everyone[4:5], everyone[5:6]
    spread_row = 2.0 * everyone[3:4] * everyone[3:4]
    tiles = count // lanes
    depth = own // 8
    shape = (depth, 8, lanes)
    lane = lax.broadcasted_iota(jnp.int32, shape, 2)
    line = lax.broadcasted_iota(jnp.int32, shape, 0) * 8 + lax.broadcasted_iota(jnp.int32, shape, 1)

    def part(row, tile):
        return row[:, tile * lanes : (tile + 1) * lanes]

    def down(row):
        return [jnp.broadcast_to(part(row, tile), (8, lanes))[None] for tile in range(tiles)]

    def along(column):
        return jnp.broadcast_to(column, (own, lanes)).reshape(shape)

    def total(value):
        return jnp.sum(value, axis=1, keepdims=True)

    axes = [down(everyone[axis : axis + 1]) for axis in range(3)]
    wide_row, rhs_row = down(spread_row), down(rhs)

    above = [jnp.zeros((8, lanes), jnp.float32) for _ in range(tiles)]
    for start in range(0, count, own):
        first = start // lanes
        column = columns[start : start + own]
        place = [along(column[:, axis : axis + 1]) for axis in range(3)]
        wide = along(2.0 * column[:, 3:4] * column[:, 3:4])
        value = along(column[:, 5:6])
        value_ref[start : start + own, :] = value.reshape(own, lanes)
        below = jnp.zeros(shape, jnp.float32)
        for tile in range(first, tiles):
            delta = [place[axis] - axes[axis][tile] for axis in range(3)]
            squared = delta[0] * delta[0] + delta[1] * delta[1] + delta[2] * delta[2]
            if tile == first:
                same = lane == line + (start - first * lanes)
                squared = jnp.where(same, 1.0, squared)
            inverse = lax.rsqrt(squared)
            scale = lax.rsqrt(wide + wide_row[tile])
            smear, decay = smeared(squared * inverse * scale)
            kernel = smear * inverse
            if start == 0:
                slope = (two_over_root_pi * scale * decay - kernel) * inverse * inverse
                slope = jnp.where(same, 0.0, slope) if tile == first else slope
                for which, kind in enumerate(delta + [slope]):
                    kept_ref[which, :, tile * lanes : (tile + 1) * lanes] = kind.reshape(own, lanes)
            if tile == first:
                kernel = jnp.where(same, 0.0, kernel)
            else:
                below = below + kernel * rhs_row[tile]
            above[tile] = above[tile] + jnp.sum(kernel * value, axis=0)
            matrix_ref[start : start + own, tile * lanes : (tile + 1) * lanes] = kernel.reshape(
                own, lanes
            )
        if first + 1 < tiles:
            side_ref[start : start + own, :] = below.reshape(own, lanes)
    image = []
    for tile in range(tiles):
        value = jnp.sum(above[tile], axis=0, keepdims=True)
        if tile + 1 < tiles:
            below = side_ref[tile * lanes : (tile + 1) * lanes, :].T
            value = value + jnp.sum(below, axis=0, keepdims=True)
        image.append(value)
    image = diag * rhs + jnp.concatenate(image, axis=1)
    across = jnp.broadcast_to(image, (8, count)).T
    norm = total(rhs * rhs)
    alpha = norm * reciprocal(total(rhs * image))
    residual = rhs - alpha * image
    fresh = total(residual * residual)
    again = fresh * reciprocal(norm)
    direction = residual + again * rhs
    onto = [jnp.zeros((8, lanes), jnp.float32) for _ in range(tiles)]
    above = [jnp.zeros((8, lanes), jnp.float32) for _ in range(tiles)]
    for start in range(0, count, own):
        first = start // lanes
        value = (1.0 + again) * value_ref[start : start + own, :]
        value = value - alpha * jnp.broadcast_to(across[start : start + own, 0:1], (own, lanes))
        value = value.reshape(shape)
        for tile in range(first, tiles):
            sums = onto if tile == first else above
            kernel = matrix_ref[start : start + own, tile * lanes : (tile + 1) * lanes]
            sums[tile] = sums[tile] + jnp.sum(kernel.reshape(shape) * value, axis=0)
    curved = jnp.zeros((8, lanes), jnp.float32)
    for tile in range(tiles):
        curved = curved + (onto[tile] + 2.0 * above[tile]) * part(direction, tile)
    curved = jnp.sum(curved, axis=0, keepdims=True)
    for tile in range(tiles):
        curved = curved + part(diag * direction * direction, tile)
    charges = alpha * rhs + fresh * reciprocal(total(curved)) * direction

    sums = [jnp.zeros(shape, jnp.float32) for _ in range(9)]
    charge_row = down(charges)
    for tile in range(tiles):
        *delta, slope = [
            kept_ref[which, :, tile * lanes : (tile + 1) * lanes].reshape(shape)
            for which in range(4)
        ]
        weight = charge_row[tile] * slope
        pulled = [weight * delta[axis] for axis in range(3)]
        terms = pulled + [
            pulled[left] * delta[right]
            for left, right in ((0, 0), (1, 1), (2, 2), (0, 1), (0, 2), (1, 2))
        ]
        sums = [old + term for old, term in zip(sums, terms)]
    table = jnp.zeros((own, lanes), jnp.float32)
    lane = lane.reshape(own, lanes)
    for place, value in enumerate(sums):
        table = jnp.where(lane == place, total(value.reshape(own, lanes)), table)
    table = table.T
    mine = charges[:, :own]
    charges_ref[...] = mine
    pull = -mine * table[0:3]
    third = lax.broadcasted_iota(jnp.int32, pull.shape, 0) == 2
    forces_ref[...] = pull + jnp.where(third, mine * field_ref[0], 0.0)
    virial_ref[...] = 0.5 * mine * table[3:9]


def kernel_call(kernel, shapes, arguments, scalars=0, far=0, scratch=(), flops=0):
    shapes = tuple(jax.ShapeDtypeStruct(shape, kind) for shape, kind in shapes)
    spaces = [pltpu.SMEM] * scalars + [pltpu.HBM] * far
    spaces = spaces + [pltpu.VMEM] * (len(arguments) - len(spaces))
    arguments = [
        pltpu.with_memory_space_constraint(value, space) if space is pltpu.HBM else value
        for value, space in zip(arguments, spaces)
    ]
    return pl.pallas_call(
        kernel,
        out_shape=shapes,
        in_specs=[pl.BlockSpec(memory_space=space) for space in spaces],
        out_specs=tuple(pl.BlockSpec(memory_space=pltpu.VMEM) for _ in shapes),
        scratch_shapes=list(scratch),
        compiler_params=pltpu.CompilerParams(vmem_limit_bytes=32 * 1024 * 1024),
        cost_estimate=pl.CostEstimate(flops=flops, bytes_accessed=1 << 20, transcendentals=0),
    )(*arguments)


def exchanged(block, axis, step):
    size = lax.axis_size(axis)
    return lax.ppermute(block, axis, [(place, place ^ step) for place in range(size)])


def few_shards(
    features,
    positions,
    species,
    ghost_list,
    edge_recv,
    edge_send,
    edge_vec,
    w_msg,
    w_rad1,
    w_rad2,
    w_up,
    w_out,
    hardness,
    width,
    chi_shift,
    field,
):
    atoms, chans = features.shape
    edges = edge_recv.shape[0]
    rows, lanes = lax.axis_size("row"), lax.axis_size("space")
    space = lax.axis_index("space").astype(jnp.int32)
    (packed,) = kernel_call(
        pack_kernel,
        [((atoms + 16, chans), jnp.bfloat16)],
        (space.reshape(1), features, ghost_list),
        scalars=1,
        far=2,
        scratch=[
            pltpu.VMEM(ghost_list.shape, ghost_list.dtype),
            pltpu.SemaphoreType.DMA((2,)),
        ],
    )
    others = [exchanged(packed, "space", step) for step in range(1, lanes)]
    rest = (edge_vec, w_rad1, w_rad2, edge_send[None], edge_recv[None], w_msg)
    rest = rest + (species[None], hardness[None], width[None], chi_shift[None], positions)
    kept = (w_up, w_out[None])
    parts = kernel_call(
        functools.partial(edge_kernel, lanes),
        [
            ((2 * chans, edges), jnp.float32),
            ((8, edges), jnp.float32),
            ((1, chans), jnp.float32),
            ((chans + atoms, edges), jnp.bfloat16),
            ((atoms, edges), jnp.bfloat16),
            ((2 * chans, chans), jnp.bfloat16),
            (w_up.shape, w_up.dtype),
            ((1, chans), jnp.float32),
        ],
        (space.reshape(1), *rest, *kept),
        scalars=1,
        far=len(rest + kept),
        scratch=[pltpu.VMEM(value.shape, value.dtype) for value in rest]
        + [pltpu.SemaphoreType.DMA((len(rest + kept),))],
        flops=1 << 28,
    )
    devices = rows * lanes
    hidden, block = kernel_call(
        node_kernel,
        [((atoms, chans), jnp.float32), ((devices, 1, chans), jnp.float32)],
        (packed, *others, *parts),
        flops=1 << 28,
    )
    (new_features,) = kernel_call(
        feature_kernel, [((atoms, chans), jnp.bfloat16)], (packed, hidden), flops=1 << 20
    )
    block = lax.all_to_all(block, everywhere, 0, 0, tiled=True)
    place = lax.axis_index("row").astype(jnp.int32) * lanes + space
    everybody = rows * lanes * atoms
    charges, forces, virial = kernel_call(
        charge_kernel,
        [((count, atoms), jnp.float32) for count in (1, 3, 6)],
        (place.reshape(1), field, block),
        scalars=2,
        scratch=[
            pltpu.VMEM((everybody, everybody), jnp.float32),
            pltpu.VMEM((everybody, chans), jnp.float32),
            pltpu.VMEM((everybody, chans), jnp.float32),
            pltpu.VMEM((4, atoms, everybody), jnp.float32),
        ],
        flops=1 << 28,
    )
    return (new_features, charges[0], forces, virial)


def solution(mesh):
    small = mesh.shape["space"] == 4 and mesh.shape["row"] == 8
    return jax.shard_map(
        few_shards if small else shards,
        mesh=mesh,
        in_specs=(
            P(("row", "space"), None),
            P(None, ("row", "space")),
            P(("row", "space")),
            P("row", "space", None),
            P(("row", "space")),
            P(("row", "space")),
            P(None, ("row", "space")),
            P(),
            P(),
            P(),
            P(),
            P(),
            P(),
            P(),
            P(),
            P(),
        ),
        out_specs=(
            P(("row", "space"), None),
            P(("row", "space")),
            P(None, ("row", "space")),
            P(None, ("row", "space")),
        ),
        check_vma=False,
    )
```

```python
import functools
import math

import jax
import jax.numpy as jnp
from jax import lax
from jax.experimental import pallas as pl
from jax.experimental.pallas import tpu as pltpu
from jax.sharding import PartitionSpec as P

ITERS = 2


cutoff = 6.0
message_scale = 0.125
two_over_root_pi = 2.0 / math.sqrt(math.pi)
inverse_root_pi = 1.0 / math.sqrt(math.pi)
replicate_limit = 1024
everywhere = ("row", "space")


def lookup(species, table):
    result = jnp.zeros(species.shape, jnp.float32)
    for kind in range(table.shape[0]):
        result = result + jnp.where(species == kind, table[kind], 0.0)
    return result


def pair_terms(target, target_labels, source, source_labels):
    delta = target[:3, :, None] - source[:3, None, :]
    squared = jnp.sum(delta * delta, axis=0)
    same = target_labels[:, None] == source_labels[None, :]
    squared = jnp.where(same, 1.0, squared)
    inverse = lax.rsqrt(squared)
    radius = squared * inverse
    spread = target[3][:, None] * target[3][:, None] + source[3][None, :] * source[3][None, :]
    scale = lax.rsqrt(2.0 * spread)
    scaled = radius * scale
    smear = lax.erf(scaled)
    return delta, same, inverse, scale, scaled, smear


def coulomb(target, target_labels, source, source_labels):
    _, same, inverse, _, _, smear = pair_terms(target, target_labels, source, source_labels)
    return jnp.where(same, 0.0, smear * inverse)


def pair_forces(target, target_labels, source, source_labels, source_charge):
    delta, same, inverse, scale, scaled, smear = pair_terms(
        target, target_labels, source, source_labels
    )
    slope = (
        two_over_root_pi * scale * jnp.exp(-scaled * scaled) * inverse - smear * inverse * inverse
    )
    weight = jnp.where(same, 0.0, source_charge[None, :] * slope * inverse)
    first = jnp.sum(weight[None] * delta, axis=2)
    pairs = ((0, 0), (1, 1), (2, 2), (0, 1), (0, 2), (1, 2))
    second = jnp.stack(
        [jnp.sum(weight * delta[left] * delta[right], axis=1) for left, right in pairs]
    )
    return jnp.concatenate([first, second], axis=0)


def edge_terms(receive, sender_rows, vectors, projected, w_rad1, w_rad2, atoms):
    length = jnp.sqrt(jnp.sum(vectors * vectors, axis=0))
    unit = vectors / length
    order = jnp.arange(1, w_rad1.shape[0] + 1, dtype=jnp.int32).astype(jnp.float32)[:, None]
    ratio = length / cutoff
    envelope = (1.0 - ratio * ratio) * (1.0 - ratio * ratio)
    basis = jnp.sin(order * math.pi * ratio) / ratio * envelope
    mixed = lax.dot_general(
        basis, w_rad1, (((0,), (0,)), ((), ())), precision=lax.Precision.HIGHEST
    )
    radial = jax.nn.silu(mixed).astype(jnp.bfloat16)
    filters = jnp.dot(radial, w_rad2, preferred_element_type=jnp.float32)
    picked = jnp.take(projected, sender_rows, axis=0).astype(jnp.float32) * filters
    chans = w_rad1.shape[1]
    scalar = picked[:, :chans]
    carried = picked[:, chans:]
    joined = [
        scalar,
        unit[0][:, None] * carried,
        unit[1][:, None] * carried,
        unit[2][:, None] * carried,
    ]
    message = jnp.concatenate(joined, axis=1).astype(jnp.bfloat16)
    onehot = (jnp.arange(atoms, dtype=jnp.int32)[:, None] == receive[None, :]).astype(jnp.bfloat16)
    return jnp.dot(onehot, message, preferred_element_type=jnp.float32)


def gathered(block, devices):
    copies = jnp.broadcast_to(block[None], (devices,) + block.shape)
    return lax.all_to_all(copies, everywhere, split_axis=0, concat_axis=0, tiled=True)


def shards(
    features,
    positions,
    species,
    ghost_list,
    edge_recv,
    edge_send,
    edge_vec,
    w_msg,
    w_rad1,
    w_rad2,
    w_up,
    w_out,
    hardness,
    width,
    chi_shift,
    field,
):
    atoms = features.shape[0]
    chans = features.shape[1]
    lanes = lax.axis_size("space")
    devices = lanes * lax.axis_size("row")
    everybody = devices * atoms
    me = lax.axis_index("row") * lanes + lax.axis_index("space")
    sigma = lookup(species, width)
    diag = lookup(species, hardness) + inverse_root_pi / sigma
    placed = jnp.concatenate([positions, sigma[None, :], diag[None, :]], axis=0)
    everyone = gathered(placed, devices).transpose(1, 0, 2).reshape(5, everybody)
    lists = ghost_list[0]
    outgoing = jnp.take(features, lists.reshape(-1), axis=0).reshape(lanes, lists.shape[1], chans)
    ghost_rows = jnp.einsum(
        "dkc,cf->dkf",
        lax.all_to_all(outgoing, "space", split_axis=0, concat_axis=0, tiled=True),
        w_msg,
        preferred_element_type=jnp.float32,
    ).astype(jnp.bfloat16)
    own_rows = jnp.dot(features, w_msg, preferred_element_type=jnp.float32).astype(jnp.bfloat16)
    projected = jnp.concatenate([own_rows, ghost_rows.reshape(-1, 2 * chans)], axis=0)
    summed = edge_terms(edge_recv, edge_send, edge_vec, projected, w_rad1, w_rad2, atoms)
    summed = summed * message_scale
    vector_part = summed[:, chans:].reshape(atoms, 3, chans)
    invariant = jnp.concatenate(
        [summed[:, :chans], jnp.sum(vector_part * vector_part, axis=1)], axis=1
    ).astype(jnp.bfloat16)
    hidden = jax.nn.silu(jnp.dot(invariant, w_up, preferred_element_type=jnp.float32))
    new_features = (features.astype(jnp.float32) + hidden).astype(jnp.bfloat16)
    chi = jnp.dot(hidden, w_out, precision=lax.Precision.HIGHEST) + lookup(species, chi_shift)
    own_labels = me * atoms + jnp.arange(atoms, dtype=jnp.int32)
    all_labels = jnp.arange(everybody, dtype=jnp.int32)
    rhs = field[0] * positions[2] - chi

    if everybody <= replicate_limit:
        kernel = coulomb(everyone, all_labels, everyone, all_labels)
        residual = gathered(rhs, devices).reshape(everybody)
        all_charges = conjugate(
            residual, lambda v: everyone[4] * v + jnp.sum(kernel * v[None, :], axis=1), jnp.sum
        )
        charges = lax.dynamic_slice(all_charges, (me * atoms,), (atoms,))
    else:
        kernel = coulomb(placed, own_labels, everyone, all_labels)

        def spread(vector):
            return gathered(vector, devices).reshape(everybody)

        charges = conjugate(
            rhs,
            lambda v: diag * v + jnp.sum(kernel * spread(v)[None, :], axis=1),
            lambda v: lax.psum(jnp.sum(v), everywhere),
        )
        all_charges = spread(charges)
    sums = pair_forces(placed, own_labels, everyone, all_labels, all_charges)
    pull = -charges[None, :] * sums[:3]
    forces = jnp.concatenate([pull[:2], pull[2:] + (charges * field[0])[None, :]], axis=0)
    virial = 0.5 * charges[None, :] * sums[3:]
    return (new_features, charges, forces, virial)


def conjugate(rhs, apply, total):
    charges = jnp.zeros_like(rhs)
    residual = rhs
    direction = rhs
    norm_now = total(residual * residual)
    for step in range(ITERS):
        image = apply(direction)
        alpha = norm_now / total(direction * image)
        charges = charges + alpha * direction
        if step + 1 < ITERS:
            residual = residual - alpha * image
            fresh = total(residual * residual)
            direction = residual + fresh / norm_now * direction
            norm_now = fresh
    return charges


def split3(value):
    first = value.astype(jnp.bfloat16).astype(jnp.float32)
    rest = value - first
    second = rest.astype(jnp.bfloat16).astype(jnp.float32)
    third = (rest - second).astype(jnp.bfloat16).astype(jnp.float32)
    return first, second, third


def over_first(left, right):
    return lax.dot_general(
        left, right, (((0,), (0,)), ((), ())), preferred_element_type=jnp.float32
    )


def over_last(left, right, precision=None):
    return lax.dot_general(
        left,
        right,
        (((1,), (1,)), ((), ())),
        precision=precision,
        preferred_element_type=jnp.float32,
    )


def silu(value):
    return value / (1.0 + jnp.exp(-value))


def silu_half(value):
    return (0.5 * value) * (1.0 + jnp.tanh(0.5 * value))


sine_series = [(-1.0) ** k * math.pi ** (2 * k + 1) / math.factorial(2 * k + 1) for k in range(7)]


def fetched(pairs, semaphores):
    copies = [
        pltpu.make_async_copy(source, target, semaphores.at[place])
        for place, (source, target) in enumerate(pairs)
    ]
    for copy in copies:
        copy.start()
    return copies


chi_segment = 3


def pack_kernel(space_ref, features_ref, lists_ref, packed_ref, held_ref, semaphores):
    atoms, chans = features_ref.shape
    copies = fetched(
        [(lists_ref, held_ref), (features_ref, packed_ref.at[pl.ds(0, atoms)])], semaphores
    )
    copies[0].wait()
    _, lanes, width = held_ref.shape
    rows = []
    for place in range(lanes):
        row = held_ref[0, pl.ds(space_ref[0] ^ place, 1), :].astype(jnp.float32) + place * atoms
        parts = [jnp.zeros((1, width), jnp.float32)] * lanes
        parts[place] = row
        rows.append(jnp.concatenate(parts, axis=1))
    rows.append(jnp.zeros((packed_ref.shape[0] - atoms - lanes, chans), jnp.float32))
    packed_ref[atoms:, :] = jnp.concatenate(rows, axis=0).astype(jnp.bfloat16)
    copies[1].wait()


def edge_kernel(lanes, space_ref, *refs):
    count = (len(refs) - 7) // 2
    far, near, semaphores = refs[:count], refs[count + 8 : -1], refs[-1]
    filter_ref, unit_ref, row_ref, slot_ref, hit_ref = refs[count : count + 5]
    turned_ref, update_ref, out_ref = refs[count + 5 : count + 8]
    vec_ref, first_ref, second_ref, send_ref, recv_ref, project_ref = near[:6]
    species_ref, hardness_ref, width_ref, shift_ref, positions_ref = near[6:]
    copies = fetched(list(zip(far, near + (update_ref, out_ref))), semaphores)
    for copy in copies[:3]:
        copy.wait()
    edges = vec_ref.shape[1]
    orders = first_ref.shape[0]
    vec = vec_ref[...]
    east, north, up = vec[0:1], vec[1:2], vec[2:3]
    squared = east * east + north * north + up * up
    inverse = lax.rsqrt(squared)
    unit_ref[0:3, :] = vec * inverse
    ratio = squared * inverse * (1.0 / cutoff)
    envelope = (1.0 - ratio * ratio) * (1.0 - ratio * ratio) * (cutoff * inverse)
    order = lax.broadcasted_iota(jnp.int32, (orders, edges), 0).astype(jnp.float32) + 1.0
    turns = order * ratio
    whole = jnp.floor(turns + 0.5)
    part = turns - whole
    sign = 1.0 - 2.0 * (whole - 2.0 * jnp.floor(whole * 0.5))
    series = jnp.full_like(part, sine_series[-1])
    for coefficient in sine_series[-2::-1]:
        series = series * (part * part) + coefficient
    basis = series * part * (sign * envelope)
    b1, b2, b3 = split3(basis)
    w1, w2, w3 = split3(first_ref[...])
    mixed = over_first(
        jnp.concatenate([w1, w1, w2, w2, w1, w3], axis=0).astype(jnp.bfloat16),
        jnp.concatenate([b1, b2, b1, b2, b3, b1], axis=0).astype(jnp.bfloat16),
    )
    radial = silu_half(mixed).astype(jnp.bfloat16)
    filter_ref[...] = over_first(second_ref[...], radial)
    for copy in copies[3:]:
        copy.wait()
    species = species_ref[...]

    def table(ref):
        result = jnp.zeros(species.shape, jnp.float32)
        for kind in range(ref.shape[1]):
            result = result + jnp.where(species == kind, ref[:, kind : kind + 1], 0.0)
        return result

    positions = positions_ref[...]
    sigma = table(width_ref)
    atoms = species.shape[1]
    chans = row_ref.shape[1]
    diag = table(hardness_ref) + inverse_root_pi / sigma
    blank = jnp.zeros((2, atoms), jnp.float32)
    rows = [positions[0:1], blank, -table(shift_ref), diag, sigma, positions[2:3], positions[1:2]]
    block = jnp.concatenate(
        [jnp.concatenate(rows, axis=0), jnp.zeros((8, chans - atoms), jnp.float32)], axis=1
    )
    block = pltpu.roll(block, 0, 1, stride=atoms, stride_axis=0)
    row_ref[...] = jnp.sum(block, axis=0, keepdims=True)
    slots = slot_ref.shape[0] - atoms
    width = slots // lanes
    send = send_ref[...]
    ghost = (send - atoms) ^ (space_ref[0] * width)

    def chosen(ref, index, value):
        hit = lax.broadcasted_iota(jnp.int32, ref.shape, 0) == index
        ref[...] = jnp.where(hit, value, 0.0).astype(ref.dtype)

    chosen(slot_ref, jnp.where(send < atoms, send + slots, ghost), 1.0)
    chosen(hit_ref, recv_ref[...], message_scale)
    turned_ref[...] = project_ref[...].astype(jnp.float32).T.astype(jnp.bfloat16)


def node_kernel(
    own_ref,
    near_ref,
    side_ref,
    far_ref,
    filter_ref,
    unit_ref,
    row_ref,
    slot_ref,
    hit_ref,
    turned_ref,
    update_ref,
    out_ref,
    hidden_ref,
    block_ref,
):
    atoms, chans = hidden_ref.shape
    packed = (own_ref, near_ref, side_ref, far_ref)
    group = jnp.concatenate([ref[:atoms, :] for ref in packed], axis=0)
    chosen = jnp.zeros((1, chans), jnp.float32)
    for place, ref in enumerate(packed):
        tail = ref[atoms:, :].astype(jnp.float32)
        chosen = chosen + tail[place : place + 1]
    member = lax.broadcasted_iota(jnp.int32, (len(packed) * atoms, chans), 0)
    fill = jnp.where(member == chosen.astype(jnp.int32), 1.0, 0.0)
    lane = lax.broadcasted_iota(jnp.int32, (len(packed) * atoms, atoms), 1)
    fill = jnp.concatenate([fill, jnp.where(member[:, :atoms] == lane, 1.0, 0.0)], axis=1)
    sender = jnp.dot(
        fill.astype(jnp.bfloat16), slot_ref[...], preferred_element_type=jnp.float32
    )
    projected = over_last(turned_ref[...], group).astype(jnp.bfloat16)
    picked = jnp.dot(projected, sender.astype(jnp.bfloat16), preferred_element_type=jnp.float32)
    scalar = picked[:chans] * filter_ref[:chans, :]
    carried = picked[chans:] * filter_ref[chans:, :]
    parts = [scalar] + [unit_ref[axis : axis + 1, :] * carried for axis in range(3)]
    message = jnp.concatenate([part.astype(jnp.bfloat16) for part in parts], axis=0)
    summed = over_last(hit_ref[...], message)
    square = jnp.zeros((atoms, chans), jnp.float32)
    for component in range(1, 4):
        part = summed[:, component * chans : (component + 1) * chans]
        square = square + part * part
    invariant = jnp.concatenate([summed[:, :chans], square], axis=1).astype(jnp.bfloat16)
    hidden = silu(jnp.dot(invariant, update_ref[...], preferred_element_type=jnp.float32))
    chi = jnp.sum(hidden * out_ref[...], axis=1, keepdims=True)
    lane = lax.broadcasted_iota(jnp.int32, (atoms, chans), 1)
    atom = lax.broadcasted_iota(jnp.int32, (atoms, chans), 0)
    chi = jnp.where(lane == atom + chi_segment * atoms, chi, 0.0)
    row = row_ref[...] - jnp.sum(chi, axis=0, keepdims=True)
    block_ref[...] = jnp.broadcast_to(row[None], block_ref.shape)
    hidden_ref[...] = hidden


def feature_kernel(packed_ref, hidden_ref, features_ref):
    atoms = features_ref.shape[0]
    old = packed_ref[...].astype(jnp.float32)[:atoms]
    features_ref[...] = (old + hidden_ref[...]).astype(jnp.bfloat16)


def reciprocal(value):
    rough = pl.reciprocal(value, approx=True)
    return rough * (2.0 - value * rough)


def smeared(scaled):
    decay = jnp.exp2(scaled * scaled * -math.log2(math.e))
    turn = reciprocal(1.0 + 0.3275911 * scaled)
    series = 1.061405429 * turn - 1.453152027
    series = series * turn + 1.421413741
    series = series * turn - 0.284496736
    series = series * turn + 0.254829592
    return 1.0 - series * turn * decay, decay


def charge_kernel(
    place_ref,
    field_ref,
    all_ref,
    charges_ref,
    forces_ref,
    virial_ref,
    matrix_ref,
    side_ref,
    value_ref,
    kept_ref,
):
    blocks, _, lanes = all_ref.shape
    own = charges_ref.shape[1]
    count = blocks * own
    fit = lanes // own
    segment = lax.broadcasted_iota(jnp.int32, (8, lanes), 1) // own
    tiles = []
    for first in range(0, blocks, fit):
        tile = jnp.zeros((8, lanes), jnp.float32)
        for place in range(fit):
            row = all_ref[(place_ref[0] + first + place) & (blocks - 1)]
            row = pltpu.roll(jnp.broadcast_to(row, (8, lanes)), 0, 1, stride=own, stride_axis=0)
            row = pltpu.roll(row, place * own, 1) if place else row
            tile = jnp.where(segment == place, row, tile)
        tiles.append(tile)
    everyone = jnp.concatenate(tiles, axis=1)
    last = lax.broadcasted_iota(jnp.int32, everyone.shape, 0) == 5
    everyone = everyone + jnp.where(last, field_ref[0] * everyone[2:3], 0.0)
    columns = everyone.T
    diag, rhs = everyone[4:5], everyone[5:6]
    spread_row = 2.0 * everyone[3:4] * everyone[3:4]
    tiles = count // lanes
    depth = own // 8
    shape = (depth, 8, lanes)
    lane = lax.broadcasted_iota(jnp.int32, shape, 2)
    line = lax.broadcasted_iota(jnp.int32, shape, 0) * 8 + lax.broadcasted_iota(jnp.int32, shape, 1)

    def part(row, tile):
        return row[:, tile * lanes : (tile + 1) * lanes]

    def down(row):
        return [jnp.broadcast_to(part(row, tile), (8, lanes))[None] for tile in range(tiles)]

    def along(column):
        return jnp.broadcast_to(column, (own, lanes)).reshape(shape)

    def total(value):
        return jnp.sum(value, axis=1, keepdims=True)

    axes = [down(everyone[axis : axis + 1]) for axis in range(3)]
    wide_row, rhs_row = down(spread_row), down(rhs)

    above = [jnp.zeros((8, lanes), jnp.float32) for _ in range(tiles)]
    image, across = [], []
    for start in range(0, count, own):
        first = start // lanes
        column = columns[start : start + own]
        place = [along(column[:, axis : axis + 1]) for axis in range(3)]
        wide = along(2.0 * column[:, 3:4] * column[:, 3:4])
        value = along(column[:, 5:6])
        value_ref[start : start + own, :] = value.reshape(own, lanes)
        below = jnp.zeros(shape, jnp.float32)
        for tile in range(first, tiles):
            delta = [place[axis] - axes[axis][tile] for axis in range(3)]
            squared = delta[0] * delta[0] + delta[1] * delta[1] + delta[2] * delta[2]
            if tile == first:
                same = lane == line + (start - first * lanes)
                squared = jnp.where(same, 1.0, squared)
            inverse = lax.rsqrt(squared)
            scale = lax.rsqrt(wide + wide_row[tile])
            smear, decay = smeared(squared * inverse * scale)
            kernel = smear * inverse
            if start == 0:
                slope = (two_over_root_pi * scale * decay - kernel) * inverse * inverse
                slope = jnp.where(same, 0.0, slope) if tile == first else slope
                for which, kind in enumerate(delta + [slope]):
                    kept_ref[which, :, tile * lanes : (tile + 1) * lanes] = kind.reshape(own, lanes)
            if tile == first:
                kernel = jnp.where(same, 0.0, kernel)
            else:
                below = below + kernel * rhs_row[tile]
            above[tile] = above[tile] + jnp.sum(kernel * value, axis=0)
            matrix_ref[start : start + own, tile * lanes : (tile + 1) * lanes] = kernel.reshape(
                own, lanes
            )
        if first + 1 < tiles:
            side_ref[start : start + own, :] = below.reshape(own, lanes)
        if (start + own) % lanes == 0:
            done = jnp.sum(above[first], axis=0, keepdims=True)
            if first + 1 < tiles:
                turned = side_ref[first * lanes : (first + 1) * lanes, :].T
                done = done + jnp.sum(turned, axis=0, keepdims=True)
            done = done + part(diag, first) * part(rhs, first)
            image.append(done)
            across.append(jnp.broadcast_to(done, (8, lanes)).T)
    image = jnp.concatenate(image, axis=1)
    norm = total(rhs * rhs)
    alpha = norm * reciprocal(total(rhs * image))
    residual = rhs - alpha * image
    fresh = total(residual * residual)
    again = fresh * reciprocal(norm)
    direction = residual + again * rhs
    onto = [jnp.zeros((8, lanes), jnp.float32) for _ in range(tiles)]
    above = [jnp.zeros((8, lanes), jnp.float32) for _ in range(tiles)]
    for start in range(0, count, own):
        first = start // lanes
        value = (1.0 + again) * value_ref[start : start + own, :]
        column = across[first][start - first * lanes : start - first * lanes + own, 0:1]
        value = value - alpha * jnp.broadcast_to(column, (own, lanes))
        value = value.reshape(shape)
        for tile in range(first, tiles):
            sums = onto if tile == first else above
            kernel = matrix_ref[start : start + own, tile * lanes : (tile + 1) * lanes]
            sums[tile] = sums[tile] + jnp.sum(kernel.reshape(shape) * value, axis=0)
    curved = jnp.zeros((8, lanes), jnp.float32)
    for tile in range(tiles):
        curved = curved + (onto[tile] + 2.0 * above[tile]) * part(direction, tile)
    curved = jnp.sum(curved, axis=0, keepdims=True)
    for tile in range(tiles):
        curved = curved + part(diag * direction * direction, tile)
    charges = alpha * rhs + fresh * reciprocal(total(curved)) * direction

    sums = [jnp.zeros(shape, jnp.float32) for _ in range(9)]
    charge_row = down(charges)
    for tile in range(tiles):
        *delta, slope = [
            kept_ref[which, :, tile * lanes : (tile + 1) * lanes].reshape(shape)
            for which in range(4)
        ]
        weight = charge_row[tile] * slope
        pulled = [weight * delta[axis] for axis in range(3)]
        terms = pulled + [
            pulled[left] * delta[right]
            for left, right in ((0, 0), (1, 1), (2, 2), (0, 1), (0, 2), (1, 2))
        ]
        sums = [old + term for old, term in zip(sums, terms)]
    table = jnp.zeros((own, lanes), jnp.float32)
    lane = lane.reshape(own, lanes)
    for place, value in enumerate(sums):
        table = jnp.where(lane == place, total(value.reshape(own, lanes)), table)
    table = table.T
    mine = charges[:, :own]
    charges_ref[...] = mine
    pull = -mine * table[0:3]
    third = lax.broadcasted_iota(jnp.int32, pull.shape, 0) == 2
    forces_ref[...] = pull + jnp.where(third, mine * field_ref[0], 0.0)
    virial_ref[...] = 0.5 * mine * table[3:9]


def kernel_call(kernel, shapes, arguments, scalars=0, far=0, scratch=(), flops=0):
    shapes = tuple(jax.ShapeDtypeStruct(shape, kind) for shape, kind in shapes)
    spaces = [pltpu.SMEM] * scalars + [pltpu.HBM] * far
    spaces = spaces + [pltpu.VMEM] * (len(arguments) - len(spaces))
    arguments = [
        pltpu.with_memory_space_constraint(value, space) if space is pltpu.HBM else value
        for value, space in zip(arguments, spaces)
    ]
    return pl.pallas_call(
        kernel,
        out_shape=shapes,
        in_specs=[pl.BlockSpec(memory_space=space) for space in spaces],
        out_specs=tuple(pl.BlockSpec(memory_space=pltpu.VMEM) for _ in shapes),
        scratch_shapes=list(scratch),
        compiler_params=pltpu.CompilerParams(vmem_limit_bytes=32 * 1024 * 1024),
        cost_estimate=pl.CostEstimate(flops=flops, bytes_accessed=1 << 20, transcendentals=0),
    )(*arguments)


def exchanged(block, axis, step):
    size = lax.axis_size(axis)
    return lax.ppermute(block, axis, [(place, place ^ step) for place in range(size)])


def few_shards(
    features,
    positions,
    species,
    ghost_list,
    edge_recv,
    edge_send,
    edge_vec,
    w_msg,
    w_rad1,
    w_rad2,
    w_up,
    w_out,
    hardness,
    width,
    chi_shift,
    field,
):
    atoms, chans = features.shape
    edges = edge_recv.shape[0]
    rows, lanes = lax.axis_size("row"), lax.axis_size("space")
    space = lax.axis_index("space").astype(jnp.int32)
    (packed,) = kernel_call(
        pack_kernel,
        [((atoms + 16, chans), jnp.bfloat16)],
        (space.reshape(1), features, ghost_list),
        scalars=1,
        far=2,
        scratch=[
            pltpu.VMEM(ghost_list.shape, ghost_list.dtype),
            pltpu.SemaphoreType.DMA((2,)),
        ],
    )
    others = [exchanged(packed, "space", step) for step in range(1, lanes)]
    rest = (edge_vec, w_rad1, w_rad2, edge_send[None], edge_recv[None], w_msg)
    rest = rest + (species[None], hardness[None], width[None], chi_shift[None], positions)
    kept = (w_up, w_out[None])
    parts = kernel_call(
        functools.partial(edge_kernel, lanes),
        [
            ((2 * chans, edges), jnp.float32),
            ((8, edges), jnp.float32),
            ((1, chans), jnp.float32),
            ((chans + atoms, edges), jnp.bfloat16),
            ((atoms, edges), jnp.bfloat16),
            ((2 * chans, chans), jnp.bfloat16),
            (w_up.shape, w_up.dtype),
            ((1, chans), jnp.float32),
        ],
        (space.reshape(1), *rest, *kept),
        scalars=1,
        far=len(rest + kept),
        scratch=[pltpu.VMEM(value.shape, value.dtype) for value in rest]
        + [pltpu.SemaphoreType.DMA((len(rest + kept),))],
        flops=1 << 28,
    )
    devices = rows * lanes
    hidden, block = kernel_call(
        node_kernel,
        [((atoms, chans), jnp.float32), ((devices, 1, chans), jnp.float32)],
        (packed, *others, *parts),
        flops=1 << 28,
    )
    (new_features,) = kernel_call(
        feature_kernel, [((atoms, chans), jnp.bfloat16)], (packed, hidden), flops=1 << 20
    )
    block = lax.all_to_all(block, everywhere, 0, 0, tiled=True)
    place = lax.axis_index("row").astype(jnp.int32) * lanes + space
    everybody = rows * lanes * atoms
    charges, forces, virial = kernel_call(
        charge_kernel,
        [((count, atoms), jnp.float32) for count in (1, 3, 6)],
        (place.reshape(1), field, block),
        scalars=2,
        scratch=[
            pltpu.VMEM((everybody, everybody), jnp.float32),
            pltpu.VMEM((everybody, chans), jnp.float32),
            pltpu.VMEM((everybody, chans), jnp.float32),
            pltpu.VMEM((4, atoms, everybody), jnp.float32),
        ],
        flops=1 << 28,
    )
    return (new_features, charges[0], forces, virial)


def solution(mesh):
    small = mesh.shape["space"] == 4 and mesh.shape["row"] == 8
    return jax.shard_map(
        few_shards if small else shards,
        mesh=mesh,
        in_specs=(
            P(("row", "space"), None),
            P(None, ("row", "space")),
            P(("row", "space")),
            P("row", "space", None),
            P(("row", "space")),
            P(("row", "space")),
            P(None, ("row", "space")),
            P(),
            P(),
            P(),
            P(),
            P(),
            P(),
            P(),
            P(),
            P(),
        ),
        out_specs=(
            P(("row", "space"), None),
            P(("row", "space")),
            P(None, ("row", "space")),
            P(None, ("row", "space")),
        ),
        check_vma=False,
    )
```

```python
import functools
import math

import jax
import jax.numpy as jnp
from jax import lax
from jax.experimental import pallas as pl
from jax.experimental.pallas import tpu as pltpu
from jax.sharding import PartitionSpec as P

ITERS = 2


cutoff = 6.0
message_scale = 0.125
two_over_root_pi = 2.0 / math.sqrt(math.pi)
inverse_root_pi = 1.0 / math.sqrt(math.pi)
replicate_limit = 1024
everywhere = ("row", "space")


def lookup(species, table):
    result = jnp.zeros(species.shape, jnp.float32)
    for kind in range(table.shape[0]):
        result = result + jnp.where(species == kind, table[kind], 0.0)
    return result


def pair_terms(target, target_labels, source, source_labels):
    delta = target[:3, :, None] - source[:3, None, :]
    squared = jnp.sum(delta * delta, axis=0)
    same = target_labels[:, None] == source_labels[None, :]
    squared = jnp.where(same, 1.0, squared)
    inverse = lax.rsqrt(squared)
    radius = squared * inverse
    spread = target[3][:, None] * target[3][:, None] + source[3][None, :] * source[3][None, :]
    scale = lax.rsqrt(2.0 * spread)
    scaled = radius * scale
    smear = lax.erf(scaled)
    return delta, same, inverse, scale, scaled, smear


def coulomb(target, target_labels, source, source_labels):
    _, same, inverse, _, _, smear = pair_terms(target, target_labels, source, source_labels)
    return jnp.where(same, 0.0, smear * inverse)


def pair_forces(target, target_labels, source, source_labels, source_charge):
    delta, same, inverse, scale, scaled, smear = pair_terms(
        target, target_labels, source, source_labels
    )
    slope = (
        two_over_root_pi * scale * jnp.exp(-scaled * scaled) * inverse - smear * inverse * inverse
    )
    weight = jnp.where(same, 0.0, source_charge[None, :] * slope * inverse)
    first = jnp.sum(weight[None] * delta, axis=2)
    pairs = ((0, 0), (1, 1), (2, 2), (0, 1), (0, 2), (1, 2))
    second = jnp.stack(
        [jnp.sum(weight * delta[left] * delta[right], axis=1) for left, right in pairs]
    )
    return jnp.concatenate([first, second], axis=0)


def edge_terms(receive, sender_rows, vectors, projected, w_rad1, w_rad2, atoms):
    length = jnp.sqrt(jnp.sum(vectors * vectors, axis=0))
    unit = vectors / length
    order = jnp.arange(1, w_rad1.shape[0] + 1, dtype=jnp.int32).astype(jnp.float32)[:, None]
    ratio = length / cutoff
    envelope = (1.0 - ratio * ratio) * (1.0 - ratio * ratio)
    basis = jnp.sin(order * math.pi * ratio) / ratio * envelope
    mixed = lax.dot_general(
        basis, w_rad1, (((0,), (0,)), ((), ())), precision=lax.Precision.HIGHEST
    )
    radial = jax.nn.silu(mixed).astype(jnp.bfloat16)
    filters = jnp.dot(radial, w_rad2, preferred_element_type=jnp.float32)
    picked = jnp.take(projected, sender_rows, axis=0).astype(jnp.float32) * filters
    chans = w_rad1.shape[1]
    scalar = picked[:, :chans]
    carried = picked[:, chans:]
    joined = [
        scalar,
        unit[0][:, None] * carried,
        unit[1][:, None] * carried,
        unit[2][:, None] * carried,
    ]
    message = jnp.concatenate(joined, axis=1).astype(jnp.bfloat16)
    onehot = (jnp.arange(atoms, dtype=jnp.int32)[:, None] == receive[None, :]).astype(jnp.bfloat16)
    return jnp.dot(onehot, message, preferred_element_type=jnp.float32)


def gathered(block, devices):
    copies = jnp.broadcast_to(block[None], (devices,) + block.shape)
    return lax.all_to_all(copies, everywhere, split_axis=0, concat_axis=0, tiled=True)


def shards(
    features,
    positions,
    species,
    ghost_list,
    edge_recv,
    edge_send,
    edge_vec,
    w_msg,
    w_rad1,
    w_rad2,
    w_up,
    w_out,
    hardness,
    width,
    chi_shift,
    field,
):
    atoms = features.shape[0]
    chans = features.shape[1]
    lanes = lax.axis_size("space")
    devices = lanes * lax.axis_size("row")
    everybody = devices * atoms
    me = lax.axis_index("row") * lanes + lax.axis_index("space")
    sigma = lookup(species, width)
    diag = lookup(species, hardness) + inverse_root_pi / sigma
    placed = jnp.concatenate([positions, sigma[None, :], diag[None, :]], axis=0)
    everyone = gathered(placed, devices).transpose(1, 0, 2).reshape(5, everybody)
    lists = ghost_list[0]
    outgoing = jnp.take(features, lists.reshape(-1), axis=0).reshape(lanes, lists.shape[1], chans)
    ghost_rows = jnp.einsum(
        "dkc,cf->dkf",
        lax.all_to_all(outgoing, "space", split_axis=0, concat_axis=0, tiled=True),
        w_msg,
        preferred_element_type=jnp.float32,
    ).astype(jnp.bfloat16)
    own_rows = jnp.dot(features, w_msg, preferred_element_type=jnp.float32).astype(jnp.bfloat16)
    projected = jnp.concatenate([own_rows, ghost_rows.reshape(-1, 2 * chans)], axis=0)
    summed = edge_terms(edge_recv, edge_send, edge_vec, projected, w_rad1, w_rad2, atoms)
    summed = summed * message_scale
    vector_part = summed[:, chans:].reshape(atoms, 3, chans)
    invariant = jnp.concatenate(
        [summed[:, :chans], jnp.sum(vector_part * vector_part, axis=1)], axis=1
    ).astype(jnp.bfloat16)
    hidden = jax.nn.silu(jnp.dot(invariant, w_up, preferred_element_type=jnp.float32))
    new_features = (features.astype(jnp.float32) + hidden).astype(jnp.bfloat16)
    chi = jnp.dot(hidden, w_out, precision=lax.Precision.HIGHEST) + lookup(species, chi_shift)
    own_labels = me * atoms + jnp.arange(atoms, dtype=jnp.int32)
    all_labels = jnp.arange(everybody, dtype=jnp.int32)
    rhs = field[0] * positions[2] - chi

    if everybody <= replicate_limit:
        kernel = coulomb(everyone, all_labels, everyone, all_labels)
        residual = gathered(rhs, devices).reshape(everybody)
        all_charges = conjugate(
            residual, lambda v: everyone[4] * v + jnp.sum(kernel * v[None, :], axis=1), jnp.sum
        )
        charges = lax.dynamic_slice(all_charges, (me * atoms,), (atoms,))
    else:
        kernel = coulomb(placed, own_labels, everyone, all_labels)

        def spread(vector):
            return gathered(vector, devices).reshape(everybody)

        charges = conjugate(
            rhs,
            lambda v: diag * v + jnp.sum(kernel * spread(v)[None, :], axis=1),
            lambda v: lax.psum(jnp.sum(v), everywhere),
        )
        all_charges = spread(charges)
    sums = pair_forces(placed, own_labels, everyone, all_labels, all_charges)
    pull = -charges[None, :] * sums[:3]
    forces = jnp.concatenate([pull[:2], pull[2:] + (charges * field[0])[None, :]], axis=0)
    virial = 0.5 * charges[None, :] * sums[3:]
    return (new_features, charges, forces, virial)


def conjugate(rhs, apply, total):
    charges = jnp.zeros_like(rhs)
    residual = rhs
    direction = rhs
    norm_now = total(residual * residual)
    for step in range(ITERS):
        image = apply(direction)
        alpha = norm_now / total(direction * image)
        charges = charges + alpha * direction
        if step + 1 < ITERS:
            residual = residual - alpha * image
            fresh = total(residual * residual)
            direction = residual + fresh / norm_now * direction
            norm_now = fresh
    return charges


def split3(value):
    first = value.astype(jnp.bfloat16).astype(jnp.float32)
    rest = value - first
    second = rest.astype(jnp.bfloat16).astype(jnp.float32)
    third = (rest - second).astype(jnp.bfloat16).astype(jnp.float32)
    return first, second, third


def over_first(left, right):
    return lax.dot_general(
        left, right, (((0,), (0,)), ((), ())), preferred_element_type=jnp.float32
    )


def over_last(left, right, precision=None):
    return lax.dot_general(
        left,
        right,
        (((1,), (1,)), ((), ())),
        precision=precision,
        preferred_element_type=jnp.float32,
    )


def reciprocal(value):
    return pl.reciprocal(value, approx=True)


def silu(value):
    return value * reciprocal(1.0 + jnp.exp(-value))


def silu_half(value):
    return (0.5 * value) * (1.0 + jnp.tanh(0.5 * value))


sine_series = [(-1.0) ** k * math.pi ** (2 * k + 1) / math.factorial(2 * k + 1) for k in range(7)]


def fetched(pairs, semaphores):
    copies = [
        pltpu.make_async_copy(source, target, semaphores.at[place])
        for place, (source, target) in enumerate(pairs)
    ]
    for copy in copies:
        copy.start()
    return copies


chi_segment = 3


def pack_kernel(space_ref, features_ref, lists_ref, packed_ref, held_ref, semaphores):
    atoms, chans = features_ref.shape
    copies = fetched(
        [(lists_ref, held_ref), (features_ref, packed_ref.at[pl.ds(0, atoms)])], semaphores
    )
    copies[0].wait()
    _, lanes, width = held_ref.shape
    rows = []
    for place in range(lanes):
        row = held_ref[0, pl.ds(space_ref[0] ^ place, 1), :].astype(jnp.float32) + place * atoms
        parts = [jnp.zeros((1, width), jnp.float32)] * lanes
        parts[place] = row
        rows.append(jnp.concatenate(parts, axis=1))
    rows.append(jnp.zeros((packed_ref.shape[0] - atoms - lanes, chans), jnp.float32))
    packed_ref[atoms:, :] = jnp.concatenate(rows, axis=0).astype(jnp.bfloat16)
    copies[1].wait()


def edge_kernel(lanes, space_ref, *refs):
    count = (len(refs) - 7) // 2
    far, near, semaphores = refs[:count], refs[count + 8 : -1], refs[-1]
    filter_ref, unit_ref, row_ref, slot_ref, hit_ref = refs[count : count + 5]
    turned_ref, update_ref, out_ref = refs[count + 5 : count + 8]
    vec_ref, first_ref, second_ref, send_ref, recv_ref, project_ref = near[:6]
    species_ref, hardness_ref, width_ref, shift_ref, positions_ref = near[6:]
    copies = fetched(list(zip(far, near + (update_ref, out_ref))), semaphores)
    for copy in copies[:3]:
        copy.wait()
    edges = vec_ref.shape[1]
    orders = first_ref.shape[0]
    vec = vec_ref[...]
    east, north, up = vec[0:1], vec[1:2], vec[2:3]
    squared = east * east + north * north + up * up
    inverse = lax.rsqrt(squared)
    unit_ref[0:3, :] = vec * inverse
    ratio = squared * inverse * (1.0 / cutoff)
    envelope = (1.0 - ratio * ratio) * (1.0 - ratio * ratio) * (cutoff * inverse)
    order = lax.broadcasted_iota(jnp.int32, (orders, edges), 0).astype(jnp.float32) + 1.0
    turns = order * ratio
    whole = jnp.floor(turns + 0.5)
    part = turns - whole
    sign = 1.0 - 2.0 * (whole - 2.0 * jnp.floor(whole * 0.5))
    series = jnp.full_like(part, sine_series[-1])
    for coefficient in sine_series[-2::-1]:
        series = series * (part * part) + coefficient
    basis = series * part * (sign * envelope)
    b1, b2, b3 = split3(basis)
    w1, w2, w3 = split3(first_ref[...])
    mixed = over_first(
        jnp.concatenate([w1, w1, w2, w2, w1, w3], axis=0).astype(jnp.bfloat16),
        jnp.concatenate([b1, b2, b1, b2, b3, b1], axis=0).astype(jnp.bfloat16),
    )
    radial = silu_half(mixed).astype(jnp.bfloat16)
    filter_ref[...] = over_first(second_ref[...], radial)
    for copy in copies[3:]:
        copy.wait()
    species = species_ref[...]

    def table(ref):
        result = jnp.zeros(species.shape, jnp.float32)
        for kind in range(ref.shape[1]):
            result = result + jnp.where(species == kind, ref[:, kind : kind + 1], 0.0)
        return result

    positions = positions_ref[...]
    sigma = table(width_ref)
    atoms = species.shape[1]
    chans = row_ref.shape[1]
    diag = table(hardness_ref) + inverse_root_pi / sigma
    blank = jnp.zeros((2, atoms), jnp.float32)
    rows = [positions[0:1], blank, -table(shift_ref), diag, sigma, positions[2:3], positions[1:2]]
    block = jnp.concatenate(
        [jnp.concatenate(rows, axis=0), jnp.zeros((8, chans - atoms), jnp.float32)], axis=1
    )
    block = pltpu.roll(block, 0, 1, stride=atoms, stride_axis=0)
    row_ref[...] = jnp.sum(block, axis=0, keepdims=True)
    slots = slot_ref.shape[0] - atoms
    width = slots // lanes
    send = send_ref[...]
    ghost = (send - atoms) ^ (space_ref[0] * width)

    def chosen(ref, index, value):
        hit = lax.broadcasted_iota(jnp.int32, ref.shape, 0) == index
        ref[...] = jnp.where(hit, value, 0.0).astype(ref.dtype)

    chosen(slot_ref, jnp.where(send < atoms, send + slots, ghost), 1.0)
    chosen(hit_ref, recv_ref[...], message_scale)
    turned_ref[...] = project_ref[...].astype(jnp.float32).T.astype(jnp.bfloat16)


def node_kernel(
    own_ref,
    near_ref,
    side_ref,
    far_ref,
    filter_ref,
    unit_ref,
    row_ref,
    slot_ref,
    hit_ref,
    turned_ref,
    update_ref,
    out_ref,
    hidden_ref,
    block_ref,
):
    atoms, chans = hidden_ref.shape
    packed = (own_ref, near_ref, side_ref, far_ref)
    group = jnp.concatenate([ref[:atoms, :] for ref in packed], axis=0)
    chosen = jnp.zeros((1, chans), jnp.float32)
    for place, ref in enumerate(packed):
        tail = ref[atoms:, :].astype(jnp.float32)
        chosen = chosen + tail[place : place + 1]
    member = lax.broadcasted_iota(jnp.int32, (len(packed) * atoms, chans), 0)
    fill = jnp.where(member == chosen.astype(jnp.int32), 1.0, 0.0)
    lane = lax.broadcasted_iota(jnp.int32, (len(packed) * atoms, atoms), 1)
    fill = jnp.concatenate([fill, jnp.where(member[:, :atoms] == lane, 1.0, 0.0)], axis=1)
    sender = jnp.dot(
        fill.astype(jnp.bfloat16), slot_ref[...], preferred_element_type=jnp.float32
    )
    projected = over_last(turned_ref[...], group).astype(jnp.bfloat16)
    picked = jnp.dot(projected, sender.astype(jnp.bfloat16), preferred_element_type=jnp.float32)
    scalar = picked[:chans] * filter_ref[:chans, :]
    carried = picked[chans:] * filter_ref[chans:, :]
    parts = [scalar] + [unit_ref[axis : axis + 1, :] * carried for axis in range(3)]
    message = jnp.concatenate([part.astype(jnp.bfloat16) for part in parts], axis=0)
    summed = over_last(hit_ref[...], message)
    square = jnp.zeros((atoms, chans), jnp.float32)
    for component in range(1, 4):
        part = summed[:, component * chans : (component + 1) * chans]
        square = square + part * part
    invariant = jnp.concatenate([summed[:, :chans], square], axis=1).astype(jnp.bfloat16)
    hidden = silu(jnp.dot(invariant, update_ref[...], preferred_element_type=jnp.float32))
    chi = jnp.sum(hidden * out_ref[...], axis=1, keepdims=True)
    lane = lax.broadcasted_iota(jnp.int32, (atoms, chans), 1)
    atom = lax.broadcasted_iota(jnp.int32, (atoms, chans), 0)
    chi = jnp.where(lane == atom + chi_segment * atoms, chi, 0.0)
    row = row_ref[...] - jnp.sum(chi, axis=0, keepdims=True)
    block_ref[...] = jnp.broadcast_to(row[None], block_ref.shape)
    hidden_ref[...] = hidden


def feature_kernel(packed_ref, hidden_ref, features_ref):
    atoms = features_ref.shape[0]
    old = packed_ref[...].astype(jnp.float32)[:atoms]
    features_ref[...] = (old + hidden_ref[...]).astype(jnp.bfloat16)


def smeared(scaled):
    decay = jnp.exp2(scaled * scaled * -math.log2(math.e))
    turn = reciprocal(1.0 + 0.3275911 * scaled)
    series = 1.061405429 * turn - 1.453152027
    series = series * turn + 1.421413741
    series = series * turn - 0.284496736
    series = series * turn + 0.254829592
    return 1.0 - series * turn * decay, decay


def charge_kernel(
    place_ref,
    field_ref,
    all_ref,
    charges_ref,
    forces_ref,
    virial_ref,
    matrix_ref,
    side_ref,
    value_ref,
    kept_ref,
):
    blocks, _, lanes = all_ref.shape
    own = charges_ref.shape[1]
    count = blocks * own
    fit = lanes // own
    segment = lax.broadcasted_iota(jnp.int32, (8, lanes), 1) // own
    tiles = []
    for first in range(0, blocks, fit):
        tile = jnp.zeros((8, lanes), jnp.float32)
        for place in range(fit):
            row = all_ref[(place_ref[0] + first + place) & (blocks - 1)]
            row = pltpu.roll(jnp.broadcast_to(row, (8, lanes)), 0, 1, stride=own, stride_axis=0)
            row = pltpu.roll(row, place * own, 1) if place else row
            tile = jnp.where(segment == place, row, tile)
        tiles.append(tile)
    everyone = jnp.concatenate(tiles, axis=1)
    last = lax.broadcasted_iota(jnp.int32, everyone.shape, 0) == 5
    everyone = everyone + jnp.where(last, field_ref[0] * everyone[2:3], 0.0)
    columns = everyone.T
    diag, rhs = everyone[4:5], everyone[5:6]
    spread_row = 2.0 * everyone[3:4] * everyone[3:4]
    tiles = count // lanes
    depth = own // 8
    shape = (depth, 8, lanes)
    lane = lax.broadcasted_iota(jnp.int32, shape, 2)
    line = lax.broadcasted_iota(jnp.int32, shape, 0) * 8 + lax.broadcasted_iota(jnp.int32, shape, 1)

    def part(row, tile):
        return row[:, tile * lanes : (tile + 1) * lanes]

    def down(row):
        return [jnp.broadcast_to(part(row, tile), (8, lanes))[None] for tile in range(tiles)]

    def along(column):
        return jnp.broadcast_to(column, (own, lanes)).reshape(shape)

    def total(value):
        return jnp.sum(value, axis=1, keepdims=True)

    axes = [down(everyone[axis : axis + 1]) for axis in range(3)]
    wide_row, rhs_row = down(spread_row), down(rhs)

    above = [jnp.zeros((8, lanes), jnp.float32) for _ in range(tiles)]
    for start in range(0, count, own):
        first = start // lanes
        column = columns[start : start + own]
        place = [along(column[:, axis : axis + 1]) for axis in range(3)]
        wide = along(2.0 * column[:, 3:4] * column[:, 3:4])
        value = along(column[:, 5:6])
        value_ref[start : start + own, :] = value.reshape(own, lanes)
        below = jnp.zeros(shape, jnp.float32)
        for tile in range(first, tiles):
            delta = [place[axis] - axes[axis][tile] for axis in range(3)]
            squared = delta[0] * delta[0] + delta[1] * delta[1] + delta[2] * delta[2]
            if tile == first:
                same = lane == line + (start - first * lanes)
                squared = jnp.where(same, 1.0, squared)
            inverse = lax.rsqrt(squared)
            scale = lax.rsqrt(wide + wide_row[tile])
            smear, decay = smeared(squared * inverse * scale)
            kernel = smear * inverse
            if start == 0:
                slope = (two_over_root_pi * scale * decay - kernel) * inverse * inverse
                slope = jnp.where(same, 0.0, slope) if tile == first else slope
                for which, kind in enumerate(delta + [slope]):
                    kept_ref[which, :, tile * lanes : (tile + 1) * lanes] = kind.reshape(own, lanes)
            if tile == first:
                kernel = jnp.where(same, 0.0, kernel)
            else:
                below = below + kernel * rhs_row[tile]
            above[tile] = above[tile] + jnp.sum(kernel * value, axis=0)
            matrix_ref[start : start + own, tile * lanes : (tile + 1) * lanes] = kernel.reshape(
                own, lanes
            )
        if first + 1 < tiles:
            side_ref[start : start + own, :] = below.reshape(own, lanes)
    image = []
    for tile in range(tiles):
        value = jnp.sum(above[tile], axis=0, keepdims=True)
        if tile + 1 < tiles:
            below = side_ref[tile * lanes : (tile + 1) * lanes, :].T
            value = value + jnp.sum(below, axis=0, keepdims=True)
        image.append(value)
    image = diag * rhs + jnp.concatenate(image, axis=1)
    across = jnp.broadcast_to(image, (8, count)).T
    norm = total(rhs * rhs)
    alpha = norm * reciprocal(total(rhs * image))
    residual = rhs - alpha * image
    fresh = total(residual * residual)
    again = fresh * reciprocal(norm)
    direction = residual + again * rhs
    onto = [jnp.zeros((8, lanes), jnp.float32) for _ in range(tiles)]
    above = [jnp.zeros((8, lanes), jnp.float32) for _ in range(tiles)]
    for start in range(0, count, own):
        first = start // lanes
        value = (1.0 + again) * value_ref[start : start + own, :]
        value = value - alpha * jnp.broadcast_to(across[start : start + own, 0:1], (own, lanes))
        value = value.reshape(shape)
        for tile in range(first, tiles):
            sums = onto if tile == first else above
            kernel = matrix_ref[start : start + own, tile * lanes : (tile + 1) * lanes]
            sums[tile] = sums[tile] + jnp.sum(kernel.reshape(shape) * value, axis=0)
    curved = jnp.zeros((8, lanes), jnp.float32)
    for tile in range(tiles):
        curved = curved + (onto[tile] + 2.0 * above[tile]) * part(direction, tile)
    curved = jnp.sum(curved, axis=0, keepdims=True)
    for tile in range(tiles):
        curved = curved + part(diag * direction * direction, tile)
    charges = alpha * rhs + fresh * reciprocal(total(curved)) * direction

    sums = [jnp.zeros(shape, jnp.float32) for _ in range(9)]
    charge_row = down(charges)
    for tile in range(tiles):
        *delta, slope = [
            kept_ref[which, :, tile * lanes : (tile + 1) * lanes].reshape(shape)
            for which in range(4)
        ]
        weight = charge_row[tile] * slope
        pulled = [weight * delta[axis] for axis in range(3)]
        terms = pulled + [
            pulled[left] * delta[right]
            for left, right in ((0, 0), (1, 1), (2, 2), (0, 1), (0, 2), (1, 2))
        ]
        sums = [old + term for old, term in zip(sums, terms)]
    table = jnp.zeros((own, lanes), jnp.float32)
    lane = lane.reshape(own, lanes)
    for place, value in enumerate(sums):
        table = jnp.where(lane == place, total(value.reshape(own, lanes)), table)
    table = table.T
    mine = charges[:, :own]
    charges_ref[...] = mine
    pull = -mine * table[0:3]
    third = lax.broadcasted_iota(jnp.int32, pull.shape, 0) == 2
    forces_ref[...] = pull + jnp.where(third, mine * field_ref[0], 0.0)
    virial_ref[...] = 0.5 * mine * table[3:9]


def kernel_call(kernel, shapes, arguments, scalars=0, far=0, scratch=(), flops=0):
    shapes = tuple(jax.ShapeDtypeStruct(shape, kind) for shape, kind in shapes)
    spaces = [pltpu.SMEM] * scalars + [pltpu.HBM] * far
    spaces = spaces + [pltpu.VMEM] * (len(arguments) - len(spaces))
    arguments = [
        pltpu.with_memory_space_constraint(value, space) if space is pltpu.HBM else value
        for value, space in zip(arguments, spaces)
    ]
    return pl.pallas_call(
        kernel,
        out_shape=shapes,
        in_specs=[pl.BlockSpec(memory_space=space) for space in spaces],
        out_specs=tuple(pl.BlockSpec(memory_space=pltpu.VMEM) for _ in shapes),
        scratch_shapes=list(scratch),
        compiler_params=pltpu.CompilerParams(vmem_limit_bytes=32 * 1024 * 1024),
        cost_estimate=pl.CostEstimate(flops=flops, bytes_accessed=1 << 20, transcendentals=0),
    )(*arguments)


def exchanged(block, axis, step):
    size = lax.axis_size(axis)
    return lax.ppermute(block, axis, [(place, place ^ step) for place in range(size)])


def few_shards(
    features,
    positions,
    species,
    ghost_list,
    edge_recv,
    edge_send,
    edge_vec,
    w_msg,
    w_rad1,
    w_rad2,
    w_up,
    w_out,
    hardness,
    width,
    chi_shift,
    field,
):
    atoms, chans = features.shape
    edges = edge_recv.shape[0]
    rows, lanes = lax.axis_size("row"), lax.axis_size("space")
    space = lax.axis_index("space").astype(jnp.int32)
    (packed,) = kernel_call(
        pack_kernel,
        [((atoms + 16, chans), jnp.bfloat16)],
        (space.reshape(1), features, ghost_list),
        scalars=1,
        far=2,
        scratch=[
            pltpu.VMEM(ghost_list.shape, ghost_list.dtype),
            pltpu.SemaphoreType.DMA((2,)),
        ],
    )
    others = [exchanged(packed, "space", step) for step in range(1, lanes)]
    rest = (edge_vec, w_rad1, w_rad2, edge_send[None], edge_recv[None], w_msg)
    rest = rest + (species[None], hardness[None], width[None], chi_shift[None], positions)
    kept = (w_up, w_out[None])
    parts = kernel_call(
        functools.partial(edge_kernel, lanes),
        [
            ((2 * chans, edges), jnp.float32),
            ((8, edges), jnp.float32),
            ((1, chans), jnp.float32),
            ((chans + atoms, edges), jnp.bfloat16),
            ((atoms, edges), jnp.bfloat16),
            ((2 * chans, chans), jnp.bfloat16),
            (w_up.shape, w_up.dtype),
            ((1, chans), jnp.float32),
        ],
        (space.reshape(1), *rest, *kept),
        scalars=1,
        far=len(rest + kept),
        scratch=[pltpu.VMEM(value.shape, value.dtype) for value in rest]
        + [pltpu.SemaphoreType.DMA((len(rest + kept),))],
        flops=1 << 28,
    )
    devices = rows * lanes
    hidden, block = kernel_call(
        node_kernel,
        [((atoms, chans), jnp.float32), ((devices, 1, chans), jnp.float32)],
        (packed, *others, *parts),
        flops=1 << 28,
    )
    (new_features,) = kernel_call(
        feature_kernel, [((atoms, chans), jnp.bfloat16)], (packed, hidden), flops=1 << 20
    )
    block = lax.all_to_all(block, everywhere, 0, 0, tiled=True)
    place = lax.axis_index("row").astype(jnp.int32) * lanes + space
    everybody = rows * lanes * atoms
    charges, forces, virial = kernel_call(
        charge_kernel,
        [((count, atoms), jnp.float32) for count in (1, 3, 6)],
        (place.reshape(1), field, block),
        scalars=2,
        scratch=[
            pltpu.VMEM((everybody, everybody), jnp.float32),
            pltpu.VMEM((everybody, chans), jnp.float32),
            pltpu.VMEM((everybody, chans), jnp.float32),
            pltpu.VMEM((4, atoms, everybody), jnp.float32),
        ],
        flops=1 << 28,
    )
    return (new_features, charges[0], forces, virial)


def solution(mesh):
    small = mesh.shape["space"] == 4 and mesh.shape["row"] == 8
    return jax.shard_map(
        few_shards if small else shards,
        mesh=mesh,
        in_specs=(
            P(("row", "space"), None),
            P(None, ("row", "space")),
            P(("row", "space")),
            P("row", "space", None),
            P(("row", "space")),
            P(("row", "space")),
            P(None, ("row", "space")),
            P(),
            P(),
            P(),
            P(),
            P(),
            P(),
            P(),
            P(),
            P(),
        ),
        out_specs=(
            P(("row", "space"), None),
            P(("row", "space")),
            P(None, ("row", "space")),
            P(None, ("row", "space")),
        ),
        check_vma=False,
    )
```

```python
import functools
import math

import jax
import jax.numpy as jnp
from jax import lax
from jax.experimental import pallas as pl
from jax.experimental.pallas import tpu as pltpu
from jax.sharding import PartitionSpec as P

ITERS = 2


cutoff = 6.0
message_scale = 0.125
two_over_root_pi = 2.0 / math.sqrt(math.pi)
inverse_root_pi = 1.0 / math.sqrt(math.pi)
replicate_limit = 1024
everywhere = ("row", "space")


def lookup(species, table):
    result = jnp.zeros(species.shape, jnp.float32)
    for kind in range(table.shape[0]):
        result = result + jnp.where(species == kind, table[kind], 0.0)
    return result


def pair_terms(target, target_labels, source, source_labels):
    delta = target[:3, :, None] - source[:3, None, :]
    squared = jnp.sum(delta * delta, axis=0)
    same = target_labels[:, None] == source_labels[None, :]
    squared = jnp.where(same, 1.0, squared)
    inverse = lax.rsqrt(squared)
    radius = squared * inverse
    spread = target[3][:, None] * target[3][:, None] + source[3][None, :] * source[3][None, :]
    scale = lax.rsqrt(2.0 * spread)
    scaled = radius * scale
    smear = lax.erf(scaled)
    return delta, same, inverse, scale, scaled, smear


def coulomb(target, target_labels, source, source_labels):
    _, same, inverse, _, _, smear = pair_terms(target, target_labels, source, source_labels)
    return jnp.where(same, 0.0, smear * inverse)


def pair_forces(target, target_labels, source, source_labels, source_charge):
    delta, same, inverse, scale, scaled, smear = pair_terms(
        target, target_labels, source, source_labels
    )
    slope = (
        two_over_root_pi * scale * jnp.exp(-scaled * scaled) * inverse - smear * inverse * inverse
    )
    weight = jnp.where(same, 0.0, source_charge[None, :] * slope * inverse)
    first = jnp.sum(weight[None] * delta, axis=2)
    pairs = ((0, 0), (1, 1), (2, 2), (0, 1), (0, 2), (1, 2))
    second = jnp.stack(
        [jnp.sum(weight * delta[left] * delta[right], axis=1) for left, right in pairs]
    )
    return jnp.concatenate([first, second], axis=0)


def edge_terms(receive, sender_rows, vectors, projected, w_rad1, w_rad2, atoms):
    length = jnp.sqrt(jnp.sum(vectors * vectors, axis=0))
    unit = vectors / length
    order = jnp.arange(1, w_rad1.shape[0] + 1, dtype=jnp.int32).astype(jnp.float32)[:, None]
    ratio = length / cutoff
    envelope = (1.0 - ratio * ratio) * (1.0 - ratio * ratio)
    basis = jnp.sin(order * math.pi * ratio) / ratio * envelope
    mixed = lax.dot_general(
        basis, w_rad1, (((0,), (0,)), ((), ())), precision=lax.Precision.HIGHEST
    )
    radial = jax.nn.silu(mixed).astype(jnp.bfloat16)
    filters = jnp.dot(radial, w_rad2, preferred_element_type=jnp.float32)
    picked = jnp.take(projected, sender_rows, axis=0).astype(jnp.float32) * filters
    chans = w_rad1.shape[1]
    scalar = picked[:, :chans]
    carried = picked[:, chans:]
    joined = [
        scalar,
        unit[0][:, None] * carried,
        unit[1][:, None] * carried,
        unit[2][:, None] * carried,
    ]
    message = jnp.concatenate(joined, axis=1).astype(jnp.bfloat16)
    onehot = (jnp.arange(atoms, dtype=jnp.int32)[:, None] == receive[None, :]).astype(jnp.bfloat16)
    return jnp.dot(onehot, message, preferred_element_type=jnp.float32)


def gathered(block, devices):
    copies = jnp.broadcast_to(block[None], (devices,) + block.shape)
    return lax.all_to_all(copies, everywhere, split_axis=0, concat_axis=0, tiled=True)


def shards(
    features,
    positions,
    species,
    ghost_list,
    edge_recv,
    edge_send,
    edge_vec,
    w_msg,
    w_rad1,
    w_rad2,
    w_up,
    w_out,
    hardness,
    width,
    chi_shift,
    field,
):
    atoms = features.shape[0]
    chans = features.shape[1]
    lanes = lax.axis_size("space")
    devices = lanes * lax.axis_size("row")
    everybody = devices * atoms
    me = lax.axis_index("row") * lanes + lax.axis_index("space")
    sigma = lookup(species, width)
    diag = lookup(species, hardness) + inverse_root_pi / sigma
    placed = jnp.concatenate([positions, sigma[None, :], diag[None, :]], axis=0)
    everyone = gathered(placed, devices).transpose(1, 0, 2).reshape(5, everybody)
    lists = ghost_list[0]
    outgoing = jnp.take(features, lists.reshape(-1), axis=0).reshape(lanes, lists.shape[1], chans)
    ghost_rows = jnp.einsum(
        "dkc,cf->dkf",
        lax.all_to_all(outgoing, "space", split_axis=0, concat_axis=0, tiled=True),
        w_msg,
        preferred_element_type=jnp.float32,
    ).astype(jnp.bfloat16)
    own_rows = jnp.dot(features, w_msg, preferred_element_type=jnp.float32).astype(jnp.bfloat16)
    projected = jnp.concatenate([own_rows, ghost_rows.reshape(-1, 2 * chans)], axis=0)
    summed = edge_terms(edge_recv, edge_send, edge_vec, projected, w_rad1, w_rad2, atoms)
    summed = summed * message_scale
    vector_part = summed[:, chans:].reshape(atoms, 3, chans)
    invariant = jnp.concatenate(
        [summed[:, :chans], jnp.sum(vector_part * vector_part, axis=1)], axis=1
    ).astype(jnp.bfloat16)
    hidden = jax.nn.silu(jnp.dot(invariant, w_up, preferred_element_type=jnp.float32))
    new_features = (features.astype(jnp.float32) + hidden).astype(jnp.bfloat16)
    chi = jnp.dot(hidden, w_out, precision=lax.Precision.HIGHEST) + lookup(species, chi_shift)
    own_labels = me * atoms + jnp.arange(atoms, dtype=jnp.int32)
    all_labels = jnp.arange(everybody, dtype=jnp.int32)
    rhs = field[0] * positions[2] - chi

    if everybody <= replicate_limit:
        kernel = coulomb(everyone, all_labels, everyone, all_labels)
        residual = gathered(rhs, devices).reshape(everybody)
        all_charges = conjugate(
            residual, lambda v: everyone[4] * v + jnp.sum(kernel * v[None, :], axis=1), jnp.sum
        )
        charges = lax.dynamic_slice(all_charges, (me * atoms,), (atoms,))
    else:
        kernel = coulomb(placed, own_labels, everyone, all_labels)

        def spread(vector):
            return gathered(vector, devices).reshape(everybody)

        charges = conjugate(
            rhs,
            lambda v: diag * v + jnp.sum(kernel * spread(v)[None, :], axis=1),
            lambda v: lax.psum(jnp.sum(v), everywhere),
        )
        all_charges = spread(charges)
    sums = pair_forces(placed, own_labels, everyone, all_labels, all_charges)
    pull = -charges[None, :] * sums[:3]
    forces = jnp.concatenate([pull[:2], pull[2:] + (charges * field[0])[None, :]], axis=0)
    virial = 0.5 * charges[None, :] * sums[3:]
    return (new_features, charges, forces, virial)


def conjugate(rhs, apply, total):
    charges = jnp.zeros_like(rhs)
    residual = rhs
    direction = rhs
    norm_now = total(residual * residual)
    for step in range(ITERS):
        image = apply(direction)
        alpha = norm_now / total(direction * image)
        charges = charges + alpha * direction
        if step + 1 < ITERS:
            residual = residual - alpha * image
            fresh = total(residual * residual)
            direction = residual + fresh / norm_now * direction
            norm_now = fresh
    return charges


def split3(value):
    first = value.astype(jnp.bfloat16).astype(jnp.float32)
    rest = value - first
    second = rest.astype(jnp.bfloat16).astype(jnp.float32)
    third = (rest - second).astype(jnp.bfloat16).astype(jnp.float32)
    return first, second, third


def over_first(left, right):
    return lax.dot_general(
        left, right, (((0,), (0,)), ((), ())), preferred_element_type=jnp.float32
    )


def over_last(left, right, precision=None):
    return lax.dot_general(
        left,
        right,
        (((1,), (1,)), ((), ())),
        precision=precision,
        preferred_element_type=jnp.float32,
    )


def reciprocal(value):
    return pl.reciprocal(value, approx=True)


def silu(value):
    return value * reciprocal(1.0 + jnp.exp(-value))


def silu_half(value):
    return (0.5 * value) * (1.0 + jnp.tanh(0.5 * value))


sine_series = [(-1.0) ** k * math.pi ** (2 * k + 1) / math.factorial(2 * k + 1) for k in range(7)]


def fetched(pairs, semaphores):
    copies = [
        pltpu.make_async_copy(source, target, semaphores.at[place])
        for place, (source, target) in enumerate(pairs)
    ]
    for copy in copies:
        copy.start()
    return copies


chi_segment = 3


def pack_kernel(space_ref, features_ref, lists_ref, packed_ref, held_ref, semaphores):
    atoms, chans = features_ref.shape
    copies = fetched(
        [(lists_ref, held_ref), (features_ref, packed_ref.at[pl.ds(0, atoms)])], semaphores
    )
    copies[0].wait()
    _, lanes, width = held_ref.shape
    rows = []
    for place in range(lanes):
        row = held_ref[0, pl.ds(space_ref[0] ^ place, 1), :].astype(jnp.float32) + place * atoms
        parts = [jnp.zeros((1, width), jnp.float32)] * lanes
        parts[place] = row
        rows.append(jnp.concatenate(parts, axis=1))
    rows.append(jnp.zeros((packed_ref.shape[0] - atoms - lanes, chans), jnp.float32))
    packed_ref[atoms:, :] = jnp.concatenate(rows, axis=0).astype(jnp.bfloat16)
    copies[1].wait()


def edge_kernel(lanes, space_ref, *refs):
    count = (len(refs) - 7) // 2
    far, near, semaphores = refs[:count], refs[count + 8 : -1], refs[-1]
    filter_ref, unit_ref, row_ref, slot_ref, hit_ref = refs[count : count + 5]
    turned_ref, update_ref, out_ref = refs[count + 5 : count + 8]
    vec_ref, first_ref, second_ref, send_ref, recv_ref, project_ref = near[:6]
    species_ref, hardness_ref, width_ref, shift_ref, positions_ref = near[6:]
    copies = fetched(list(zip(far, near + (update_ref, out_ref))), semaphores)
    for copy in copies[:3]:
        copy.wait()
    edges = vec_ref.shape[1]
    orders = first_ref.shape[0]
    vec = vec_ref[...]
    east, north, up = vec[0:1], vec[1:2], vec[2:3]
    squared = east * east + north * north + up * up
    inverse = lax.rsqrt(squared)
    unit_ref[0:3, :] = vec * inverse
    ratio = squared * inverse * (1.0 / cutoff)
    envelope = (1.0 - ratio * ratio) * (1.0 - ratio * ratio) * (cutoff * inverse)
    order = lax.broadcasted_iota(jnp.int32, (orders, edges), 0).astype(jnp.float32) + 1.0
    turns = order * ratio
    whole = jnp.floor(turns + 0.5)
    part = turns - whole
    sign = 1.0 - 2.0 * (whole - 2.0 * jnp.floor(whole * 0.5))
    series = jnp.full_like(part, sine_series[-1])
    for coefficient in sine_series[-2::-1]:
        series = series * (part * part) + coefficient
    basis = series * part * (sign * envelope)
    b1, b2, b3 = split3(basis)
    w1, w2, w3 = split3(first_ref[...])
    mixed = over_first(
        jnp.concatenate([w1, w1, w2, w2, w1, w3], axis=0).astype(jnp.bfloat16),
        jnp.concatenate([b1, b2, b1, b2, b3, b1], axis=0).astype(jnp.bfloat16),
    )
    radial = silu_half(mixed).astype(jnp.bfloat16)
    filter_ref[...] = over_first(second_ref[...], radial)
    for copy in copies[3:]:
        copy.wait()
    species = species_ref[...]

    def table(ref):
        result = jnp.zeros(species.shape, jnp.float32)
        for kind in range(ref.shape[1]):
            result = result + jnp.where(species == kind, ref[:, kind : kind + 1], 0.0)
        return result

    positions = positions_ref[...]
    sigma = table(width_ref)
    atoms = species.shape[1]
    chans = row_ref.shape[1]
    diag = table(hardness_ref) + inverse_root_pi / sigma
    blank = jnp.zeros((2, atoms), jnp.float32)
    rows = [positions[0:1], blank, -table(shift_ref), diag, sigma, positions[2:3], positions[1:2]]
    block = jnp.concatenate(
        [jnp.concatenate(rows, axis=0), jnp.zeros((8, chans - atoms), jnp.float32)], axis=1
    )
    block = pltpu.roll(block, 0, 1, stride=atoms, stride_axis=0)
    row_ref[...] = jnp.sum(block, axis=0, keepdims=True)
    slots = slot_ref.shape[0] - atoms
    width = slots // lanes
    send = send_ref[...]
    ghost = (send - atoms) ^ (space_ref[0] * width)

    def chosen(ref, index, value):
        hit = lax.broadcasted_iota(jnp.int32, ref.shape, 0) == index
        ref[...] = jnp.where(hit, value, 0.0).astype(ref.dtype)

    chosen(slot_ref, jnp.where(send < atoms, send + slots, ghost), 1.0)
    chosen(hit_ref, recv_ref[...], message_scale)
    turned_ref[...] = project_ref[...].astype(jnp.float32).T.astype(jnp.bfloat16)


def node_kernel(
    own_ref,
    near_ref,
    side_ref,
    far_ref,
    filter_ref,
    unit_ref,
    row_ref,
    slot_ref,
    hit_ref,
    turned_ref,
    update_ref,
    out_ref,
    hidden_ref,
    block_ref,
):
    atoms, chans = hidden_ref.shape
    packed = (own_ref, near_ref, side_ref, far_ref)
    group = jnp.concatenate([ref[:atoms, :] for ref in packed], axis=0)
    chosen = jnp.zeros((1, chans), jnp.float32)
    for place, ref in enumerate(packed):
        tail = ref[atoms:, :].astype(jnp.float32)
        chosen = chosen + tail[place : place + 1]
    member = lax.broadcasted_iota(jnp.int32, (len(packed) * atoms, chans), 0)
    fill = jnp.where(member == chosen.astype(jnp.int32), 1.0, 0.0)
    lane = lax.broadcasted_iota(jnp.int32, (len(packed) * atoms, atoms), 1)
    fill = jnp.concatenate([fill, jnp.where(member[:, :atoms] == lane, 1.0, 0.0)], axis=1)
    sender = jnp.dot(
        fill.astype(jnp.bfloat16), slot_ref[...], preferred_element_type=jnp.float32
    )
    projected = over_last(turned_ref[...], group).astype(jnp.bfloat16)
    picked = jnp.dot(projected, sender.astype(jnp.bfloat16), preferred_element_type=jnp.float32)
    scalar = picked[:chans] * filter_ref[:chans, :]
    carried = picked[chans:] * filter_ref[chans:, :]
    parts = [scalar] + [unit_ref[axis : axis + 1, :] * carried for axis in range(3)]
    message = jnp.concatenate([part.astype(jnp.bfloat16) for part in parts], axis=0)
    summed = over_last(hit_ref[...], message)
    square = jnp.zeros((atoms, chans), jnp.float32)
    for component in range(1, 4):
        part = summed[:, component * chans : (component + 1) * chans]
        square = square + part * part
    invariant = jnp.concatenate([summed[:, :chans], square], axis=1).astype(jnp.bfloat16)
    hidden = silu(jnp.dot(invariant, update_ref[...], preferred_element_type=jnp.float32))
    chi = jnp.sum(hidden * out_ref[...], axis=1, keepdims=True)
    lane = lax.broadcasted_iota(jnp.int32, (atoms, chans), 1)
    atom = lax.broadcasted_iota(jnp.int32, (atoms, chans), 0)
    chi = jnp.where(lane == atom + chi_segment * atoms, chi, 0.0)
    row = row_ref[...] - jnp.sum(chi, axis=0, keepdims=True)
    block_ref[...] = jnp.broadcast_to(row[None], block_ref.shape)
    hidden_ref[...] = hidden


def feature_kernel(packed_ref, hidden_ref, features_ref):
    atoms = features_ref.shape[0]
    old = packed_ref[...].astype(jnp.float32)[:atoms]
    features_ref[...] = (old + hidden_ref[...]).astype(jnp.bfloat16)


turn_rate = 0.3275911


def smeared(scaled):
    decay = jnp.exp2(scaled * scaled * (-math.log2(math.e) / turn_rate**2))
    turn = reciprocal(1.0 + scaled)
    series = 1.061405429 * turn - 1.453152027
    series = series * turn + 1.421413741
    series = series * turn - 0.284496736
    series = series * turn + 0.254829592
    return 1.0 - series * turn * decay, decay


def charge_kernel(
    place_ref,
    field_ref,
    all_ref,
    charges_ref,
    forces_ref,
    virial_ref,
    matrix_ref,
    side_ref,
    value_ref,
    kept_ref,
):
    blocks, _, lanes = all_ref.shape
    own = charges_ref.shape[1]
    count = blocks * own
    fit = lanes // own
    segment = lax.broadcasted_iota(jnp.int32, (8, lanes), 1) // own
    tiles = []
    for first in range(0, blocks, fit):
        tile = jnp.zeros((8, lanes), jnp.float32)
        for place in range(fit):
            row = all_ref[(place_ref[0] + first + place) & (blocks - 1)]
            row = pltpu.roll(jnp.broadcast_to(row, (8, lanes)), 0, 1, stride=own, stride_axis=0)
            row = pltpu.roll(row, place * own, 1) if place else row
            tile = jnp.where(segment == place, row, tile)
        tiles.append(tile)
    everyone = jnp.concatenate(tiles, axis=1)
    last = lax.broadcasted_iota(jnp.int32, everyone.shape, 0) == 5
    everyone = everyone + jnp.where(last, field_ref[0] * everyone[2:3], 0.0)
    columns = everyone.T
    diag, rhs = everyone[4:5], everyone[5:6]
    twice = 2.0 / turn_rate**2
    spread_row = twice * everyone[3:4] * everyone[3:4]
    tiles = count // lanes
    depth = own // 8
    shape = (depth, 8, lanes)
    lane = lax.broadcasted_iota(jnp.int32, shape, 2)
    line = lax.broadcasted_iota(jnp.int32, shape, 0) * 8 + lax.broadcasted_iota(jnp.int32, shape, 1)

    def part(row, tile):
        return row[:, tile * lanes : (tile + 1) * lanes]

    def down(row):
        return [jnp.broadcast_to(part(row, tile), (8, lanes))[None] for tile in range(tiles)]

    def along(column):
        return jnp.broadcast_to(column, (own, lanes)).reshape(shape)

    def total(value):
        return jnp.sum(value, axis=1, keepdims=True)

    axes = [down(everyone[axis : axis + 1]) for axis in range(3)]
    wide_row, rhs_row = down(spread_row), down(rhs)

    above = [jnp.zeros((8, lanes), jnp.float32) for _ in range(tiles)]
    for start in range(0, count, own):
        first = start // lanes
        column = columns[start : start + own]
        place = [along(column[:, axis : axis + 1]) for axis in range(3)]
        wide = along(twice * column[:, 3:4] * column[:, 3:4])
        value = along(column[:, 5:6])
        value_ref[start : start + own, :] = value.reshape(own, lanes)
        below = jnp.zeros(shape, jnp.float32)
        for tile in range(first, tiles):
            delta = [place[axis] - axes[axis][tile] for axis in range(3)]
            squared = delta[0] * delta[0] + delta[1] * delta[1] + delta[2] * delta[2]
            if tile == first:
                same = lane == line + (start - first * lanes)
                squared = jnp.where(same, 1.0, squared)
            inverse = lax.rsqrt(squared)
            scale = lax.rsqrt(wide + wide_row[tile])
            smear, decay = smeared(squared * inverse * scale)
            kernel = smear * inverse
            if start == 0:
                slope = (two_over_root_pi / turn_rate * scale * decay - kernel) * inverse * inverse
                slope = jnp.where(same, 0.0, slope) if tile == first else slope
                for which, kind in enumerate(delta + [slope]):
                    kept_ref[which, :, tile * lanes : (tile + 1) * lanes] = kind.reshape(own, lanes)
            if tile == first:
                kernel = jnp.where(same, 0.0, kernel)
            else:
                below = below + kernel * rhs_row[tile]
            above[tile] = above[tile] + jnp.sum(kernel * value, axis=0)
            matrix_ref[start : start + own, tile * lanes : (tile + 1) * lanes] = kernel.reshape(
                own, lanes
            )
        if first + 1 < tiles:
            side_ref[start : start + own, :] = below.reshape(own, lanes)
    image = []
    for tile in range(tiles):
        value = jnp.sum(above[tile], axis=0, keepdims=True)
        if tile + 1 < tiles:
            below = side_ref[tile * lanes : (tile + 1) * lanes, :].T
            value = value + jnp.sum(below, axis=0, keepdims=True)
        image.append(value)
    image = diag * rhs + jnp.concatenate(image, axis=1)
    across = jnp.broadcast_to(image, (8, count)).T
    norm = total(rhs * rhs)
    alpha = norm * reciprocal(total(rhs * image))
    residual = rhs - alpha * image
    fresh = total(residual * residual)
    again = fresh * reciprocal(norm)
    direction = residual + again * rhs
    onto = [jnp.zeros((8, lanes), jnp.float32) for _ in range(tiles)]
    above = [jnp.zeros((8, lanes), jnp.float32) for _ in range(tiles)]
    for start in range(0, count, own):
        first = start // lanes
        value = (1.0 + again) * value_ref[start : start + own, :]
        value = value - alpha * jnp.broadcast_to(across[start : start + own, 0:1], (own, lanes))
        value = value.reshape(shape)
        for tile in range(first, tiles):
            sums = onto if tile == first else above
            kernel = matrix_ref[start : start + own, tile * lanes : (tile + 1) * lanes]
            sums[tile] = sums[tile] + jnp.sum(kernel.reshape(shape) * value, axis=0)
    curved = jnp.zeros((8, lanes), jnp.float32)
    for tile in range(tiles):
        curved = curved + (onto[tile] + 2.0 * above[tile]) * part(direction, tile)
    curved = jnp.sum(curved, axis=0, keepdims=True)
    for tile in range(tiles):
        curved = curved + part(diag * direction * direction, tile)
    charges = alpha * rhs + fresh * reciprocal(total(curved)) * direction

    sums = [jnp.zeros(shape, jnp.float32) for _ in range(9)]
    charge_row = down(charges)
    for tile in range(tiles):
        *delta, slope = [
            kept_ref[which, :, tile * lanes : (tile + 1) * lanes].reshape(shape)
            for which in range(4)
        ]
        weight = charge_row[tile] * slope
        pulled = [weight * delta[axis] for axis in range(3)]
        terms = pulled + [
            pulled[left] * delta[right]
            for left, right in ((0, 0), (1, 1), (2, 2), (0, 1), (0, 2), (1, 2))
        ]
        sums = [old + term for old, term in zip(sums, terms)]
    table = jnp.zeros((own, lanes), jnp.float32)
    lane = lane.reshape(own, lanes)
    for place, value in enumerate(sums):
        table = jnp.where(lane == place, total(value.reshape(own, lanes)), table)
    table = table.T
    mine = charges[:, :own]
    charges_ref[...] = mine
    pull = -mine * table[0:3]
    third = lax.broadcasted_iota(jnp.int32, pull.shape, 0) == 2
    forces_ref[...] = pull + jnp.where(third, mine * field_ref[0], 0.0)
    virial_ref[...] = 0.5 * mine * table[3:9]


def kernel_call(kernel, shapes, arguments, scalars=0, far=0, scratch=(), flops=0):
    shapes = tuple(jax.ShapeDtypeStruct(shape, kind) for shape, kind in shapes)
    spaces = [pltpu.SMEM] * scalars + [pltpu.HBM] * far
    spaces = spaces + [pltpu.VMEM] * (len(arguments) - len(spaces))
    arguments = [
        pltpu.with_memory_space_constraint(value, space) if space is pltpu.HBM else value
        for value, space in zip(arguments, spaces)
    ]
    return pl.pallas_call(
        kernel,
        out_shape=shapes,
        in_specs=[pl.BlockSpec(memory_space=space) for space in spaces],
        out_specs=tuple(pl.BlockSpec(memory_space=pltpu.VMEM) for _ in shapes),
        scratch_shapes=list(scratch),
        compiler_params=pltpu.CompilerParams(vmem_limit_bytes=32 * 1024 * 1024),
        cost_estimate=pl.CostEstimate(flops=flops, bytes_accessed=1 << 20, transcendentals=0),
    )(*arguments)


def exchanged(block, axis, step):
    size = lax.axis_size(axis)
    return lax.ppermute(block, axis, [(place, place ^ step) for place in range(size)])


def few_shards(
    features,
    positions,
    species,
    ghost_list,
    edge_recv,
    edge_send,
    edge_vec,
    w_msg,
    w_rad1,
    w_rad2,
    w_up,
    w_out,
    hardness,
    width,
    chi_shift,
    field,
):
    atoms, chans = features.shape
    edges = edge_recv.shape[0]
    rows, lanes = lax.axis_size("row"), lax.axis_size("space")
    space = lax.axis_index("space").astype(jnp.int32)
    (packed,) = kernel_call(
        pack_kernel,
        [((atoms + 16, chans), jnp.bfloat16)],
        (space.reshape(1), features, ghost_list),
        scalars=1,
        far=2,
        scratch=[
            pltpu.VMEM(ghost_list.shape, ghost_list.dtype),
            pltpu.SemaphoreType.DMA((2,)),
        ],
    )
    others = [exchanged(packed, "space", step) for step in range(1, lanes)]
    rest = (edge_vec, w_rad1, w_rad2, edge_send[None], edge_recv[None], w_msg)
    rest = rest + (species[None], hardness[None], width[None], chi_shift[None], positions)
    kept = (w_up, w_out[None])
    parts = kernel_call(
        functools.partial(edge_kernel, lanes),
        [
            ((2 * chans, edges), jnp.float32),
            ((8, edges), jnp.float32),
            ((1, chans), jnp.float32),
            ((chans + atoms, edges), jnp.bfloat16),
            ((atoms, edges), jnp.bfloat16),
            ((2 * chans, chans), jnp.bfloat16),
            (w_up.shape, w_up.dtype),
            ((1, chans), jnp.float32),
        ],
        (space.reshape(1), *rest, *kept),
        scalars=1,
        far=len(rest + kept),
        scratch=[pltpu.VMEM(value.shape, value.dtype) for value in rest]
        + [pltpu.SemaphoreType.DMA((len(rest + kept),))],
        flops=1 << 28,
    )
    devices = rows * lanes
    hidden, block = kernel_call(
        node_kernel,
        [((atoms, chans), jnp.float32), ((devices, 1, chans), jnp.float32)],
        (packed, *others, *parts),
        flops=1 << 28,
    )
    (new_features,) = kernel_call(
        feature_kernel, [((atoms, chans), jnp.bfloat16)], (packed, hidden), flops=1 << 20
    )
    block = lax.all_to_all(block, everywhere, 0, 0, tiled=True)
    place = lax.axis_index("row").astype(jnp.int32) * lanes + space
    everybody = rows * lanes * atoms
    charges, forces, virial = kernel_call(
        charge_kernel,
        [((count, atoms), jnp.float32) for count in (1, 3, 6)],
        (place.reshape(1), field, block),
        scalars=2,
        scratch=[
            pltpu.VMEM((everybody, everybody), jnp.float32),
            pltpu.VMEM((everybody, chans), jnp.float32),
            pltpu.VMEM((everybody, chans), jnp.float32),
            pltpu.VMEM((4, atoms, everybody), jnp.float32),
        ],
        flops=1 << 28,
    )
    return (new_features, charges[0], forces, virial)


def solution(mesh):
    small = mesh.shape["space"] == 4 and mesh.shape["row"] == 8
    return jax.shard_map(
        few_shards if small else shards,
        mesh=mesh,
        in_specs=(
            P(("row", "space"), None),
            P(None, ("row", "space")),
            P(("row", "space")),
            P("row", "space", None),
            P(("row", "space")),
            P(("row", "space")),
            P(None, ("row", "space")),
            P(),
            P(),
            P(),
            P(),
            P(),
            P(),
            P(),
            P(),
            P(),
        ),
        out_specs=(
            P(("row", "space"), None),
            P(("row", "space")),
            P(None, ("row", "space")),
            P(None, ("row", "space")),
        ),
        check_vma=False,
    )
```

```python
import functools
import math

import jax
import jax.numpy as jnp
from jax import lax
from jax.experimental import pallas as pl
from jax.experimental.pallas import tpu as pltpu
from jax.sharding import PartitionSpec as P

ITERS = 2


cutoff = 6.0
message_scale = 0.125
two_over_root_pi = 2.0 / math.sqrt(math.pi)
inverse_root_pi = 1.0 / math.sqrt(math.pi)
replicate_limit = 1024
everywhere = ("row", "space")


def lookup(species, table):
    result = jnp.zeros(species.shape, jnp.float32)
    for kind in range(table.shape[0]):
        result = result + jnp.where(species == kind, table[kind], 0.0)
    return result


def pair_terms(target, target_labels, source, source_labels):
    delta = target[:3, :, None] - source[:3, None, :]
    squared = jnp.sum(delta * delta, axis=0)
    same = target_labels[:, None] == source_labels[None, :]
    squared = jnp.where(same, 1.0, squared)
    inverse = lax.rsqrt(squared)
    radius = squared * inverse
    spread = target[3][:, None] * target[3][:, None] + source[3][None, :] * source[3][None, :]
    scale = lax.rsqrt(2.0 * spread)
    scaled = radius * scale
    smear = lax.erf(scaled)
    return delta, same, inverse, scale, scaled, smear


def coulomb(target, target_labels, source, source_labels):
    _, same, inverse, _, _, smear = pair_terms(target, target_labels, source, source_labels)
    return jnp.where(same, 0.0, smear * inverse)


def pair_forces(target, target_labels, source, source_labels, source_charge):
    delta, same, inverse, scale, scaled, smear = pair_terms(
        target, target_labels, source, source_labels
    )
    slope = (
        two_over_root_pi * scale * jnp.exp(-scaled * scaled) * inverse - smear * inverse * inverse
    )
    weight = jnp.where(same, 0.0, source_charge[None, :] * slope * inverse)
    first = jnp.sum(weight[None] * delta, axis=2)
    pairs = ((0, 0), (1, 1), (2, 2), (0, 1), (0, 2), (1, 2))
    second = jnp.stack(
        [jnp.sum(weight * delta[left] * delta[right], axis=1) for left, right in pairs]
    )
    return jnp.concatenate([first, second], axis=0)


def edge_terms(receive, sender_rows, vectors, projected, w_rad1, w_rad2, atoms):
    length = jnp.sqrt(jnp.sum(vectors * vectors, axis=0))
    unit = vectors / length
    order = jnp.arange(1, w_rad1.shape[0] + 1, dtype=jnp.int32).astype(jnp.float32)[:, None]
    ratio = length / cutoff
    envelope = (1.0 - ratio * ratio) * (1.0 - ratio * ratio)
    basis = jnp.sin(order * math.pi * ratio) / ratio * envelope
    mixed = lax.dot_general(
        basis, w_rad1, (((0,), (0,)), ((), ())), precision=lax.Precision.HIGHEST
    )
    radial = jax.nn.silu(mixed).astype(jnp.bfloat16)
    filters = jnp.dot(radial, w_rad2, preferred_element_type=jnp.float32)
    picked = jnp.take(projected, sender_rows, axis=0).astype(jnp.float32) * filters
    chans = w_rad1.shape[1]
    scalar = picked[:, :chans]
    carried = picked[:, chans:]
    joined = [
        scalar,
        unit[0][:, None] * carried,
        unit[1][:, None] * carried,
        unit[2][:, None] * carried,
    ]
    message = jnp.concatenate(joined, axis=1).astype(jnp.bfloat16)
    onehot = (jnp.arange(atoms, dtype=jnp.int32)[:, None] == receive[None, :]).astype(jnp.bfloat16)
    return jnp.dot(onehot, message, preferred_element_type=jnp.float32)


def gathered(block, devices):
    copies = jnp.broadcast_to(block[None], (devices,) + block.shape)
    return lax.all_to_all(copies, everywhere, split_axis=0, concat_axis=0, tiled=True)


def shards(
    features,
    positions,
    species,
    ghost_list,
    edge_recv,
    edge_send,
    edge_vec,
    w_msg,
    w_rad1,
    w_rad2,
    w_up,
    w_out,
    hardness,
    width,
    chi_shift,
    field,
):
    atoms = features.shape[0]
    chans = features.shape[1]
    lanes = lax.axis_size("space")
    devices = lanes * lax.axis_size("row")
    everybody = devices * atoms
    me = lax.axis_index("row") * lanes + lax.axis_index("space")
    sigma = lookup(species, width)
    diag = lookup(species, hardness) + inverse_root_pi / sigma
    placed = jnp.concatenate([positions, sigma[None, :], diag[None, :]], axis=0)
    everyone = gathered(placed, devices).transpose(1, 0, 2).reshape(5, everybody)
    lists = ghost_list[0]
    outgoing = jnp.take(features, lists.reshape(-1), axis=0).reshape(lanes, lists.shape[1], chans)
    ghost_rows = jnp.einsum(
        "dkc,cf->dkf",
        lax.all_to_all(outgoing, "space", split_axis=0, concat_axis=0, tiled=True),
        w_msg,
        preferred_element_type=jnp.float32,
    ).astype(jnp.bfloat16)
    own_rows = jnp.dot(features, w_msg, preferred_element_type=jnp.float32).astype(jnp.bfloat16)
    projected = jnp.concatenate([own_rows, ghost_rows.reshape(-1, 2 * chans)], axis=0)
    summed = edge_terms(edge_recv, edge_send, edge_vec, projected, w_rad1, w_rad2, atoms)
    summed = summed * message_scale
    vector_part = summed[:, chans:].reshape(atoms, 3, chans)
    invariant = jnp.concatenate(
        [summed[:, :chans], jnp.sum(vector_part * vector_part, axis=1)], axis=1
    ).astype(jnp.bfloat16)
    hidden = jax.nn.silu(jnp.dot(invariant, w_up, preferred_element_type=jnp.float32))
    new_features = (features.astype(jnp.float32) + hidden).astype(jnp.bfloat16)
    chi = jnp.dot(hidden, w_out, precision=lax.Precision.HIGHEST) + lookup(species, chi_shift)
    own_labels = me * atoms + jnp.arange(atoms, dtype=jnp.int32)
    all_labels = jnp.arange(everybody, dtype=jnp.int32)
    rhs = field[0] * positions[2] - chi

    if everybody <= replicate_limit:
        kernel = coulomb(everyone, all_labels, everyone, all_labels)
        residual = gathered(rhs, devices).reshape(everybody)
        all_charges = conjugate(
            residual, lambda v: everyone[4] * v + jnp.sum(kernel * v[None, :], axis=1), jnp.sum
        )
        charges = lax.dynamic_slice(all_charges, (me * atoms,), (atoms,))
    else:
        kernel = coulomb(placed, own_labels, everyone, all_labels)

        def spread(vector):
            return gathered(vector, devices).reshape(everybody)

        charges = conjugate(
            rhs,
            lambda v: diag * v + jnp.sum(kernel * spread(v)[None, :], axis=1),
            lambda v: lax.psum(jnp.sum(v), everywhere),
        )
        all_charges = spread(charges)
    sums = pair_forces(placed, own_labels, everyone, all_labels, all_charges)
    pull = -charges[None, :] * sums[:3]
    forces = jnp.concatenate([pull[:2], pull[2:] + (charges * field[0])[None, :]], axis=0)
    virial = 0.5 * charges[None, :] * sums[3:]
    return (new_features, charges, forces, virial)


def conjugate(rhs, apply, total):
    charges = jnp.zeros_like(rhs)
    residual = rhs
    direction = rhs
    norm_now = total(residual * residual)
    for step in range(ITERS):
        image = apply(direction)
        alpha = norm_now / total(direction * image)
        charges = charges + alpha * direction
        if step + 1 < ITERS:
            residual = residual - alpha * image
            fresh = total(residual * residual)
            direction = residual + fresh / norm_now * direction
            norm_now = fresh
    return charges


def split3(value):
    first = value.astype(jnp.bfloat16).astype(jnp.float32)
    rest = value - first
    second = rest.astype(jnp.bfloat16).astype(jnp.float32)
    third = (rest - second).astype(jnp.bfloat16).astype(jnp.float32)
    return first, second, third


def over_first(left, right):
    return lax.dot_general(
        left, right, (((0,), (0,)), ((), ())), preferred_element_type=jnp.float32
    )


def over_last(left, right, precision=None):
    return lax.dot_general(
        left,
        right,
        (((1,), (1,)), ((), ())),
        precision=precision,
        preferred_element_type=jnp.float32,
    )


def reciprocal(value):
    return pl.reciprocal(value, approx=True)


def silu(value):
    return value * reciprocal(1.0 + jnp.exp(-value))


def silu_half(value):
    return (0.5 * value) * (1.0 + jnp.tanh(0.5 * value))


sine_series = [(-1.0) ** k * math.pi ** (2 * k + 1) / math.factorial(2 * k + 1) for k in range(7)]


def fetched(pairs, semaphores):
    copies = [
        pltpu.make_async_copy(source, target, semaphores.at[place])
        for place, (source, target) in enumerate(pairs)
    ]
    for copy in copies:
        copy.start()
    return copies


chi_segment = 3


def pack_kernel(space_ref, features_ref, lists_ref, packed_ref, held_ref, semaphores):
    atoms, chans = features_ref.shape
    copies = fetched(
        [(lists_ref, held_ref), (features_ref, packed_ref.at[pl.ds(0, atoms)])], semaphores
    )
    copies[0].wait()
    _, lanes, width = held_ref.shape
    rows = []
    for place in range(lanes):
        row = held_ref[0, pl.ds(space_ref[0] ^ place, 1), :].astype(jnp.float32) + place * atoms
        parts = [jnp.zeros((1, width), jnp.float32)] * lanes
        parts[place] = row
        rows.append(jnp.concatenate(parts, axis=1))
    rows.append(jnp.zeros((packed_ref.shape[0] - atoms - lanes, chans), jnp.float32))
    packed_ref[atoms:, :] = jnp.concatenate(rows, axis=0).astype(jnp.bfloat16)
    copies[1].wait()


def edge_kernel(lanes, space_ref, *refs):
    count = (len(refs) - 7) // 2
    far, near, semaphores = refs[:count], refs[count + 8 : -1], refs[-1]
    filter_ref, unit_ref, row_ref, slot_ref, hit_ref = refs[count : count + 5]
    turned_ref, update_ref, out_ref = refs[count + 5 : count + 8]
    vec_ref, first_ref, second_ref, send_ref, recv_ref, project_ref = near[:6]
    species_ref, hardness_ref, width_ref, shift_ref, positions_ref = near[6:]
    copies = fetched(list(zip(far, near + (update_ref, out_ref))), semaphores)
    for copy in copies[:3]:
        copy.wait()
    edges = vec_ref.shape[1]
    orders = first_ref.shape[0]
    vec = vec_ref[...]
    east, north, up = vec[0:1], vec[1:2], vec[2:3]
    squared = east * east + north * north + up * up
    inverse = lax.rsqrt(squared)
    unit_ref[0:3, :] = vec * inverse
    ratio = squared * inverse * (1.0 / cutoff)
    envelope = (1.0 - ratio * ratio) * (1.0 - ratio * ratio) * (cutoff * inverse)
    order = lax.broadcasted_iota(jnp.int32, (orders, edges), 0).astype(jnp.float32) + 1.0
    turns = order * ratio
    whole = jnp.floor(turns + 0.5)
    part = turns - whole
    sign = 1.0 - 2.0 * (whole - 2.0 * jnp.floor(whole * 0.5))
    series = jnp.full_like(part, sine_series[-1])
    for coefficient in sine_series[-2::-1]:
        series = series * (part * part) + coefficient
    basis = series * part * (sign * envelope)
    b1, b2, b3 = split3(basis)
    w1, w2, w3 = split3(first_ref[...])
    mixed = over_first(
        jnp.concatenate([w1, w1, w2, w2, w1, w3], axis=0).astype(jnp.bfloat16),
        jnp.concatenate([b1, b2, b1, b2, b3, b1], axis=0).astype(jnp.bfloat16),
    )
    radial = silu_half(mixed).astype(jnp.bfloat16)
    filter_ref[...] = over_first(second_ref[...], radial)
    for copy in copies[3:]:
        copy.wait()
    species = species_ref[...]

    def table(ref):
        result = jnp.zeros(species.shape, jnp.float32)
        for kind in range(ref.shape[1]):
            result = result + jnp.where(species == kind, ref[:, kind : kind + 1], 0.0)
        return result

    positions = positions_ref[...]
    sigma = table(width_ref)
    atoms = species.shape[1]
    chans = row_ref.shape[1]
    diag = table(hardness_ref) + inverse_root_pi / sigma
    blank = jnp.zeros((2, atoms), jnp.float32)
    rows = [positions[0:1], blank, -table(shift_ref), diag, sigma, positions[2:3], positions[1:2]]
    block = jnp.concatenate(
        [jnp.concatenate(rows, axis=0), jnp.zeros((8, chans - atoms), jnp.float32)], axis=1
    )
    block = pltpu.roll(block, 0, 1, stride=atoms, stride_axis=0)
    row_ref[...] = jnp.sum(block, axis=0, keepdims=True)
    slots = slot_ref.shape[0] - atoms
    width = slots // lanes
    send = send_ref[...]
    ghost = (send - atoms) ^ (space_ref[0] * width)

    def chosen(ref, index, value):
        hit = lax.broadcasted_iota(jnp.int32, ref.shape, 0) == index
        ref[...] = jnp.where(hit, value, 0.0).astype(ref.dtype)

    chosen(slot_ref, jnp.where(send < atoms, send + slots, ghost), 1.0)
    chosen(hit_ref, recv_ref[...], message_scale)
    turned_ref[...] = project_ref[...].astype(jnp.float32).T.astype(jnp.bfloat16)


def node_kernel(
    own_ref,
    near_ref,
    side_ref,
    far_ref,
    filter_ref,
    unit_ref,
    row_ref,
    slot_ref,
    hit_ref,
    turned_ref,
    update_ref,
    out_ref,
    hidden_ref,
    block_ref,
):
    atoms, chans = hidden_ref.shape
    packed = (own_ref, near_ref, side_ref, far_ref)
    group = jnp.concatenate([ref[:atoms, :] for ref in packed], axis=0)
    chosen = jnp.zeros((1, chans), jnp.float32)
    for place, ref in enumerate(packed):
        tail = ref[atoms:, :].astype(jnp.float32)
        chosen = chosen + tail[place : place + 1]
    member = lax.broadcasted_iota(jnp.int32, (len(packed) * atoms, chans), 0)
    fill = jnp.where(member == chosen.astype(jnp.int32), 1.0, 0.0)
    lane = lax.broadcasted_iota(jnp.int32, (len(packed) * atoms, atoms), 1)
    fill = jnp.concatenate([fill, jnp.where(member[:, :atoms] == lane, 1.0, 0.0)], axis=1)
    sender = jnp.dot(
        fill.astype(jnp.bfloat16), slot_ref[...], preferred_element_type=jnp.float32
    )
    projected = over_last(turned_ref[...], group).astype(jnp.bfloat16)
    picked = jnp.dot(projected, sender.astype(jnp.bfloat16), preferred_element_type=jnp.float32)
    scalar = picked[:chans] * filter_ref[:chans, :]
    carried = picked[chans:] * filter_ref[chans:, :]
    parts = [scalar] + [unit_ref[axis : axis + 1, :] * carried for axis in range(3)]
    message = jnp.concatenate([part.astype(jnp.bfloat16) for part in parts], axis=0)
    summed = over_last(hit_ref[...], message)
    square = jnp.zeros((atoms, chans), jnp.float32)
    for component in range(1, 4):
        part = summed[:, component * chans : (component + 1) * chans]
        square = square + part * part
    invariant = jnp.concatenate([summed[:, :chans], square], axis=1).astype(jnp.bfloat16)
    hidden = silu(jnp.dot(invariant, update_ref[...], preferred_element_type=jnp.float32))
    chi = jnp.sum(hidden * out_ref[...], axis=1, keepdims=True)
    lane = lax.broadcasted_iota(jnp.int32, (atoms, chans), 1)
    atom = lax.broadcasted_iota(jnp.int32, (atoms, chans), 0)
    chi = jnp.where(lane == atom + chi_segment * atoms, chi, 0.0)
    row = row_ref[...] - jnp.sum(chi, axis=0, keepdims=True)
    block_ref[...] = jnp.broadcast_to(row[None], block_ref.shape)
    hidden_ref[...] = hidden


def feature_kernel(packed_ref, hidden_ref, features_ref):
    atoms = features_ref.shape[0]
    old = packed_ref[...].astype(jnp.float32)[:atoms]
    features_ref[...] = (old + hidden_ref[...]).astype(jnp.bfloat16)


turn_rate = 0.3275911


def smeared(scaled):
    decay = jnp.exp2(scaled * scaled * (-math.log2(math.e) / turn_rate**2))
    turn = reciprocal(1.0 + scaled)
    series = 1.061405429 * turn - 1.453152027
    series = series * turn + 1.421413741
    series = series * turn - 0.284496736
    series = series * turn + 0.254829592
    return 1.0 - series * turn * decay, decay


def charge_kernel(
    place_ref,
    field_ref,
    all_ref,
    charges_ref,
    forces_ref,
    virial_ref,
    matrix_ref,
    side_ref,
    value_ref,
    kept_ref,
):
    blocks, _, lanes = all_ref.shape
    own = charges_ref.shape[1]
    count = blocks * own
    fit = lanes // own
    segment = lax.broadcasted_iota(jnp.int32, (8, lanes), 1) // own
    tiles = []
    for first in range(0, blocks, fit):
        tile = jnp.zeros((8, lanes), jnp.float32)
        for place in range(fit):
            row = all_ref[(place_ref[0] + first + place) & (blocks - 1)]
            row = pltpu.roll(jnp.broadcast_to(row, (8, lanes)), 0, 1, stride=own, stride_axis=0)
            row = pltpu.roll(row, place * own, 1) if place else row
            tile = jnp.where(segment == place, row, tile)
        tiles.append(tile)
    everyone = jnp.concatenate(tiles, axis=1)
    last = lax.broadcasted_iota(jnp.int32, everyone.shape, 0) == 5
    everyone = everyone + jnp.where(last, field_ref[0] * everyone[2:3], 0.0)
    columns = everyone.T
    diag, rhs = everyone[4:5], everyone[5:6]
    twice = 2.0 / turn_rate**2
    spread_row = twice * everyone[3:4] * everyone[3:4]
    tiles = count // lanes
    depth = own // 8
    shape = (depth, 8, lanes)
    lane = lax.broadcasted_iota(jnp.int32, shape, 2)
    line = lax.broadcasted_iota(jnp.int32, shape, 0) * 8 + lax.broadcasted_iota(jnp.int32, shape, 1)

    def part(row, tile):
        return row[:, tile * lanes : (tile + 1) * lanes]

    def down(row):
        return [jnp.broadcast_to(part(row, tile), (8, lanes))[None] for tile in range(tiles)]

    def along(column):
        return jnp.broadcast_to(column, (own, lanes)).reshape(shape)

    def total(value):
        return jnp.sum(value, axis=1, keepdims=True)

    axes = [down(everyone[axis : axis + 1]) for axis in range(3)]
    wide_row, rhs_row = down(spread_row), down(rhs)

    above = [jnp.zeros((8, lanes), jnp.float32) for _ in range(tiles)]
    for start in range(0, count, own):
        first = start // lanes
        column = columns[start : start + own]
        place = [along(column[:, axis : axis + 1]) for axis in range(3)]
        wide = along(twice * column[:, 3:4] * column[:, 3:4])
        value = along(column[:, 5:6])
        value_ref[start : start + own, :] = value.reshape(own, lanes)
        below = jnp.zeros(shape, jnp.float32)
        for tile in range(first, tiles):
            delta = [place[axis] - axes[axis][tile] for axis in range(3)]
            squared = delta[0] * delta[0] + delta[1] * delta[1] + delta[2] * delta[2]
            inverse = lax.rsqrt(squared)
            if tile == first:
                same = lane == line + (start - first * lanes)
                inverse = jnp.where(same, 0.0, inverse)
            scale = lax.rsqrt(wide + wide_row[tile])
            smear, decay = smeared(squared * inverse * scale)
            kernel = smear * inverse
            if start == 0:
                slope = (two_over_root_pi / turn_rate * scale * decay - kernel) * inverse * inverse
                for which, kind in enumerate(delta + [slope]):
                    kept_ref[which, :, tile * lanes : (tile + 1) * lanes] = kind.reshape(own, lanes)
            if tile > first:
                below = below + kernel * rhs_row[tile]
            above[tile] = above[tile] + jnp.sum(kernel * value, axis=0)
            matrix_ref[start : start + own, tile * lanes : (tile + 1) * lanes] = kernel.reshape(
                own, lanes
            )
        if first + 1 < tiles:
            side_ref[start : start + own, :] = below.reshape(own, lanes)
    image = []
    for tile in range(tiles):
        value = jnp.sum(above[tile], axis=0, keepdims=True)
        if tile + 1 < tiles:
            below = side_ref[tile * lanes : (tile + 1) * lanes, :].T
            value = value + jnp.sum(below, axis=0, keepdims=True)
        image.append(value)
    image = diag * rhs + jnp.concatenate(image, axis=1)
    across = jnp.broadcast_to(image, (8, count)).T
    norm = total(rhs * rhs)
    alpha = norm * reciprocal(total(rhs * image))
    residual = rhs - alpha * image
    fresh = total(residual * residual)
    again = fresh * reciprocal(norm)
    direction = residual + again * rhs
    onto = [jnp.zeros((8, lanes), jnp.float32) for _ in range(tiles)]
    above = [jnp.zeros((8, lanes), jnp.float32) for _ in range(tiles)]
    for start in range(0, count, own):
        first = start // lanes
        value = (1.0 + again) * value_ref[start : start + own, :]
        value = value - alpha * jnp.broadcast_to(across[start : start + own, 0:1], (own, lanes))
        value = value.reshape(shape)
        for tile in range(first, tiles):
            sums = onto if tile == first else above
            kernel = matrix_ref[start : start + own, tile * lanes : (tile + 1) * lanes]
            sums[tile] = sums[tile] + jnp.sum(kernel.reshape(shape) * value, axis=0)
    curved = jnp.zeros((8, lanes), jnp.float32)
    for tile in range(tiles):
        curved = curved + (onto[tile] + 2.0 * above[tile]) * part(direction, tile)
    curved = jnp.sum(curved, axis=0, keepdims=True)
    for tile in range(tiles):
        curved = curved + part(diag * direction * direction, tile)
    charges = alpha * rhs + fresh * reciprocal(total(curved)) * direction

    sums = [jnp.zeros(shape, jnp.float32) for _ in range(9)]
    charge_row = down(charges)
    for tile in range(tiles):
        *delta, slope = [
            kept_ref[which, :, tile * lanes : (tile + 1) * lanes].reshape(shape)
            for which in range(4)
        ]
        weight = charge_row[tile] * slope
        pulled = [weight * delta[axis] for axis in range(3)]
        terms = pulled + [
            pulled[left] * delta[right]
            for left, right in ((0, 0), (1, 1), (2, 2), (0, 1), (0, 2), (1, 2))
        ]
        sums = [old + term for old, term in zip(sums, terms)]
    table = jnp.zeros((own, lanes), jnp.float32)
    lane = lane.reshape(own, lanes)
    for place, value in enumerate(sums):
        table = jnp.where(lane == place, total(value.reshape(own, lanes)), table)
    table = table.T
    mine = charges[:, :own]
    charges_ref[...] = mine
    pull = -mine * table[0:3]
    third = lax.broadcasted_iota(jnp.int32, pull.shape, 0) == 2
    forces_ref[...] = pull + jnp.where(third, mine * field_ref[0], 0.0)
    virial_ref[...] = 0.5 * mine * table[3:9]


def kernel_call(kernel, shapes, arguments, scalars=0, far=0, scratch=(), flops=0):
    shapes = tuple(jax.ShapeDtypeStruct(shape, kind) for shape, kind in shapes)
    spaces = [pltpu.SMEM] * scalars + [pltpu.HBM] * far
    spaces = spaces + [pltpu.VMEM] * (len(arguments) - len(spaces))
    arguments = [
        pltpu.with_memory_space_constraint(value, space) if space is pltpu.HBM else value
        for value, space in zip(arguments, spaces)
    ]
    return pl.pallas_call(
        kernel,
        out_shape=shapes,
        in_specs=[pl.BlockSpec(memory_space=space) for space in spaces],
        out_specs=tuple(pl.BlockSpec(memory_space=pltpu.VMEM) for _ in shapes),
        scratch_shapes=list(scratch),
        compiler_params=pltpu.CompilerParams(vmem_limit_bytes=32 * 1024 * 1024),
        cost_estimate=pl.CostEstimate(flops=flops, bytes_accessed=1 << 20, transcendentals=0),
    )(*arguments)


def exchanged(block, axis, step):
    size = lax.axis_size(axis)
    return lax.ppermute(block, axis, [(place, place ^ step) for place in range(size)])


def few_shards(
    features,
    positions,
    species,
    ghost_list,
    edge_recv,
    edge_send,
    edge_vec,
    w_msg,
    w_rad1,
    w_rad2,
    w_up,
    w_out,
    hardness,
    width,
    chi_shift,
    field,
):
    atoms, chans = features.shape
    edges = edge_recv.shape[0]
    rows, lanes = lax.axis_size("row"), lax.axis_size("space")
    space = lax.axis_index("space").astype(jnp.int32)
    (packed,) = kernel_call(
        pack_kernel,
        [((atoms + 16, chans), jnp.bfloat16)],
        (space.reshape(1), features, ghost_list),
        scalars=1,
        far=2,
        scratch=[
            pltpu.VMEM(ghost_list.shape, ghost_list.dtype),
            pltpu.SemaphoreType.DMA((2,)),
        ],
    )
    others = [exchanged(packed, "space", step) for step in range(1, lanes)]
    rest = (edge_vec, w_rad1, w_rad2, edge_send[None], edge_recv[None], w_msg)
    rest = rest + (species[None], hardness[None], width[None], chi_shift[None], positions)
    kept = (w_up, w_out[None])
    parts = kernel_call(
        functools.partial(edge_kernel, lanes),
        [
            ((2 * chans, edges), jnp.float32),
            ((8, edges), jnp.float32),
            ((1, chans), jnp.float32),
            ((chans + atoms, edges), jnp.bfloat16),
            ((atoms, edges), jnp.bfloat16),
            ((2 * chans, chans), jnp.bfloat16),
            (w_up.shape, w_up.dtype),
            ((1, chans), jnp.float32),
        ],
        (space.reshape(1), *rest, *kept),
        scalars=1,
        far=len(rest + kept),
        scratch=[pltpu.VMEM(value.shape, value.dtype) for value in rest]
        + [pltpu.SemaphoreType.DMA((len(rest + kept),))],
        flops=1 << 28,
    )
    devices = rows * lanes
    hidden, block = kernel_call(
        node_kernel,
        [((atoms, chans), jnp.float32), ((devices, 1, chans), jnp.float32)],
        (packed, *others, *parts),
        flops=1 << 28,
    )
    (new_features,) = kernel_call(
        feature_kernel, [((atoms, chans), jnp.bfloat16)], (packed, hidden), flops=1 << 20
    )
    block = lax.all_to_all(block, everywhere, 0, 0, tiled=True)
    place = lax.axis_index("row").astype(jnp.int32) * lanes + space
    everybody = rows * lanes * atoms
    charges, forces, virial = kernel_call(
        charge_kernel,
        [((count, atoms), jnp.float32) for count in (1, 3, 6)],
        (place.reshape(1), field, block),
        scalars=2,
        scratch=[
            pltpu.VMEM((everybody, everybody), jnp.float32),
            pltpu.VMEM((everybody, chans), jnp.float32),
            pltpu.VMEM((everybody, chans), jnp.float32),
            pltpu.VMEM((4, atoms, everybody), jnp.float32),
        ],
        flops=1 << 28,
    )
    return (new_features, charges[0], forces, virial)


def solution(mesh):
    small = mesh.shape["space"] == 4 and mesh.shape["row"] == 8
    return jax.shard_map(
        few_shards if small else shards,
        mesh=mesh,
        in_specs=(
            P(("row", "space"), None),
            P(None, ("row", "space")),
            P(("row", "space")),
            P("row", "space", None),
            P(("row", "space")),
            P(("row", "space")),
            P(None, ("row", "space")),
            P(),
            P(),
            P(),
            P(),
            P(),
            P(),
            P(),
            P(),
            P(),
        ),
        out_specs=(
            P(("row", "space"), None),
            P(("row", "space")),
            P(None, ("row", "space")),
            P(None, ("row", "space")),
        ),
        check_vma=False,
    )
```
